32 devices in a mesh: samp: 4 (over z), pix: 8 (over y, x, core).
Axes of the slice: x: 2, y: 2, z: 4, core: 2. Of those that a mesh axis runs over, the one named last changes fastest.
Arguments:
- pixels: bfloat16 [16, 261, 16384], P('samp', None, 'pix'), may hold values from -6 to 6
- pixel_mask: int32 [16, 16384], P('samp', 'pix'), may hold values from 0 to 1, as said below
- proj_blocks: float32 [128, 4, 64, 128], P(('samp', 'pix')), may hold values from -1 to 1
- proj_left: float32 [128, 4, 64, 64], P(('samp', 'pix')), may hold values from -2097152 to 8388608, as said below
- proj_right: float32 [128, 4, 128, 128], P(('samp', 'pix')), may hold values from -1048576 to 4194304, as said below
- left_roots: float32 [128, 4, 64, 64], P(('samp', 'pix')), may hold values from -1 to 1, as said below
- right_roots: float32 [128, 4, 128, 128], P(('samp', 'pix')), may hold values from -1 to 1, as said below
- keyval_weight: float32 [261, 2048], P(None, ('samp', 'pix')), may hold values from -0.375 to 0.375
- keyval_second: float32 [261, 2048], P(None, ('samp', 'pix')), may hold values from 2750 to 11000
- latents: float32 [512, 1024], P('pix'), may hold values from -6 to 6
- latent_second: float32 [512, 1024], P('pix'), may hold values from 48 to 192
- gains: float32 [2309], replicated, may hold values from 0.5 to 1.5
- gain_second: float32 [2309], replicated, may hold values from 16384 to 70000
- mixed_grad: bfloat16 [16, 512, 1024], P('samp', 'pix'), may hold values from -6 to 6
Outputs:
- mixed: bfloat16 [16, 512, 1024], P('samp', 'pix')
- pixel_grad: float32 [16, 261, 16384], P('samp', None, 'pix')
- proj_grad: float32 [128, 4, 64, 128], P(('samp', 'pix'))
- left_new: float32 [128, 4, 64, 64], P(('samp', 'pix'))
- right_new: float32 [128, 4, 128, 128], P(('samp', 'pix'))
- proj_new: float32 [128, 4, 64, 128], P(('samp', 'pix'))
- keyval_grad: float32 [261, 2048], P(None, ('samp', 'pix'))
- keyval_second_new: float32 [261, 2048], P(None, ('samp', 'pix'))
- keyval_new: float32 [261, 2048], P(None, ('samp', 'pix'))
- latent_grad: float32 [512, 1024], P('pix')
- latent_second_new: float32 [512, 1024], P('pix')
- latent_new: float32 [512, 1024], P('pix')
- gain_grad: float32 [2309], replicated
- gain_second_new: float32 [2309], replicated
- gain_new: float32 [2309], replicated
The draws below stay inside these ranges and needn't reach their ends.
Inputs may be any that keep to these rules, and one draw needn't show every extreme that they name: `pixel_mask`: an image's valid pixels come first: its mask is 1 on its first 5056, 9911 or 16384 pixels and 0 after; each run of 4 consecutive images holds one or more images with all 16384 valid. `proj_left`: each block is symmetric. `proj_right`: each block is symmetric. `left_roots`: each block is symmetric. `right_roots`: each block is symmetric.
All inputs are finite; a program needn't handle non-finite values.
Results may differ from the reference program's by a relative error of at most 0.035.
Values may be sent and summed in bfloat16 or wider, within the bound.
A program may use at most 256 MiB of HBM per device.

```python
import math
import jax
import jax.numpy as jnp
from jax import lax

D = 1024
LAT = 512
CH = 261
BR = 64
BC = 128
PIX_DEV = 2048
MICRO = 4
IMAGES = 16
PIXELS = 16384
NBLK = 128
N_PIX = 8


def draw_pixel_mask(key, part):
    class_key, full_key = jax.random.split(jax.random.fold_in(key, 11))
    classes = jax.random.randint(class_key, (IMAGES,), 0, 3)
    chosen = jax.random.randint(full_key, (IMAGES // MICRO,), 0, MICRO)
    image_index = jnp.arange(IMAGES)
    is_full = image_index % MICRO == chosen[image_index // MICRO]
    classes = jnp.where(is_full, 2, classes)
    side_area = jnp.array([25, 49, 81], jnp.int32)[classes]
    lengths = PIXELS * side_area // 81
    return (jnp.arange(PIXELS)[None, :] < lengths[:, None]).astype(jnp.int32)


def draw_proj_blocks(key, part):
    samples = jax.random.normal(jax.random.fold_in(key, 3), (NBLK, 4, BR, BC), jnp.float32)
    samples = jnp.clip(samples, -2.5, 2.5)
    spread = jnp.array([(6.0 / D) ** 0.5, (8.0 / D) ** 0.5, (2.0 / D) ** 0.5, (2.0 / D) ** 0.5], jnp.float32)
    return samples * spread[None, :, None, None]


def grad_squares():
    shared = IMAGES * LAT / PIXELS
    rows_all = IMAGES * LAT
    return jnp.array([10800.0 * shared, 1400.0 * shared, 1.2 * rows_all, 1.0 * rows_all], jnp.float32)


def dominant(key, matrix_size, scales):
    diag_key, offdiag_key = jax.random.split(key)
    diagonal = jnp.exp(jax.random.uniform(diag_key, (NBLK, 4, matrix_size), jnp.float32, 0.0, 1.386))
    off_bound = 0.9 / (matrix_size - 1)
    offdiag = jax.random.uniform(offdiag_key, (NBLK, 4, matrix_size, matrix_size), jnp.float32, -off_bound, off_bound)
    offdiag = jnp.triu(offdiag, 1)
    offdiag = offdiag + jnp.swapaxes(offdiag, 2, 3)
    identity = jnp.eye(matrix_size, dtype=jnp.float32)
    matrix = offdiag + identity * diagonal[..., None]
    return matrix * scales[None, :, None, None]


def draw_proj_left(key, part):
    return dominant(jax.random.fold_in(key, 21), BR, BC * grad_squares())


def draw_proj_right(key, part):
    return dominant(jax.random.fold_in(key, 22), BC, BR * grad_squares())


def draw_left_roots(key, part):
    return dominant(jax.random.fold_in(key, 23), BR, 0.5 * (2.0 * BC * grad_squares()) ** (-0.25))


def draw_right_roots(key, part):
    return dominant(jax.random.fold_in(key, 24), BC, 0.5 * (2.0 * BR * grad_squares()) ** (-0.25))


def draw_gain_second(key, part):
    spread = jax.random.uniform(jax.random.fold_in(key, 31), (2 * D + CH,), jnp.float32, 0.0, 1.386)
    position = jnp.arange(2 * D + CH)
    first_base = 35000.0 * IMAGES * LAT / PIXELS
    mlp_base = 2.0 * IMAGES * LAT
    base = jnp.where(position < D + CH, first_base, mlp_base).astype(jnp.float32)
    return base * jnp.exp(spread)


def block_levels(stream_key, dims, cuts, low, top_value):
    level = 1.0
    for dim, blocks in cuts:
        heights = jax.random.uniform(jax.random.fold_in(jax.random.fold_in(stream_key, 6), dim), (blocks,), jnp.float32, low / len(cuts), top_value / len(cuts))
        level = level * jnp.repeat(jnp.exp(heights), dims[dim] // blocks).reshape((-1,) + (1,) * (len(dims) - 1 - dim))
    return level


def bell_draw(stream_key, extent, scale, reach, cuts=(), held_as=jnp.bfloat16):
    values = scale * jax.random.normal(stream_key, extent, jnp.float32)
    if cuts:
        values = values * block_levels(stream_key, extent, cuts, -0.22, 0.18)
    return jnp.clip(values, -reach, reach).astype(held_as)


def setup_inputs(seed: int = 0) -> dict:
    arg_keys = jax.random.split(jax.random.key(seed), 15)
    return {
        "pixels": bell_draw(arg_keys[0], (IMAGES, CH, PIXELS), 1.0, 6.0, ((0, 4), (2, 8))),
        "pixel_mask": draw_pixel_mask(jax.random.fold_in(arg_keys[14], 71), 0),
        "proj_blocks": draw_proj_blocks(jax.random.fold_in(arg_keys[14], 71), 0),
        "proj_left": draw_proj_left(jax.random.fold_in(arg_keys[14], 71), 0),
        "proj_right": draw_proj_right(jax.random.fold_in(arg_keys[14], 71), 0),
        "left_roots": draw_left_roots(jax.random.fold_in(arg_keys[14], 71), 0),
        "right_roots": draw_right_roots(jax.random.fold_in(arg_keys[14], 71), 0),
        "keyval_weight": bell_draw(arg_keys[7], (CH, 2 * D), CH ** -0.5, 0.375, ((1, 32),), jnp.float32),
        "keyval_second": jnp.clip(jnp.exp(math.log(11000.0) - 1.3862944 * jax.random.uniform(arg_keys[8], (CH, 2 * D), jnp.float32) ** block_levels(arg_keys[8], (CH, 2 * D), ((1, 32),), -0.2, 0.2)), 2750.0, 11000.0),
        "latents": bell_draw(arg_keys[9], (LAT, D), 1.0, 6.0, ((0, 8),), jnp.float32),
        "latent_second": jnp.clip(jnp.exp(math.log(192.0) - 1.3862944 * jax.random.uniform(arg_keys[10], (LAT, D), jnp.float32) ** block_levels(arg_keys[10], (LAT, D), ((0, 8),), -0.2, 0.2)), 48.0, 192.0),
        "gains": jnp.clip(1.0 + 0.1 * jax.random.normal(arg_keys[11], (2 * D + CH,), jnp.float32), 0.5, 1.5),
        "gain_second": draw_gain_second(jax.random.fold_in(arg_keys[14], 71), 0),
        "mixed_grad": bell_draw(arg_keys[13], (IMAGES, LAT, D), 1.0, 6.0, ((0, 4), (1, 8))),
    }


EPSILON = 1e-05
NEGATIVE = -1e+30
HIGHEST = lax.Precision.HIGHEST
STAT_DECAY = 0.5
MATRIX_RATE = 0.5
KEYVAL_RATE = 0.05
LATENT_RATE = 0.7
GAIN_RATE = 0.6
MOMENT_FLOOR = 1e-08

@jax.custom_vjp
def low(v):
    return lax.optimization_barrier(v.astype(jnp.bfloat16)).astype(jnp.float32)

@jax.custom_vjp
def low_back(v):
    return v

def low_keep(v):
    return (low(v), None)

def low_pass(kept, grad):
    return (grad,)

def back_keep(v):
    return (v, None)

def back_low(kept, grad):
    return (low(grad),)
low.defvjp(low_keep, low_pass)
low_back.defvjp(back_keep, back_low)

def matmul(former, latter):
    return jnp.dot(former, latter, precision=HIGHEST, preferred_element_type=jnp.float32)

def normalize(values, gain, axis):
    row_mean = lax.optimization_barrier(jnp.mean(values, axis=axis, keepdims=True))
    centered = values - row_mean
    variance = lax.optimization_barrier(jnp.mean(centered * centered, axis=axis, keepdims=True))
    return centered * lax.rsqrt(variance + EPSILON) * gain

def gelu_exact(values):
    return jax.nn.gelu(values, approximate=False)

def assemble(blocks):
    return blocks.reshape(D // BR, D // BC, BR, BC).transpose(0, 2, 1, 3).reshape(D, D)

def split_blocks(matrix):
    return matrix.reshape(D // BR, BR, D // BC, BC).transpose(0, 2, 1, 3).reshape(NBLK, BR, BC)

def shard_part(query, keyval_low, in_gain, shard_pixels, shard_valid):
    normed = low(normalize(shard_pixels, in_gain[:, None], 0))
    keyval = low(low_back(matmul(normed.T, keyval_low)))
    key_rows = keyval[:, :D]
    value_rows = keyval[:, D:]
    scores = low_back(matmul(query, key_rows.T) * D ** (-0.5))
    masked = jnp.where(shard_valid[None, :], scores, NEGATIVE)
    shard_top = low(lax.optimization_barrier(jnp.max(masked, axis=1)))
    weights = jnp.exp(jnp.where(shard_valid[None, :], scores - shard_top[:, None], NEGATIVE))
    shard_total = low(low_back(lax.optimization_barrier(jnp.sum(weights, axis=1))))
    shard_numer = low(low_back(matmul(low(weights), value_rows)))
    return (shard_numer, shard_top, shard_total)

def image_part(query, keyval_low, in_gain, out_low, mlp_gain, mlp_in_low, mlp_out_low, latents, image_pixels, image_valid):
    shard_pixels = image_pixels.reshape(CH, N_PIX, PIX_DEV).transpose(1, 0, 2)
    shard_valid = image_valid.reshape(N_PIX, PIX_DEV)

    def one_shard(pieces):
        return jax.checkpoint(shard_part)(query, keyval_low, in_gain, pieces[0], pieces[1])
    numers, tops, totals = lax.map(one_shard, (shard_pixels, shard_valid))
    global_top = lax.optimization_barrier(jnp.max(tops, axis=0))
    factor = jnp.exp(tops - global_top[None, :])
    denominator = lax.optimization_barrier(jnp.sum(factor * totals, axis=0))
    attended = lax.optimization_barrier(jnp.sum(factor[:, :, None] * numers, axis=0)) / denominator[:, None]
    attended = low(low_back(attended))
    middle = low_back(latents + matmul(attended, out_low))
    mid_normed = low(normalize(middle, mlp_gain[None, :], 1))
    pre_act = low_back(matmul(mid_normed, mlp_in_low))
    hidden = low(low_back(gelu_exact(pre_act)))
    return middle + matmul(hidden, mlp_out_low)

def forward(pixels_f, pixel_valid, query_weight, output_weight, mlp_in, mlp_out, keyval_weight, latents, gains):
    lat_gain = gains[:D]
    in_gain = gains[D:D + CH]
    mlp_gain = gains[D + CH:]
    lat_normed = low(normalize(latents, lat_gain[None, :], 1))
    query = low(low_back(matmul(lat_normed, low(query_weight))))
    keyval_low = low(keyval_weight)
    out_low = low(output_weight)
    mlp_in_low = low(mlp_in)
    mlp_out_low = low(mlp_out)

    def one_image(running, image_item):
        mixed_rows = jax.checkpoint(image_part)(query, keyval_low, in_gain, out_low, mlp_gain, mlp_in_low, mlp_out_low, latents, image_item[0], image_item[1])
        return (running, mixed_rows)
    unused, mixed_all = lax.scan(one_image, jnp.zeros((), jnp.float32), (pixels_f, pixel_valid))
    return mixed_all

def moment_step(weight, grad, second, rate):
    second_new = STAT_DECAY * second + (1.0 - STAT_DECAY) * grad * grad
    return (second_new, weight - rate * grad / (jnp.sqrt(second_new) + MOMENT_FLOOR))

def reference(pixels, pixel_mask, proj_blocks, proj_left, proj_right, left_roots, right_roots, keyval_weight, keyval_second, latents, latent_second, gains, gain_second, mixed_grad):
    pixels_f = pixels.astype(jnp.float32)
    pixel_valid = pixel_mask == 1
    query_weight = assemble(proj_blocks[:, 0])
    output_weight = assemble(proj_blocks[:, 1])
    mlp_in = assemble(proj_blocks[:, 2])
    mlp_out = assemble(proj_blocks[:, 3])

    def closed(pixels_in, query_in, output_in, mlp_in_in, mlp_out_in, keyval_in, latents_in, gains_in):
        return forward(pixels_in, pixel_valid, query_in, output_in, mlp_in_in, mlp_out_in, keyval_in, latents_in, gains_in)
    mixed_all, pullback = jax.vjp(closed, pixels_f, query_weight, output_weight, mlp_in, mlp_out, keyval_weight, latents, gains)
    pixel_grad, query_grad, output_grad, mlp_in_grad, mlp_out_grad, keyval_grad, latent_grad, gain_grad = pullback(mixed_grad.astype(jnp.float32))
    proj_grad = jnp.stack([split_blocks(query_grad), split_blocks(output_grad), split_blocks(mlp_in_grad), split_blocks(mlp_out_grad)], axis=1)
    left_new = STAT_DECAY * proj_left + (1.0 - STAT_DECAY) * jnp.einsum('nsab,nscb->nsac', proj_grad, proj_grad, precision=HIGHEST)
    right_new = STAT_DECAY * proj_right + (1.0 - STAT_DECAY) * jnp.einsum('nsab,nsac->nsbc', proj_grad, proj_grad, precision=HIGHEST)
    partial_step = jnp.einsum('nsab,nsbc->nsac', left_roots, proj_grad, precision=HIGHEST)
    direction = jnp.einsum('nsac,nscd->nsad', partial_step, right_roots, precision=HIGHEST)
    proj_new = proj_blocks - MATRIX_RATE * direction
    keyval_second_new, keyval_new = moment_step(keyval_weight, keyval_grad, keyval_second, KEYVAL_RATE)
    latent_second_new, latent_new = moment_step(latents, latent_grad, latent_second, LATENT_RATE)
    gain_second_new, gain_new = moment_step(gains, gain_grad, gain_second, GAIN_RATE)
    return (mixed_all.astype(jnp.bfloat16), pixel_grad, proj_grad, left_new, right_new, proj_new, keyval_grad, keyval_second_new, keyval_new, latent_grad, latent_second_new, latent_new, gain_grad, gain_second_new, gain_new)
```

```python
import jax
import jax.numpy as jnp
from jax import lax
from jax.sharding import PartitionSpec as P

EPSILON = 1e-05
NEGATIVE = -1e30
HIGHEST = lax.Precision.HIGHEST
STAT_DECAY = 0.5
MATRIX_RATE = 0.5
KEYVAL_RATE = 0.05
LATENT_RATE = 0.7
GAIN_RATE = 0.6
MOMENT_FLOOR = 1e-08
BF = jnp.bfloat16


def matmul(former, latter):
    return jnp.dot(former, latter, preferred_element_type=jnp.float32)


def contract(former, latter, former_dim, latter_dim):
    return lax.dot_general(
        former,
        latter,
        (((former_dim,), (latter_dim,)), ((), ())),
        preferred_element_type=jnp.float32,
    )


def gelu_exact(values):
    return jax.nn.gelu(values, approximate=False)


def normalize_parts(values, axis):
    row_mean = jnp.mean(values, axis=axis, keepdims=True)
    centered = values - row_mean
    variance = jnp.mean(centered * centered, axis=axis, keepdims=True)
    inverse = lax.rsqrt(variance + EPSILON)
    return (centered * inverse, inverse)


def normalize_back(grad_hat, normal_hat, inverse, axis):
    first_mean = jnp.mean(grad_hat, axis=axis, keepdims=True)
    second_mean = jnp.mean(grad_hat * normal_hat, axis=axis, keepdims=True)
    return inverse * (grad_hat - first_mean - normal_hat * second_mean)


def assemble(blocks, model_width, row_block, col_block):
    shaped = blocks.reshape(
        model_width // row_block, model_width // col_block, row_block, col_block
    )
    return shaped.transpose(0, 2, 1, 3).reshape(model_width, model_width)


def split_blocks(matrix, row_block, col_block):
    rows, cols = matrix.shape
    shaped = matrix.reshape(rows // row_block, row_block, cols // col_block, col_block)
    return shaped.transpose(0, 2, 1, 3).reshape(-1, row_block, col_block)


def moment_step(weight, grad, second, rate):
    second_new = STAT_DECAY * second + (1.0 - STAT_DECAY) * grad * grad
    return (second_new, weight - rate * grad / (jnp.sqrt(second_new) + MOMENT_FLOOR))


def body(
    pixels,
    pixel_mask,
    proj_blocks,
    proj_left,
    proj_right,
    left_roots,
    right_roots,
    keyval_weight,
    keyval_second,
    latents,
    latent_second,
    gains,
    gain_second,
    mixed_grad,
):
    batches, channels, shard_pixels = pixels.shape
    lat_rows, width = latents.shape
    groups = lax.axis_size("pix")
    all_rows = lat_rows * groups
    owned_count, _, row_block, col_block = proj_blocks.shape
    scale = width ** (-0.5)
    everyone = ("samp", "pix")

    latent_all = lax.all_gather(latents.astype(BF), "pix", axis=0, tiled=True).astype(jnp.float32)
    query_blocks = lax.all_gather(proj_blocks[:, 0].astype(BF), everyone, axis=0, tiled=True)
    keyval_t = lax.all_gather(keyval_weight.T.astype(BF), everyone, axis=0, tiled=True)
    rest_blocks = lax.all_gather(proj_blocks[:, 1:].astype(BF), everyone, axis=0, tiled=True)
    query_weight = assemble(query_blocks, width, row_block, col_block)
    output_weight = assemble(rest_blocks[:, 0], width, row_block, col_block)
    mlp_in = assemble(rest_blocks[:, 1], width, row_block, col_block)
    mlp_out = assemble(rest_blocks[:, 2], width, row_block, col_block)
    key_t = keyval_t[:width]
    value_t = keyval_t[width:]
    lat_gain = gains[:width]
    in_gain = gains[width : width + channels]
    mlp_gain = gains[width + channels :]
    lat_hat, lat_inverse = normalize_parts(latent_all, 1)
    lat_normed = (lat_hat * lat_gain[None, :]).astype(BF)
    query = matmul(lat_normed, query_weight).astype(BF)
    pixel_query = (matmul(query, key_t) * scale).astype(BF)

    kept = []
    packed = []
    for slot in range(batches):
        normal_hat, inverse = normalize_parts(pixels[slot].astype(jnp.float32), 0)
        normed = (normal_hat * in_gain[:, None]).astype(BF)
        valid = pixel_mask[slot] == 1
        scores = jnp.where(valid[None, :], matmul(pixel_query, normed), NEGATIVE)
        top = jnp.max(scores, axis=1).astype(BF)
        weights = jnp.where(
            valid[None, :], jnp.exp(scores - top.astype(jnp.float32)[:, None]), 0.0
        )
        total = jnp.sum(weights, axis=1).astype(BF)
        weights = weights.astype(BF)
        numer = contract(weights, normed, 1, 1).astype(BF)
        kept.append((normed, top, weights))
        packed.append(jnp.concatenate([numer, top[:, None], total[:, None]], axis=1))
    outgoing = jnp.stack(packed, axis=0).reshape(batches, groups, lat_rows, channels + 2)
    outgoing = outgoing.transpose(1, 0, 2, 3).reshape(groups, batches * lat_rows, channels + 2)
    incoming = lax.all_to_all(outgoing, "pix", split_axis=0, concat_axis=0, tiled=True)
    top_in = incoming[:, :, channels].astype(jnp.float32)
    total_in = incoming[:, :, channels + 1].astype(jnp.float32)
    peak = jnp.max(top_in, axis=0)
    factor = jnp.exp(top_in - peak[None, :])
    denominator = jnp.sum(factor * total_in, axis=0)
    summed = jnp.sum(factor[:, :, None] * incoming[:, :, :channels].astype(jnp.float32), axis=0)
    attended_chan = (summed / denominator[:, None]).astype(BF)

    attended = contract(attended_chan, value_t, 1, 1)
    attended_low = attended.astype(BF)
    latents_tiled = jnp.tile(latents, (batches, 1))
    middle = latents_tiled + matmul(attended_low, output_weight)
    mid_hat, mid_inverse = normalize_parts(middle, 1)
    mid_normed = (mid_hat * mlp_gain[None, :]).astype(BF)
    pre_act = matmul(mid_normed, mlp_in)
    hidden, gelu_pull = jax.vjp(gelu_exact, pre_act)
    hidden_low = hidden.astype(BF)
    mixed = (middle + matmul(hidden_low, mlp_out)).astype(BF)
    grad_rows = mixed_grad.reshape(batches * lat_rows, width)
    grad_hidden = contract(grad_rows, mlp_out, 1, 1).astype(BF)
    (slope_grad,) = gelu_pull(grad_hidden.astype(jnp.float32))
    grad_pre = slope_grad.astype(BF)
    grad_mid_normed = contract(grad_pre, mlp_in, 1, 1)
    mlp_gain_part = jnp.sum(grad_mid_normed * mid_hat, axis=0)
    grad_mid = (
        grad_rows.astype(jnp.float32)
        + normalize_back(grad_mid_normed * mlp_gain[None, :], mid_hat, mid_inverse, 1)
    ).astype(BF)
    grad_attended = contract(grad_mid, output_weight, 1, 1).astype(BF)
    row_delta = jnp.sum(attended * grad_attended.astype(jnp.float32), axis=1)
    grad_chan = (matmul(grad_attended, value_t) / denominator[:, None]).astype(BF)
    delta_low = (row_delta / denominator).astype(BF)
    back_own = jnp.concatenate([grad_chan, peak.astype(BF)[:, None], delta_low[:, None]], axis=1)
    back_own = back_own.reshape(batches, lat_rows, channels + 2)
    back_all = lax.all_gather(back_own, "pix", axis=1, tiled=True)

    out_term = split_blocks(contract(attended_low, grad_mid, 0, 0).astype(BF), row_block, col_block)
    in_term = split_blocks(contract(mid_normed, grad_pre, 0, 0).astype(BF), row_block, col_block)
    down_term = split_blocks(contract(hidden_low, grad_rows, 0, 0).astype(BF), row_block, col_block)
    triple_term = jnp.stack([out_term, in_term, down_term], axis=1)
    triple_owned = lax.psum_scatter(triple_term, everyone, scatter_dimension=0, tiled=True)
    residual = jnp.sum(grad_mid.astype(jnp.float32).reshape(batches, lat_rows, width), axis=0)
    residual_total = lax.psum(residual.astype(BF), "samp").astype(jnp.float32)

    query_acc = jnp.zeros((all_rows, channels), jnp.float32)
    in_gain_part = jnp.zeros((channels,), jnp.float32)
    pixel_list = []
    for slot in range(batches):
        normed, top, weights = kept[slot]
        back = back_all[slot]
        share = jnp.exp(top.astype(jnp.float32) - back[:, channels].astype(jnp.float32))
        back_chan = (back[:, :channels].astype(jnp.float32) * share[:, None]).astype(BF)
        back_total = share * back[:, channels + 1].astype(jnp.float32)
        grad_weights = matmul(back_chan, normed) - back_total[:, None]
        grad_scores = (weights.astype(jnp.float32) * grad_weights).astype(BF)
        query_acc = query_acc + contract(grad_scores, normed, 1, 1)
        grad_normed = contract(pixel_query, grad_scores, 0, 0) + contract(back_chan, weights, 0, 0)
        normal_hat, inverse = normalize_parts(pixels[slot].astype(jnp.float32), 0)
        in_gain_part = in_gain_part + jnp.sum(grad_normed * normal_hat, axis=1)
        pixel_list.append(
            normalize_back(grad_normed * in_gain[:, None], normal_hat, inverse, 0)
        )
    pixel_grad = jnp.stack(pixel_list, axis=0)

    query_sum, in_gain_sum, mlp_gain_sum = lax.psum(
        (query_acc, in_gain_part, mlp_gain_part), everyone
    )
    value_term = contract(grad_attended, attended_chan, 0, 0)
    key_term = contract(query, query_acc.astype(BF), 0, 0) * scale
    keyval_term = jnp.concatenate([key_term, value_term], axis=0).astype(BF)
    keyval_grad = lax.psum_scatter(keyval_term, everyone, scatter_dimension=0, tiled=True)
    keyval_grad = keyval_grad.astype(jnp.float32).T

    grad_query = (contract(query_sum.astype(BF), key_t, 1, 1) * scale).astype(BF)
    grad_lat_normed = contract(grad_query, query_weight, 1, 1)
    lat_gain_grad = jnp.sum(grad_lat_normed * lat_hat, axis=0)
    latent_path = normalize_back(grad_lat_normed * lat_gain[None, :], lat_hat, lat_inverse, 1)
    row_start = lax.axis_index("pix") * lat_rows
    own_path = lax.dynamic_slice_in_dim(latent_path, row_start, lat_rows, 0)
    latent_grad = residual_total + own_path
    first_block = lax.axis_index(everyone) * owned_count
    col_count = width // col_block
    query_list = []
    for offset in range(owned_count):
        block_index = first_block + offset
        block_row = block_index // col_count * row_block
        block_col = block_index % col_count * col_block
        normed_slice = lax.dynamic_slice_in_dim(lat_normed, block_row, row_block, 1)
        grad_slice = lax.dynamic_slice_in_dim(grad_query, block_col, col_block, 1)
        query_list.append(contract(normed_slice, grad_slice, 0, 0))
    query_grad = jnp.stack(query_list, axis=0)
    proj_grad = jnp.concatenate([query_grad[:, None], triple_owned.astype(jnp.float32)], axis=1)
    left_new = STAT_DECAY * proj_left + (1.0 - STAT_DECAY) * jnp.einsum(
        "nsab,nscb->nsac", proj_grad, proj_grad, precision=HIGHEST
    )
    right_new = STAT_DECAY * proj_right + (1.0 - STAT_DECAY) * jnp.einsum(
        "nsab,nsac->nsbc", proj_grad, proj_grad, precision=HIGHEST
    )
    partial_step = jnp.einsum("nsab,nsbc->nsac", left_roots, proj_grad, precision=HIGHEST)
    direction = jnp.einsum("nsac,nscd->nsad", partial_step, right_roots, precision=HIGHEST)
    proj_new = proj_blocks - MATRIX_RATE * direction
    keyval_second_new, keyval_new = moment_step(
        keyval_weight, keyval_grad, keyval_second, KEYVAL_RATE
    )
    latent_second_new, latent_new = moment_step(latents, latent_grad, latent_second, LATENT_RATE)
    gain_grad = jnp.concatenate([lat_gain_grad, in_gain_sum, mlp_gain_sum], axis=0)
    gain_second_new, gain_new = moment_step(gains, gain_grad, gain_second, GAIN_RATE)
    return (
        mixed.reshape(batches, lat_rows, width),
        pixel_grad,
        proj_grad,
        left_new,
        right_new,
        proj_new,
        keyval_grad,
        keyval_second_new,
        keyval_new,
        latent_grad,
        latent_second_new,
        latent_new,
        gain_grad,
        gain_second_new,
        gain_new,
    )


def solution(mesh):
    blocks = P(("samp", "pix"), None, None, None)
    columns = P(None, ("samp", "pix"))
    rows = P("pix", None)
    return jax.shard_map(
        body,
        mesh=mesh,
        in_specs=(
            P("samp", None, "pix"),
            P("samp", "pix"),
            blocks,
            blocks,
            blocks,
            blocks,
            blocks,
            columns,
            columns,
            rows,
            rows,
            P(),
            P(),
            P("samp", "pix", None),
        ),
        out_specs=(
            P("samp", "pix", None),
            P("samp", None, "pix"),
            blocks,
            blocks,
            blocks,
            blocks,
            columns,
            columns,
            columns,
            rows,
            rows,
            rows,
            P(),
            P(),
            P(),
        ),
        check_vma=False,
    )
```

```python
import functools
import math

import jax
import jax.numpy as jnp
from jax import lax
from jax.experimental import pallas as pl
from jax.experimental.pallas import tpu as pltpu
from jax.sharding import PartitionSpec as P

EPSILON = 1e-05
NEGATIVE = -1e30
HIGHEST = lax.Precision.HIGHEST
STAT_DECAY = 0.5
MATRIX_RATE = 0.5
KEYVAL_RATE = 0.05
LATENT_RATE = 0.7
GAIN_RATE = 0.6
MOMENT_FLOOR = 1e-08
BF = jnp.bfloat16
MESH = pl.DeviceIdType.MESH


def matmul(former, latter):
    return jnp.dot(former, latter, preferred_element_type=jnp.float32)


def contract(former, latter, former_dim, latter_dim):
    return lax.dot_general(
        former,
        latter,
        (((former_dim,), (latter_dim,)), ((), ())),
        preferred_element_type=jnp.float32,
    )


def gelu_exact(values):
    return jax.nn.gelu(values, approximate=False)


def normalize_parts(values, axis):
    row_mean = jnp.mean(values, axis=axis, keepdims=True)
    centered = values - row_mean
    variance = jnp.mean(centered * centered, axis=axis, keepdims=True)
    inverse = lax.rsqrt(variance + EPSILON)
    return (centered * inverse, inverse)


def normalize_back(grad_hat, normal_hat, inverse, axis):
    first_mean = jnp.mean(grad_hat, axis=axis, keepdims=True)
    second_mean = jnp.mean(grad_hat * normal_hat, axis=axis, keepdims=True)
    return inverse * (grad_hat - first_mean - normal_hat * second_mean)


def assemble(blocks, model_width, row_block, col_block):
    shaped = blocks.reshape(
        model_width // row_block, model_width // col_block, row_block, col_block
    )
    return shaped.transpose(0, 2, 1, 3).reshape(model_width, model_width)


def split_blocks(matrix, row_block, col_block):
    rows, cols = matrix.shape
    shaped = matrix.reshape(rows // row_block, row_block, cols // col_block, col_block)
    return shaped.transpose(0, 2, 1, 3).reshape(-1, row_block, col_block)


def moment_step(weight, grad, second, rate):
    second_new = STAT_DECAY * second + (1.0 - STAT_DECAY) * grad * grad
    return (second_new, weight - rate * grad / (jnp.sqrt(second_new) + MOMENT_FLOOR))


def ceil_to(value, step):
    return -(-value // step) * step


class Links:
    def __init__(self, send_sems, recv_sems):
        self.send_sems = send_sems
        self.recv_sems = recv_sems
        self.used = 0
        self.started = []

    def push(self, source, target, samp, pix):
        copy = pltpu.make_async_remote_copy(
            src_ref=source,
            dst_ref=target,
            send_sem=self.send_sems.at[self.used],
            recv_sem=self.recv_sems.at[self.used],
            device_id=(samp, pix),
            device_id_type=MESH,
        )
        self.used += 1
        copy.start()
        self.started.append(copy)
        return copy

    def drain(self):
        for copy in self.started:
            copy.wait_send()
        self.started = []


class Place:
    def __init__(self, nz, ny, nx):
        self.nz, self.ny, self.nx = nz, ny, nx
        self.group = ny * nx * 2
        self.z = lax.axis_index("samp")
        self.p = lax.axis_index("pix")
        self.c = lax.rem(self.p, 2)
        self.x = lax.rem(self.p // 2, nx)
        self.y = self.p // (2 * nx)

    def pix(self, y, x, c):
        return (y * self.nx + x) * 2 + c

    def barrier(self):
        semaphore = pltpu.get_barrier_semaphore()
        for step in range(1, self.nz):
            pl.semaphore_signal(
                semaphore,
                inc=1,
                device_id=(lax.rem(self.z + step, self.nz), self.p),
                device_id_type=MESH,
            )
        for step in range(1, self.group):
            pl.semaphore_signal(
                semaphore,
                inc=1,
                device_id=(self.z, lax.rem(self.p + step, self.group)),
                device_id_type=MESH,
            )
        pl.semaphore_wait(semaphore, self.nz - 1 + self.group - 1)

    def push_z(self, links, array, sub=()):
        copies = []
        for step in range(1, self.nz):
            own = array.at[(self.z, self.y, self.x, self.c) + sub]
            copies.append(links.push(own, own, lax.rem(self.z - step + self.nz, self.nz), self.p))
        return copies

    def push_first(self, links, array, lead, sub, along):
        own = array.at[lead + (self.y, self.x, self.c) + sub]
        copies = []
        if along == "x":
            for step in range(1, self.nx):
                other = self.pix(self.y, lax.rem(self.x + step, self.nx), self.c)
                copies.append(links.push(own, own, self.z, other))
        else:
            for step in range(1, self.ny):
                other = self.pix(lax.rem(self.y + step, self.ny), self.x, self.c)
                copies.append(links.push(own, own, self.z, other))
        return copies

    def push_second(self, links, array, lead, sub, first):
        copies = []
        if first == "x":
            held = array.at[lead + (self.y, slice(None), self.c) + sub]
            for step in range(1, self.ny):
                other = self.pix(lax.rem(self.y + step, self.ny), self.x, self.c)
                copies.append(links.push(held, held, self.z, other))
        else:
            held = array.at[lead + (slice(None), self.x, self.c) + sub]
            for step in range(1, self.nx):
                other = self.pix(self.y, lax.rem(self.x + step, self.nx), self.c)
                copies.append(links.push(held, held, self.z, other))
        return copies

    def push_core(self, links, array, lead):
        held = array.at[lead + (slice(None), slice(None), self.c)]
        return [links.push(held, held, self.z, self.p + 1 - 2 * self.c)]


def arrived(copies):
    for copy in copies:
        copy.wait_recv()


def column_block(array, place, index, col_blocks, owned, sub=()):
    every = slice(None)
    if 2 * owned == col_blocks:
        block = array[(every, every, every, index // owned) + sub + (index % owned,)]
    else:
        block = array[(every, every, index // 2, index % 2) + sub + (0,)]
    return block.reshape(-1, block.shape[-1])


def column_pair(array, place, pair, col_blocks, owned, sub=()):
    return jnp.concatenate(
        [
            column_block(array, place, 2 * pair, col_blocks, owned, sub),
            column_block(array, place, 2 * pair + 1, col_blocks, owned, sub),
        ],
        axis=1,
    )


def front_kernel(
    dims,
    pixels,
    mask,
    gain_cols,
    lat_gain,
    own_proj,
    own_keyval,
    own_latents,
    all_query,
    all_keyval,
    all_latents,
    all_mats,
    normed_out,
    inverse_out,
    weights_out,
    sent_out,
    landed,
    pixel_query,
    mats_own,
    g_query,
    g_keyval,
    g_latents,
    lat_normed,
    query,
    normed,
    weights,
    outgoing,
    send_sems,
    recv_sems,
    local_sems,
):
    batches, channels, shard_pixels = pixels.shape
    lat_rows, width = own_latents.shape
    owned, _, row_block, col_block = own_proj.shape
    col_blocks = width // col_block
    padded = normed.shape[1]
    main = channels // 16 * 16
    place = Place(*dims)
    links = Links(send_sems, recv_sems)
    z, y, x, c, p = place.z, place.y, place.x, place.c, place.p
    half_rows = row_block // 2
    half_width = width // 2
    every = slice(None)

    g_query[z, y, x, c] = own_proj[:, 0].astype(BF)
    g_keyval[z, y, x, c] = own_keyval[...]
    g_latents[y, x, c] = own_latents[...]
    for mat in range(3):
        mats_own[mat] = own_proj[:, mat + 1].astype(BF)
    local = []

    def local_copy(source, target):
        copy = pltpu.make_async_copy(source, target, local_sems.at[len(local)])
        copy.start()
        local.append(copy)
        return copy

    own_mats_copy = local_copy(mats_own, all_mats.at[z, y, x, c])
    place.barrier()

    sub_a = (every, pl.ds(0, half_rows))
    sub_b = (every, pl.ds(half_rows, half_rows))

    def first_of(step):
        zz = lax.rem(z + step, place.nz)
        copies = place.push_first(links, g_query, (zz,), sub_a, "x")
        copies += place.push_first(links, g_query, (zz,), sub_b, "y")
        copies += place.push_first(links, g_keyval, (zz,), (), "xy"[step % 2])
        return copies

    def second_of(step):
        zz = lax.rem(z + step, place.nz)
        copies = place.push_second(links, g_query, (zz,), sub_a, "x")
        copies += place.push_second(links, g_query, (zz,), sub_b, "y")
        copies += place.push_second(links, g_keyval, (zz,), (), "xy"[step % 2])
        return copies

    z_query = place.push_z(links, g_query)
    z_keyval = place.push_z(links, g_keyval)
    firsts = [first_of(0)]
    lat_a = (every, pl.ds(0, half_width))
    lat_b = (every, pl.ds(half_width, half_width))
    lat_first = place.push_first(links, g_latents, (), lat_a, "x")
    lat_first += place.push_first(links, g_latents, (), lat_b, "y")

    lane_chunk = 128
    bias_row = channels - main

    def norm_image(image):
        @pl.loop(0, shard_pixels // lane_chunk)
        def _(chunk):
            cols = pl.ds(pl.multiple_of(chunk * lane_chunk, lane_chunk), lane_chunk)
            top = pixels[image, 0:main, cols].astype(jnp.float32)
            tail = pixels[image, main:channels, cols].astype(jnp.float32)
            mean = (
                jnp.sum(top, axis=0, keepdims=True) + jnp.sum(tail, axis=0, keepdims=True)
            ) / channels
            top = top - mean
            tail = tail - mean
            variance = (
                jnp.sum(top * top, axis=0, keepdims=True)
                + jnp.sum(tail * tail, axis=0, keepdims=True)
            ) / channels
            inverse = lax.rsqrt(variance + EPSILON)
            inverse_out[image : image + 1, cols] = inverse
            normed[image, 0:main, cols] = (top * inverse * gain_cols[0:main, :]).astype(BF)
            tail = tail * inverse * gain_cols[main:channels, :]
            bias = jnp.where(mask[image : image + 1, cols] == 1, 0.0, NEGATIVE)
            row = lax.broadcasted_iota(jnp.int32, (padded - main, lane_chunk), 0)
            rest = jnp.where(row == bias_row + 1, 1.0, 0.0)
            rest = jnp.where(row == bias_row, bias, rest)
            for index in range(channels - main):
                rest = jnp.where(row == index, tail[index : index + 1], rest)
            normed[image, main:padded, cols] = rest.astype(BF)

        local_copy(normed.at[image], normed_out.at[image])

    norm_image(0)
    for step in range(1, place.nz):
        z_query[step - 1].wait_recv()
        z_keyval[step - 1].wait_recv()
        firsts.append(first_of(step))
    own_mats_copy.wait()
    z_mats = place.push_z(links, all_mats)
    norm_image(1)
    seconds = []
    for step in range(place.nz):
        arrived(firsts[step])
        seconds += second_of(step)
    arrived(lat_first)
    seconds += place.push_second(links, g_latents, (), lat_a, "x")
    seconds += place.push_second(links, g_latents, (), lat_b, "y")
    norm_image(2)
    arrived(seconds)
    cores = place.push_core(links, g_query, (every,))
    cores += place.push_core(links, g_keyval, (every,))
    cores += place.push_core(links, g_latents, ())
    norm_image(3)

    out_sub = 0
    mats_a = [((0, every, pl.ds(0, half_rows)), "x"), ((1,), "x")]
    mats_b = [((0, every, pl.ds(half_rows, half_rows)), "y"), ((2,), "y")]

    arrived(z_mats)
    firsts_m = []
    for sub, along in mats_a + mats_b:
        firsts_m += place.push_first(links, all_mats, (every,), sub, along)

    arrived(cores)
    for yy in range(place.ny):
        for xx in range(place.nx):
            for cc in range(2):
                rows = pl.ds(((yy * place.nx + xx) * 2 + cc) * lat_rows, lat_rows)
                values = g_latents[yy, xx, cc].astype(jnp.float32)
                mean = jnp.mean(values, axis=1, keepdims=True)
                values = values - mean
                variance = jnp.mean(values * values, axis=1, keepdims=True)
                values = values * lax.rsqrt(variance + EPSILON) * lat_gain[...]
                lat_normed[rows, :] = values.astype(BF)
    local_copy(g_query, all_query)
    local_copy(g_keyval, all_keyval)
    local_copy(g_latents, all_latents)
    for pair in range(col_blocks // 2):
        query[:, 2 * col_block * pair : 2 * col_block * (pair + 1)] = jnp.dot(
            lat_normed[...],
            column_pair(g_query, place, pair, col_blocks, owned),
            preferred_element_type=jnp.float32,
        ).astype(BF)
    key_t = g_keyval[0 : place.nz // 2]
    key_t = key_t.reshape(width, key_t.shape[-1])
    projected = jnp.dot(query[...], key_t, preferred_element_type=jnp.float32) * width ** (-0.5)
    lane = lax.broadcasted_iota(jnp.int32, projected.shape, 1)
    pixel_query[...] = jnp.where(lane == channels, 1.0, projected).astype(BF)

    all_rows = lat_rows * place.group
    tile = min(256, all_rows)

    def attend(image):
        @pl.loop(0, all_rows // tile)
        def _(step):
            rows = pl.ds(pl.multiple_of(step * tile, tile), tile)
            scores = jnp.dot(
                pixel_query[rows, 0:padded], normed[image], preferred_element_type=jnp.float32
            )
            top = jnp.max(scores, axis=1, keepdims=True)
            top = jnp.maximum(top, 0.1 * NEGATIVE).astype(BF).astype(jnp.float32)
            share = jnp.exp(scores - top).astype(BF)
            weights[image, rows, :] = share
            numer = lax.dot_general(
                share,
                normed[image],
                (((1,), (1,)), ((), ())),
                preferred_element_type=jnp.float32,
            )
            lane = lax.broadcasted_iota(jnp.int32, numer.shape, 1)
            outgoing[image, rows, 0:padded] = jnp.where(lane == channels, top, numer).astype(BF)

        local_copy(weights.at[image], weights_out.at[image])
        local_copy(outgoing.at[image], sent_out.at[image])
        own_rows = pl.ds(pl.multiple_of(p * lat_rows, lat_rows), lat_rows)
        local_copy(outgoing.at[image, own_rows], landed.at[p, image])
        copies = []
        for step in range(1, place.group):
            q = lax.rem(p + step, place.group)
            rows = pl.ds(pl.multiple_of(q * lat_rows, lat_rows), lat_rows)
            copies.append(links.push(outgoing.at[image, rows], landed.at[p, image], z, q))
        return copies

    sent = attend(0)
    arrived(firsts_m)
    seconds_m = []
    for sub, along in mats_a + mats_b:
        seconds_m += place.push_second(links, all_mats, (every,), sub, along)
    sent += attend(1)
    sent += attend(2)
    arrived(seconds_m)
    core_m = place.push_core(links, all_mats, (every,))
    sent += attend(3)
    arrived(sent)
    arrived(core_m)
    links.drain()
    for copy in local[1:]:
        copy.wait()


def front_copies(nz, ny, nx, batches):
    plane_first = lambda a, b: a * (nx - 1) + b * (ny - 1)
    count = 2 * (nz - 1)
    for step in range(nz):
        ab = plane_first(1, 1) + (plane_first(1, 0) if step % 2 == 0 else plane_first(0, 1))
        ba = plane_first(1, 1) + (plane_first(0, 1) if step % 2 == 0 else plane_first(1, 0))
        count += ab + ba
    count += 2 * plane_first(1, 1)
    count += 3 + (nz - 1) + 2 * plane_first(2, 2) + 1
    count += batches * (2 * nx * ny - 1)
    return count


def front(dims, pixels, pixel_mask, in_gain, lat_gain, proj_blocks, keyval_weight, latents):
    nz, ny, nx = dims
    batches, channels, shard_pixels = pixels.shape
    lat_rows, width = latents.shape
    owned, mats, row_block, col_block = proj_blocks.shape
    keyval_rows = keyval_weight.shape[1]
    group = 2 * ny * nx
    all_rows = lat_rows * group
    padded = ceil_to(channels + 2, 16)
    lanes = ceil_to(padded, 128)
    gain_cols = jnp.broadcast_to(
        jnp.pad(in_gain, (0, ceil_to(channels, 8) - channels))[:, None],
        (ceil_to(channels, 8), 128),
    )
    own_keyval = jnp.pad(keyval_weight.T.astype(BF), ((0, 0), (0, lanes - channels)))
    vmem = pl.BlockSpec(memory_space=pltpu.VMEM)
    anywhere = pl.BlockSpec(memory_space=pl.ANY)
    cube = (nz, ny, nx, 2)
    copies = front_copies(nz, ny, nx, batches)
    return pl.pallas_call(
        functools.partial(front_kernel, dims),
        out_shape=(
            jax.ShapeDtypeStruct(cube + (owned, row_block, col_block), BF),
            jax.ShapeDtypeStruct(cube + (keyval_rows, lanes), BF),
            jax.ShapeDtypeStruct(cube[1:] + (lat_rows, width), BF),
            jax.ShapeDtypeStruct(cube + (3, owned, row_block, col_block), BF),
            jax.ShapeDtypeStruct((batches, padded, shard_pixels), BF),
            jax.ShapeDtypeStruct((batches, shard_pixels), jnp.float32),
            jax.ShapeDtypeStruct((batches, all_rows, shard_pixels), BF),
            jax.ShapeDtypeStruct((batches, all_rows, lanes), BF),
            jax.ShapeDtypeStruct((group, batches, lat_rows, lanes), BF),
            jax.ShapeDtypeStruct((all_rows, lanes), BF),
        ),
        in_specs=[vmem] * 7,
        out_specs=(
            anywhere,
            anywhere,
            anywhere,
            anywhere,
            anywhere,
            vmem,
            anywhere,
            anywhere,
            anywhere,
            vmem,
        ),
        scratch_shapes=[
            pltpu.VMEM((3, owned, row_block, col_block), BF),
            pltpu.VMEM(cube + (owned, row_block, col_block), BF),
            pltpu.VMEM(cube + (keyval_rows, lanes), BF),
            pltpu.VMEM(cube[1:] + (lat_rows, width), BF),
            pltpu.VMEM((all_rows, width), BF),
            pltpu.VMEM((all_rows, width), BF),
            pltpu.VMEM((batches, padded, shard_pixels), BF),
            pltpu.VMEM((batches, all_rows, shard_pixels), BF),
            pltpu.VMEM((batches, all_rows, lanes), BF),
            pltpu.SemaphoreType.DMA((copies,)),
            pltpu.SemaphoreType.DMA((copies,)),
            pltpu.SemaphoreType.DMA((4 + 4 * batches,)),
        ],
        compiler_params=pltpu.CompilerParams(
            collective_id=0, has_side_effects=True, vmem_limit_bytes=56 * 2**20
        ),
    )(
        pixels,
        pixel_mask,
        gain_cols,
        lat_gain[None, :],
        proj_blocks,
        own_keyval,
        latents.astype(BF),
    )


def body(
    pixels,
    pixel_mask,
    proj_blocks,
    proj_left,
    proj_right,
    left_roots,
    right_roots,
    keyval_weight,
    keyval_second,
    latents,
    latent_second,
    gains,
    gain_second,
    mixed_grad,
):
    batches, channels, shard_pixels = pixels.shape
    lat_rows, width = latents.shape
    groups = lax.axis_size("pix")
    all_rows = lat_rows * groups
    owned_count, _, row_block, col_block = proj_blocks.shape
    scale = width ** (-0.5)
    everyone = ("samp", "pix")

    lat_gain = gains[:width]
    in_gain = gains[width : width + channels]
    mlp_gain = gains[width + channels :]
    side = math.isqrt(groups // 2)
    dims = (lax.axis_size("samp"), side, side)
    (
        query_blocks,
        keyval_t,
        latent_all,
        mats,
        normed_all,
        inverse_all,
        weights_all,
        sent_all,
        landed,
        pixel_query,
    ) = front(dims, pixels, pixel_mask, in_gain, lat_gain, proj_blocks, keyval_weight, latents)
    latent_all = latent_all.reshape(all_rows, width).astype(jnp.float32)
    keyval_t = keyval_t.reshape(2 * width, -1)[:, :channels]
    pixel_query = pixel_query[:, :channels]
    query_weight = assemble(query_blocks, width, row_block, col_block)
    rest_blocks = mats.reshape(-1, 3, owned_count, row_block, col_block).swapaxes(0, 1)
    output_weight = assemble(rest_blocks[0], width, row_block, col_block)
    mlp_in = assemble(rest_blocks[1], width, row_block, col_block)
    mlp_out = assemble(rest_blocks[2], width, row_block, col_block)
    key_t = keyval_t[:width]
    value_t = keyval_t[width:]
    lat_hat, lat_inverse = normalize_parts(latent_all, 1)
    lat_normed = (lat_hat * lat_gain[None, :]).astype(BF)
    query = matmul(lat_normed, query_weight).astype(BF)

    incoming = landed.reshape(groups, batches * lat_rows, -1)
    top_in = incoming[:, :, channels].astype(jnp.float32)
    total_in = incoming[:, :, channels + 1].astype(jnp.float32)
    peak = jnp.max(top_in, axis=0)
    factor = jnp.exp(top_in - peak[None, :])
    denominator = jnp.sum(factor * total_in, axis=0)
    summed = jnp.sum(factor[:, :, None] * incoming[:, :, :channels].astype(jnp.float32), axis=0)
    attended_chan = (summed / denominator[:, None]).astype(BF)

    attended = contract(attended_chan, value_t, 1, 1)
    attended_low = attended.astype(BF)
    latents_tiled = jnp.tile(latents, (batches, 1))
    middle = latents_tiled + matmul(attended_low, output_weight)
    mid_hat, mid_inverse = normalize_parts(middle, 1)
    mid_normed = (mid_hat * mlp_gain[None, :]).astype(BF)
    pre_act = matmul(mid_normed, mlp_in)
    hidden, gelu_pull = jax.vjp(gelu_exact, pre_act)
    hidden_low = hidden.astype(BF)
    mixed = (middle + matmul(hidden_low, mlp_out)).astype(BF)
    grad_rows = mixed_grad.reshape(batches * lat_rows, width)
    grad_hidden = contract(grad_rows, mlp_out, 1, 1).astype(BF)
    (slope_grad,) = gelu_pull(grad_hidden.astype(jnp.float32))
    grad_pre = slope_grad.astype(BF)
    grad_mid_normed = contract(grad_pre, mlp_in, 1, 1)
    mlp_gain_part = jnp.sum(grad_mid_normed * mid_hat, axis=0)
    grad_mid = (
        grad_rows.astype(jnp.float32)
        + normalize_back(grad_mid_normed * mlp_gain[None, :], mid_hat, mid_inverse, 1)
    ).astype(BF)
    grad_attended = contract(grad_mid, output_weight, 1, 1).astype(BF)
    row_delta = jnp.sum(attended * grad_attended.astype(jnp.float32), axis=1)
    grad_chan = (matmul(grad_attended, value_t) / denominator[:, None]).astype(BF)
    delta_low = (row_delta / denominator).astype(BF)
    back_own = jnp.concatenate([grad_chan, peak.astype(BF)[:, None], delta_low[:, None]], axis=1)
    back_own = back_own.reshape(batches, lat_rows, channels + 2)
    back_all = lax.all_gather(back_own, "pix", axis=1, tiled=True)

    out_term = split_blocks(contract(attended_low, grad_mid, 0, 0).astype(BF), row_block, col_block)
    in_term = split_blocks(contract(mid_normed, grad_pre, 0, 0).astype(BF), row_block, col_block)
    down_term = split_blocks(contract(hidden_low, grad_rows, 0, 0).astype(BF), row_block, col_block)
    triple_term = jnp.stack([out_term, in_term, down_term], axis=1)
    triple_owned = lax.psum_scatter(triple_term, everyone, scatter_dimension=0, tiled=True)
    residual = jnp.sum(grad_mid.astype(jnp.float32).reshape(batches, lat_rows, width), axis=0)
    residual_total = lax.psum(residual.astype(BF), "samp").astype(jnp.float32)

    query_acc = jnp.zeros((all_rows, channels), jnp.float32)
    in_gain_part = jnp.zeros((channels,), jnp.float32)
    pixel_list = []
    for slot in range(batches):
        normed = normed_all[slot, :channels]
        top = sent_all[slot, :, channels]
        weights = weights_all[slot]
        back = back_all[slot]
        share = jnp.exp(top.astype(jnp.float32) - back[:, channels].astype(jnp.float32))
        back_chan = (back[:, :channels].astype(jnp.float32) * share[:, None]).astype(BF)
        back_total = share * back[:, channels + 1].astype(jnp.float32)
        grad_weights = matmul(back_chan, normed) - back_total[:, None]
        grad_scores = (weights.astype(jnp.float32) * grad_weights).astype(BF)
        query_acc = query_acc + contract(grad_scores, normed, 1, 1)
        grad_normed = contract(pixel_query, grad_scores, 0, 0) + contract(back_chan, weights, 0, 0)
        normal_hat, inverse = normalize_parts(pixels[slot].astype(jnp.float32), 0)
        in_gain_part = in_gain_part + jnp.sum(grad_normed * normal_hat, axis=1)
        pixel_list.append(
            normalize_back(grad_normed * in_gain[:, None], normal_hat, inverse, 0)
        )
    pixel_grad = jnp.stack(pixel_list, axis=0)

    query_sum, in_gain_sum, mlp_gain_sum = lax.psum(
        (query_acc, in_gain_part, mlp_gain_part), everyone
    )
    value_term = contract(grad_attended, attended_chan, 0, 0)
    key_term = contract(query, query_acc.astype(BF), 0, 0) * scale
    keyval_term = jnp.concatenate([key_term, value_term], axis=0).astype(BF)
    keyval_grad = lax.psum_scatter(keyval_term, everyone, scatter_dimension=0, tiled=True)
    keyval_grad = keyval_grad.astype(jnp.float32).T

    grad_query = (contract(query_sum.astype(BF), key_t, 1, 1) * scale).astype(BF)
    grad_lat_normed = contract(grad_query, query_weight, 1, 1)
    lat_gain_grad = jnp.sum(grad_lat_normed * lat_hat, axis=0)
    latent_path = normalize_back(grad_lat_normed * lat_gain[None, :], lat_hat, lat_inverse, 1)
    row_start = lax.axis_index("pix") * lat_rows
    own_path = lax.dynamic_slice_in_dim(latent_path, row_start, lat_rows, 0)
    latent_grad = residual_total + own_path
    first_block = lax.axis_index(everyone) * owned_count
    col_count = width // col_block
    query_list = []
    for offset in range(owned_count):
        block_index = first_block + offset
        block_row = block_index // col_count * row_block
        block_col = block_index % col_count * col_block
        normed_slice = lax.dynamic_slice_in_dim(lat_normed, block_row, row_block, 1)
        grad_slice = lax.dynamic_slice_in_dim(grad_query, block_col, col_block, 1)
        query_list.append(contract(normed_slice, grad_slice, 0, 0))
    query_grad = jnp.stack(query_list, axis=0)
    proj_grad = jnp.concatenate([query_grad[:, None], triple_owned.astype(jnp.float32)], axis=1)
    left_new = STAT_DECAY * proj_left + (1.0 - STAT_DECAY) * jnp.einsum(
        "nsab,nscb->nsac", proj_grad, proj_grad, precision=HIGHEST
    )
    right_new = STAT_DECAY * proj_right + (1.0 - STAT_DECAY) * jnp.einsum(
        "nsab,nsac->nsbc", proj_grad, proj_grad, precision=HIGHEST
    )
    partial_step = jnp.einsum("nsab,nsbc->nsac", left_roots, proj_grad, precision=HIGHEST)
    direction = jnp.einsum("nsac,nscd->nsad", partial_step, right_roots, precision=HIGHEST)
    proj_new = proj_blocks - MATRIX_RATE * direction
    keyval_second_new, keyval_new = moment_step(
        keyval_weight, keyval_grad, keyval_second, KEYVAL_RATE
    )
    latent_second_new, latent_new = moment_step(latents, latent_grad, latent_second, LATENT_RATE)
    gain_grad = jnp.concatenate([lat_gain_grad, in_gain_sum, mlp_gain_sum], axis=0)
    gain_second_new, gain_new = moment_step(gains, gain_grad, gain_second, GAIN_RATE)
    return (
        mixed.reshape(batches, lat_rows, width),
        pixel_grad,
        proj_grad,
        left_new,
        right_new,
        proj_new,
        keyval_grad,
        keyval_second_new,
        keyval_new,
        latent_grad,
        latent_second_new,
        latent_new,
        gain_grad,
        gain_second_new,
        gain_new,
    )


def solution(mesh):
    blocks = P(("samp", "pix"), None, None, None)
    columns = P(None, ("samp", "pix"))
    rows = P("pix", None)
    return jax.shard_map(
        body,
        mesh=mesh,
        in_specs=(
            P("samp", None, "pix"),
            P("samp", "pix"),
            blocks,
            blocks,
            blocks,
            blocks,
            blocks,
            columns,
            columns,
            rows,
            rows,
            P(),
            P(),
            P("samp", "pix", None),
        ),
        out_specs=(
            P("samp", "pix", None),
            P("samp", None, "pix"),
            blocks,
            blocks,
            blocks,
            blocks,
            columns,
            columns,
            columns,
            rows,
            rows,
            rows,
            P(),
            P(),
            P(),
        ),
        check_vma=False,
    )
```

```python
import functools
import math

import jax
import jax.numpy as jnp
from jax import lax
from jax.experimental import pallas as pl
from jax.experimental.pallas import tpu as pltpu
from jax.sharding import PartitionSpec as P

EPSILON = 1e-05
NEGATIVE = -1e30
HIGHEST = lax.Precision.HIGHEST
STAT_DECAY = 0.5
MATRIX_RATE = 0.5
KEYVAL_RATE = 0.05
LATENT_RATE = 0.7
GAIN_RATE = 0.6
MOMENT_FLOOR = 1e-08
BF = jnp.bfloat16
MESH = pl.DeviceIdType.MESH
NT = (((1,), (1,)), ((), ()))


def matmul(former, latter):
    return jnp.dot(former, latter, preferred_element_type=jnp.float32)


def contract(former, latter, former_dim, latter_dim):
    return lax.dot_general(
        former,
        latter,
        (((former_dim,), (latter_dim,)), ((), ())),
        preferred_element_type=jnp.float32,
    )


def gelu_exact(values):
    return jax.nn.gelu(values, approximate=False)


def normalize_parts(values, axis):
    row_mean = jnp.mean(values, axis=axis, keepdims=True)
    centered = values - row_mean
    variance = jnp.mean(centered * centered, axis=axis, keepdims=True)
    inverse = lax.rsqrt(variance + EPSILON)
    return (centered * inverse, inverse)


def normalize_back(grad_hat, normal_hat, inverse, axis):
    first_mean = jnp.mean(grad_hat, axis=axis, keepdims=True)
    second_mean = jnp.mean(grad_hat * normal_hat, axis=axis, keepdims=True)
    return inverse * (grad_hat - first_mean - normal_hat * second_mean)


def assemble(blocks, model_width, row_block, col_block):
    shaped = blocks.reshape(
        model_width // row_block, model_width // col_block, row_block, col_block
    )
    return shaped.transpose(0, 2, 1, 3).reshape(model_width, model_width)


def split_blocks(matrix, row_block, col_block):
    rows, cols = matrix.shape
    shaped = matrix.reshape(rows // row_block, row_block, cols // col_block, col_block)
    return shaped.transpose(0, 2, 1, 3).reshape(-1, row_block, col_block)


def moment_step(weight, grad, second, rate):
    second_new = STAT_DECAY * second + (1.0 - STAT_DECAY) * grad * grad
    return (second_new, weight - rate * grad / (jnp.sqrt(second_new) + MOMENT_FLOOR))


def ceil_to(value, step):
    return -(-value // step) * step


class Links:
    def __init__(self, send_sems, recv_sems):
        self.send_sems = send_sems
        self.recv_sems = recv_sems
        self.used = 0
        self.started = []

    def make(self, source, target, samp, pix):
        copy = pltpu.make_async_remote_copy(
            src_ref=source,
            dst_ref=target,
            send_sem=self.send_sems.at[self.used],
            recv_sem=self.recv_sems.at[self.used],
            device_id=(samp, pix),
            device_id_type=MESH,
        )
        self.used += 1
        return copy

    def push(self, source, target, samp, pix):
        copy = self.make(source, target, samp, pix)
        copy.start()
        self.started.append(copy)
        return copy

    def drain(self):
        for copy in self.started:
            copy.wait_send()
        self.started = []


class Place:
    def __init__(self, nz, ny, nx):
        self.nz, self.ny, self.nx = nz, ny, nx
        self.group = ny * nx * 2
        self.z = lax.axis_index("samp")
        self.p = lax.axis_index("pix")
        self.c = lax.rem(self.p, 2)
        self.x = lax.rem(self.p // 2, nx)
        self.y = self.p // (2 * nx)

    def pix(self, y, x, c):
        return (y * self.nx + x) * 2 + c

    def barrier(self):
        semaphore = pltpu.get_barrier_semaphore()
        for step in range(1, self.nz):
            pl.semaphore_signal(
                semaphore,
                inc=1,
                device_id=(lax.rem(self.z + step, self.nz), self.p),
                device_id_type=MESH,
            )
        for step in range(1, self.group):
            pl.semaphore_signal(
                semaphore,
                inc=1,
                device_id=(self.z, lax.rem(self.p + step, self.group)),
                device_id_type=MESH,
            )
        pl.semaphore_wait(semaphore, self.nz - 1 + self.group - 1)

    def push_z(self, links, array, sub=()):
        copies = []
        for step in range(1, self.nz):
            own = array.at[(self.z, self.y, self.x, self.c) + sub]
            copies.append(links.push(own, own, lax.rem(self.z - step + self.nz, self.nz), self.p))
        return copies

    def push_first(self, links, array, lead, sub, along):
        own = array.at[lead + (self.y, self.x, self.c) + sub]
        copies = []
        if along == "x":
            for step in range(1, self.nx):
                other = self.pix(self.y, lax.rem(self.x + step, self.nx), self.c)
                copies.append(links.push(own, own, self.z, other))
        else:
            for step in range(1, self.ny):
                other = self.pix(lax.rem(self.y + step, self.ny), self.x, self.c)
                copies.append(links.push(own, own, self.z, other))
        return copies

    def push_second(self, links, array, lead, sub, first):
        copies = []
        if first == "x":
            held = array.at[lead + (self.y, slice(None), self.c) + sub]
            for step in range(1, self.ny):
                other = self.pix(lax.rem(self.y + step, self.ny), self.x, self.c)
                copies.append(links.push(held, held, self.z, other))
        else:
            held = array.at[lead + (slice(None), self.x, self.c) + sub]
            for step in range(1, self.nx):
                other = self.pix(self.y, lax.rem(self.x + step, self.nx), self.c)
                copies.append(links.push(held, held, self.z, other))
        return copies

    def push_core(self, links, array, lead):
        held = array.at[lead + (slice(None), slice(None), self.c)]
        return [links.push(held, held, self.z, self.p + 1 - 2 * self.c)]


def arrived(copies):
    for copy in copies:
        copy.wait_recv()


def column_block(array, place, index, col_blocks, owned, sub=()):
    every = slice(None)
    if 2 * owned == col_blocks:
        block = array[(every, every, every, index // owned) + sub + (index % owned,)]
    else:
        block = array[(every, every, index // 2, index % 2) + sub + (0,)]
    return block.reshape(-1, block.shape[-1])


def column_pair(array, place, pair, col_blocks, owned, sub=()):
    return jnp.concatenate(
        [
            column_block(array, place, 2 * pair, col_blocks, owned, sub),
            column_block(array, place, 2 * pair + 1, col_blocks, owned, sub),
        ],
        axis=1,
    )


def front_kernel(
    dims,
    pixels,
    mask,
    gain_cols,
    lat_gain,
    own_proj,
    own_keyval,
    own_latents,
    all_query,
    all_keyval,
    all_latents,
    all_mats,
    normed_out,
    inverse_out,
    weights_out,
    sent_out,
    landed,
    pixel_query,
    query_out,
    mats_own,
    g_query,
    g_keyval,
    g_latents,
    lat_normed,
    query,
    normed,
    weights,
    outgoing,
    send_sems,
    recv_sems,
    local_sems,
):
    batches, channels, shard_pixels = pixels.shape
    lat_rows, width = own_latents.shape
    owned, _, row_block, col_block = own_proj.shape
    col_blocks = width // col_block
    padded = normed.shape[1]
    main = channels // 16 * 16
    place = Place(*dims)
    links = Links(send_sems, recv_sems)
    z, y, x, c, p = place.z, place.y, place.x, place.c, place.p
    half_rows = row_block // 2
    half_width = width // 2
    every = slice(None)

    g_query[z, y, x, c] = own_proj[:, 0].astype(BF)
    g_keyval[z, y, x, c] = own_keyval[...]
    g_latents[y, x, c] = own_latents[...]
    for mat in range(3):
        mats_own[mat] = own_proj[:, mat + 1].astype(BF)
    local = []

    def local_copy(source, target):
        copy = pltpu.make_async_copy(source, target, local_sems.at[len(local)])
        copy.start()
        local.append(copy)
        return copy

    own_mats_copy = local_copy(mats_own, all_mats.at[z, y, x, c])
    place.barrier()

    sub_a = (every, pl.ds(0, half_rows))
    sub_b = (every, pl.ds(half_rows, half_rows))

    def first_of(step):
        zz = lax.rem(z + step, place.nz)
        copies = place.push_first(links, g_query, (zz,), sub_a, "x")
        copies += place.push_first(links, g_query, (zz,), sub_b, "y")
        copies += place.push_first(links, g_keyval, (zz,), (), "xy"[step % 2])
        return copies

    def second_of(step):
        zz = lax.rem(z + step, place.nz)
        copies = place.push_second(links, g_query, (zz,), sub_a, "x")
        copies += place.push_second(links, g_query, (zz,), sub_b, "y")
        copies += place.push_second(links, g_keyval, (zz,), (), "xy"[step % 2])
        return copies

    z_query = place.push_z(links, g_query)
    z_keyval = place.push_z(links, g_keyval)
    firsts = [first_of(0)]
    lat_a = (every, pl.ds(0, half_width))
    lat_b = (every, pl.ds(half_width, half_width))
    lat_first = place.push_first(links, g_latents, (), lat_a, "x")
    lat_first += place.push_first(links, g_latents, (), lat_b, "y")

    lane_chunk = 128
    bias_row = channels - main

    def norm_image(image):
        @pl.loop(0, shard_pixels // lane_chunk)
        def _(chunk):
            cols = pl.ds(pl.multiple_of(chunk * lane_chunk, lane_chunk), lane_chunk)
            top = pixels[image, 0:main, cols].astype(jnp.float32)
            tail = pixels[image, main:channels, cols].astype(jnp.float32)
            mean = (
                jnp.sum(top, axis=0, keepdims=True) + jnp.sum(tail, axis=0, keepdims=True)
            ) / channels
            top = top - mean
            tail = tail - mean
            variance = (
                jnp.sum(top * top, axis=0, keepdims=True)
                + jnp.sum(tail * tail, axis=0, keepdims=True)
            ) / channels
            inverse = lax.rsqrt(variance + EPSILON)
            inverse_out[image : image + 1, cols] = inverse
            normed[image, 0:main, cols] = (top * inverse * gain_cols[0:main, :]).astype(BF)
            tail = tail * inverse * gain_cols[main:channels, :]
            bias = jnp.where(mask[image : image + 1, cols] == 1, 0.0, NEGATIVE)
            row = lax.broadcasted_iota(jnp.int32, (padded - main, lane_chunk), 0)
            rest = jnp.where(row == bias_row + 1, 1.0, 0.0)
            rest = jnp.where(row == bias_row, bias, rest)
            for index in range(channels - main):
                rest = jnp.where(row == index, tail[index : index + 1], rest)
            normed[image, main:padded, cols] = rest.astype(BF)

        local_copy(normed.at[image], normed_out.at[image])

    norm_image(0)
    for step in range(1, place.nz):
        z_query[step - 1].wait_recv()
        z_keyval[step - 1].wait_recv()
        firsts.append(first_of(step))
    own_mats_copy.wait()
    z_mats = place.push_z(links, all_mats)
    norm_image(1)
    seconds = []
    for step in range(place.nz):
        arrived(firsts[step])
        seconds += second_of(step)
    arrived(lat_first)
    seconds += place.push_second(links, g_latents, (), lat_a, "x")
    seconds += place.push_second(links, g_latents, (), lat_b, "y")
    norm_image(2)
    arrived(seconds)
    cores = place.push_core(links, g_query, (every,))
    cores += place.push_core(links, g_keyval, (every,))
    cores += place.push_core(links, g_latents, ())
    norm_image(3)

    out_sub = 0
    mats_a = [((0, every, pl.ds(0, half_rows)), "x"), ((1,), "x")]
    mats_b = [((0, every, pl.ds(half_rows, half_rows)), "y"), ((2,), "y")]

    arrived(z_mats)
    firsts_m = []
    for sub, along in mats_a + mats_b:
        firsts_m += place.push_first(links, all_mats, (every,), sub, along)

    arrived(cores)
    for yy in range(place.ny):
        for xx in range(place.nx):
            for cc in range(2):
                rows = pl.ds(((yy * place.nx + xx) * 2 + cc) * lat_rows, lat_rows)
                values = g_latents[yy, xx, cc].astype(jnp.float32)
                mean = jnp.mean(values, axis=1, keepdims=True)
                values = values - mean
                variance = jnp.mean(values * values, axis=1, keepdims=True)
                values = values * lax.rsqrt(variance + EPSILON) * lat_gain[...]
                lat_normed[rows, :] = values.astype(BF)
    local_copy(g_query, all_query)
    local_copy(g_keyval, all_keyval)
    local_copy(g_latents, all_latents)
    for pair in range(col_blocks // 2):
        query[:, 2 * col_block * pair : 2 * col_block * (pair + 1)] = jnp.dot(
            lat_normed[...],
            column_pair(g_query, place, pair, col_blocks, owned),
            preferred_element_type=jnp.float32,
        ).astype(BF)
    local_copy(query, query_out)
    key_t = g_keyval[0 : place.nz // 2]
    key_t = key_t.reshape(width, key_t.shape[-1])
    projected = jnp.dot(query[...], key_t, preferred_element_type=jnp.float32) * width ** (-0.5)
    lane = lax.broadcasted_iota(jnp.int32, projected.shape, 1)
    pixel_query[...] = jnp.where(lane == channels, 1.0, projected).astype(BF)

    all_rows = lat_rows * place.group
    tile = min(256, all_rows)

    def attend(image):
        @pl.loop(0, all_rows // tile)
        def _(step):
            rows = pl.ds(pl.multiple_of(step * tile, tile), tile)
            scores = jnp.dot(
                pixel_query[rows, 0:padded], normed[image], preferred_element_type=jnp.float32
            )
            top = jnp.max(scores, axis=1, keepdims=True)
            top = jnp.maximum(top, 0.1 * NEGATIVE).astype(BF).astype(jnp.float32)
            share = jnp.exp(scores - top).astype(BF)
            weights[image, rows, :] = share
            numer = lax.dot_general(
                share, normed[image], NT, preferred_element_type=jnp.float32
            )
            lane = lax.broadcasted_iota(jnp.int32, numer.shape, 1)
            outgoing[image, rows, 0:padded] = jnp.where(lane == channels, top, numer).astype(BF)

        local_copy(weights.at[image], weights_out.at[image])
        local_copy(outgoing.at[image], sent_out.at[image])
        own_rows = pl.ds(pl.multiple_of(p * lat_rows, lat_rows), lat_rows)
        local_copy(outgoing.at[image, own_rows], landed.at[p, image])
        copies = []
        for step in range(1, place.group):
            q = lax.rem(p + step, place.group)
            rows = pl.ds(pl.multiple_of(q * lat_rows, lat_rows), lat_rows)
            copies.append(links.push(outgoing.at[image, rows], landed.at[p, image], z, q))
        return copies

    sent = attend(0)
    arrived(firsts_m)
    seconds_m = []
    for sub, along in mats_a + mats_b:
        seconds_m += place.push_second(links, all_mats, (every,), sub, along)
    sent += attend(1)
    sent += attend(2)
    arrived(seconds_m)
    core_m = place.push_core(links, all_mats, (every,))
    sent += attend(3)
    arrived(sent)
    arrived(core_m)
    links.drain()
    for copy in local[1:]:
        copy.wait()


def front_copies(nz, ny, nx, batches):
    plane_first = lambda a, b: a * (nx - 1) + b * (ny - 1)
    count = 2 * (nz - 1)
    for step in range(nz):
        ab = plane_first(1, 1) + (plane_first(1, 0) if step % 2 == 0 else plane_first(0, 1))
        ba = plane_first(1, 1) + (plane_first(0, 1) if step % 2 == 0 else plane_first(1, 0))
        count += ab + ba
    count += 2 * plane_first(1, 1)
    count += 3 + (nz - 1) + 2 * plane_first(2, 2) + 1
    count += batches * (2 * nx * ny - 1)
    return count


def front(dims, pixels, pixel_mask, in_gain, lat_gain, proj_blocks, keyval_weight, latents):
    nz, ny, nx = dims
    batches, channels, shard_pixels = pixels.shape
    lat_rows, width = latents.shape
    owned, mats, row_block, col_block = proj_blocks.shape
    keyval_rows = keyval_weight.shape[1]
    group = 2 * ny * nx
    all_rows = lat_rows * group
    padded = ceil_to(channels + 2, 16)
    lanes = ceil_to(padded, 128)
    gain_cols = jnp.broadcast_to(
        jnp.pad(in_gain, (0, ceil_to(channels, 8) - channels))[:, None],
        (ceil_to(channels, 8), 128),
    )
    own_keyval = jnp.pad(keyval_weight.T.astype(BF), ((0, 0), (0, lanes - channels)))
    vmem = pl.BlockSpec(memory_space=pltpu.VMEM)
    anywhere = pl.BlockSpec(memory_space=pl.ANY)
    cube = (nz, ny, nx, 2)
    copies = front_copies(nz, ny, nx, batches)
    return pl.pallas_call(
        functools.partial(front_kernel, dims),
        out_shape=(
            jax.ShapeDtypeStruct(cube + (owned, row_block, col_block), BF),
            jax.ShapeDtypeStruct(cube + (keyval_rows, lanes), BF),
            jax.ShapeDtypeStruct(cube[1:] + (lat_rows, width), BF),
            jax.ShapeDtypeStruct(cube + (3, owned, row_block, col_block), BF),
            jax.ShapeDtypeStruct((batches, padded, shard_pixels), BF),
            jax.ShapeDtypeStruct((batches, shard_pixels), jnp.float32),
            jax.ShapeDtypeStruct((batches, all_rows, shard_pixels), BF),
            jax.ShapeDtypeStruct((batches, all_rows, lanes), BF),
            jax.ShapeDtypeStruct((group, batches, lat_rows, lanes), BF),
            jax.ShapeDtypeStruct((all_rows, lanes), BF),
            jax.ShapeDtypeStruct((all_rows, width), BF),
        ),
        in_specs=[vmem] * 7,
        out_specs=(
            anywhere,
            anywhere,
            anywhere,
            anywhere,
            anywhere,
            vmem,
            anywhere,
            anywhere,
            anywhere,
            vmem,
            anywhere,
        ),
        scratch_shapes=[
            pltpu.VMEM((3, owned, row_block, col_block), BF),
            pltpu.VMEM(cube + (owned, row_block, col_block), BF),
            pltpu.VMEM(cube + (keyval_rows, lanes), BF),
            pltpu.VMEM(cube[1:] + (lat_rows, width), BF),
            pltpu.VMEM((all_rows, width), BF),
            pltpu.VMEM((all_rows, width), BF),
            pltpu.VMEM((batches, padded, shard_pixels), BF),
            pltpu.VMEM((batches, all_rows, shard_pixels), BF),
            pltpu.VMEM((batches, all_rows, lanes), BF),
            pltpu.SemaphoreType.DMA((copies,)),
            pltpu.SemaphoreType.DMA((copies,)),
            pltpu.SemaphoreType.DMA((5 + 4 * batches,)),
        ],
        compiler_params=pltpu.CompilerParams(
            collective_id=0, has_side_effects=True, vmem_limit_bytes=56 * 2**20
        ),
    )(
        pixels,
        pixel_mask,
        gain_cols,
        lat_gain[None, :],
        proj_blocks,
        own_keyval,
        latents.astype(BF),
    )


def add_low(former, latter):
    return (former.astype(jnp.float32) + latter.astype(jnp.float32)).astype(BF)


class Reduce:
    def __init__(self, place, links, term, buffers, along, base=0):
        self.place, self.links, self.term, self.along = place, links, term, along
        self.by_core, self.by_first, self.by_second, self.by_z = buffers
        self.base = base
        self.waiting = []

    def wait(self):
        arrived(self.waiting)
        self.waiting = []

    def push_core(self):
        place = self.place
        every = slice(None)
        self.waiting = [
            self.links.push(
                self.term.at[every, every, every, 1 - place.c],
                self.by_core,
                place.z,
                place.p + 1 - 2 * place.c,
            )
        ]

    def push_first(self):
        place = self.place
        self.wait()

        @pl.loop(0, self.by_core.shape[0])
        def _(level):
            self.by_core[level] = add_low(
                self.by_core[level], self.term[level, :, :, place.c]
            )

        every = slice(None)
        for step in range(1, place.nx if self.along == "x" else place.ny):
            if self.along == "x":
                xx = lax.rem(place.x + step, place.nx)
                source = self.by_core.at[every, every, xx]
                target = place.pix(place.y, xx, place.c)
            else:
                yy = lax.rem(place.y + step, place.ny)
                source = self.by_core.at[every, yy]
                target = place.pix(yy, place.x, place.c)
            self.waiting.append(
                self.links.push(source, self.by_first.at[step - 1], place.z, target)
            )

    def push_second(self):
        place = self.place
        self.wait()
        if self.along == "x":
            held = self.by_core[:, :, place.x].astype(jnp.float32)
        else:
            held = self.by_core[:, place.y].astype(jnp.float32)
        for slot in range(self.by_first.shape[0]):
            held = held + self.by_first[slot].astype(jnp.float32)
        self.by_first[0] = held.astype(BF)
        every = slice(None)
        for step in range(1, place.ny if self.along == "x" else place.nx):
            if self.along == "x":
                other = lax.rem(place.y + step, place.ny)
                target = place.pix(other, place.x, place.c)
            else:
                other = lax.rem(place.x + step, place.nx)
                target = place.pix(place.y, other, place.c)
            self.waiting.append(
                self.links.push(
                    self.by_first.at[0, every, other],
                    self.by_second.at[step - 1],
                    place.z,
                    target,
                )
            )

    def push_z(self):
        place = self.place
        self.wait()
        mine = place.y if self.along == "x" else place.x
        held = self.by_first[0, :, mine].astype(jnp.float32)
        for slot in range(self.by_second.shape[0]):
            held = held + self.by_second[slot].astype(jnp.float32)
        self.by_second[0] = held.astype(BF)
        self.sends = []
        for step in range(1, place.nz):
            zz = lax.rem(place.z - step + place.nz, place.nz)
            if self.base == 0:
                self.waiting.append(
                    self.links.push(
                        self.by_second.at[0, zz], self.by_z.at[step - 1], zz, place.p
                    )
                )
            else:
                level = jnp.maximum(zz - self.base, 0)
                copy = self.links.make(
                    self.by_second.at[0, level], self.by_z.at[step - 1], zz, place.p
                )
                pl.when(zz >= self.base)(copy.start)
                self.sends.append((zz, copy))

    def total(self):
        place = self.place
        level = place.z
        if self.base == 0:
            self.wait()
        else:
            level = jnp.maximum(place.z - self.base, 0)

            @pl.when(place.z >= self.base)
            def _():
                for _, copy in self.sends:
                    copy.wait_recv()

            for zz, copy in self.sends:
                pl.when(zz >= self.base)(copy.wait_send)
        held = self.by_second[0, level].astype(jnp.float32)
        return held, [self.by_z.at[slot] for slot in range(self.by_z.shape[0])]


def block_index(block, col_blocks, owned):
    every = slice(None)
    if 2 * owned == col_blocks:
        return (every, every, every, block // owned, block % owned)
    return (every, every, block // 2, block % 2, 0)


def back_kernel(
    dims,
    channels,
    landed,
    all_keyval,
    all_mats,
    normed_all,
    inverse,
    weights_all,
    sent_all,
    pixel_query,
    latents,
    mlp_gain,
    grad_rows,
    gain_cols,
    gain_back,
    mixed,
    pixel_grad,
    mats_grad,
    value_grad,
    query_total,
    gain_total,
    residual_total,
    came,
    values,
    mats,
    normed,
    weights,
    tops,
    attended_chan,
    attended,
    middle,
    mid_hat,
    mid_inverse,
    mid_normed,
    slope,
    hidden,
    grad_pre,
    grad_mid_normed,
    grad_mid,
    grad_attended,
    shares,
    query_turned,
    query_acc,
    gain_acc,
    staged,
    terms,
    buffers,
    query_low,
    query_came,
    query_levels,
    gain_plane,
    gain_levels,
    residual_levels,
    send_sems,
    recv_sems,
    local_sems,
):
    place = Place(*dims)
    links = Links(send_sems, recv_sems)
    z, y, x, c, p = place.z, place.y, place.x, place.c, place.p
    group, batches, lat_rows, lanes = landed.shape
    rows = batches * lat_rows
    all_rows = group * lat_rows
    width = latents.shape[1]
    padded, shard_pixels = normed_all.shape[1:]
    owned, row_block, col_block = all_mats.shape[5:]
    col_blocks = width // col_block
    every = slice(None)
    tile = 256
    tiles = width // tile
    local = []

    def local_copy(source, target):
        copy = pltpu.make_async_copy(source, target, local_sems.at[len(local)])
        copy.start()
        local.append(copy)
        return copy

    came_copy = local_copy(landed, came)
    values_copy = local_copy(all_keyval.at[pl.ds(place.nz // 2, place.nz // 2)], values)
    mats_copies = []
    for mat in range(3):
        copies = []
        for block in range(col_blocks):
            where = block_index(block, col_blocks, owned)
            source = all_mats.at[where[:4] + (mat,) + where[4:]]
            cols = pl.ds(block * col_block, col_block)
            lead = (mat,) + (every,) * (len(mats.shape) - 2)
            copies.append(local_copy(source, mats.at[lead + (cols,)]))
        mats_copies.append(copies)
    tops_copy = local_copy(sent_all.at[:, :, pl.ds(lanes - 128, 128)], tops)

    def fetch(image):
        slot = image % 2
        return [
            local_copy(normed_all.at[image], normed.at[slot]),
            local_copy(weights_all.at[image], weights.at[slot]),
        ]

    fetched = [fetch(0), fetch(1)]
    place.barrier()

    def columns_of(mat, index):
        lead = (mat,) + (every,) * (len(mats.shape) - 2)
        return mats[lead + (slice(index * tile, (index + 1) * tile),)].reshape(width, tile)

    def rows_of(mat, index):
        return mats[mat, index].reshape(-1, width)

    row_tile = width // place.nz

    came_copy.wait()
    lane = lax.broadcasted_iota(jnp.int32, (rows, lanes), 1)
    parts = [came[g].reshape(rows, lanes).astype(jnp.float32) for g in range(group)]
    top = [part[:, channels : channels + 1] for part in parts]
    peak = functools.reduce(jnp.maximum, top)
    factor = [jnp.exp(value - peak) for value in top]
    denominator = sum(f * part[:, channels + 1 : channels + 2] for f, part in zip(factor, parts))
    summed = sum(f * part for f, part in zip(factor, parts))
    attended_chan[...] = jnp.where(lane < channels, summed / denominator, 0.0).astype(BF)

    values_copy.wait()
    value_t = values[...].reshape(width, lanes)
    attended[...] = lax.dot_general(
        attended_chan[...], value_t, NT, preferred_element_type=jnp.float32
    ).astype(BF)
    arrived_local(mats_copies[0])
    for index in range(tiles):
        cols = slice(index * tile, (index + 1) * tile)
        own = latents[:, cols]
        middle[:, cols] = jnp.concatenate([own] * batches, axis=0) + jnp.dot(
            attended[...], columns_of(0, index), preferred_element_type=jnp.float32
        )

    @pl.loop(0, rows // lat_rows)
    def _(step):
        part = pl.ds(pl.multiple_of(step * lat_rows, lat_rows), lat_rows)
        value = middle[part, :]
        value = value - jnp.mean(value, axis=1, keepdims=True)
        scale = lax.rsqrt(jnp.mean(value * value, axis=1, keepdims=True) + EPSILON)
        value = value * scale
        mid_hat[part, :] = value
        mid_inverse[part, :] = jnp.broadcast_to(scale, (lat_rows, 128))
        mid_normed[part, :] = (value * mlp_gain[...]).astype(BF)

    arrived_local(mats_copies[1])
    for index in range(tiles):
        cols = slice(index * tile, (index + 1) * tile)
        pre = jnp.dot(mid_normed[...], columns_of(1, index), preferred_element_type=jnp.float32)
        below = 0.5 + 0.5 * lax.erf(pre * 0.5**0.5)
        hidden[:, cols] = (pre * below).astype(BF)
        slope[:, cols] = below + pre * jnp.exp(-0.5 * pre * pre) * (0.5 / math.pi) ** 0.5

    half_rows = row_block // 2

    def store_term(targets, left, right):
        turned = left[...].T
        for pair in range(col_blocks // 2):
            cols = slice(2 * pair * col_block, 2 * (pair + 1) * col_block)
            product = jnp.dot(turned, right[:, cols], preferred_element_type=jnp.float32).astype(
                BF
            )
            for side in range(2):
                where = block_index(2 * pair + side, col_blocks, owned)
                block = product[:, side * col_block : (side + 1) * col_block]
                taken = 0
                for target in targets:
                    height = target.shape[-2]
                    pieces = block.reshape(-1, row_block, col_block)[:, taken : taken + height]
                    taken += height
                    shape = target.shape
                    lead = shape[:3] if 2 * owned == col_blocks else shape[:2]
                    target[where] = pieces.reshape(lead + (height, col_block))

    jobs = [
        Reduce(place, links, terms[0], buffers[0], "y"),
        Reduce(place, links, terms[1], buffers[1], "x"),
        Reduce(place, links, terms[2], buffers[2], "x"),
        Reduce(place, links, terms[3], buffers[3], "y"),
        Reduce(place, links, terms[4], buffers[4], "x", place.nz // 2),
    ]
    down, inward, out_a, out_b, value_job = jobs
    store_term([terms[0]], hidden, grad_rows)
    down.push_core()

    arrived_local(mats_copies[2])
    for index in range(place.nz):
        cols = slice(index * row_tile, (index + 1) * row_tile)
        grad_hidden = lax.dot_general(
            grad_rows[...], rows_of(2, index), NT, preferred_element_type=jnp.float32
        )
        grad_pre[:, cols] = (
            grad_hidden.astype(BF).astype(jnp.float32) * slope[:, cols]
        ).astype(BF)
    down.push_first()
    gain_plane[p] = jnp.zeros(gain_plane.shape[1:], jnp.float32)
    for index in range(place.nz):
        cols = slice(index * row_tile, (index + 1) * row_tile)
        part = lax.dot_general(
            grad_pre[...], rows_of(1, index), NT, preferred_element_type=jnp.float32
        )
        grad_mid_normed[:, cols] = part
        summed_rows = jnp.sum(part * mid_hat[:, cols], axis=0, keepdims=True)
        for sub in range(row_tile // 128):
            row = index * (row_tile // 128) + sub
            gain_plane[p, row : row + 1, :] = summed_rows[:, sub * 128 : (sub + 1) * 128]

    @pl.loop(0, rows // lat_rows)
    def _(step):
        part = pl.ds(pl.multiple_of(step * lat_rows, lat_rows), lat_rows)
        grad = grad_mid_normed[part, :] * mlp_gain[...]
        hat = mid_hat[part, :]
        grad = (
            grad
            - jnp.mean(grad, axis=1, keepdims=True)
            - hat * jnp.mean(grad * hat, axis=1, keepdims=True)
        ) * mid_inverse[part, 0:1]
        grad_mid[part, :] = (grad_rows[part, :].astype(jnp.float32) + grad).astype(BF)

    for index in range(place.nz):
        cols = slice(index * row_tile, (index + 1) * row_tile)
        grad_attended[:, cols] = lax.dot_general(
            grad_mid[...], rows_of(0, index), NT, preferred_element_type=jnp.float32
        ).astype(BF)
    grad_chan = jnp.dot(grad_attended[...], value_t, preferred_element_type=jnp.float32)
    row_delta = jnp.sum(attended_chan[...].astype(jnp.float32) * grad_chan, axis=1, keepdims=True)
    back = jnp.where(lane == channels + 1, row_delta, grad_chan) / denominator
    back = jnp.where(lane == channels, peak, back)
    shares[y, x, c] = back.astype(BF).reshape(batches, lat_rows, lanes)

    share_first = []
    for image in range(batches):
        share_first.append(
            place.push_first(links, shares, (), (image,), "xy"[image % 2])
        )
    store_term([terms[1]], mid_normed, grad_pre)
    inward.push_core()
    share_second = []
    for image in range(batches):
        arrived(share_first[image])
        share_second.append(
            place.push_second(links, shares, (), (image,), "xy"[image % 2])
        )
    store_term([terms[2], terms[3]], attended, grad_mid)
    out_a.push_core()
    out_b.push_core()
    share_core = []
    for image in range(batches):
        arrived(share_second[image])
        held = shares.at[:, :, c, image]
        share_core.append([links.push(held, held, z, p + 1 - 2 * c)])
    terms[4][...] = (
        jnp.dot(grad_attended[...].T, attended_chan[...], preferred_element_type=jnp.float32)
        .astype(BF)
        .reshape(terms[4].shape)
    )
    value_job.push_core()
    residual = sum(
        grad_mid[image * lat_rows : (image + 1) * lat_rows].astype(jnp.float32)
        for image in range(batches)
    )
    residual_levels[z] = residual.astype(BF)
    residual_sent = []
    for step in range(1, place.nz):
        level = residual_levels.at[z]
        residual_sent.append(
            links.push(level, level, lax.rem(z + step, place.nz), p)
        )
    inward.push_first()
    down.push_second()

    lane_all = lax.broadcasted_iota(jnp.int32, (all_rows, lanes), 1)
    query_turned[...] = jnp.where(
        lane_all < channels, pixel_query[...].astype(jnp.float32), 0.0
    ).T[0:padded].astype(BF)
    query_acc[...] = jnp.zeros(query_acc.shape, jnp.float32)
    gain_acc[...] = jnp.zeros(gain_acc.shape, jnp.float32)
    chunk = min(512, shard_pixels)
    staged_out = []
    tops_copy.wait()

    def attend_back(image):
        slot = image % 2
        arrived(share_core[image])
        arrived_local(fetched[image])
        if image >= 2:
            staged_out[image - 2].wait()
        back = shares[:, :, :, image].reshape(all_rows, lanes).astype(jnp.float32)
        top = tops[image].astype(jnp.float32)[:, channels - (lanes - 128) :][:, 0:1]
        share = jnp.exp(top - back[:, channels : channels + 1])
        back = jnp.where(lane_all == channels, 0.0, back * share)
        back = jnp.where(lane_all > channels + 1, 0.0, back)
        back_low = jnp.where(lane_all == channels + 1, -back, back).astype(BF)[:, 0:padded]
        back_turned = jnp.where(lane_all < channels, back, 0.0).T[0:padded].astype(BF)

        @pl.loop(0, shard_pixels // chunk)
        def _(step):
            cols = pl.ds(pl.multiple_of(step * chunk, chunk), chunk)
            normed_chunk = normed[slot, :, cols]
            share_chunk = weights[slot, :, cols]
            grad_weights = jnp.dot(back_low, normed_chunk, preferred_element_type=jnp.float32)
            grad_scores = (share_chunk.astype(jnp.float32) * grad_weights).astype(BF)
            query_acc[:, 0:padded] += lax.dot_general(
                grad_scores, normed_chunk, NT, preferred_element_type=jnp.float32
            )
            grad_normed = jnp.dot(
                query_turned[...], grad_scores, preferred_element_type=jnp.float32
            ) + jnp.dot(back_turned, share_chunk, preferred_element_type=jnp.float32)
            normal = normed_chunk.astype(jnp.float32)
            product = grad_normed * normal
            folded = sum(product[:, at : at + 128] for at in range(0, chunk, 128))
            gain_acc[0:padded, :] += folded
            second_mean = jnp.sum(product, axis=0, keepdims=True) / channels
            spread = jnp.concatenate([gain_cols[...]] * (chunk // 128), axis=1)
            spread_back = jnp.concatenate([gain_back[...]] * (chunk // 128), axis=1)
            grad_hat = grad_normed * spread
            first_mean = jnp.sum(grad_hat, axis=0, keepdims=True) / channels
            result = (grad_hat - first_mean - normal * spread_back * second_mean) * inverse[
                image : image + 1, cols
            ]
            staged[slot, :, cols] = result[0:channels]

        staged_out.append(local_copy(staged.at[slot], pixel_grad.at[image]))
        if image + 2 < batches:
            fetched.append(fetch(image + 2))

    attend_back(0)
    out_a.push_first()
    out_b.push_first()
    value_job.push_first()
    inward.push_second()
    down.push_z()
    attend_back(1)
    out_a.push_second()
    out_b.push_second()
    value_job.push_second()
    inward.push_z()
    attend_back(2)
    out_a.push_z()
    out_b.push_z()
    value_job.push_z()
    attend_back(3)

    query_low[...] = query_acc[...].astype(BF)
    query_sent = []
    for step in range(1, group):
        q = lax.rem(p + step, group)
        part = pl.ds(pl.multiple_of(q * lat_rows, lat_rows), lat_rows)
        query_sent.append(links.push(query_low.at[part], query_came.at[step - 1], z, q))
    gain_rows = lax.dot_general(
        jnp.ones((8, 128), jnp.float32),
        gain_acc[...],
        NT,
        precision=HIGHEST,
        preferred_element_type=jnp.float32,
    )
    for sub in range(lanes // 128):
        row = width // 128 + sub
        gain_plane[p, row : row + 1, :] = gain_rows[0:1, sub * 128 : (sub + 1) * 128]
    gain_sent = []
    for step in range(1, group):
        own = gain_plane.at[p]
        gain_sent.append(links.push(own, own, z, lax.rem(p + step, group)))

    def finish(job, target):
        held, came_z = job.total()
        for part in came_z:
            held = held + part[...].astype(jnp.float32)
        target[...] = held

    finish(down, mats_grad.at[2])
    finish(inward, mats_grad.at[1])
    finish(out_a, mats_grad.at[0, :, pl.ds(0, half_rows)])
    finish(out_b, mats_grad.at[0, :, pl.ds(half_rows, half_rows)])

    arrived(query_sent)
    own_rows = pl.ds(pl.multiple_of(p * lat_rows, lat_rows), lat_rows)
    held = query_acc[own_rows, :]
    for slot in range(group - 1):
        held = held + query_came[slot].astype(jnp.float32)
    query_levels[z] = held.astype(BF)
    query_up = []
    for step in range(1, place.nz):
        own = query_levels.at[z]
        query_up.append(links.push(own, own, lax.rem(z + step, place.nz), p))
    arrived(gain_sent)
    gain_levels[z] = sum(gain_plane[g] for g in range(group))
    gain_up = []
    for step in range(1, place.nz):
        own = gain_levels.at[z]
        gain_up.append(links.push(own, own, lax.rem(z + step, place.nz), p))

    held, came_z = value_job.total()
    above = place.z >= place.nz // 2
    for part in came_z:
        held = held + part[...].astype(jnp.float32)
    value_grad[...] = jnp.where(above, held, 0.0)
    arrived(residual_sent)
    residual_total[...] = sum(residual_levels[zz].astype(jnp.float32) for zz in range(place.nz))

    arrived(query_up)
    query_total[p] = sum(query_levels[zz].astype(jnp.float32) for zz in range(place.nz)).astype(BF)
    query_all = []
    for step in range(1, group):
        own = query_total.at[p]
        query_all.append(links.push(own, own, z, lax.rem(p + step, group)))
    arrived(gain_up)
    gain_total[...] = sum(gain_levels[zz] for zz in range(place.nz))
    for index in range(tiles):
        cols = slice(index * tile, (index + 1) * tile)
        mixed[:, cols] = (
            middle[:, cols]
            + jnp.dot(hidden[...], columns_of(2, index), preferred_element_type=jnp.float32)
        ).astype(BF)
    arrived(query_all)
    links.drain()
    for copy in staged_out[batches - 2 :]:
        copy.wait()


def arrived_local(copies):
    for copy in copies:
        copy.wait()


def back_copies(nz, ny, nx, batches):
    group = 2 * ny * nx
    both = nx + ny - 2
    count = batches // 2 * 2 * both + batches
    count += 5 * (1 + both + nz - 1)
    count += 2 * (nz - 1) + group - 1 + group - 1 + nz - 1 + group - 1
    return count


def back(dims, channels, gathered, latents, mlp_gain, in_gain, mixed_grad):
    landed, all_keyval, all_mats, normed_all, inverse, weights_all, sent_all, pixel_query = gathered
    nz, ny, nx = dims
    group, batches, lat_rows, lanes = landed.shape
    rows = batches * lat_rows
    all_rows = group * lat_rows
    width = latents.shape[1]
    padded, shard_pixels = normed_all.shape[1:]
    owned, row_block, col_block = all_mats.shape[5:]
    keyval_rows = all_keyval.shape[4]
    half_rows = row_block // 2
    column = jnp.pad(in_gain, (0, padded - channels))[:, None]
    column_back = jnp.pad(1.0 / in_gain, (0, padded - channels))[:, None]
    gain_cols = jnp.broadcast_to(column, (padded, 128))
    gain_back = jnp.broadcast_to(column_back, (padded, 128))
    vmem = pl.BlockSpec(memory_space=pltpu.VMEM)
    anywhere = pl.BlockSpec(memory_space=pl.ANY)
    lead = (nz, ny, nx) if 2 * owned * col_block == width else (nz, ny)
    cube = (nz, ny, nx, 2)
    inners = [
        (nz, (owned, row_block, col_block), "y"),
        (nz, (owned, row_block, col_block), "x"),
        (nz, (owned, half_rows, col_block), "x"),
        (nz, (owned, half_rows, col_block), "y"),
        (nz // 2, (keyval_rows, lanes), "x"),
    ]
    terms = [pltpu.VMEM((levels, ny, nx, 2) + inner, BF) for levels, inner, _ in inners]
    buffers = []
    for levels, inner, along in inners:
        one, two = (nx, ny) if along == "x" else (ny, nx)
        buffers.append(
            [
                pltpu.VMEM((levels, ny, nx) + inner, BF),
                pltpu.VMEM((one - 1, levels, two) + inner, BF),
                pltpu.VMEM((two - 1, levels) + inner, BF),
                pltpu.VMEM((nz - 1,) + inner, BF),
            ]
        )
    wide = lambda kind: pltpu.VMEM((rows, width), kind)
    copies = back_copies(nz, ny, nx, batches)
    return pl.pallas_call(
        functools.partial(back_kernel, dims, channels),
        out_shape=(
            jax.ShapeDtypeStruct((rows, width), BF),
            jax.ShapeDtypeStruct((batches, channels, shard_pixels), jnp.float32),
            jax.ShapeDtypeStruct((3, owned, row_block, col_block), jnp.float32),
            jax.ShapeDtypeStruct((keyval_rows, lanes), jnp.float32),
            jax.ShapeDtypeStruct((group, lat_rows, lanes), BF),
            jax.ShapeDtypeStruct((16, 128), jnp.float32),
            jax.ShapeDtypeStruct((lat_rows, width), jnp.float32),
        ),
        in_specs=[
            anywhere,
            anywhere,
            anywhere,
            anywhere,
            vmem,
            anywhere,
            anywhere,
            vmem,
            vmem,
            vmem,
            vmem,
            vmem,
            vmem,
        ],
        out_specs=(vmem, anywhere, vmem, vmem, vmem, vmem, vmem),
        scratch_shapes=[
            pltpu.VMEM((group, batches, lat_rows, lanes), BF),
            pltpu.VMEM((nz // 2, ny, nx, 2, keyval_rows, lanes), BF),
            pltpu.VMEM((3,) + lead + (row_block, width), BF),
            pltpu.VMEM((2, padded, shard_pixels), BF),
            pltpu.VMEM((2, all_rows, shard_pixels), BF),
            pltpu.VMEM((batches, all_rows, 128), BF),
            pltpu.VMEM((rows, lanes), BF),
            wide(BF),
            wide(jnp.float32),
            wide(jnp.float32),
            pltpu.VMEM((rows, 128), jnp.float32),
            wide(BF),
            wide(jnp.float32),
            wide(BF),
            wide(BF),
            wide(jnp.float32),
            wide(BF),
            wide(BF),
            pltpu.VMEM(cube[1:] + (batches, lat_rows, lanes), BF),
            pltpu.VMEM((padded, all_rows), BF),
            pltpu.VMEM((all_rows, lanes), jnp.float32),
            pltpu.VMEM((lanes, 128), jnp.float32),
            pltpu.VMEM((2, channels, shard_pixels), jnp.float32),
            terms,
            buffers,
            pltpu.VMEM((all_rows, lanes), BF),
            pltpu.VMEM((group - 1, lat_rows, lanes), BF),
            pltpu.VMEM((nz, lat_rows, lanes), BF),
            pltpu.VMEM((group, 16, 128), jnp.float32),
            pltpu.VMEM((nz, 16, 128), jnp.float32),
            pltpu.VMEM((nz, lat_rows, width), BF),
            pltpu.SemaphoreType.DMA((copies,)),
            pltpu.SemaphoreType.DMA((copies,)),
            pltpu.SemaphoreType.DMA((3 + 3 * (width // col_block) + 3 * batches,)),
        ],
        compiler_params=pltpu.CompilerParams(
            collective_id=1, has_side_effects=True, vmem_limit_bytes=61 * 2**20
        ),
    )(
        landed,
        all_keyval,
        all_mats,
        normed_all,
        inverse,
        weights_all,
        sent_all,
        pixel_query,
        latents,
        mlp_gain[None, :],
        mixed_grad.reshape(rows, width),
        gain_cols,
        gain_back,
    )


def body(
    pixels,
    pixel_mask,
    proj_blocks,
    proj_left,
    proj_right,
    left_roots,
    right_roots,
    keyval_weight,
    keyval_second,
    latents,
    latent_second,
    gains,
    gain_second,
    mixed_grad,
):
    batches, channels, shard_pixels = pixels.shape
    lat_rows, width = latents.shape
    groups = lax.axis_size("pix")
    all_rows = lat_rows * groups
    owned_count, _, row_block, col_block = proj_blocks.shape
    scale = width ** (-0.5)
    everyone = ("samp", "pix")

    lat_gain = gains[:width]
    in_gain = gains[width : width + channels]
    mlp_gain = gains[width + channels :]
    side = math.isqrt(groups // 2)
    dims = (lax.axis_size("samp"), side, side)
    (
        query_blocks,
        keyval_t,
        latent_all,
        mats,
        normed_all,
        inverse_all,
        weights_all,
        sent_all,
        landed,
        pixel_query,
        query,
    ) = front(dims, pixels, pixel_mask, in_gain, lat_gain, proj_blocks, keyval_weight, latents)
    gathered = (
        landed,
        keyval_t,
        mats,
        normed_all,
        inverse_all,
        weights_all,
        sent_all,
        pixel_query,
    )
    mixed, pixel_grad, triple_owned, value_grad, query_total, gain_total, residual_total = back(
        dims, channels, gathered, latents, mlp_gain, in_gain, mixed_grad
    )
    query_sum = query_total.reshape(all_rows, -1)[:, :channels]
    gain_rows = gain_total.reshape(-1)
    mlp_gain_sum = gain_rows[:width]
    in_gain_sum = gain_rows[width : width + channels] / in_gain
    latent_all = latent_all.reshape(all_rows, width).astype(jnp.float32)
    key_t = keyval_t.reshape(2 * width, -1)[:width, :channels]
    query_weight = assemble(query_blocks, width, row_block, col_block)
    lat_hat, lat_inverse = normalize_parts(latent_all, 1)
    lat_normed = (lat_hat * lat_gain[None, :]).astype(BF)

    key_rows = keyval_weight.shape[1]
    device = lax.axis_index(everyone)
    half_devices = width // key_rows
    own_query = lax.dynamic_slice_in_dim(query, device % half_devices * key_rows, key_rows, 1)
    key_grad = contract(query_sum, own_query, 0, 0) * scale
    keyval_grad = jnp.where(device < half_devices, key_grad, value_grad[:, :channels].T)

    grad_query = (contract(query_sum, key_t, 1, 1) * scale).astype(BF)
    grad_lat_normed = contract(grad_query, query_weight, 1, 1)
    lat_gain_grad = jnp.sum(grad_lat_normed * lat_hat, axis=0)
    latent_path = normalize_back(grad_lat_normed * lat_gain[None, :], lat_hat, lat_inverse, 1)
    row_start = lax.axis_index("pix") * lat_rows
    own_path = lax.dynamic_slice_in_dim(latent_path, row_start, lat_rows, 0)
    latent_grad = residual_total + own_path
    first_block = device * owned_count
    col_count = width // col_block
    query_list = []
    for offset in range(owned_count):
        block_index = first_block + offset
        block_row = block_index // col_count * row_block
        block_col = block_index % col_count * col_block
        normed_slice = lax.dynamic_slice_in_dim(lat_normed, block_row, row_block, 1)
        grad_slice = lax.dynamic_slice_in_dim(grad_query, block_col, col_block, 1)
        query_list.append(contract(normed_slice, grad_slice, 0, 0))
    query_grad = jnp.stack(query_list, axis=0)
    proj_grad = jnp.concatenate([query_grad[:, None], triple_owned.swapaxes(0, 1)], axis=1)
    left_new = STAT_DECAY * proj_left + (1.0 - STAT_DECAY) * jnp.einsum(
        "nsab,nscb->nsac", proj_grad, proj_grad, precision=HIGHEST
    )
    right_new = STAT_DECAY * proj_right + (1.0 - STAT_DECAY) * jnp.einsum(
        "nsab,nsac->nsbc", proj_grad, proj_grad, precision=HIGHEST
    )
    partial_step = jnp.einsum("nsab,nsbc->nsac", left_roots, proj_grad, precision=HIGHEST)
    direction = jnp.einsum("nsac,nscd->nsad", partial_step, right_roots, precision=HIGHEST)
    proj_new = proj_blocks - MATRIX_RATE * direction
    keyval_second_new, keyval_new = moment_step(
        keyval_weight, keyval_grad, keyval_second, KEYVAL_RATE
    )
    latent_second_new, latent_new = moment_step(latents, latent_grad, latent_second, LATENT_RATE)
    gain_grad = jnp.concatenate([lat_gain_grad, in_gain_sum, mlp_gain_sum], axis=0)
    gain_second_new, gain_new = moment_step(gains, gain_grad, gain_second, GAIN_RATE)
    return (
        mixed.reshape(batches, lat_rows, width),
        pixel_grad,
        proj_grad,
        left_new,
        right_new,
        proj_new,
        keyval_grad,
        keyval_second_new,
        keyval_new,
        latent_grad,
        latent_second_new,
        latent_new,
        gain_grad,
        gain_second_new,
        gain_new,
    )


def solution(mesh):
    blocks = P(("samp", "pix"), None, None, None)
    columns = P(None, ("samp", "pix"))
    rows = P("pix", None)
    return jax.shard_map(
        body,
        mesh=mesh,
        in_specs=(
            P("samp", None, "pix"),
            P("samp", "pix"),
            blocks,
            blocks,
            blocks,
            blocks,
            blocks,
            columns,
            columns,
            rows,
            rows,
            P(),
            P(),
            P("samp", "pix", None),
        ),
        out_specs=(
            P("samp", "pix", None),
            P("samp", None, "pix"),
            blocks,
            blocks,
            blocks,
            blocks,
            columns,
            columns,
            columns,
            rows,
            rows,
            rows,
            P(),
            P(),
            P(),
        ),
        check_vma=False,
    )
```

```python
import functools
import math

import jax
import jax.numpy as jnp
from jax import lax
from jax.experimental import pallas as pl
from jax.experimental.pallas import tpu as pltpu
from jax.sharding import PartitionSpec as P

EPSILON = 1e-05
NEGATIVE = -1e30
HIGHEST = lax.Precision.HIGHEST
STAT_DECAY = 0.5
MATRIX_RATE = 0.5
KEYVAL_RATE = 0.05
LATENT_RATE = 0.7
GAIN_RATE = 0.6
MOMENT_FLOOR = 1e-08
BF = jnp.bfloat16
MESH = pl.DeviceIdType.MESH
NT = (((1,), (1,)), ((), ()))


def moment_step(weight, grad, second, rate):
    second_new = STAT_DECAY * second + (1.0 - STAT_DECAY) * grad * grad
    return (second_new, weight - rate * grad / (jnp.sqrt(second_new) + MOMENT_FLOOR))


def ceil_to(value, step):
    return -(-value // step) * step


class Links:
    def __init__(self, send_sems, recv_sems):
        self.send_sems = send_sems
        self.recv_sems = recv_sems
        self.used = 0
        self.started = []

    def make(self, source, target, samp, pix):
        copy = pltpu.make_async_remote_copy(
            src_ref=source,
            dst_ref=target,
            send_sem=self.send_sems.at[self.used],
            recv_sem=self.recv_sems.at[self.used],
            device_id=(samp, pix),
            device_id_type=MESH,
        )
        self.used += 1
        return copy

    def push(self, source, target, samp, pix):
        copy = self.make(source, target, samp, pix)
        copy.start()
        self.started.append(copy)
        return copy

    def drain(self):
        for copy in self.started:
            copy.wait_send()
        self.started = []


class Place:
    def __init__(self, nz, ny, nx):
        self.nz, self.ny, self.nx = nz, ny, nx
        self.group = ny * nx * 2
        self.z = lax.axis_index("samp")
        self.p = lax.axis_index("pix")
        self.c = lax.rem(self.p, 2)
        self.x = lax.rem(self.p // 2, nx)
        self.y = self.p // (2 * nx)

    def pix(self, y, x, c):
        return (y * self.nx + x) * 2 + c

    def barrier(self):
        semaphore = pltpu.get_barrier_semaphore()
        for step in range(1, self.nz):
            pl.semaphore_signal(
                semaphore,
                inc=1,
                device_id=(lax.rem(self.z + step, self.nz), self.p),
                device_id_type=MESH,
            )
        for step in range(1, self.group):
            pl.semaphore_signal(
                semaphore,
                inc=1,
                device_id=(self.z, lax.rem(self.p + step, self.group)),
                device_id_type=MESH,
            )
        pl.semaphore_wait(semaphore, self.nz - 1 + self.group - 1)

    def push_z(self, links, array, sub=()):
        copies = []
        for step in range(1, self.nz):
            own = array.at[(self.z, self.y, self.x, self.c) + sub]
            copies.append(links.push(own, own, lax.rem(self.z - step + self.nz, self.nz), self.p))
        return copies

    def push_first(self, links, array, lead, sub, along):
        own = array.at[lead + (self.y, self.x, self.c) + sub]
        copies = []
        if along == "x":
            for step in range(1, self.nx):
                other = self.pix(self.y, lax.rem(self.x + step, self.nx), self.c)
                copies.append(links.push(own, own, self.z, other))
        else:
            for step in range(1, self.ny):
                other = self.pix(lax.rem(self.y + step, self.ny), self.x, self.c)
                copies.append(links.push(own, own, self.z, other))
        return copies

    def push_second(self, links, array, lead, sub, first):
        copies = []
        if first == "x":
            held = array.at[lead + (self.y, slice(None), self.c) + sub]
            for step in range(1, self.ny):
                other = self.pix(lax.rem(self.y + step, self.ny), self.x, self.c)
                copies.append(links.push(held, held, self.z, other))
        else:
            held = array.at[lead + (slice(None), self.x, self.c) + sub]
            for step in range(1, self.nx):
                other = self.pix(self.y, lax.rem(self.x + step, self.nx), self.c)
                copies.append(links.push(held, held, self.z, other))
        return copies

    def push_core(self, links, array, lead):
        held = array.at[lead + (slice(None), slice(None), self.c)]
        return [links.push(held, held, self.z, self.p + 1 - 2 * self.c)]


def arrived(copies):
    for copy in copies:
        copy.wait_recv()


def column_block(array, place, index, col_blocks, owned, sub=()):
    every = slice(None)
    if 2 * owned == col_blocks:
        block = array[(every, every, every, index // owned) + sub + (index % owned,)]
    else:
        block = array[(every, every, index // 2, index % 2) + sub + (0,)]
    return block.reshape(-1, block.shape[-1])


def column_pair(array, place, pair, col_blocks, owned, sub=()):
    return jnp.concatenate(
        [
            column_block(array, place, 2 * pair, col_blocks, owned, sub),
            column_block(array, place, 2 * pair + 1, col_blocks, owned, sub),
        ],
        axis=1,
    )


def front_kernel(
    dims,
    pixels,
    mask,
    gain_rows,
    own_proj,
    own_keyval,
    own_latents,
    all_query,
    all_keyval,
    all_latents,
    all_mats,
    normed_out,
    inverse_out,
    weights_out,
    sent_out,
    landed,
    pixel_query,
    query_out,
    raw,
    gain_cols,
    mats_own,
    g_query,
    g_keyval,
    g_latents,
    lat_normed,
    query,
    normed,
    weights,
    outgoing,
    send_sems,
    recv_sems,
    local_sems,
):
    channels, batches, shard_pixels = pixels.shape
    lat_rows, width = own_latents.shape
    owned, _, row_block, col_block = own_proj.shape
    col_blocks = width // col_block
    padded = normed.shape[1]
    main = channels // 16 * 16
    place = Place(*dims)
    links = Links(send_sems, recv_sems)
    z, y, x, c, p = place.z, place.y, place.x, place.c, place.p
    half_rows = row_block // 2
    half_width = width // 2
    every = slice(None)
    quarter = shard_pixels // 4
    local = []

    def local_copy(source, target):
        copy = pltpu.make_async_copy(source, target, local_sems.at[len(local)])
        copy.start()
        local.append(copy)
        return copy

    g_query[z, y, x, c] = own_proj[:, 0].astype(BF)
    pixel_copies = [
        local_copy(pixels.at[:, :, pl.ds(part, quarter)], raw.at[:, :, pl.ds(part, quarter)])
        for part in range(0, shard_pixels, quarter)
    ]
    keyval_rows, lanes = g_keyval.shape[4:]
    g_keyval[z, y, x, c] = jnp.zeros((keyval_rows, lanes), BF)
    g_keyval[z, y, x, c, :, 0:channels] = own_keyval[...].astype(BF)
    gain_cols[...] = jnp.broadcast_to(gain_rows[1:2, 0:lanes], (128, lanes)).T
    g_latents[y, x, c] = own_latents[...].astype(BF)
    for mat in range(3):
        mats_own[mat] = own_proj[:, mat + 1].astype(BF)
    own_mats_copy = local_copy(mats_own, all_mats.at[z, y, x, c])
    place.barrier()

    sub_a = (every, pl.ds(0, half_rows))
    sub_b = (every, pl.ds(half_rows, half_rows))

    def first_of(step):
        zz = lax.rem(z + step, place.nz)
        copies = place.push_first(links, g_query, (zz,), sub_a, "x")
        copies += place.push_first(links, g_query, (zz,), sub_b, "y")
        copies += place.push_first(links, g_keyval, (zz,), (), "xy"[step % 2])
        return copies

    def second_of(step):
        zz = lax.rem(z + step, place.nz)
        copies = place.push_second(links, g_query, (zz,), sub_a, "x")
        copies += place.push_second(links, g_query, (zz,), sub_b, "y")
        copies += place.push_second(links, g_keyval, (zz,), (), "xy"[step % 2])
        return copies

    z_query = place.push_z(links, g_query)
    z_keyval = place.push_z(links, g_keyval)
    firsts = [first_of(0)]
    lat_a = (every, pl.ds(0, half_width))
    lat_b = (every, pl.ds(half_width, half_width))
    lat_first = place.push_first(links, g_latents, (), lat_a, "x")
    lat_first += place.push_first(links, g_latents, (), lat_b, "y")

    lane_chunk = 128
    bias_row = channels - main
    row = lax.broadcasted_iota(jnp.int32, (padded - main, lane_chunk), 0)

    def norm_quarter(part):
        pixel_copies[part].wait()

        @pl.loop(0, quarter // lane_chunk)
        def _(chunk):
            start = part * quarter + chunk * lane_chunk
            cols = pl.ds(pl.multiple_of(start, lane_chunk), lane_chunk)
            together = raw[:, :, cols].astype(jnp.float32)
            for image in range(batches):
                value = together[:, image, :]
                value = value - jnp.sum(value, axis=0, keepdims=True) / channels
                variance = jnp.sum(value * value, axis=0, keepdims=True) / channels
                inverse = lax.rsqrt(variance + EPSILON)
                inverse_out[image : image + 1, cols] = inverse
                value = value * inverse * gain_cols[0:channels, :]
                normed[image, 0:main, cols] = value[0:main].astype(BF)
                tail = value[main:channels]
                bias = jnp.where(mask[image : image + 1, cols] == 1, 0.0, NEGATIVE)
                rest = jnp.where(row == bias_row + 1, 1.0, 0.0)
                rest = jnp.where(row == bias_row, bias, rest)
                for index in range(channels - main):
                    rest = jnp.where(row == index, tail[index : index + 1], rest)
                normed[image, main:padded, cols] = rest.astype(BF)

    norm_quarter(0)
    for step in range(1, place.nz):
        z_query[step - 1].wait_recv()
        z_keyval[step - 1].wait_recv()
        firsts.append(first_of(step))
    own_mats_copy.wait()
    z_mats = place.push_z(links, all_mats)
    norm_quarter(1)
    seconds = []
    for step in range(place.nz):
        arrived(firsts[step])
        seconds += second_of(step)
    arrived(lat_first)
    seconds += place.push_second(links, g_latents, (), lat_a, "x")
    seconds += place.push_second(links, g_latents, (), lat_b, "y")
    norm_quarter(2)
    arrived(seconds)
    cores = place.push_core(links, g_query, (every,))
    cores += place.push_core(links, g_keyval, (every,))
    cores += place.push_core(links, g_latents, ())
    norm_quarter(3)
    local_copy(normed, normed_out)

    out_sub = 0
    mats_a = [((0, every, pl.ds(0, half_rows)), "x"), ((1,), "x")]
    mats_b = [((0, every, pl.ds(half_rows, half_rows)), "y"), ((2,), "y")]

    arrived(z_mats)
    firsts_m = []
    for sub, along in mats_a + mats_b:
        firsts_m += place.push_first(links, all_mats, (every,), sub, along)

    arrived(cores)
    for yy in range(place.ny):
        for xx in range(place.nx):
            for cc in range(2):
                rows = pl.ds(((yy * place.nx + xx) * 2 + cc) * lat_rows, lat_rows)
                values = g_latents[yy, xx, cc].astype(jnp.float32)
                mean = jnp.mean(values, axis=1, keepdims=True)
                values = values - mean
                variance = jnp.mean(values * values, axis=1, keepdims=True)
                values = values * lax.rsqrt(variance + EPSILON) * gain_rows[0:1, :]
                lat_normed[rows, :] = values.astype(BF)
    local_copy(g_query, all_query)
    local_copy(g_keyval, all_keyval)
    local_copy(lat_normed, all_latents)
    for pair in range(col_blocks // 2):
        query[:, 2 * col_block * pair : 2 * col_block * (pair + 1)] = jnp.dot(
            lat_normed[...],
            column_pair(g_query, place, pair, col_blocks, owned),
            preferred_element_type=jnp.float32,
        ).astype(BF)
    local_copy(query, query_out)
    key_t = g_keyval[0 : place.nz // 2]
    key_t = key_t.reshape(width, key_t.shape[-1])
    projected = jnp.dot(query[...], key_t, preferred_element_type=jnp.float32) * width ** (-0.5)
    lane = lax.broadcasted_iota(jnp.int32, projected.shape, 1)
    pixel_query[...] = jnp.where(lane == channels, 1.0, projected).astype(BF)

    all_rows = lat_rows * place.group
    tile = min(256, all_rows)

    def attend(image):
        @pl.loop(0, all_rows // tile)
        def _(step):
            rows = pl.ds(pl.multiple_of(step * tile, tile), tile)
            scores = jnp.dot(
                pixel_query[rows, 0:padded], normed[image], preferred_element_type=jnp.float32
            )
            top = jnp.max(scores, axis=1, keepdims=True)
            top = jnp.maximum(top, 0.1 * NEGATIVE).astype(BF).astype(jnp.float32)
            share = jnp.exp(scores - top).astype(BF)
            weights[image, rows, :] = share
            numer = lax.dot_general(
                share, normed[image], NT, preferred_element_type=jnp.float32
            )
            lane = lax.broadcasted_iota(jnp.int32, numer.shape, 1)
            outgoing[image, rows, 0:padded] = jnp.where(lane == channels, top, numer).astype(BF)

        local_copy(weights.at[image], weights_out.at[image])
        local_copy(outgoing.at[image], sent_out.at[image])
        own_rows = pl.ds(pl.multiple_of(p * lat_rows, lat_rows), lat_rows)
        local_copy(outgoing.at[image, own_rows], landed.at[p, image])
        copies = []
        for step in range(1, place.group):
            q = lax.rem(p + step, place.group)
            rows = pl.ds(pl.multiple_of(q * lat_rows, lat_rows), lat_rows)
            copies.append(links.push(outgoing.at[image, rows], landed.at[p, image], z, q))
        return copies

    sent = attend(0)
    arrived(firsts_m)
    seconds_m = []
    for sub, along in mats_a + mats_b:
        seconds_m += place.push_second(links, all_mats, (every,), sub, along)
    sent += attend(1)
    sent += attend(2)
    arrived(seconds_m)
    core_m = place.push_core(links, all_mats, (every,))
    sent += attend(3)
    arrived(sent)
    arrived(core_m)
    links.drain()
    for copy in local[5:]:
        copy.wait()


def front_copies(nz, ny, nx, batches):
    plane_first = lambda a, b: a * (nx - 1) + b * (ny - 1)
    count = 2 * (nz - 1)
    for step in range(nz):
        ab = plane_first(1, 1) + (plane_first(1, 0) if step % 2 == 0 else plane_first(0, 1))
        ba = plane_first(1, 1) + (plane_first(0, 1) if step % 2 == 0 else plane_first(1, 0))
        count += ab + ba
    count += 2 * plane_first(1, 1)
    count += 3 + (nz - 1) + 2 * plane_first(2, 2) + 1
    count += batches * (2 * nx * ny - 1)
    return count


def front(dims, pixels, pixel_mask, gain_rows, proj_blocks, keyval_t, latents):
    nz, ny, nx = dims
    channels, batches, shard_pixels = pixels.shape
    lat_rows, width = latents.shape
    owned, mats, row_block, col_block = proj_blocks.shape
    keyval_rows = keyval_t.shape[0]
    group = 2 * ny * nx
    all_rows = lat_rows * group
    padded = ceil_to(channels + 2, 16)
    lanes = ceil_to(padded, 128)
    vmem = pl.BlockSpec(memory_space=pltpu.VMEM)
    anywhere = pl.BlockSpec(memory_space=pl.ANY)
    cube = (nz, ny, nx, 2)
    copies = front_copies(nz, ny, nx, batches)
    return pl.pallas_call(
        functools.partial(front_kernel, dims),
        out_shape=(
            jax.ShapeDtypeStruct(cube + (owned, row_block, col_block), BF),
            jax.ShapeDtypeStruct(cube + (keyval_rows, lanes), BF),
            jax.ShapeDtypeStruct((all_rows, width), BF),
            jax.ShapeDtypeStruct(cube + (3, owned, row_block, col_block), BF),
            jax.ShapeDtypeStruct((batches, padded, shard_pixels), BF),
            jax.ShapeDtypeStruct((batches, shard_pixels), jnp.float32),
            jax.ShapeDtypeStruct((batches, all_rows, shard_pixels), BF),
            jax.ShapeDtypeStruct((batches, all_rows, lanes), BF),
            jax.ShapeDtypeStruct((group, batches, lat_rows, lanes), BF),
            jax.ShapeDtypeStruct((all_rows, lanes), BF),
            jax.ShapeDtypeStruct((all_rows, width), BF),
        ),
        in_specs=[anywhere] + [vmem] * 5,
        out_specs=(
            anywhere,
            anywhere,
            anywhere,
            anywhere,
            anywhere,
            vmem,
            anywhere,
            anywhere,
            anywhere,
            vmem,
            anywhere,
        ),
        scratch_shapes=[
            pltpu.VMEM(pixels.shape, BF),
            pltpu.VMEM((lanes, 128), jnp.float32),
            pltpu.VMEM((3, owned, row_block, col_block), BF),
            pltpu.VMEM(cube + (owned, row_block, col_block), BF),
            pltpu.VMEM(cube + (keyval_rows, lanes), BF),
            pltpu.VMEM(cube[1:] + (lat_rows, width), BF),
            pltpu.VMEM((all_rows, width), BF),
            pltpu.VMEM((all_rows, width), BF),
            pltpu.VMEM((batches, padded, shard_pixels), BF),
            pltpu.VMEM((batches, all_rows, shard_pixels), BF),
            pltpu.VMEM((batches, all_rows, lanes), BF),
            pltpu.SemaphoreType.DMA((copies,)),
            pltpu.SemaphoreType.DMA((copies,)),
            pltpu.SemaphoreType.DMA((10 + 3 * batches,)),
        ],
        compiler_params=pltpu.CompilerParams(
            collective_id=0, has_side_effects=True, vmem_limit_bytes=56 * 2**20
        ),
    )(
        pixels,
        pixel_mask,
        gain_rows,
        proj_blocks,
        keyval_t,
        latents,
    )


def add_low(former, latter):
    return (former.astype(jnp.float32) + latter.astype(jnp.float32)).astype(BF)


class Reduce:
    def __init__(self, place, links, term, buffers, along, base=0):
        self.place, self.links, self.term, self.along = place, links, term, along
        self.by_core, self.by_first, self.by_second, self.by_z = buffers
        self.base = base
        self.waiting = []

    def wait(self):
        arrived(self.waiting)
        self.waiting = []

    def push_core(self):
        place = self.place
        every = slice(None)
        self.waiting = [
            self.links.push(
                self.term.at[every, every, every, 1 - place.c],
                self.by_core,
                place.z,
                place.p + 1 - 2 * place.c,
            )
        ]

    def push_first(self):
        place = self.place
        self.wait()

        @pl.loop(0, self.by_core.shape[0])
        def _(level):
            self.by_core[level] = add_low(
                self.by_core[level], self.term[level, :, :, place.c]
            )

        every = slice(None)
        for step in range(1, place.nx if self.along == "x" else place.ny):
            if self.along == "x":
                xx = lax.rem(place.x + step, place.nx)
                source = self.by_core.at[every, every, xx]
                target = place.pix(place.y, xx, place.c)
            else:
                yy = lax.rem(place.y + step, place.ny)
                source = self.by_core.at[every, yy]
                target = place.pix(yy, place.x, place.c)
            self.waiting.append(
                self.links.push(source, self.by_first.at[step - 1], place.z, target)
            )

    def push_second(self):
        place = self.place
        self.wait()
        if self.along == "x":
            held = self.by_core[:, :, place.x].astype(jnp.float32)
        else:
            held = self.by_core[:, place.y].astype(jnp.float32)
        for slot in range(self.by_first.shape[0]):
            held = held + self.by_first[slot].astype(jnp.float32)
        self.by_first[0] = held.astype(BF)
        every = slice(None)
        for step in range(1, place.ny if self.along == "x" else place.nx):
            if self.along == "x":
                other = lax.rem(place.y + step, place.ny)
                target = place.pix(other, place.x, place.c)
            else:
                other = lax.rem(place.x + step, place.nx)
                target = place.pix(place.y, other, place.c)
            self.waiting.append(
                self.links.push(
                    self.by_first.at[0, every, other],
                    self.by_second.at[step - 1],
                    place.z,
                    target,
                )
            )

    def push_z(self):
        place = self.place
        self.wait()
        mine = place.y if self.along == "x" else place.x
        held = self.by_first[0, :, mine].astype(jnp.float32)
        for slot in range(self.by_second.shape[0]):
            held = held + self.by_second[slot].astype(jnp.float32)
        self.by_second[0] = held.astype(BF)
        self.sends = []
        for step in range(1, place.nz):
            zz = lax.rem(place.z - step + place.nz, place.nz)
            if self.base == 0:
                self.waiting.append(
                    self.links.push(
                        self.by_second.at[0, zz], self.by_z.at[step - 1], zz, place.p
                    )
                )
            else:
                level = jnp.maximum(zz - self.base, 0)
                copy = self.links.make(
                    self.by_second.at[0, level], self.by_z.at[step - 1], zz, place.p
                )
                pl.when(zz >= self.base)(copy.start)
                self.sends.append((zz, copy))

    def total(self):
        place = self.place
        level = place.z
        if self.base == 0:
            self.wait()
        else:
            level = jnp.maximum(place.z - self.base, 0)

            @pl.when(place.z >= self.base)
            def _():
                for _, copy in self.sends:
                    copy.wait_recv()

            for zz, copy in self.sends:
                pl.when(zz >= self.base)(copy.wait_send)
        held = self.by_second[0, level].astype(jnp.float32)
        return held, [self.by_z.at[slot] for slot in range(self.by_z.shape[0])]


def block_index(block, col_blocks, owned):
    every = slice(None)
    if 2 * owned == col_blocks:
        return (every, every, every, block // owned, block % owned)
    return (every, every, block // 2, block % 2, 0)


def back_kernel(
    dims,
    channels,
    landed,
    all_keyval,
    all_mats,
    normed_all,
    inverse,
    weights_all,
    sent_all,
    pixel_query,
    latents,
    gain_rows,
    grad_rows,
    mixed,
    pixel_grad,
    mats_grad,
    value_grad,
    query_total,
    gain_total,
    residual_total,
    came,
    values,
    mats,
    normed,
    weights,
    tops,
    attended_chan,
    attended,
    middle,
    mid_hat,
    mid_inverse,
    mid_normed,
    slope,
    hidden,
    grad_pre,
    grad_mid_normed,
    grad_mid,
    grad_attended,
    shares,
    query_turned,
    query_acc,
    gain_acc,
    gain_cols,
    staged,
    terms,
    buffers,
    query_low,
    query_came,
    query_levels,
    gain_plane,
    gain_levels,
    residual_levels,
    send_sems,
    recv_sems,
    local_sems,
):
    place = Place(*dims)
    links = Links(send_sems, recv_sems)
    z, y, x, c, p = place.z, place.y, place.x, place.c, place.p
    group, batches, lat_rows, lanes = landed.shape
    rows = batches * lat_rows
    all_rows = group * lat_rows
    width = latents.shape[1]
    padded, shard_pixels = normed_all.shape[1:]
    owned, row_block, col_block = all_mats.shape[5:]
    col_blocks = width // col_block
    every = slice(None)
    tile = 256
    tiles = width // tile
    local = []

    def local_copy(source, target):
        copy = pltpu.make_async_copy(source, target, local_sems.at[len(local)])
        copy.start()
        local.append(copy)
        return copy

    came_copy = local_copy(landed, came)
    values_copy = local_copy(all_keyval.at[pl.ds(place.nz // 2, place.nz // 2)], values)
    mats_copies = []
    for mat in range(3):
        copies = []
        for block in range(col_blocks):
            where = block_index(block, col_blocks, owned)
            source = all_mats.at[where[:4] + (mat,) + where[4:]]
            cols = pl.ds(block * col_block, col_block)
            lead = (mat,) + (every,) * (len(mats.shape) - 2)
            copies.append(local_copy(source, mats.at[lead + (cols,)]))
        mats_copies.append(copies)
    tops_copy = local_copy(sent_all.at[:, :, pl.ds(lanes - 128, 128)], tops)

    def fetch(image):
        slot = image % 2
        return [
            local_copy(normed_all.at[image], normed.at[slot]),
            local_copy(weights_all.at[image], weights.at[slot]),
        ]

    fetched = [fetch(0), fetch(1)]
    place.barrier()

    def columns_of(mat, index):
        lead = (mat,) + (every,) * (len(mats.shape) - 2)
        return mats[lead + (slice(index * tile, (index + 1) * tile),)].reshape(width, tile)

    def rows_of(mat, index):
        return mats[mat, index].reshape(-1, width)

    row_tile = width // place.nz

    came_copy.wait()
    lane = lax.broadcasted_iota(jnp.int32, (rows, lanes), 1)
    parts = [came[g].reshape(rows, lanes).astype(jnp.float32) for g in range(group)]
    top = [part[:, channels : channels + 1] for part in parts]
    peak = functools.reduce(jnp.maximum, top)
    factor = [jnp.exp(value - peak) for value in top]
    denominator = sum(f * part[:, channels + 1 : channels + 2] for f, part in zip(factor, parts))
    summed = sum(f * part for f, part in zip(factor, parts))
    attended_chan[...] = jnp.where(lane < channels, summed / denominator, 0.0).astype(BF)

    values_copy.wait()
    value_t = values[...].reshape(width, lanes)
    attended[...] = lax.dot_general(
        attended_chan[...], value_t, NT, preferred_element_type=jnp.float32
    ).astype(BF)
    arrived_local(mats_copies[0])
    for index in range(tiles):
        cols = slice(index * tile, (index + 1) * tile)
        own = latents[:, cols]
        middle[:, cols] = jnp.concatenate([own] * batches, axis=0) + jnp.dot(
            attended[...], columns_of(0, index), preferred_element_type=jnp.float32
        )

    @pl.loop(0, rows // lat_rows)
    def _(step):
        part = pl.ds(pl.multiple_of(step * lat_rows, lat_rows), lat_rows)
        value = middle[part, :]
        value = value - jnp.mean(value, axis=1, keepdims=True)
        scale = lax.rsqrt(jnp.mean(value * value, axis=1, keepdims=True) + EPSILON)
        value = value * scale
        mid_hat[part, :] = value
        mid_inverse[part, :] = jnp.broadcast_to(scale, (lat_rows, 128))
        mid_normed[part, :] = (value * gain_rows[2:3, :]).astype(BF)

    arrived_local(mats_copies[1])
    for index in range(tiles):
        cols = slice(index * tile, (index + 1) * tile)
        pre = jnp.dot(mid_normed[...], columns_of(1, index), preferred_element_type=jnp.float32)
        below = 0.5 + 0.5 * lax.erf(pre * 0.5**0.5)
        hidden[:, cols] = (pre * below).astype(BF)
        slope[:, cols] = below + pre * jnp.exp(-0.5 * pre * pre) * (0.5 / math.pi) ** 0.5

    half_rows = row_block // 2

    def store_term(targets, left, right):
        turned = left[...].T
        for pair in range(col_blocks // 2):
            cols = slice(2 * pair * col_block, 2 * (pair + 1) * col_block)
            product = jnp.dot(turned, right[:, cols], preferred_element_type=jnp.float32).astype(
                BF
            )
            for side in range(2):
                where = block_index(2 * pair + side, col_blocks, owned)
                block = product[:, side * col_block : (side + 1) * col_block]
                taken = 0
                for target in targets:
                    height = target.shape[-2]
                    pieces = block.reshape(-1, row_block, col_block)[:, taken : taken + height]
                    taken += height
                    shape = target.shape
                    lead = shape[:3] if 2 * owned == col_blocks else shape[:2]
                    target[where] = pieces.reshape(lead + (height, col_block))

    jobs = [
        Reduce(place, links, terms[0], buffers[0], "y"),
        Reduce(place, links, terms[1], buffers[1], "x"),
        Reduce(place, links, terms[2], buffers[2], "x"),
        Reduce(place, links, terms[3], buffers[3], "y"),
        Reduce(place, links, terms[4], buffers[4], "x", place.nz // 2),
    ]
    down, inward, out_a, out_b, value_job = jobs
    store_term([terms[0]], hidden, grad_rows)
    down.push_core()

    arrived_local(mats_copies[2])
    for index in range(place.nz):
        cols = slice(index * row_tile, (index + 1) * row_tile)
        grad_hidden = lax.dot_general(
            grad_rows[...], rows_of(2, index), NT, preferred_element_type=jnp.float32
        )
        grad_pre[:, cols] = (
            grad_hidden.astype(BF).astype(jnp.float32) * slope[:, cols]
        ).astype(BF)
    down.push_first()
    gain_plane[p] = jnp.zeros(gain_plane.shape[1:], jnp.float32)
    for index in range(place.nz):
        cols = slice(index * row_tile, (index + 1) * row_tile)
        part = lax.dot_general(
            grad_pre[...], rows_of(1, index), NT, preferred_element_type=jnp.float32
        )
        grad_mid_normed[:, cols] = part
        summed_rows = jnp.sum(part * mid_hat[:, cols], axis=0, keepdims=True)
        for sub in range(row_tile // 128):
            row = index * (row_tile // 128) + sub
            gain_plane[p, row : row + 1, :] = summed_rows[:, sub * 128 : (sub + 1) * 128]

    @pl.loop(0, rows // lat_rows)
    def _(step):
        part = pl.ds(pl.multiple_of(step * lat_rows, lat_rows), lat_rows)
        grad = grad_mid_normed[part, :] * gain_rows[2:3, :]
        hat = mid_hat[part, :]
        grad = (
            grad
            - jnp.mean(grad, axis=1, keepdims=True)
            - hat * jnp.mean(grad * hat, axis=1, keepdims=True)
        ) * mid_inverse[part, 0:1]
        grad_mid[part, :] = (grad_rows[part, :].astype(jnp.float32) + grad).astype(BF)

    for index in range(place.nz):
        cols = slice(index * row_tile, (index + 1) * row_tile)
        grad_attended[:, cols] = lax.dot_general(
            grad_mid[...], rows_of(0, index), NT, preferred_element_type=jnp.float32
        ).astype(BF)
    grad_chan = jnp.dot(grad_attended[...], value_t, preferred_element_type=jnp.float32)
    row_delta = jnp.sum(attended_chan[...].astype(jnp.float32) * grad_chan, axis=1, keepdims=True)
    back = jnp.where(lane == channels + 1, row_delta, grad_chan) / denominator
    back = jnp.where(lane == channels, peak, back)
    shares[y, x, c] = back.astype(BF).reshape(batches, lat_rows, lanes)

    share_first = []
    for image in range(batches):
        share_first.append(
            place.push_first(links, shares, (), (image,), "xy"[image % 2])
        )
    store_term([terms[1]], mid_normed, grad_pre)
    inward.push_core()
    share_second = []
    for image in range(batches):
        arrived(share_first[image])
        share_second.append(
            place.push_second(links, shares, (), (image,), "xy"[image % 2])
        )
    store_term([terms[2], terms[3]], attended, grad_mid)
    out_a.push_core()
    out_b.push_core()
    share_core = []
    for image in range(batches):
        arrived(share_second[image])
        held = shares.at[:, :, c, image]
        share_core.append([links.push(held, held, z, p + 1 - 2 * c)])
    terms[4][...] = (
        jnp.dot(grad_attended[...].T, attended_chan[...], preferred_element_type=jnp.float32)
        .astype(BF)
        .reshape(terms[4].shape)
    )
    value_job.push_core()
    residual = sum(
        grad_mid[image * lat_rows : (image + 1) * lat_rows].astype(jnp.float32)
        for image in range(batches)
    )
    residual_levels[z] = residual.astype(BF)
    residual_sent = []
    for step in range(1, place.nz):
        level = residual_levels.at[z]
        residual_sent.append(
            links.push(level, level, lax.rem(z + step, place.nz), p)
        )
    inward.push_first()
    down.push_second()

    lane_all = lax.broadcasted_iota(jnp.int32, (all_rows, lanes), 1)
    query_turned[...] = jnp.where(
        lane_all < channels, pixel_query[...].astype(jnp.float32), 0.0
    ).T[0:padded].astype(BF)
    query_acc[...] = jnp.zeros(query_acc.shape, jnp.float32)
    gain_acc[...] = jnp.zeros(gain_acc.shape, jnp.float32)
    gain_cols[0] = jnp.broadcast_to(gain_rows[1:2, 0:lanes], (128, lanes)).T[0:padded]
    gain_cols[1] = jnp.broadcast_to(gain_rows[3:4, 0:lanes], (128, lanes)).T[0:padded]
    chunk = min(512, shard_pixels)
    staged_out = []
    tops_copy.wait()

    def attend_back(image):
        slot = image % 2
        arrived(share_core[image])
        arrived_local(fetched[image])
        if image >= 2:
            staged_out[image - 2].wait()
        back = shares[:, :, :, image].reshape(all_rows, lanes).astype(jnp.float32)
        top = tops[image].astype(jnp.float32)[:, channels - (lanes - 128) :][:, 0:1]
        share = jnp.exp(top - back[:, channels : channels + 1])
        back = jnp.where(lane_all == channels, 0.0, back * share)
        back = jnp.where(lane_all > channels + 1, 0.0, back)
        back_low = jnp.where(lane_all == channels + 1, -back, back).astype(BF)[:, 0:padded]
        back_turned = jnp.where(lane_all < channels, back, 0.0).T[0:padded].astype(BF)

        @pl.loop(0, shard_pixels // chunk)
        def _(step):
            cols = pl.ds(pl.multiple_of(step * chunk, chunk), chunk)
            normed_chunk = normed[slot, :, cols]
            share_chunk = weights[slot, :, cols]
            grad_weights = jnp.dot(back_low, normed_chunk, preferred_element_type=jnp.float32)
            grad_scores = (share_chunk.astype(jnp.float32) * grad_weights).astype(BF)
            query_acc[:, 0:padded] += lax.dot_general(
                grad_scores, normed_chunk, NT, preferred_element_type=jnp.float32
            )
            grad_normed = jnp.dot(
                query_turned[...], grad_scores, preferred_element_type=jnp.float32
            ) + jnp.dot(back_turned, share_chunk, preferred_element_type=jnp.float32)
            normal = normed_chunk.astype(jnp.float32)
            product = grad_normed * normal
            folded = sum(product[:, at : at + 128] for at in range(0, chunk, 128))
            gain_acc[0:padded, :] += folded
            second_mean = jnp.sum(product, axis=0, keepdims=True) / channels
            spread = jnp.concatenate([gain_cols[0]] * (chunk // 128), axis=1)
            spread_back = jnp.concatenate([gain_cols[1]] * (chunk // 128), axis=1)
            grad_hat = grad_normed * spread
            first_mean = jnp.sum(grad_hat, axis=0, keepdims=True) / channels
            result = (grad_hat - first_mean - normal * spread_back * second_mean) * inverse[
                image : image + 1, cols
            ]
            staged[slot, :, cols] = result[0:channels].astype(BF)

        staged_out.append(local_copy(staged.at[slot], pixel_grad.at[image]))
        if image + 2 < batches:
            fetched.append(fetch(image + 2))

    attend_back(0)
    out_a.push_first()
    out_b.push_first()
    value_job.push_first()
    inward.push_second()
    down.push_z()
    attend_back(1)
    out_a.push_second()
    out_b.push_second()
    value_job.push_second()
    inward.push_z()
    attend_back(2)
    out_a.push_z()
    out_b.push_z()
    value_job.push_z()
    attend_back(3)

    query_low[...] = query_acc[...].astype(BF)
    query_sent = []
    for step in range(1, group):
        q = lax.rem(p + step, group)
        part = pl.ds(pl.multiple_of(q * lat_rows, lat_rows), lat_rows)
        query_sent.append(links.push(query_low.at[part], query_came.at[step - 1], z, q))
    gain_rows = lax.dot_general(
        jnp.ones((8, 128), jnp.float32),
        gain_acc[...],
        NT,
        precision=HIGHEST,
        preferred_element_type=jnp.float32,
    )
    for sub in range(lanes // 128):
        row = width // 128 + sub
        gain_plane[p, row : row + 1, :] = gain_rows[0:1, sub * 128 : (sub + 1) * 128]
    gain_sent = []
    for step in range(1, group):
        own = gain_plane.at[p]
        gain_sent.append(links.push(own, own, z, lax.rem(p + step, group)))

    def finish(job, target):
        held, came_z = job.total()
        for part in came_z:
            held = held + part[...].astype(jnp.float32)
        target[...] = held

    finish(down, mats_grad.at[2])
    finish(inward, mats_grad.at[1])
    finish(out_a, mats_grad.at[0, :, pl.ds(0, half_rows)])
    finish(out_b, mats_grad.at[0, :, pl.ds(half_rows, half_rows)])

    arrived(query_sent)
    own_rows = pl.ds(pl.multiple_of(p * lat_rows, lat_rows), lat_rows)
    held = query_acc[own_rows, :]
    for slot in range(group - 1):
        held = held + query_came[slot].astype(jnp.float32)
    query_levels[z] = held.astype(BF)
    query_up = []
    for step in range(1, place.nz):
        own = query_levels.at[z]
        query_up.append(links.push(own, own, lax.rem(z + step, place.nz), p))
    arrived(gain_sent)
    gain_levels[z] = sum(gain_plane[g] for g in range(group))
    gain_up = []
    for step in range(1, place.nz):
        own = gain_levels.at[z]
        gain_up.append(links.push(own, own, lax.rem(z + step, place.nz), p))

    held, came_z = value_job.total()
    above = place.z >= place.nz // 2
    for part in came_z:
        held = held + part[...].astype(jnp.float32)
    value_grad[...] = jnp.where(above, held, 0.0)
    arrived(residual_sent)
    residual_total[...] = sum(residual_levels[zz].astype(jnp.float32) for zz in range(place.nz))

    arrived(query_up)
    query_total[p] = sum(query_levels[zz].astype(jnp.float32) for zz in range(place.nz)).astype(BF)
    query_all = []
    for step in range(1, group):
        own = query_total.at[p]
        query_all.append(links.push(own, own, z, lax.rem(p + step, group)))
    arrived(gain_up)
    gain_total[...] = sum(gain_levels[zz] for zz in range(place.nz))
    for index in range(tiles):
        cols = slice(index * tile, (index + 1) * tile)
        mixed[:, cols] = (
            middle[:, cols]
            + jnp.dot(hidden[...], columns_of(2, index), preferred_element_type=jnp.float32)
        ).astype(BF)
    arrived(query_all)
    links.drain()
    for copy in staged_out[batches - 2 :]:
        copy.wait()


def arrived_local(copies):
    for copy in copies:
        copy.wait()


def back_copies(nz, ny, nx, batches):
    group = 2 * ny * nx
    both = nx + ny - 2
    count = batches // 2 * 2 * both + batches
    count += 5 * (1 + both + nz - 1)
    count += 2 * (nz - 1) + group - 1 + group - 1 + nz - 1 + group - 1
    return count


def back(dims, channels, gathered, latents, gain_rows, mixed_grad):
    landed, all_keyval, all_mats, normed_all, inverse, weights_all, sent_all, pixel_query = gathered
    nz, ny, nx = dims
    group, batches, lat_rows, lanes = landed.shape
    rows = batches * lat_rows
    all_rows = group * lat_rows
    width = latents.shape[1]
    padded, shard_pixels = normed_all.shape[1:]
    owned, row_block, col_block = all_mats.shape[5:]
    keyval_rows = all_keyval.shape[4]
    half_rows = row_block // 2
    vmem = pl.BlockSpec(memory_space=pltpu.VMEM)
    anywhere = pl.BlockSpec(memory_space=pl.ANY)
    lead = (nz, ny, nx) if 2 * owned * col_block == width else (nz, ny)
    cube = (nz, ny, nx, 2)
    inners = [
        (nz, (owned, row_block, col_block), "y"),
        (nz, (owned, row_block, col_block), "x"),
        (nz, (owned, half_rows, col_block), "x"),
        (nz, (owned, half_rows, col_block), "y"),
        (nz // 2, (keyval_rows, lanes), "x"),
    ]
    terms = [pltpu.VMEM((levels, ny, nx, 2) + inner, BF) for levels, inner, _ in inners]
    buffers = []
    for levels, inner, along in inners:
        one, two = (nx, ny) if along == "x" else (ny, nx)
        buffers.append(
            [
                pltpu.VMEM((levels, ny, nx) + inner, BF),
                pltpu.VMEM((one - 1, levels, two) + inner, BF),
                pltpu.VMEM((two - 1, levels) + inner, BF),
                pltpu.VMEM((nz - 1,) + inner, BF),
            ]
        )
    wide = lambda kind: pltpu.VMEM((rows, width), kind)
    copies = back_copies(nz, ny, nx, batches)
    return pl.pallas_call(
        functools.partial(back_kernel, dims, channels),
        out_shape=(
            jax.ShapeDtypeStruct((rows, width), BF),
            jax.ShapeDtypeStruct((batches, channels, shard_pixels), BF),
            jax.ShapeDtypeStruct((3, owned, row_block, col_block), jnp.float32),
            jax.ShapeDtypeStruct((keyval_rows, lanes), jnp.float32),
            jax.ShapeDtypeStruct((group, lat_rows, lanes), BF),
            jax.ShapeDtypeStruct((16, 128), jnp.float32),
            jax.ShapeDtypeStruct((lat_rows, width), jnp.float32),
        ),
        in_specs=[
            anywhere,
            anywhere,
            anywhere,
            anywhere,
            vmem,
            anywhere,
            anywhere,
            vmem,
            vmem,
            vmem,
            vmem,
        ],
        out_specs=(vmem, anywhere, vmem, vmem, vmem, vmem, vmem),
        scratch_shapes=[
            pltpu.VMEM((group, batches, lat_rows, lanes), BF),
            pltpu.VMEM((nz // 2, ny, nx, 2, keyval_rows, lanes), BF),
            pltpu.VMEM((3,) + lead + (row_block, width), BF),
            pltpu.VMEM((2, padded, shard_pixels), BF),
            pltpu.VMEM((2, all_rows, shard_pixels), BF),
            pltpu.VMEM((batches, all_rows, 128), BF),
            pltpu.VMEM((rows, lanes), BF),
            wide(BF),
            wide(jnp.float32),
            wide(jnp.float32),
            pltpu.VMEM((rows, 128), jnp.float32),
            wide(BF),
            wide(jnp.float32),
            wide(BF),
            wide(BF),
            wide(jnp.float32),
            wide(BF),
            wide(BF),
            pltpu.VMEM(cube[1:] + (batches, lat_rows, lanes), BF),
            pltpu.VMEM((padded, all_rows), BF),
            pltpu.VMEM((all_rows, lanes), jnp.float32),
            pltpu.VMEM((lanes, 128), jnp.float32),
            pltpu.VMEM((2, padded, 128), jnp.float32),
            pltpu.VMEM((2, channels, shard_pixels), BF),
            terms,
            buffers,
            pltpu.VMEM((all_rows, lanes), BF),
            pltpu.VMEM((group - 1, lat_rows, lanes), BF),
            pltpu.VMEM((nz, lat_rows, lanes), BF),
            pltpu.VMEM((group, 16, 128), jnp.float32),
            pltpu.VMEM((nz, 16, 128), jnp.float32),
            pltpu.VMEM((nz, lat_rows, width), BF),
            pltpu.SemaphoreType.DMA((copies,)),
            pltpu.SemaphoreType.DMA((copies,)),
            pltpu.SemaphoreType.DMA((3 + 3 * (width // col_block) + 3 * batches,)),
        ],
        compiler_params=pltpu.CompilerParams(
            collective_id=1, has_side_effects=True, vmem_limit_bytes=61 * 2**20
        ),
    )(
        landed,
        all_keyval,
        all_mats,
        normed_all,
        inverse,
        weights_all,
        sent_all,
        pixel_query,
        latents,
        gain_rows,
        mixed_grad.reshape(rows, width),
    )


TN = (((0,), (0,)), ((), ()))


def tail_kernel(
    dims,
    channels,
    query_total,
    residual_total,
    mats_grad,
    value_grad,
    proj_blocks,
    proj_left,
    proj_right,
    left_roots,
    right_roots,
    keyval_weight,
    keyval_second,
    latents,
    latent_second,
    gain_rows,
    query_in,
    lat_normed_in,
    query_blocks,
    all_keyval,
    pixel_low,
    pixel_grad,
    proj_grad,
    left_new,
    right_new,
    proj_new,
    keyval_grad,
    keyval_second_new,
    keyval_new,
    latent_grad,
    latent_second_new,
    latent_new,
    lat_gain_grad,
    query,
    lat_normed,
    query_weight,
    keys,
    pixel_came,
    pixel_wide,
    grad_query,
    grad_normed,
    query_grad,
    key_rows,
    local_sems,
):
    place = Place(*dims)
    group, lat_rows, lanes = query_total.shape
    all_rows = group * lat_rows
    width = latents.shape[1]
    batches = pixel_low.shape[0]
    owned, mats, row_block, col_block = proj_blocks.shape
    col_blocks = width // col_block
    keyval_rows = keyval_weight.shape[0]
    device = place.z * group + place.p
    every = slice(None)
    local = []

    def local_copy(source, target):
        copy = pltpu.make_async_copy(source, target, local_sems.at[len(local)])
        copy.start()
        local.append(copy)
        return copy

    keys_copy = local_copy(all_keyval.at[pl.ds(0, place.nz // 2)], keys)
    weight_copies = []
    for block in range(col_blocks):
        lead = (every,) * (len(query_weight.shape) - 1)
        weight_copies.append(
            local_copy(
                query_blocks.at[block_index(block, col_blocks, owned)],
                query_weight.at[lead + (pl.ds(block * col_block, col_block),)],
            )
        )
    normed_copy = local_copy(lat_normed_in, lat_normed)
    query_copy = local_copy(query_in, query)
    pixel_copies = [local_copy(pixel_low.at[i], pixel_came.at[i]) for i in range(batches)]
    pixel_sent = []

    def widen(image):
        pixel_copies[image].wait()

        @pl.loop(0, pixel_low.shape[2] // 256)
        def _(step):
            cols = pl.ds(pl.multiple_of(step * 256, 256), 256)
            pixel_wide[image, :, cols] = pixel_came[image, :, cols].astype(jnp.float32)

        pixel_sent.append(local_copy(pixel_wide.at[image], pixel_grad.at[:, image]))

    def moments(weight, grad, second, rate, second_out, weight_out):
        second_value = STAT_DECAY * second[...] + (1.0 - STAT_DECAY) * grad * grad
        second_out[...] = second_value
        weight_out[...] = weight[...] - rate * grad / (jnp.sqrt(second_value) + MOMENT_FLOOR)

    def precondition(mat, index, grad):
        low = grad.astype(BF)
        proj_grad[index, mat] = grad
        left_new[index, mat] = STAT_DECAY * proj_left[index, mat] + (
            1.0 - STAT_DECAY
        ) * lax.dot_general(low, low, NT, preferred_element_type=jnp.float32)
        right_new[index, mat] = STAT_DECAY * proj_right[index, mat] + (
            1.0 - STAT_DECAY
        ) * lax.dot_general(low, low, TN, preferred_element_type=jnp.float32)
        step = jnp.dot(
            left_roots[index, mat].astype(BF), low, preferred_element_type=jnp.float32
        ).astype(BF)
        step = jnp.dot(
            step, right_roots[index, mat].astype(BF), preferred_element_type=jnp.float32
        )
        proj_new[index, mat] = proj_blocks[index, mat] - MATRIX_RATE * step

    for mat in range(3):
        for index in range(owned):
            precondition(mat + 1, index, mats_grad[mat, index])
    widen(0)
    keys_copy.wait()
    scale = width ** (-0.5)
    query_sum = query_total[...].reshape(all_rows, lanes)
    key_t = keys[...].reshape(width, lanes)
    for start in range(0, width, 256):
        grad_query[:, start : start + 256] = (
            lax.dot_general(
                query_sum, key_t[start : start + 256], NT, preferred_element_type=jnp.float32
            )
            * scale
        ).astype(BF)
    widen(1)
    arrived_local(weight_copies)
    normed_copy.wait()
    row_tile = width // place.nz
    for index in range(place.nz):
        cols = slice(index * row_tile, (index + 1) * row_tile)
        part = lax.dot_general(
            grad_query[...],
            query_weight[index].reshape(row_tile, width),
            NT,
            preferred_element_type=jnp.float32,
        )
        grad_normed[:, cols] = part
        lat_gain_grad[:, cols] = (
            jnp.sum(part * lat_normed[:, cols].astype(jnp.float32), axis=0, keepdims=True)
            / gain_rows[0:1, cols]
        )
    widen(2)
    values = latents[...]
    centered = values - jnp.mean(values, axis=1, keepdims=True)
    inverse = lax.rsqrt(jnp.mean(centered * centered, axis=1, keepdims=True) + EPSILON)
    hat = centered * inverse
    own = pl.ds(pl.multiple_of(place.p * lat_rows, lat_rows), lat_rows)
    grad = grad_normed[own, :] * gain_rows[0:1, :]
    grad = (
        grad
        - jnp.mean(grad, axis=1, keepdims=True)
        - hat * jnp.mean(grad * hat, axis=1, keepdims=True)
    ) * inverse
    grad = residual_total[...] + grad
    latent_grad[...] = grad
    moments(latents, grad, latent_second, LATENT_RATE, latent_second_new, latent_new)

    block_row = device * owned // col_blocks
    block_col = lax.rem(device * owned, col_blocks)
    per_lane = 128 // row_block
    rows = pl.ds(pl.multiple_of(block_row // per_lane * 128, 128), 128)
    cols = pl.ds(pl.multiple_of(block_col * col_block, col_block), owned * col_block)
    query_grad[...] = lax.dot_general(
        lat_normed[:, rows], grad_query[:, cols], TN, preferred_element_type=jnp.float32
    )
    part = pl.ds(pl.multiple_of(lax.rem(block_row, per_lane) * row_block, row_block), row_block)
    for index in range(owned):
        precondition(0, index, query_grad[part, index * col_block : (index + 1) * col_block])
    widen(3)

    query_copy.wait()
    half_devices = width // keyval_rows
    start = lax.rem(device, half_devices) * keyval_rows
    cols = pl.ds(pl.multiple_of(start // 128 * 128, 128), 128)
    key_rows[...] = (
        lax.dot_general(query[:, cols], query_sum, TN, preferred_element_type=jnp.float32) * scale
    )
    part = pl.ds(pl.multiple_of(lax.rem(start, 128), keyval_rows), keyval_rows)
    grad = jnp.where(device < half_devices, key_rows[part, :], value_grad[...])[:, 0:channels]
    keyval_grad[...] = grad
    moments(keyval_weight, grad, keyval_second, KEYVAL_RATE, keyval_second_new, keyval_new)
    for copy in pixel_sent:
        copy.wait()


def tail(
    dims,
    query_total,
    residual_total,
    mats_grad,
    value_grad,
    owned_arrays,
    gain_rows,
    query,
    lat_normed,
    query_blocks,
    all_keyval,
    pixel_low,
):
    nz, ny, nx = dims
    proj_blocks, keyval_weight, latents = owned_arrays[0], owned_arrays[5], owned_arrays[7]
    group, lat_rows, lanes = query_total.shape
    all_rows = group * lat_rows
    width = latents.shape[1]
    batches, channels, shard_pixels = pixel_low.shape
    owned, mats, row_block, col_block = proj_blocks.shape
    lead = (nz, ny, nx) if 2 * owned * col_block == width else (nz, ny)
    vmem = pl.BlockSpec(memory_space=pltpu.VMEM)
    anywhere = pl.BlockSpec(memory_space=pl.ANY)
    like = lambda array: jax.ShapeDtypeStruct(array.shape, array.dtype)
    wide = jax.ShapeDtypeStruct((channels, batches, shard_pixels), jnp.float32)
    results = [
        wide,
        like(proj_blocks),
        like(owned_arrays[1]),
        like(owned_arrays[2]),
        like(proj_blocks),
        like(keyval_weight),
        like(keyval_weight),
        like(keyval_weight),
        like(latents),
        like(latents),
        like(latents),
        jax.ShapeDtypeStruct((1, width), jnp.float32),
    ]
    return pl.pallas_call(
        functools.partial(tail_kernel, dims, channels),
        out_shape=results,
        in_specs=[vmem] * 14 + [anywhere] * 5,
        out_specs=[anywhere] + [vmem] * 11,
        scratch_shapes=[
            pltpu.VMEM((all_rows, width), BF),
            pltpu.VMEM((all_rows, width), BF),
            pltpu.VMEM(lead + (row_block, width), BF),
            pltpu.VMEM((nz // 2, ny, nx, 2) + all_keyval.shape[4:], BF),
            pltpu.VMEM((batches, channels, shard_pixels), BF),
            pltpu.VMEM((batches, channels, shard_pixels), jnp.float32),
            pltpu.VMEM((all_rows, width), BF),
            pltpu.VMEM((all_rows, width), jnp.float32),
            pltpu.VMEM((128, owned * col_block), jnp.float32),
            pltpu.VMEM((128, lanes), jnp.float32),
            pltpu.SemaphoreType.DMA((3 + width // col_block + 2 * batches,)),
        ],
        compiler_params=pltpu.CompilerParams(vmem_limit_bytes=56 * 2**20),
    )(
        query_total,
        residual_total,
        mats_grad,
        value_grad,
        *owned_arrays,
        gain_rows,
        query,
        lat_normed,
        query_blocks,
        all_keyval,
        pixel_low,
    )


def body(
    pixels,
    pixel_mask,
    proj_blocks,
    proj_left,
    proj_right,
    left_roots,
    right_roots,
    keyval_weight,
    keyval_second,
    latents,
    latent_second,
    gains,
    gain_second,
    mixed_grad,
):
    batches, channels, shard_pixels = pixels.shape
    lat_rows, width = latents.shape
    groups = lax.axis_size("pix")
    scale = width ** (-0.5)

    lat_gain = gains[:width]
    in_gain = gains[width : width + channels]
    mlp_gain = gains[width + channels :]
    side = math.isqrt(groups // 2)
    dims = (lax.axis_size("samp"), side, side)
    widen = lambda row: jnp.pad(row, (0, width - row.shape[0]))
    gain_rows = jnp.stack([lat_gain, widen(in_gain), mlp_gain, widen(1.0 / in_gain)])
    keyval_own = keyval_weight.T
    (
        query_blocks,
        keyval_t,
        lat_normed,
        mats,
        normed_all,
        inverse_all,
        weights_all,
        sent_all,
        landed,
        pixel_query,
        query,
    ) = front(
        dims, pixels.swapaxes(0, 1), pixel_mask, gain_rows, proj_blocks, keyval_own, latents
    )
    gathered = (
        landed,
        keyval_t,
        mats,
        normed_all,
        inverse_all,
        weights_all,
        sent_all,
        pixel_query,
    )
    mixed, pixel_low, mats_grad, value_grad, query_total, gain_total, residual_total = back(
        dims, channels, gathered, latents, gain_rows, mixed_grad
    )
    (
        pixel_grad,
        proj_grad,
        left_new,
        right_new,
        proj_new,
        keyval_grad,
        keyval_second_new,
        keyval_new,
        latent_grad,
        latent_second_new,
        latent_new,
        lat_gain_grad,
    ) = tail(
        dims,
        query_total,
        residual_total,
        mats_grad,
        value_grad,
        (
            proj_blocks,
            proj_left,
            proj_right,
            left_roots,
            right_roots,
            keyval_own,
            keyval_second.T,
            latents,
            latent_second,
        ),
        gain_rows,
        query,
        lat_normed,
        query_blocks,
        keyval_t,
        pixel_low,
    )
    gain_sums = gain_total.reshape(-1)
    gain_grad = jnp.concatenate(
        [
            lat_gain_grad[0],
            gain_sums[width : width + channels] / in_gain,
            gain_sums[:width],
        ],
        axis=0,
    )
    gain_second_new, gain_new = moment_step(gains, gain_grad, gain_second, GAIN_RATE)
    return (
        mixed.reshape(batches, lat_rows, width),
        pixel_grad.swapaxes(0, 1),
        proj_grad,
        left_new,
        right_new,
        proj_new,
        keyval_grad.T,
        keyval_second_new.T,
        keyval_new.T,
        latent_grad,
        latent_second_new,
        latent_new,
        gain_grad,
        gain_second_new,
        gain_new,
    )


def solution(mesh):
    blocks = P(("samp", "pix"), None, None, None)
    columns = P(None, ("samp", "pix"))
    rows = P("pix", None)
    return jax.shard_map(
        body,
        mesh=mesh,
        in_specs=(
            P("samp", None, "pix"),
            P("samp", "pix"),
            blocks,
            blocks,
            blocks,
            blocks,
            blocks,
            columns,
            columns,
            rows,
            rows,
            P(),
            P(),
            P("samp", "pix", None),
        ),
        out_specs=(
            P("samp", "pix", None),
            P("samp", None, "pix"),
            blocks,
            blocks,
            blocks,
            blocks,
            columns,
            columns,
            columns,
            rows,
            rows,
            rows,
            P(),
            P(),
            P(),
        ),
        check_vma=False,
    )
```

```python
import functools
import math

import jax
import jax.numpy as jnp
from jax import lax
from jax.experimental import pallas as pl
from jax.experimental.pallas import tpu as pltpu
from jax.sharding import PartitionSpec as P

EPSILON = 1e-05
NEGATIVE = -1e30
HIGHEST = lax.Precision.HIGHEST
STAT_DECAY = 0.5
MATRIX_RATE = 0.5
KEYVAL_RATE = 0.05
LATENT_RATE = 0.7
GAIN_RATE = 0.6
MOMENT_FLOOR = 1e-08
BF = jnp.bfloat16
MESH = pl.DeviceIdType.MESH
NT = (((1,), (1,)), ((), ()))


def moment_step(weight, grad, second, rate):
    second_new = STAT_DECAY * second + (1.0 - STAT_DECAY) * grad * grad
    return (second_new, weight - rate * grad / (jnp.sqrt(second_new) + MOMENT_FLOOR))


def ceil_to(value, step):
    return -(-value // step) * step


class Links:
    def __init__(self, send_sems, recv_sems):
        self.send_sems = send_sems
        self.recv_sems = recv_sems
        self.used = 0
        self.started = []

    def make(self, source, target, samp, pix):
        copy = pltpu.make_async_remote_copy(
            src_ref=source,
            dst_ref=target,
            send_sem=self.send_sems.at[self.used],
            recv_sem=self.recv_sems.at[self.used],
            device_id=(samp, pix),
            device_id_type=MESH,
        )
        self.used += 1
        return copy

    def push(self, source, target, samp, pix):
        copy = self.make(source, target, samp, pix)
        copy.start()
        self.started.append(copy)
        return copy

    def drain(self):
        for copy in self.started:
            copy.wait_send()
        self.started = []


class Place:
    def __init__(self, nz, ny, nx):
        self.nz, self.ny, self.nx = nz, ny, nx
        self.group = ny * nx * 2
        self.z = lax.axis_index("samp")
        self.p = lax.axis_index("pix")
        self.c = lax.rem(self.p, 2)
        self.x = lax.rem(self.p // 2, nx)
        self.y = self.p // (2 * nx)

    def pix(self, y, x, c):
        return (y * self.nx + x) * 2 + c

    def barrier(self):
        semaphore = pltpu.get_barrier_semaphore()
        for step in range(1, self.nz):
            pl.semaphore_signal(
                semaphore,
                inc=1,
                device_id=(lax.rem(self.z + step, self.nz), self.p),
                device_id_type=MESH,
            )
        for step in range(1, self.group):
            pl.semaphore_signal(
                semaphore,
                inc=1,
                device_id=(self.z, lax.rem(self.p + step, self.group)),
                device_id_type=MESH,
            )
        pl.semaphore_wait(semaphore, self.nz - 1 + self.group - 1)

    def push_z(self, links, array, step):
        own = array.at[self.z, self.y, self.x, self.c]
        return [links.push(own, own, lax.rem(self.z - step + self.nz, self.nz), self.p)]

    def push_first(self, links, array, lead, sub, along):
        own = array.at[lead + (self.y, self.x, self.c) + sub]
        copies = []
        if along == "x":
            for step in range(1, self.nx):
                other = self.pix(self.y, lax.rem(self.x + step, self.nx), self.c)
                copies.append(links.push(own, own, self.z, other))
        else:
            for step in range(1, self.ny):
                other = self.pix(lax.rem(self.y + step, self.ny), self.x, self.c)
                copies.append(links.push(own, own, self.z, other))
        return copies

    def push_second(self, links, array, lead, sub, first):
        copies = []
        if first == "x":
            held = array.at[lead + (self.y, slice(None), self.c) + sub]
            for step in range(1, self.ny):
                other = self.pix(lax.rem(self.y + step, self.ny), self.x, self.c)
                copies.append(links.push(held, held, self.z, other))
        else:
            held = array.at[lead + (slice(None), self.x, self.c) + sub]
            for step in range(1, self.nx):
                other = self.pix(self.y, lax.rem(self.x + step, self.nx), self.c)
                copies.append(links.push(held, held, self.z, other))
        return copies

    def push_core(self, links, array, lead):
        held = array.at[lead + (slice(None), slice(None), self.c)]
        return [links.push(held, held, self.z, self.p + 1 - 2 * self.c)]


def arrived(copies):
    for copy in copies:
        copy.wait_recv()


def column_block(array, place, index, col_blocks, owned, sub=()):
    every = slice(None)
    if 2 * owned == col_blocks:
        block = array[(every, every, every, index // owned) + sub + (index % owned,)]
    else:
        block = array[(every, every, index // 2, index % 2) + sub + (0,)]
    return block.reshape(-1, block.shape[-1])


def column_pair(array, place, pair, col_blocks, owned, sub=()):
    return jnp.concatenate(
        [
            column_block(array, place, 2 * pair, col_blocks, owned, sub),
            column_block(array, place, 2 * pair + 1, col_blocks, owned, sub),
        ],
        axis=1,
    )


def front_kernel(
    dims,
    pixels,
    mask,
    gain_rows,
    own_proj,
    own_keyval,
    own_latents,
    all_query,
    all_keyval,
    all_latents,
    all_mats,
    normed_out,
    inverse_out,
    weights_out,
    sent_out,
    landed,
    pixel_query,
    query_out,
    raw,
    gain_cols,
    mats_own,
    g_query,
    g_keyval,
    g_latents,
    lat_normed,
    query,
    normed,
    weights,
    outgoing,
    paired,
    merged,
    send_sems,
    recv_sems,
    local_sems,
):
    channels, batches, shard_pixels = pixels.shape
    lat_rows, width = own_latents.shape
    owned, _, row_block, col_block = own_proj.shape
    col_blocks = width // col_block
    padded = normed.shape[1]
    main = channels // 16 * 16
    place = Place(*dims)
    links = Links(send_sems, recv_sems)
    z, y, x, c, p = place.z, place.y, place.x, place.c, place.p
    half_rows = row_block // 2
    half_width = width // 2
    every = slice(None)
    quarter = shard_pixels // 8
    local = []

    def local_copy(source, target):
        copy = pltpu.make_async_copy(source, target, local_sems.at[len(local)])
        copy.start()
        local.append(copy)
        return copy

    g_query[z, y, x, c] = own_proj[:, 0].astype(BF)
    pixel_copies = [
        local_copy(pixels.at[:, :, pl.ds(part, quarter)], raw.at[:, :, pl.ds(part, quarter)])
        for part in range(0, shard_pixels, quarter)
    ]
    keyval_rows, lanes = g_keyval.shape[4:]
    g_keyval[z, y, x, c] = jnp.zeros((keyval_rows, lanes), BF)
    g_keyval[z, y, x, c, :, 0:channels] = own_keyval[...].astype(BF)
    gain_cols[...] = jnp.broadcast_to(gain_rows[1:2, 0:lanes], (128, lanes)).T
    g_latents[y, x, c] = own_latents[...].astype(BF)
    for mat in range(3):
        mats_own[mat] = own_proj[:, mat + 1].astype(BF)
    own_mats_copy = local_copy(mats_own, all_mats.at[z, y, x, c])
    place.barrier()

    sub_a = (every, pl.ds(0, half_rows))
    sub_b = (every, pl.ds(half_rows, half_rows))
    mats_subs = [
        ((1,), "x"),
        ((2,), "y"),
        ((0, every, pl.ds(0, half_rows)), "x"),
        ((0, every, pl.ds(half_rows, half_rows)), "y"),
    ]

    def level(step):
        return lax.rem(z + step, place.nz)

    def hand_on(push, step):
        copies = push(links, g_query, (level(step),), sub_a, "x")
        copies += push(links, g_query, (level(step),), sub_b, "y")
        copies += push(links, g_keyval, (level(step),), (), "xy"[step % 2])
        return copies

    def hand_on_mats(push, step):
        copies = []
        for sub, along in mats_subs:
            copies += push(links, all_mats, (level(step),), sub, along)
        return copies

    z_group = []
    for step in range(1, place.nz):
        z_group.append(
            place.push_z(links, g_query, step) + place.push_z(links, g_keyval, step)
        )
    firsts = [hand_on(place.push_first, 0)]
    lat_a = (every, pl.ds(0, half_width))
    lat_b = (every, pl.ds(half_width, half_width))
    lat_first = place.push_first(links, g_latents, (), lat_a, "x")
    lat_first += place.push_first(links, g_latents, (), lat_b, "y")
    own_mats_copy.wait()
    z_mats = [place.push_z(links, all_mats, step) for step in range(1, place.nz)]
    firsts_m = [hand_on_mats(place.push_first, 0)]

    lane_chunk = 128
    bias_row = channels - main
    row = lax.broadcasted_iota(jnp.int32, (padded - main, lane_chunk), 0)

    def norm_quarter(part):
        pixel_copies[part].wait()

        @pl.loop(0, quarter // lane_chunk)
        def _(chunk):
            start = part * quarter + chunk * lane_chunk
            cols = pl.ds(pl.multiple_of(start, lane_chunk), lane_chunk)
            together = raw[:, :, cols].astype(jnp.float32)
            for image in range(batches):
                value = together[:, image, :]
                value = value - jnp.sum(value, axis=0, keepdims=True) / channels
                variance = jnp.sum(value * value, axis=0, keepdims=True) / channels
                inverse = lax.rsqrt(variance + EPSILON)
                inverse_out[image : image + 1, cols] = inverse
                value = value * inverse * gain_cols[0:channels, :]
                normed[image, 0:main, cols] = value[0:main].astype(BF)
                tail = value[main:channels]
                bias = jnp.where(mask[image : image + 1, cols] == 1, 0.0, NEGATIVE)
                rest = jnp.where(row == bias_row + 1, 1.0, 0.0)
                rest = jnp.where(row == bias_row, bias, rest)
                for index in range(channels - main):
                    rest = jnp.where(row == index, tail[index : index + 1], rest)
                normed[image, main:padded, cols] = rest.astype(BF)

    seconds = []
    seconds_m = []
    cores_m = []

    def first(step):
        arrived(z_group[step - 1])
        firsts.append(hand_on(place.push_first, step))

    def second(step):
        arrived(firsts[step])
        seconds.extend(hand_on(place.push_second, step))

    def first_m(step):
        arrived(z_mats[step - 1])
        firsts_m.append(hand_on_mats(place.push_first, step))

    def second_m(step):
        arrived(firsts_m[step])
        seconds_m.append(hand_on_mats(place.push_second, step))

    def core_m(step):
        arrived(seconds_m[step])
        cores_m.extend(place.push_core(links, all_mats, (level(step),)))

    norm_quarter(0)
    norm_quarter(1)
    second(0)
    arrived(lat_first)
    seconds += place.push_second(links, g_latents, (), lat_a, "x")
    seconds += place.push_second(links, g_latents, (), lat_b, "y")
    norm_quarter(2)
    first(1)
    norm_quarter(3)
    norm_quarter(4)
    first(2)
    second(1)
    norm_quarter(5)
    for step in range(3, place.nz):
        first(step)
    second(2)
    norm_quarter(6)
    for step in range(3, place.nz):
        second(step)
    norm_quarter(7)
    second_m(0)
    first_m(1)
    local_copy(normed, normed_out)
    arrived(seconds)
    cores = place.push_core(links, g_query, (every,))
    cores += place.push_core(links, g_keyval, (every,))
    cores += place.push_core(links, g_latents, ())
    second_m(1)
    first_m(2)

    arrived(cores)
    for yy in range(place.ny):
        for xx in range(place.nx):
            for cc in range(2):
                rows = pl.ds(((yy * place.nx + xx) * 2 + cc) * lat_rows, lat_rows)
                values = g_latents[yy, xx, cc].astype(jnp.float32)
                mean = jnp.mean(values, axis=1, keepdims=True)
                values = values - mean
                variance = jnp.mean(values * values, axis=1, keepdims=True)
                values = values * lax.rsqrt(variance + EPSILON) * gain_rows[0:1, :]
                lat_normed[rows, :] = values.astype(BF)
    second_m(2)
    local_copy(g_query, all_query)
    local_copy(g_keyval, all_keyval)
    local_copy(lat_normed, all_latents)
    for pair in range(col_blocks // 2):
        query[:, 2 * col_block * pair : 2 * col_block * (pair + 1)] = jnp.dot(
            lat_normed[...],
            column_pair(g_query, place, pair, col_blocks, owned),
            preferred_element_type=jnp.float32,
        ).astype(BF)
    local_copy(query, query_out)
    key_t = g_keyval[0 : place.nz // 2]
    key_t = key_t.reshape(width, key_t.shape[-1])
    projected = jnp.dot(query[...], key_t, preferred_element_type=jnp.float32) * width ** (-0.5)
    lane = lax.broadcasted_iota(jnp.int32, projected.shape, 1)
    pixel_query[...] = jnp.where(lane == channels, 1.0, projected).astype(BF)

    tile = place.nx * 2 * lat_rows
    rows_here = place.ny * place.nx * lat_rows

    def attend(image):
        @pl.loop(0, place.ny)
        def _(step):
            rows = pl.ds(pl.multiple_of(step * tile, tile), tile)
            scores = jnp.dot(
                pixel_query[rows, 0:padded], normed[image], preferred_element_type=jnp.float32
            )
            top = jnp.max(scores, axis=1, keepdims=True)
            top = jnp.maximum(top, 0.1 * NEGATIVE).astype(BF).astype(jnp.float32)
            share = jnp.exp(scores - top).astype(BF)
            weights[image, rows, :] = share
            numer = lax.dot_general(
                share, normed[image], NT, preferred_element_type=jnp.float32
            )
            lane = lax.broadcasted_iota(jnp.int32, numer.shape, 1)
            numer = jnp.where(lane == channels, top, numer).astype(BF)
            outgoing[image, step, :, :, :, 0:padded] = numer.reshape(
                place.nx, 2, lat_rows, padded
            )

        local_copy(weights.at[image], weights_out.at[image])
        last = pl.ds(lanes - 128, 128)
        local_copy(
            outgoing.at[image, :, :, :, :, last], sent_out.at[image]
        )
        return [
            links.push(
                outgoing.at[image, :, :, 1 - c], paired.at[image], z, p + 1 - 2 * c
            )
        ]

    def merge(image, pair):
        arrived(pair)
        mine = outgoing[image, :, :, c].reshape(rows_here, lanes).astype(jnp.float32)
        other = paired[image].reshape(rows_here, lanes).astype(jnp.float32)
        my_top = mine[:, channels : channels + 1]
        other_top = other[:, channels : channels + 1]
        top = jnp.maximum(my_top, other_top)
        lane = lax.broadcasted_iota(jnp.int32, mine.shape, 1)
        both = jnp.exp(my_top - top) * mine + jnp.exp(other_top - top) * other
        both = jnp.where(lane == channels, top, both)
        merged[image] = both.astype(BF).reshape(place.ny, place.nx, lat_rows, lanes)
        chip = y * place.nx + x
        chips = place.ny * place.nx
        local_copy(merged.at[image, y, x], landed.at[chip, image])
        copies = []
        for step in range(1, chips):
            q = lax.rem(chip + step, chips)
            copies.append(
                links.push(
                    merged.at[image, q // place.nx, lax.rem(q, place.nx)],
                    landed.at[chip, image],
                    z,
                    2 * q + c,
                )
            )
        return copies

    for step in range(3, place.nz):
        first_m(step)
    core_m(0)
    pair = attend(0)
    sent = []
    for step in range(3, place.nz):
        second_m(step)
    core_m(1)
    for image in range(1, batches):
        following = attend(image)
        sent += merge(image - 1, pair)
        pair = following
        if image == 1:
            core_m(2)
    sent += merge(batches - 1, pair)
    for step in range(3, place.nz):
        core_m(step)
    arrived(sent)
    arrived(cores_m)
    links.drain()
    for copy in local[9:]:
        copy.wait()


def front_copies(nz, ny, nx, batches):
    both = nx + ny - 2
    count = 3 * (nz - 1) + 2 * nz * (both + max(nx, ny) - 1) + 2 * both
    count += 2 * nz * 2 * both + 3 + nz
    return count + batches * nx * ny


def front(dims, pixels, pixel_mask, gain_rows, proj_blocks, keyval_t, latents):
    nz, ny, nx = dims
    channels, batches, shard_pixels = pixels.shape
    lat_rows, width = latents.shape
    owned, mats, row_block, col_block = proj_blocks.shape
    keyval_rows = keyval_t.shape[0]
    group = 2 * ny * nx
    all_rows = lat_rows * group
    padded = ceil_to(channels + 2, 16)
    lanes = ceil_to(padded, 128)
    vmem = pl.BlockSpec(memory_space=pltpu.VMEM)
    anywhere = pl.BlockSpec(memory_space=pl.ANY)
    cube = (nz, ny, nx, 2)
    copies = front_copies(nz, ny, nx, batches)
    return pl.pallas_call(
        functools.partial(front_kernel, dims),
        out_shape=(
            jax.ShapeDtypeStruct(cube + (owned, row_block, col_block), BF),
            jax.ShapeDtypeStruct(cube + (keyval_rows, lanes), BF),
            jax.ShapeDtypeStruct((all_rows, width), BF),
            jax.ShapeDtypeStruct(cube + (3, owned, row_block, col_block), BF),
            jax.ShapeDtypeStruct((batches, padded, shard_pixels), BF),
            jax.ShapeDtypeStruct((batches, shard_pixels), jnp.float32),
            jax.ShapeDtypeStruct((batches, all_rows, shard_pixels), BF),
            jax.ShapeDtypeStruct((batches, ny, nx, 2, lat_rows, 128), BF),
            jax.ShapeDtypeStruct((ny * nx, batches, lat_rows, lanes), BF),
            jax.ShapeDtypeStruct((all_rows, lanes), BF),
            jax.ShapeDtypeStruct((all_rows, width), BF),
        ),
        in_specs=[anywhere] + [vmem] * 5,
        out_specs=(
            anywhere,
            anywhere,
            anywhere,
            anywhere,
            anywhere,
            vmem,
            anywhere,
            anywhere,
            anywhere,
            vmem,
            anywhere,
        ),
        scratch_shapes=[
            pltpu.VMEM(pixels.shape, BF),
            pltpu.VMEM((lanes, 128), jnp.float32),
            pltpu.VMEM((3, owned, row_block, col_block), BF),
            pltpu.VMEM(cube + (owned, row_block, col_block), BF),
            pltpu.VMEM(cube + (keyval_rows, lanes), BF),
            pltpu.VMEM(cube[1:] + (lat_rows, width), BF),
            pltpu.VMEM((all_rows, width), BF),
            pltpu.VMEM((all_rows, width), BF),
            pltpu.VMEM((batches, padded, shard_pixels), BF),
            pltpu.VMEM((batches, all_rows, shard_pixels), BF),
            pltpu.VMEM((batches, ny, nx, 2, lat_rows, lanes), BF),
            pltpu.VMEM((batches, ny, nx, lat_rows, lanes), BF),
            pltpu.VMEM((batches, ny, nx, lat_rows, lanes), BF),
            pltpu.SemaphoreType.DMA((copies,)),
            pltpu.SemaphoreType.DMA((copies,)),
            pltpu.SemaphoreType.DMA((14 + 3 * batches,)),
        ],
        compiler_params=pltpu.CompilerParams(
            collective_id=0, has_side_effects=True, vmem_limit_bytes=56 * 2**20
        ),
    )(
        pixels,
        pixel_mask,
        gain_rows,
        proj_blocks,
        keyval_t,
        latents,
    )


def add_low(former, latter):
    return (former.astype(jnp.float32) + latter.astype(jnp.float32)).astype(BF)


class Reduce:
    def __init__(self, place, links, term, buffers, along, base=0):
        self.place, self.links, self.term, self.along = place, links, term, along
        self.by_core, self.by_first, self.by_second, self.by_z = buffers
        self.base = base
        self.waiting = []

    def wait(self):
        arrived(self.waiting)
        self.waiting = []

    def push_core(self):
        place = self.place
        every = slice(None)
        self.waiting = [
            self.links.push(
                self.term.at[every, every, every, 1 - place.c],
                self.by_core,
                place.z,
                place.p + 1 - 2 * place.c,
            )
        ]

    def push_first(self):
        place = self.place
        self.wait()

        @pl.loop(0, self.by_core.shape[0])
        def _(level):
            self.by_core[level] = add_low(
                self.by_core[level], self.term[level, :, :, place.c]
            )

        every = slice(None)
        for step in range(1, place.nx if self.along == "x" else place.ny):
            if self.along == "x":
                xx = lax.rem(place.x + step, place.nx)
                source = self.by_core.at[every, every, xx]
                target = place.pix(place.y, xx, place.c)
            else:
                yy = lax.rem(place.y + step, place.ny)
                source = self.by_core.at[every, yy]
                target = place.pix(yy, place.x, place.c)
            self.waiting.append(
                self.links.push(source, self.by_first.at[step - 1], place.z, target)
            )

    def push_second(self):
        place = self.place
        self.wait()
        if self.along == "x":
            held = self.by_core[:, :, place.x].astype(jnp.float32)
        else:
            held = self.by_core[:, place.y].astype(jnp.float32)
        for slot in range(self.by_first.shape[0]):
            held = held + self.by_first[slot].astype(jnp.float32)
        self.by_first[0] = held.astype(BF)
        every = slice(None)
        for step in range(1, place.ny if self.along == "x" else place.nx):
            if self.along == "x":
                other = lax.rem(place.y + step, place.ny)
                target = place.pix(other, place.x, place.c)
            else:
                other = lax.rem(place.x + step, place.nx)
                target = place.pix(place.y, other, place.c)
            self.waiting.append(
                self.links.push(
                    self.by_first.at[0, every, other],
                    self.by_second.at[step - 1],
                    place.z,
                    target,
                )
            )

    def push_z(self):
        place = self.place
        self.wait()
        mine = place.y if self.along == "x" else place.x
        held = self.by_first[0, :, mine].astype(jnp.float32)
        for slot in range(self.by_second.shape[0]):
            held = held + self.by_second[slot].astype(jnp.float32)
        self.by_second[0] = held.astype(BF)
        self.sends = []
        for step in range(1, place.nz):
            zz = lax.rem(place.z - step + place.nz, place.nz)
            if self.base == 0:
                self.waiting.append(
                    self.links.push(
                        self.by_second.at[0, zz], self.by_z.at[step - 1], zz, place.p
                    )
                )
            else:
                level = jnp.maximum(zz - self.base, 0)
                copy = self.links.make(
                    self.by_second.at[0, level], self.by_z.at[step - 1], zz, place.p
                )
                pl.when(zz >= self.base)(copy.start)
                self.sends.append((zz, copy))

    def total(self):
        place = self.place
        level = place.z
        if self.base == 0:
            self.wait()
        else:
            level = jnp.maximum(place.z - self.base, 0)

            @pl.when(place.z >= self.base)
            def _():
                for _, copy in self.sends:
                    copy.wait_recv()

            for zz, copy in self.sends:
                pl.when(zz >= self.base)(copy.wait_send)
        held = self.by_second[0, level].astype(jnp.float32)
        return held, [self.by_z.at[slot] for slot in range(self.by_z.shape[0])]


def block_index(block, col_blocks, owned):
    every = slice(None)
    if 2 * owned == col_blocks:
        return (every, every, every, block // owned, block % owned)
    return (every, every, block // 2, block % 2, 0)


def back_kernel(
    dims,
    channels,
    landed,
    all_keyval,
    all_mats,
    normed_all,
    inverse,
    weights_all,
    sent_all,
    pixel_query,
    latents,
    gain_rows,
    grad_rows,
    mixed,
    pixel_grad,
    mats_grad,
    value_grad,
    query_total,
    gain_total,
    residual_total,
    came,
    values,
    mats,
    normed,
    weights,
    tops,
    attended_chan,
    attended,
    middle,
    mid_hat,
    mid_inverse,
    mid_normed,
    slope,
    hidden,
    grad_pre,
    grad_mid_normed,
    grad_mid,
    grad_attended,
    shares,
    query_turned,
    query_acc,
    back_turned,
    grad_scores,
    gain_cols,
    staged,
    terms,
    buffers,
    query_low,
    query_came,
    query_levels,
    gain_plane,
    gain_levels,
    residual_parts,
    residual_came,
    residual_levels,
    send_sems,
    recv_sems,
    local_sems,
):
    place = Place(*dims)
    links = Links(send_sems, recv_sems)
    z, y, x, c, p = place.z, place.y, place.x, place.c, place.p
    chips, batches, lat_rows, lanes = landed.shape
    group = place.group
    rows = batches * lat_rows
    all_rows = group * lat_rows
    width = latents.shape[1]
    padded, shard_pixels = normed_all.shape[1:]
    owned, row_block, col_block = all_mats.shape[5:]
    col_blocks = width // col_block
    every = slice(None)
    tile = 256
    tiles = width // tile
    local = []

    def local_copy(source, target):
        copy = pltpu.make_async_copy(source, target, local_sems.at[len(local)])
        copy.start()
        local.append(copy)
        return copy

    came_copy = local_copy(landed, came)
    values_copy = local_copy(all_keyval.at[pl.ds(place.nz // 2, place.nz // 2)], values)
    mats_copies = []
    for mat in range(3):
        copies = []
        for block in range(col_blocks):
            where = block_index(block, col_blocks, owned)
            source = all_mats.at[where[:4] + (mat,) + where[4:]]
            cols = pl.ds(block * col_block, col_block)
            lead = (mat,) + (every,) * (len(mats.shape) - 2)
            copies.append(local_copy(source, mats.at[lead + (cols,)]))
        mats_copies.append(copies)
    tops_copy = local_copy(sent_all, tops)

    def fetch(image):
        slot = image % 2
        return [
            local_copy(normed_all.at[image], normed.at[slot]),
            local_copy(weights_all.at[image], weights.at[slot]),
        ]

    fetched = [fetch(0), fetch(1)]
    place.barrier()

    def columns_of(mat, index):
        lead = (mat,) + (every,) * (len(mats.shape) - 2)
        return mats[lead + (slice(index * tile, (index + 1) * tile),)].reshape(width, tile)

    def rows_of(mat, index):
        return mats[mat, index].reshape(-1, width)

    row_tile = width // place.nz

    came_copy.wait()
    lane = lax.broadcasted_iota(jnp.int32, (rows, lanes), 1)
    parts = [came[g].reshape(rows, lanes).astype(jnp.float32) for g in range(chips)]
    top = [part[:, channels : channels + 1] for part in parts]
    peak = functools.reduce(jnp.maximum, top)
    factor = [jnp.exp(value - peak) for value in top]
    denominator = sum(f * part[:, channels + 1 : channels + 2] for f, part in zip(factor, parts))
    summed = sum(f * part for f, part in zip(factor, parts))
    attended_chan[...] = jnp.where(lane < channels, summed / denominator, 0.0).astype(BF)

    values_copy.wait()
    value_t = values[...].reshape(width, lanes)
    attended[...] = lax.dot_general(
        attended_chan[...], value_t, NT, preferred_element_type=jnp.float32
    ).astype(BF)
    arrived_local(mats_copies[0])
    for index in range(tiles):
        cols = slice(index * tile, (index + 1) * tile)
        own = latents[:, cols]
        middle[:, cols] = jnp.concatenate([own] * batches, axis=0) + jnp.dot(
            attended[...], columns_of(0, index), preferred_element_type=jnp.float32
        )

    @pl.loop(0, rows // lat_rows)
    def _(step):
        part = pl.ds(pl.multiple_of(step * lat_rows, lat_rows), lat_rows)
        value = middle[part, :]
        value = value - jnp.mean(value, axis=1, keepdims=True)
        scale = lax.rsqrt(jnp.mean(value * value, axis=1, keepdims=True) + EPSILON)
        value = value * scale
        mid_hat[part, :] = value
        mid_inverse[part, :] = jnp.broadcast_to(scale, (lat_rows, 128))
        mid_normed[part, :] = (value * gain_rows[2:3, :]).astype(BF)

    arrived_local(mats_copies[1])
    for index in range(tiles):
        cols = slice(index * tile, (index + 1) * tile)
        pre = jnp.dot(mid_normed[...], columns_of(1, index), preferred_element_type=jnp.float32)
        below = 0.5 + 0.5 * lax.erf(pre * 0.5**0.5)
        hidden[:, cols] = (pre * below).astype(BF)
        slope[:, cols] = below + pre * jnp.exp(-0.5 * pre * pre) * (0.5 / math.pi) ** 0.5

    half_rows = row_block // 2

    def store_term(targets, left, right):
        turned = left[...].T
        for pair in range(col_blocks // 2):
            cols = slice(2 * pair * col_block, 2 * (pair + 1) * col_block)
            product = jnp.dot(turned, right[:, cols], preferred_element_type=jnp.float32).astype(
                BF
            )
            for side in range(2):
                where = block_index(2 * pair + side, col_blocks, owned)
                block = product[:, side * col_block : (side + 1) * col_block]
                taken = 0
                for target in targets:
                    height = target.shape[-2]
                    pieces = block.reshape(-1, row_block, col_block)[:, taken : taken + height]
                    taken += height
                    shape = target.shape
                    lead = shape[:3] if 2 * owned == col_blocks else shape[:2]
                    target[where] = pieces.reshape(lead + (height, col_block))

    pairs = []
    for index in range(3):
        pairs.append(
            [
                Reduce(place, links, terms[2 * index + side], buffers[2 * index + side], along)
                for side, along in enumerate("xy")
            ]
        )
    down, inward, outer = pairs
    value_job = Reduce(place, links, terms[6], buffers[6], "x", place.nz // 2)
    store_term(terms[0:2], hidden, grad_rows)
    for job in down:
        job.push_core()

    arrived_local(mats_copies[2])
    for index in range(place.nz):
        cols = slice(index * row_tile, (index + 1) * row_tile)
        grad_hidden = lax.dot_general(
            grad_rows[...], rows_of(2, index), NT, preferred_element_type=jnp.float32
        )
        grad_pre[:, cols] = (
            grad_hidden.astype(BF).astype(jnp.float32) * slope[:, cols]
        ).astype(BF)
    for job in down:
        job.push_first()
    gain_plane[p] = jnp.zeros(gain_plane.shape[1:], jnp.float32)
    for index in range(place.nz):
        cols = slice(index * row_tile, (index + 1) * row_tile)
        part = lax.dot_general(
            grad_pre[...], rows_of(1, index), NT, preferred_element_type=jnp.float32
        )
        grad_mid_normed[:, cols] = part
        summed_rows = jnp.sum(part * mid_hat[:, cols], axis=0, keepdims=True)
        for sub in range(row_tile // 128):
            row = index * (row_tile // 128) + sub
            gain_plane[p, row : row + 1, :] = summed_rows[:, sub * 128 : (sub + 1) * 128]

    @pl.loop(0, rows // lat_rows)
    def _(step):
        part = pl.ds(pl.multiple_of(step * lat_rows, lat_rows), lat_rows)
        grad = grad_mid_normed[part, :] * gain_rows[2:3, :]
        hat = mid_hat[part, :]
        grad = (
            grad
            - jnp.mean(grad, axis=1, keepdims=True)
            - hat * jnp.mean(grad * hat, axis=1, keepdims=True)
        ) * mid_inverse[part, 0:1]
        grad_mid[part, :] = (grad_rows[part, :].astype(jnp.float32) + grad).astype(BF)

    for index in range(place.nz):
        cols = slice(index * row_tile, (index + 1) * row_tile)
        grad_attended[:, cols] = lax.dot_general(
            grad_mid[...], rows_of(0, index), NT, preferred_element_type=jnp.float32
        ).astype(BF)
    grad_chan = jnp.dot(grad_attended[...], value_t, preferred_element_type=jnp.float32)
    products = attended_chan[...].astype(jnp.float32) * grad_chan
    row_delta = jnp.sum(products, axis=1, keepdims=True)
    channel_sums = jnp.sum(products, axis=0, keepdims=True)
    for sub in range(lanes // 128):
        row = width // 128 + sub
        gain_plane[p, row : row + 1, :] = channel_sums[:, sub * 128 : (sub + 1) * 128]
    back = jnp.where(lane == channels + 1, row_delta, grad_chan) / denominator
    back = jnp.where(lane == channels, peak, back)
    shares[y, x, c] = back.astype(BF).reshape(batches, lat_rows, lanes)

    share_first = []
    for image in range(batches):
        share_first.append(
            place.push_first(links, shares, (), (image,), "xy"[image % 2])
        )
    gain_sent = []
    for step in range(1, group):
        own = gain_plane.at[p]
        gain_sent.append(links.push(own, own, z, lax.rem(p + step, group)))
    share_second = []
    share_core = []

    def share_on(image):
        arrived(share_first[image])
        share_second.append(place.push_second(links, shares, (), (image,), "xy"[image % 2]))

    def share_pair(image):
        arrived(share_second[image])
        held = shares.at[:, :, c, image]
        share_core.append([links.push(held, held, z, p + 1 - 2 * c)])

    store_term(terms[2:4], mid_normed, grad_pre)
    for job in inward:
        job.push_core()
    share_on(0)
    share_on(1)
    store_term(terms[4:6], attended, grad_mid)
    for job in outer:
        job.push_core()
    share_on(2)
    share_on(3)
    terms[6][...] = (
        jnp.dot(grad_attended[...].T, attended_chan[...], preferred_element_type=jnp.float32)
        .astype(BF)
        .reshape(terms[6].shape)
    )
    value_job.push_core()
    residual = sum(
        grad_mid[image * lat_rows : (image + 1) * lat_rows].astype(jnp.float32)
        for image in range(batches)
    )
    part_width = width // place.nz
    residual_sent = []
    for zz in range(place.nz):
        residual_parts[zz] = residual[:, zz * part_width : (zz + 1) * part_width].astype(BF)
    for step in range(1, place.nz):
        zz = lax.rem(z + step, place.nz)
        residual_sent.append(
            links.push(residual_parts.at[zz], residual_came.at[step - 1], zz, p)
        )
    share_pair(0)
    share_pair(1)
    for job in inward:
        job.push_first()
    for job in down:
        job.push_second()

    lane_all = lax.broadcasted_iota(jnp.int32, (all_rows, lanes), 1)
    query_turned[...] = jnp.where(
        lane_all < channels, pixel_query[...].astype(jnp.float32), 0.0
    ).T[0:padded].astype(BF)
    query_acc[...] = jnp.zeros(query_acc.shape, jnp.float32)
    gain_cols[0] = jnp.broadcast_to(gain_rows[1:2, 0:lanes], (128, lanes)).T[0:padded]
    gain_cols[1] = jnp.broadcast_to(gain_rows[3:4, 0:lanes], (128, lanes)).T[0:padded]
    chunk = min(512, shard_pixels)
    tops_copy.wait()

    def attend_query(image):
        slot = image % 2
        arrived(share_core[image])
        arrived_local(fetched[image])
        back = shares[:, :, :, image].reshape(all_rows, lanes).astype(jnp.float32)
        top = tops[image].reshape(all_rows, 128).astype(jnp.float32)[
            :, channels - (lanes - 128) :
        ][:, 0:1]
        share = jnp.exp(top - back[:, channels : channels + 1])
        back = jnp.where(lane_all == channels, 0.0, back * share)
        back = jnp.where(lane_all > channels + 1, 0.0, back)
        back_low = jnp.where(lane_all == channels + 1, -back, back).astype(BF)[:, 0:padded]
        back_turned[image] = jnp.where(lane_all < channels, back, 0.0).T[0:padded].astype(BF)

        @pl.loop(0, shard_pixels // chunk)
        def _(step):
            cols = pl.ds(pl.multiple_of(step * chunk, chunk), chunk)
            normed_chunk = normed[slot, :, cols]
            grad_weights = jnp.dot(back_low, normed_chunk, preferred_element_type=jnp.float32)
            grad_chunk = (weights[slot, :, cols].astype(jnp.float32) * grad_weights).astype(BF)
            grad_scores[image, :, cols] = grad_chunk
            query_acc[:, 0:padded] += lax.dot_general(
                grad_chunk, normed_chunk, NT, preferred_element_type=jnp.float32
            )

        if image + 2 < batches:
            fetched.append(fetch(image + 2))

    order = list(range(2, batches)) + [0, 1]
    staged_out = []

    def attend_pixels(turn):
        image = order[turn]
        slot = image % 2
        if turn >= 2:
            arrived_local(fetched[batches + turn - 2])
            staged_out[turn - 2].wait()

        @pl.loop(0, shard_pixels // chunk)
        def _(step):
            cols = pl.ds(pl.multiple_of(step * chunk, chunk), chunk)
            grad_normed = jnp.dot(
                query_turned[...], grad_scores[image, :, cols], preferred_element_type=jnp.float32
            ) + jnp.dot(
                back_turned[image], weights[slot, :, cols], preferred_element_type=jnp.float32
            )
            normal = normed[slot, :, cols].astype(jnp.float32)
            second_mean = jnp.sum(grad_normed * normal, axis=0, keepdims=True) / channels
            spread = jnp.concatenate([gain_cols[0]] * (chunk // 128), axis=1)
            spread_back = jnp.concatenate([gain_cols[1]] * (chunk // 128), axis=1)
            grad_hat = grad_normed * spread
            first_mean = jnp.sum(grad_hat, axis=0, keepdims=True) / channels
            result = (grad_hat - first_mean - normal * spread_back * second_mean) * inverse[
                image : image + 1, cols
            ]
            staged[turn % 2, :, cols] = result[0:channels].astype(BF)

        staged_out.append(local_copy(staged.at[turn % 2], pixel_grad.at[image]))
        if turn + 2 < batches:
            fetched.append(fetch(order[turn + 2]))

    attend_query(0)
    share_pair(2)
    share_pair(3)
    attend_query(1)
    arrived(gain_sent)
    gain_levels[z] = sum(gain_plane[g] for g in range(group))
    gain_up = []
    for step in range(1, place.nz):
        own = gain_levels.at[z]
        gain_up.append(links.push(own, own, lax.rem(z + step, place.nz), p))
    arrived(residual_sent)
    residual_levels[z] = (
        residual_parts[z].astype(jnp.float32)
        + sum(residual_came[slot].astype(jnp.float32) for slot in range(place.nz - 1))
    ).astype(BF)
    residual_up = []
    for step in range(1, place.nz):
        own = residual_levels.at[z]
        residual_up.append(links.push(own, own, lax.rem(z + step, place.nz), p))
    attend_query(2)
    for job in down:
        job.push_z()
    attend_query(3)

    query_low[...] = query_acc[...].astype(BF)
    query_sent = []
    for step in range(1, group):
        q = lax.rem(p + step, group)
        part = pl.ds(pl.multiple_of(q * lat_rows, lat_rows), lat_rows)
        query_sent.append(links.push(query_low.at[part], query_came.at[step - 1], z, q))
    for job in outer:
        job.push_first()
    value_job.push_first()
    attend_pixels(0)
    for job in inward:
        job.push_second()
    arrived(query_sent)
    own_rows = pl.ds(pl.multiple_of(p * lat_rows, lat_rows), lat_rows)
    held = query_acc[own_rows, :]
    for slot in range(group - 1):
        held = held + query_came[slot].astype(jnp.float32)
    query_levels[z] = held.astype(BF)
    query_up = []
    for step in range(1, place.nz):
        own = query_levels.at[z]
        query_up.append(links.push(own, own, lax.rem(z + step, place.nz), p))
    attend_pixels(1)
    arrived(query_up)
    query_total[p] = sum(query_levels[zz].astype(jnp.float32) for zz in range(place.nz)).astype(BF)
    query_all = []
    for step in range(1, group):
        own = query_total.at[p]
        query_all.append(links.push(own, own, z, lax.rem(p + step, group)))
    attend_pixels(2)
    for job in outer:
        job.push_second()
    value_job.push_second()
    for job in inward:
        job.push_z()
    attend_pixels(3)
    for index in range(tiles):
        cols = slice(index * tile, (index + 1) * tile)
        mixed[:, cols] = (
            middle[:, cols]
            + jnp.dot(hidden[...], columns_of(2, index), preferred_element_type=jnp.float32)
        ).astype(BF)
    for job in outer:
        job.push_z()
    value_job.push_z()

    def finish(job, target):
        held, came_z = job.total()
        for part in came_z:
            held = held + part[...].astype(jnp.float32)
        target[...] = held

    def finish_mat(mat, jobs):
        for side, job in enumerate(jobs):
            finish(job, mats_grad.at[mat, :, pl.ds(side * half_rows, half_rows)])

    finish_mat(2, down)
    arrived(gain_up)
    gain_total[...] = sum(gain_levels[zz] for zz in range(place.nz))
    arrived(residual_up)
    for zz in range(place.nz):
        residual_total[:, zz * part_width : (zz + 1) * part_width] = residual_levels[zz].astype(
            jnp.float32
        )
    finish_mat(1, inward)
    finish_mat(0, outer)
    held, came_z = value_job.total()
    for part in came_z:
        held = held + part[...].astype(jnp.float32)
    value_grad[...] = jnp.where(place.z >= place.nz // 2, held, 0.0)
    arrived(query_all)
    links.drain()
    for copy in staged_out[batches - 2 :]:
        copy.wait()


def arrived_local(copies):
    for copy in copies:
        copy.wait()


def back_copies(nz, ny, nx, batches):
    group = 2 * ny * nx
    both = nx + ny - 2
    count = batches // 2 * 2 * both + batches
    count += 7 * (1 + both + nz - 1)
    count += 4 * (nz - 1) + 3 * (group - 1)
    return count


def back(dims, channels, gathered, latents, gain_rows, mixed_grad):
    landed, all_keyval, all_mats, normed_all, inverse, weights_all, sent_all, pixel_query = gathered
    nz, ny, nx = dims
    batches, lat_rows, lanes = landed.shape[1:]
    group = 2 * ny * nx
    rows = batches * lat_rows
    all_rows = group * lat_rows
    width = latents.shape[1]
    padded, shard_pixels = normed_all.shape[1:]
    owned, row_block, col_block = all_mats.shape[5:]
    keyval_rows = all_keyval.shape[4]
    half_rows = row_block // 2
    vmem = pl.BlockSpec(memory_space=pltpu.VMEM)
    anywhere = pl.BlockSpec(memory_space=pl.ANY)
    lead = (nz, ny, nx) if 2 * owned * col_block == width else (nz, ny)
    cube = (nz, ny, nx, 2)
    inners = [(nz, (owned, half_rows, col_block), along) for along in "xyxyxy"]
    inners.append((nz // 2, (keyval_rows, lanes), "x"))
    terms = [pltpu.VMEM((levels, ny, nx, 2) + inner, BF) for levels, inner, _ in inners]
    buffers = []
    for levels, inner, along in inners:
        one, two = (nx, ny) if along == "x" else (ny, nx)
        buffers.append(
            [
                pltpu.VMEM((levels, ny, nx) + inner, BF),
                pltpu.VMEM((one - 1, levels, two) + inner, BF),
                pltpu.VMEM((two - 1, levels) + inner, BF),
                pltpu.VMEM((nz - 1,) + inner, BF),
            ]
        )
    wide = lambda kind: pltpu.VMEM((rows, width), kind)
    copies = back_copies(nz, ny, nx, batches)
    return pl.pallas_call(
        functools.partial(back_kernel, dims, channels),
        out_shape=(
            jax.ShapeDtypeStruct((rows, width), BF),
            jax.ShapeDtypeStruct((batches, channels, shard_pixels), BF),
            jax.ShapeDtypeStruct((3, owned, row_block, col_block), jnp.float32),
            jax.ShapeDtypeStruct((keyval_rows, lanes), jnp.float32),
            jax.ShapeDtypeStruct((group, lat_rows, lanes), BF),
            jax.ShapeDtypeStruct((16, 128), jnp.float32),
            jax.ShapeDtypeStruct((lat_rows, width), jnp.float32),
        ),
        in_specs=[
            anywhere,
            anywhere,
            anywhere,
            anywhere,
            vmem,
            anywhere,
            anywhere,
            vmem,
            vmem,
            vmem,
            vmem,
        ],
        out_specs=(vmem, anywhere, vmem, vmem, vmem, vmem, vmem),
        scratch_shapes=[
            pltpu.VMEM((ny * nx, batches, lat_rows, lanes), BF),
            pltpu.VMEM((nz // 2, ny, nx, 2, keyval_rows, lanes), BF),
            pltpu.VMEM((3,) + lead + (row_block, width), BF),
            pltpu.VMEM((2, padded, shard_pixels), BF),
            pltpu.VMEM((2, all_rows, shard_pixels), BF),
            pltpu.VMEM((batches, ny, nx, 2, lat_rows, 128), BF),
            pltpu.VMEM((rows, lanes), BF),
            wide(BF),
            wide(jnp.float32),
            wide(jnp.float32),
            pltpu.VMEM((rows, 128), jnp.float32),
            wide(BF),
            wide(jnp.float32),
            wide(BF),
            wide(BF),
            wide(jnp.float32),
            wide(BF),
            wide(BF),
            pltpu.VMEM(cube[1:] + (batches, lat_rows, lanes), BF),
            pltpu.VMEM((padded, all_rows), BF),
            pltpu.VMEM((all_rows, lanes), jnp.float32),
            pltpu.VMEM((batches, padded, all_rows), BF),
            pltpu.VMEM((batches, all_rows, shard_pixels), BF),
            pltpu.VMEM((2, padded, 128), jnp.float32),
            pltpu.VMEM((2, channels, shard_pixels), BF),
            terms,
            buffers,
            pltpu.VMEM((all_rows, lanes), BF),
            pltpu.VMEM((group - 1, lat_rows, lanes), BF),
            pltpu.VMEM((nz, lat_rows, lanes), BF),
            pltpu.VMEM((group, 16, 128), jnp.float32),
            pltpu.VMEM((nz, 16, 128), jnp.float32),
            pltpu.VMEM((nz, lat_rows, width // nz), BF),
            pltpu.VMEM((nz - 1, lat_rows, width // nz), BF),
            pltpu.VMEM((nz, lat_rows, width // nz), BF),
            pltpu.SemaphoreType.DMA((copies,)),
            pltpu.SemaphoreType.DMA((copies,)),
            pltpu.SemaphoreType.DMA((3 + 3 * (width // col_block) + 5 * batches,)),
        ],
        compiler_params=pltpu.CompilerParams(
            collective_id=1, has_side_effects=True, vmem_limit_bytes=61 * 2**20
        ),
    )(
        landed,
        all_keyval,
        all_mats,
        normed_all,
        inverse,
        weights_all,
        sent_all,
        pixel_query,
        latents,
        gain_rows,
        mixed_grad.reshape(rows, width),
    )


TN = (((0,), (0,)), ((), ()))


def tail_kernel(
    dims,
    channels,
    query_total,
    residual_total,
    mats_grad,
    value_grad,
    proj_blocks,
    proj_left,
    proj_right,
    left_roots,
    right_roots,
    keyval_weight,
    keyval_second,
    latents,
    latent_second,
    gain_rows,
    query_in,
    lat_normed_in,
    query_blocks,
    all_keyval,
    pixel_low,
    pixel_query,
    gain_total,
    pixel_grad,
    proj_grad,
    left_new,
    right_new,
    proj_new,
    keyval_grad,
    keyval_second_new,
    keyval_new,
    latent_grad,
    latent_second_new,
    latent_new,
    lat_gain_grad,
    channel_gain_grad,
    query,
    lat_normed,
    query_weight,
    keys,
    pixel_came,
    pixel_wide,
    grad_query,
    grad_normed,
    query_grad,
    key_rows,
    local_sems,
):
    place = Place(*dims)
    group, lat_rows, lanes = query_total.shape
    all_rows = group * lat_rows
    width = latents.shape[1]
    batches = pixel_low.shape[0]
    owned, mats, row_block, col_block = proj_blocks.shape
    col_blocks = width // col_block
    keyval_rows = keyval_weight.shape[0]
    device = place.z * group + place.p
    every = slice(None)
    local = []

    def local_copy(source, target):
        copy = pltpu.make_async_copy(source, target, local_sems.at[len(local)])
        copy.start()
        local.append(copy)
        return copy

    keys_copy = local_copy(all_keyval.at[pl.ds(0, place.nz // 2)], keys)
    weight_copies = []
    for block in range(col_blocks):
        lead = (every,) * (len(query_weight.shape) - 1)
        weight_copies.append(
            local_copy(
                query_blocks.at[block_index(block, col_blocks, owned)],
                query_weight.at[lead + (pl.ds(block * col_block, col_block),)],
            )
        )
    normed_copy = local_copy(lat_normed_in, lat_normed)
    query_copy = local_copy(query_in, query)
    pixel_copies = [local_copy(pixel_low.at[i], pixel_came.at[i]) for i in range(batches)]
    pixel_sent = []

    def widen(image):
        pixel_copies[image].wait()

        @pl.loop(0, pixel_low.shape[2] // 256)
        def _(step):
            cols = pl.ds(pl.multiple_of(step * 256, 256), 256)
            pixel_wide[image, :, cols] = pixel_came[image, :, cols].astype(jnp.float32)

        pixel_sent.append(local_copy(pixel_wide.at[image], pixel_grad.at[:, image]))

    def moments(weight, grad, second, rate, second_out, weight_out):
        second_value = STAT_DECAY * second[...] + (1.0 - STAT_DECAY) * grad * grad
        second_out[...] = second_value
        weight_out[...] = weight[...] - rate * grad / (jnp.sqrt(second_value) + MOMENT_FLOOR)

    def precondition(mat, index, grad):
        low = grad.astype(BF)
        proj_grad[index, mat] = grad
        left_new[index, mat] = STAT_DECAY * proj_left[index, mat] + (
            1.0 - STAT_DECAY
        ) * lax.dot_general(low, low, NT, preferred_element_type=jnp.float32)
        right_new[index, mat] = STAT_DECAY * proj_right[index, mat] + (
            1.0 - STAT_DECAY
        ) * lax.dot_general(low, low, TN, preferred_element_type=jnp.float32)
        step = jnp.dot(
            left_roots[index, mat].astype(BF), low, preferred_element_type=jnp.float32
        ).astype(BF)
        step = jnp.dot(
            step, right_roots[index, mat].astype(BF), preferred_element_type=jnp.float32
        )
        proj_new[index, mat] = proj_blocks[index, mat] - MATRIX_RATE * step

    for mat in range(3):
        for index in range(owned):
            precondition(mat + 1, index, mats_grad[mat, index])
    widen(0)
    keys_copy.wait()
    scale = width ** (-0.5)
    query_sum = query_total[...].reshape(all_rows, lanes)
    key_t = keys[...].reshape(width, lanes)
    products = query_sum.astype(jnp.float32) * pixel_query[...].astype(jnp.float32)
    sums = jnp.sum(products, axis=0, keepdims=True)
    first = width // 128
    for sub in range(lanes // 128):
        cols = slice(sub * 128, (sub + 1) * 128)
        channel_gain_grad[:, cols] = (
            sums[:, cols] + gain_total[first + sub : first + sub + 1, :]
        ) * gain_rows[3:4, cols]
    for start in range(0, width, 256):
        grad_query[:, start : start + 256] = (
            lax.dot_general(
                query_sum, key_t[start : start + 256], NT, preferred_element_type=jnp.float32
            )
            * scale
        ).astype(BF)
    widen(1)
    arrived_local(weight_copies)
    normed_copy.wait()
    row_tile = width // place.nz
    for index in range(place.nz):
        cols = slice(index * row_tile, (index + 1) * row_tile)
        part = lax.dot_general(
            grad_query[...],
            query_weight[index].reshape(row_tile, width),
            NT,
            preferred_element_type=jnp.float32,
        )
        grad_normed[:, cols] = part
        lat_gain_grad[:, cols] = (
            jnp.sum(part * lat_normed[:, cols].astype(jnp.float32), axis=0, keepdims=True)
            / gain_rows[0:1, cols]
        )
    widen(2)
    values = latents[...]
    centered = values - jnp.mean(values, axis=1, keepdims=True)
    inverse = lax.rsqrt(jnp.mean(centered * centered, axis=1, keepdims=True) + EPSILON)
    hat = centered * inverse
    own = pl.ds(pl.multiple_of(place.p * lat_rows, lat_rows), lat_rows)
    grad = grad_normed[own, :] * gain_rows[0:1, :]
    grad = (
        grad
        - jnp.mean(grad, axis=1, keepdims=True)
        - hat * jnp.mean(grad * hat, axis=1, keepdims=True)
    ) * inverse
    grad = residual_total[...] + grad
    latent_grad[...] = grad
    moments(latents, grad, latent_second, LATENT_RATE, latent_second_new, latent_new)

    block_row = device * owned // col_blocks
    block_col = lax.rem(device * owned, col_blocks)
    per_lane = 128 // row_block
    rows = pl.ds(pl.multiple_of(block_row // per_lane * 128, 128), 128)
    cols = pl.ds(pl.multiple_of(block_col * col_block, col_block), owned * col_block)
    query_grad[...] = lax.dot_general(
        lat_normed[:, rows], grad_query[:, cols], TN, preferred_element_type=jnp.float32
    )
    part = pl.ds(pl.multiple_of(lax.rem(block_row, per_lane) * row_block, row_block), row_block)
    for index in range(owned):
        precondition(0, index, query_grad[part, index * col_block : (index + 1) * col_block])
    widen(3)

    query_copy.wait()
    half_devices = width // keyval_rows
    start = lax.rem(device, half_devices) * keyval_rows
    cols = pl.ds(pl.multiple_of(start // 128 * 128, 128), 128)
    key_rows[...] = (
        lax.dot_general(query[:, cols], query_sum, TN, preferred_element_type=jnp.float32) * scale
    )
    part = pl.ds(pl.multiple_of(lax.rem(start, 128), keyval_rows), keyval_rows)
    grad = jnp.where(device < half_devices, key_rows[part, :], value_grad[...])[:, 0:channels]
    keyval_grad[...] = grad
    moments(keyval_weight, grad, keyval_second, KEYVAL_RATE, keyval_second_new, keyval_new)
    for copy in pixel_sent:
        copy.wait()


def tail(
    dims,
    query_total,
    residual_total,
    mats_grad,
    value_grad,
    owned_arrays,
    gain_rows,
    query,
    lat_normed,
    query_blocks,
    all_keyval,
    pixel_low,
    pixel_query,
    gain_total,
):
    nz, ny, nx = dims
    proj_blocks, keyval_weight, latents = owned_arrays[0], owned_arrays[5], owned_arrays[7]
    group, lat_rows, lanes = query_total.shape
    all_rows = group * lat_rows
    width = latents.shape[1]
    batches, channels, shard_pixels = pixel_low.shape
    owned, mats, row_block, col_block = proj_blocks.shape
    lead = (nz, ny, nx) if 2 * owned * col_block == width else (nz, ny)
    vmem = pl.BlockSpec(memory_space=pltpu.VMEM)
    anywhere = pl.BlockSpec(memory_space=pl.ANY)
    like = lambda array: jax.ShapeDtypeStruct(array.shape, array.dtype)
    wide = jax.ShapeDtypeStruct((channels, batches, shard_pixels), jnp.float32)
    results = [
        wide,
        like(proj_blocks),
        like(owned_arrays[1]),
        like(owned_arrays[2]),
        like(proj_blocks),
        like(keyval_weight),
        like(keyval_weight),
        like(keyval_weight),
        like(latents),
        like(latents),
        like(latents),
        jax.ShapeDtypeStruct((1, width), jnp.float32),
        jax.ShapeDtypeStruct((1, lanes), jnp.float32),
    ]
    return pl.pallas_call(
        functools.partial(tail_kernel, dims, channels),
        out_shape=results,
        in_specs=[vmem] * 14 + [anywhere] * 5 + [vmem] * 2,
        out_specs=[anywhere] + [vmem] * 12,
        scratch_shapes=[
            pltpu.VMEM((all_rows, width), BF),
            pltpu.VMEM((all_rows, width), BF),
            pltpu.VMEM(lead + (row_block, width), BF),
            pltpu.VMEM((nz // 2, ny, nx, 2) + all_keyval.shape[4:], BF),
            pltpu.VMEM((batches, channels, shard_pixels), BF),
            pltpu.VMEM((batches, channels, shard_pixels), jnp.float32),
            pltpu.VMEM((all_rows, width), BF),
            pltpu.VMEM((all_rows, width), jnp.float32),
            pltpu.VMEM((128, owned * col_block), jnp.float32),
            pltpu.VMEM((128, lanes), jnp.float32),
            pltpu.SemaphoreType.DMA((3 + width // col_block + 2 * batches,)),
        ],
        compiler_params=pltpu.CompilerParams(vmem_limit_bytes=56 * 2**20),
    )(
        query_total,
        residual_total,
        mats_grad,
        value_grad,
        *owned_arrays,
        gain_rows,
        query,
        lat_normed,
        query_blocks,
        all_keyval,
        pixel_low,
        pixel_query,
        gain_total,
    )


def body(
    pixels,
    pixel_mask,
    proj_blocks,
    proj_left,
    proj_right,
    left_roots,
    right_roots,
    keyval_weight,
    keyval_second,
    latents,
    latent_second,
    gains,
    gain_second,
    mixed_grad,
):
    batches, channels, shard_pixels = pixels.shape
    lat_rows, width = latents.shape
    groups = lax.axis_size("pix")
    scale = width ** (-0.5)

    lat_gain = gains[:width]
    in_gain = gains[width : width + channels]
    mlp_gain = gains[width + channels :]
    side = math.isqrt(groups // 2)
    dims = (lax.axis_size("samp"), side, side)
    widen = lambda row: jnp.pad(row, (0, width - row.shape[0]))
    gain_rows = jnp.stack([lat_gain, widen(in_gain), mlp_gain, widen(1.0 / in_gain)])
    keyval_own = keyval_weight.T
    (
        query_blocks,
        keyval_t,
        lat_normed,
        mats,
        normed_all,
        inverse_all,
        weights_all,
        sent_all,
        landed,
        pixel_query,
        query,
    ) = front(
        dims, pixels.swapaxes(0, 1), pixel_mask, gain_rows, proj_blocks, keyval_own, latents
    )
    gathered = (
        landed,
        keyval_t,
        mats,
        normed_all,
        inverse_all,
        weights_all,
        sent_all,
        pixel_query,
    )
    mixed, pixel_low, mats_grad, value_grad, query_total, gain_total, residual_total = back(
        dims, channels, gathered, latents, gain_rows, mixed_grad
    )
    (
        pixel_grad,
        proj_grad,
        left_new,
        right_new,
        proj_new,
        keyval_grad,
        keyval_second_new,
        keyval_new,
        latent_grad,
        latent_second_new,
        latent_new,
        lat_gain_grad,
        channel_gain_grad,
    ) = tail(
        dims,
        query_total,
        residual_total,
        mats_grad,
        value_grad,
        (
            proj_blocks,
            proj_left,
            proj_right,
            left_roots,
            right_roots,
            keyval_own,
            keyval_second.T,
            latents,
            latent_second,
        ),
        gain_rows,
        query,
        lat_normed,
        query_blocks,
        keyval_t,
        pixel_low,
        pixel_query,
        gain_total,
    )
    gain_sums = gain_total.reshape(-1)
    gain_grad = jnp.concatenate(
        [
            lat_gain_grad[0],
            channel_gain_grad[0, :channels],
            gain_sums[:width],
        ],
        axis=0,
    )
    gain_second_new, gain_new = moment_step(gains, gain_grad, gain_second, GAIN_RATE)
    return (
        mixed.reshape(batches, lat_rows, width),
        pixel_grad.swapaxes(0, 1),
        proj_grad,
        left_new,
        right_new,
        proj_new,
        keyval_grad.T,
        keyval_second_new.T,
        keyval_new.T,
        latent_grad,
        latent_second_new,
        latent_new,
        gain_grad,
        gain_second_new,
        gain_new,
    )


def solution(mesh):
    blocks = P(("samp", "pix"), None, None, None)
    columns = P(None, ("samp", "pix"))
    rows = P("pix", None)
    return jax.shard_map(
        body,
        mesh=mesh,
        in_specs=(
            P("samp", None, "pix"),
            P("samp", "pix"),
            blocks,
            blocks,
            blocks,
            blocks,
            blocks,
            columns,
            columns,
            rows,
            rows,
            P(),
            P(),
            P("samp", "pix", None),
        ),
        out_specs=(
            P("samp", "pix", None),
            P("samp", None, "pix"),
            blocks,
            blocks,
            blocks,
            blocks,
            columns,
            columns,
            columns,
            rows,
            rows,
            rows,
            P(),
            P(),
            P(),
        ),
        check_vma=False,
    )
```

```python
import functools
import math

import jax
import jax.numpy as jnp
from jax import lax
from jax.experimental import pallas as pl
from jax.experimental.pallas import tpu as pltpu
from jax.sharding import PartitionSpec as P

EPSILON = 1e-05
NEGATIVE = -1e30
HIGHEST = lax.Precision.HIGHEST
STAT_DECAY = 0.5
MATRIX_RATE = 0.5
KEYVAL_RATE = 0.05
LATENT_RATE = 0.7
GAIN_RATE = 0.6
MOMENT_FLOOR = 1e-08
BF = jnp.bfloat16
MESH = pl.DeviceIdType.MESH
NT = (((1,), (1,)), ((), ()))


def moment_step(weight, grad, second, rate):
    second_new = STAT_DECAY * second + (1.0 - STAT_DECAY) * grad * grad
    return (second_new, weight - rate * grad / (jnp.sqrt(second_new) + MOMENT_FLOOR))


def ceil_to(value, step):
    return -(-value // step) * step


class Links:
    def __init__(self, send_sems, recv_sems):
        self.send_sems = send_sems
        self.recv_sems = recv_sems
        self.used = 0
        self.started = []

    def make(self, source, target, samp, pix):
        copy = pltpu.make_async_remote_copy(
            src_ref=source,
            dst_ref=target,
            send_sem=self.send_sems.at[self.used],
            recv_sem=self.recv_sems.at[self.used],
            device_id=(samp, pix),
            device_id_type=MESH,
        )
        self.used += 1
        return copy

    def push(self, source, target, samp, pix):
        copy = self.make(source, target, samp, pix)
        copy.start()
        self.started.append(copy)
        return copy

    def drain(self):
        for copy in self.started:
            copy.wait_send()
        self.started = []


class Place:
    def __init__(self, nz, ny, nx):
        self.nz, self.ny, self.nx = nz, ny, nx
        self.group = ny * nx * 2
        self.z = lax.axis_index("samp")
        self.p = lax.axis_index("pix")
        self.c = lax.rem(self.p, 2)
        self.x = lax.rem(self.p // 2, nx)
        self.y = self.p // (2 * nx)

    def pix(self, y, x, c):
        return (y * self.nx + x) * 2 + c

    def barrier(self):
        semaphore = pltpu.get_barrier_semaphore()
        for step in range(1, self.nz):
            pl.semaphore_signal(
                semaphore,
                inc=1,
                device_id=(lax.rem(self.z + step, self.nz), self.p),
                device_id_type=MESH,
            )
        for step in range(1, self.group):
            pl.semaphore_signal(
                semaphore,
                inc=1,
                device_id=(self.z, lax.rem(self.p + step, self.group)),
                device_id_type=MESH,
            )
        pl.semaphore_wait(semaphore, self.nz - 1 + self.group - 1)

    def push_z(self, links, array, step):
        own = array.at[self.z, self.y, self.x, self.c]
        return [links.push(own, own, lax.rem(self.z - step + self.nz, self.nz), self.p)]

    def push_first(self, links, array, lead, sub, along):
        own = array.at[lead + (self.y, self.x, self.c) + sub]
        copies = []
        if along == "x":
            for step in range(1, self.nx):
                other = self.pix(self.y, lax.rem(self.x + step, self.nx), self.c)
                copies.append(links.push(own, own, self.z, other))
        else:
            for step in range(1, self.ny):
                other = self.pix(lax.rem(self.y + step, self.ny), self.x, self.c)
                copies.append(links.push(own, own, self.z, other))
        return copies

    def push_second(self, links, array, lead, sub, first):
        copies = []
        if first == "x":
            held = array.at[lead + (self.y, slice(None), self.c) + sub]
            for step in range(1, self.ny):
                other = self.pix(lax.rem(self.y + step, self.ny), self.x, self.c)
                copies.append(links.push(held, held, self.z, other))
        else:
            held = array.at[lead + (slice(None), self.x, self.c) + sub]
            for step in range(1, self.nx):
                other = self.pix(self.y, lax.rem(self.x + step, self.nx), self.c)
                copies.append(links.push(held, held, self.z, other))
        return copies

    def push_core(self, links, array, lead):
        held = array.at[lead + (slice(None), slice(None), self.c)]
        return [links.push(held, held, self.z, self.p + 1 - 2 * self.c)]


def arrived(copies):
    for copy in copies:
        copy.wait_recv()


def column_block(array, place, index, col_blocks, owned, sub=()):
    every = slice(None)
    if 2 * owned == col_blocks:
        block = array[(every, every, every, index // owned) + sub + (index % owned,)]
    else:
        block = array[(every, every, index // 2, index % 2) + sub + (0,)]
    return block.reshape(-1, block.shape[-1])


def column_pair(array, place, pair, col_blocks, owned, sub=()):
    return jnp.concatenate(
        [
            column_block(array, place, 2 * pair, col_blocks, owned, sub),
            column_block(array, place, 2 * pair + 1, col_blocks, owned, sub),
        ],
        axis=1,
    )


def front_kernel(
    dims,
    pixels,
    mask,
    gain_rows,
    own_proj,
    own_keyval,
    own_latents,
    all_query,
    all_keyval,
    all_latents,
    all_mats,
    normed_out,
    inverse_out,
    weights_out,
    sent_out,
    landed,
    pixel_query,
    query_out,
    raw,
    gain_cols,
    mats_own,
    g_query,
    g_keyval,
    g_latents,
    lat_normed,
    query,
    normed,
    weights,
    outgoing,
    paired,
    merged,
    send_sems,
    recv_sems,
    local_sems,
):
    channels, batches, shard_pixels = pixels.shape
    lat_rows, width = own_latents.shape
    owned, _, row_block, col_block = own_proj.shape
    col_blocks = width // col_block
    padded = normed.shape[1]
    main = channels // 16 * 16
    place = Place(*dims)
    links = Links(send_sems, recv_sems)
    z, y, x, c, p = place.z, place.y, place.x, place.c, place.p
    half_rows = row_block // 2
    half_width = width // 2
    every = slice(None)
    quarter = shard_pixels // 8
    local = []

    def local_copy(source, target):
        copy = pltpu.make_async_copy(source, target, local_sems.at[len(local)])
        copy.start()
        local.append(copy)
        return copy

    g_query[z, y, x, c] = own_proj[:, 0].astype(BF)
    pixel_copies = [
        local_copy(pixels.at[:, :, pl.ds(part, quarter)], raw.at[:, :, pl.ds(part, quarter)])
        for part in range(0, shard_pixels, quarter)
    ]
    keyval_rows, lanes = g_keyval.shape[4:]
    g_keyval[z, y, x, c] = jnp.zeros((keyval_rows, lanes), BF)
    g_keyval[z, y, x, c, :, 0:channels] = own_keyval[...].astype(BF)
    gain_cols[...] = jnp.broadcast_to(gain_rows[1:2, 0:lanes], (128, lanes)).T
    g_latents[y, x, c] = own_latents[...].astype(BF)
    for mat in range(3):
        mats_own[mat] = own_proj[:, mat + 1].astype(BF)
    own_mats_copy = local_copy(mats_own, all_mats.at[z, y, x, c])
    place.barrier()

    sub_a = (every, pl.ds(0, half_rows))
    sub_b = (every, pl.ds(half_rows, half_rows))
    mats_subs = [
        ((1,), "x"),
        ((2,), "y"),
        ((0, every, pl.ds(0, half_rows)), "x"),
        ((0, every, pl.ds(half_rows, half_rows)), "y"),
    ]

    def level(step):
        return lax.rem(z + step, place.nz)

    def hand_on(push, step):
        copies = push(links, g_query, (level(step),), sub_a, "x")
        copies += push(links, g_query, (level(step),), sub_b, "y")
        copies += push(links, g_keyval, (level(step),), (), "xy"[step % 2])
        return copies

    def hand_on_mats(push, step):
        copies = []
        for sub, along in mats_subs:
            copies += push(links, all_mats, (level(step),), sub, along)
        return copies

    z_group = []
    for step in range(1, place.nz):
        z_group.append(
            place.push_z(links, g_query, step) + place.push_z(links, g_keyval, step)
        )
    firsts = [hand_on(place.push_first, 0)]
    lat_a = (every, pl.ds(0, half_width))
    lat_b = (every, pl.ds(half_width, half_width))
    lat_first = place.push_first(links, g_latents, (), lat_a, "x")
    lat_first += place.push_first(links, g_latents, (), lat_b, "y")
    own_mats_copy.wait()
    z_mats = [place.push_z(links, all_mats, step) for step in range(1, place.nz)]
    firsts_m = [hand_on_mats(place.push_first, 0)]

    lane_chunk = 128
    bias_row = channels - main
    row = lax.broadcasted_iota(jnp.int32, (padded - main, lane_chunk), 0)

    def norm_quarter(part):
        pixel_copies[part].wait()

        @pl.loop(0, quarter // lane_chunk)
        def _(chunk):
            start = part * quarter + chunk * lane_chunk
            cols = pl.ds(pl.multiple_of(start, lane_chunk), lane_chunk)
            together = raw[:, :, cols].astype(jnp.float32)
            for image in range(batches):
                value = together[:, image, :]
                value = value - jnp.sum(value, axis=0, keepdims=True) / channels
                variance = jnp.sum(value * value, axis=0, keepdims=True) / channels
                inverse = lax.rsqrt(variance + EPSILON)
                inverse_out[image : image + 1, cols] = inverse
                value = value * inverse * gain_cols[0:channels, :]
                normed[image, 0:main, cols] = value[0:main].astype(BF)
                tail = value[main:channels]
                bias = jnp.where(mask[image : image + 1, cols] == 1, 0.0, NEGATIVE)
                rest = jnp.where(row == bias_row + 1, 1.0, 0.0)
                rest = jnp.where(row == bias_row, bias, rest)
                for index in range(channels - main):
                    rest = jnp.where(row == index, tail[index : index + 1], rest)
                normed[image, main:padded, cols] = rest.astype(BF)

    seconds = []
    seconds_m = []
    cores_m = []

    def first(step):
        arrived(z_group[step - 1])
        firsts.append(hand_on(place.push_first, step))

    def second(step):
        arrived(firsts[step])
        seconds.extend(hand_on(place.push_second, step))

    def first_m(step):
        arrived(z_mats[step - 1])
        firsts_m.append(hand_on_mats(place.push_first, step))

    def second_m(step):
        arrived(firsts_m[step])
        seconds_m.append(hand_on_mats(place.push_second, step))

    def core_m(step):
        arrived(seconds_m[step])
        cores_m.extend(place.push_core(links, all_mats, (level(step),)))

    norm_quarter(0)
    norm_quarter(1)
    second(0)
    arrived(lat_first)
    seconds += place.push_second(links, g_latents, (), lat_a, "x")
    seconds += place.push_second(links, g_latents, (), lat_b, "y")
    norm_quarter(2)
    first(1)
    norm_quarter(3)
    norm_quarter(4)
    first(2)
    second(1)
    norm_quarter(5)
    for step in range(3, place.nz):
        first(step)
    second(2)
    norm_quarter(6)
    for step in range(3, place.nz):
        second(step)
    norm_quarter(7)
    second_m(0)
    first_m(1)
    local_copy(normed, normed_out)
    arrived(seconds)
    cores = place.push_core(links, g_query, (every,))
    cores += place.push_core(links, g_keyval, (every,))
    cores += place.push_core(links, g_latents, ())
    second_m(1)
    first_m(2)

    arrived(cores)
    for yy in range(place.ny):
        for xx in range(place.nx):
            for cc in range(2):
                rows = pl.ds(((yy * place.nx + xx) * 2 + cc) * lat_rows, lat_rows)
                values = g_latents[yy, xx, cc].astype(jnp.float32)
                mean = jnp.mean(values, axis=1, keepdims=True)
                values = values - mean
                variance = jnp.mean(values * values, axis=1, keepdims=True)
                values = values * lax.rsqrt(variance + EPSILON) * gain_rows[0:1, :]
                lat_normed[rows, :] = values.astype(BF)
    second_m(2)
    local_copy(g_query, all_query)
    local_copy(g_keyval, all_keyval)
    local_copy(lat_normed, all_latents)
    for pair in range(col_blocks // 2):
        query[:, 2 * col_block * pair : 2 * col_block * (pair + 1)] = jnp.dot(
            lat_normed[...],
            column_pair(g_query, place, pair, col_blocks, owned),
            preferred_element_type=jnp.float32,
        ).astype(BF)
    local_copy(query, query_out)
    key_t = g_keyval[0 : place.nz // 2]
    key_t = key_t.reshape(width, key_t.shape[-1])
    projected = jnp.dot(query[...], key_t, preferred_element_type=jnp.float32) * width ** (-0.5)
    lane = lax.broadcasted_iota(jnp.int32, projected.shape, 1)
    pixel_query[...] = jnp.where(lane == channels, 1.0, projected).astype(BF)

    tile = place.nx * 2 * lat_rows
    rows_here = place.ny * place.nx * lat_rows

    def attend(image):
        @pl.loop(0, place.ny)
        def _(step):
            rows = pl.ds(pl.multiple_of(step * tile, tile), tile)
            scores = jnp.dot(
                pixel_query[rows, 0:padded], normed[image], preferred_element_type=jnp.float32
            )
            top = jnp.max(scores, axis=1, keepdims=True)
            top = jnp.maximum(top, 0.1 * NEGATIVE).astype(BF).astype(jnp.float32)
            share = jnp.exp(scores - top).astype(BF)
            weights[image, rows, :] = share
            numer = lax.dot_general(
                share, normed[image], NT, preferred_element_type=jnp.float32
            )
            lane = lax.broadcasted_iota(jnp.int32, numer.shape, 1)
            numer = jnp.where(lane == channels, top, numer).astype(BF)
            outgoing[image, step, :, :, :, 0:padded] = numer.reshape(
                place.nx, 2, lat_rows, padded
            )

        local_copy(weights.at[image], weights_out.at[image])
        last = pl.ds(lanes - 128, 128)
        local_copy(
            outgoing.at[image, :, :, :, :, last], sent_out.at[image]
        )
        return [
            links.push(
                outgoing.at[image, :, :, 1 - c], paired.at[image], z, p + 1 - 2 * c
            )
        ]

    def merge(image, pair):
        arrived(pair)
        mine = outgoing[image, :, :, c].reshape(rows_here, lanes).astype(jnp.float32)
        other = paired[image].reshape(rows_here, lanes).astype(jnp.float32)
        my_top = mine[:, channels : channels + 1]
        other_top = other[:, channels : channels + 1]
        top = jnp.maximum(my_top, other_top)
        lane = lax.broadcasted_iota(jnp.int32, mine.shape, 1)
        both = jnp.exp(my_top - top) * mine + jnp.exp(other_top - top) * other
        both = jnp.where(lane == channels, top, both)
        merged[image] = both.astype(BF).reshape(place.ny, place.nx, lat_rows, lanes)
        chip = y * place.nx + x
        chips = place.ny * place.nx
        local_copy(merged.at[image, y, x], landed.at[chip, image])
        copies = []
        for step in range(1, chips):
            q = lax.rem(chip + step, chips)
            copies.append(
                links.push(
                    merged.at[image, q // place.nx, lax.rem(q, place.nx)],
                    landed.at[chip, image],
                    z,
                    2 * q + c,
                )
            )
        return copies

    for step in range(3, place.nz):
        first_m(step)
    core_m(0)
    pair = attend(0)
    sent = []
    for step in range(3, place.nz):
        second_m(step)
    core_m(1)
    for image in range(1, batches):
        following = attend(image)
        sent += merge(image - 1, pair)
        pair = following
        if image == 1:
            core_m(2)
    sent += merge(batches - 1, pair)
    for step in range(3, place.nz):
        core_m(step)
    arrived(sent)
    arrived(cores_m)
    links.drain()
    for copy in local[9:]:
        copy.wait()


def front_copies(nz, ny, nx, batches):
    both = nx + ny - 2
    count = 3 * (nz - 1) + 2 * nz * (both + max(nx, ny) - 1) + 2 * both
    count += 2 * nz * 2 * both + 3 + nz
    return count + batches * nx * ny


def front(dims, pixels, pixel_mask, gain_rows, proj_blocks, keyval_t, latents):
    nz, ny, nx = dims
    channels, batches, shard_pixels = pixels.shape
    lat_rows, width = latents.shape
    owned, mats, row_block, col_block = proj_blocks.shape
    keyval_rows = keyval_t.shape[0]
    group = 2 * ny * nx
    all_rows = lat_rows * group
    padded = ceil_to(channels + 2, 16)
    lanes = ceil_to(padded, 128)
    vmem = pl.BlockSpec(memory_space=pltpu.VMEM)
    anywhere = pl.BlockSpec(memory_space=pl.ANY)
    cube = (nz, ny, nx, 2)
    copies = front_copies(nz, ny, nx, batches)
    return pl.pallas_call(
        functools.partial(front_kernel, dims),
        out_shape=(
            jax.ShapeDtypeStruct(cube + (owned, row_block, col_block), BF),
            jax.ShapeDtypeStruct(cube + (keyval_rows, lanes), BF),
            jax.ShapeDtypeStruct((all_rows, width), BF),
            jax.ShapeDtypeStruct(cube + (3, owned, row_block, col_block), BF),
            jax.ShapeDtypeStruct((batches, padded, shard_pixels), BF),
            jax.ShapeDtypeStruct((batches, shard_pixels), jnp.float32),
            jax.ShapeDtypeStruct((batches, all_rows, shard_pixels), BF),
            jax.ShapeDtypeStruct((batches, ny, nx, 2, lat_rows, 128), BF),
            jax.ShapeDtypeStruct((ny * nx, batches, lat_rows, lanes), BF),
            jax.ShapeDtypeStruct((all_rows, lanes), BF),
            jax.ShapeDtypeStruct((all_rows, width), BF),
        ),
        in_specs=[anywhere] + [vmem] * 5,
        out_specs=(
            anywhere,
            anywhere,
            anywhere,
            anywhere,
            anywhere,
            vmem,
            anywhere,
            anywhere,
            anywhere,
            vmem,
            anywhere,
        ),
        scratch_shapes=[
            pltpu.VMEM(pixels.shape, BF),
            pltpu.VMEM((lanes, 128), jnp.float32),
            pltpu.VMEM((3, owned, row_block, col_block), BF),
            pltpu.VMEM(cube + (owned, row_block, col_block), BF),
            pltpu.VMEM(cube + (keyval_rows, lanes), BF),
            pltpu.VMEM(cube[1:] + (lat_rows, width), BF),
            pltpu.VMEM((all_rows, width), BF),
            pltpu.VMEM((all_rows, width), BF),
            pltpu.VMEM((batches, padded, shard_pixels), BF),
            pltpu.VMEM((batches, all_rows, shard_pixels), BF),
            pltpu.VMEM((batches, ny, nx, 2, lat_rows, lanes), BF),
            pltpu.VMEM((batches, ny, nx, lat_rows, lanes), BF),
            pltpu.VMEM((batches, ny, nx, lat_rows, lanes), BF),
            pltpu.SemaphoreType.DMA((copies,)),
            pltpu.SemaphoreType.DMA((copies,)),
            pltpu.SemaphoreType.DMA((14 + 3 * batches,)),
        ],
        compiler_params=pltpu.CompilerParams(
            collective_id=0, has_side_effects=True, vmem_limit_bytes=56 * 2**20
        ),
    )(
        pixels,
        pixel_mask,
        gain_rows,
        proj_blocks,
        keyval_t,
        latents,
    )


def add_low(former, latter):
    return (former.astype(jnp.float32) + latter.astype(jnp.float32)).astype(BF)


class Reduce:
    def __init__(self, place, links, term, buffers, along):
        self.place, self.links, self.term, self.along = place, links, term, along
        self.by_core, self.by_first, self.by_second, self.by_z = buffers
        self.waiting = []

    def wait(self):
        arrived(self.waiting)
        self.waiting = []

    def push_core(self):
        place = self.place
        every = slice(None)
        self.waiting = [
            self.links.push(
                self.term.at[every, every, every, 1 - place.c],
                self.by_core,
                place.z,
                place.p + 1 - 2 * place.c,
            )
        ]

    def push_first(self):
        place = self.place
        self.wait()

        @pl.loop(0, self.by_core.shape[0])
        def _(level):
            self.by_core[level] = add_low(
                self.by_core[level], self.term[level, :, :, place.c]
            )

        every = slice(None)
        for step in range(1, place.nx if self.along == "x" else place.ny):
            if self.along == "x":
                xx = lax.rem(place.x + step, place.nx)
                source = self.by_core.at[every, every, xx]
                target = place.pix(place.y, xx, place.c)
            else:
                yy = lax.rem(place.y + step, place.ny)
                source = self.by_core.at[every, yy]
                target = place.pix(yy, place.x, place.c)
            self.waiting.append(
                self.links.push(source, self.by_first.at[step - 1], place.z, target)
            )

    def push_second(self):
        place = self.place
        self.wait()
        if self.along == "x":
            held = self.by_core[:, :, place.x].astype(jnp.float32)
        else:
            held = self.by_core[:, place.y].astype(jnp.float32)
        for slot in range(self.by_first.shape[0]):
            held = held + self.by_first[slot].astype(jnp.float32)
        self.by_first[0] = held.astype(BF)
        every = slice(None)
        for step in range(1, place.ny if self.along == "x" else place.nx):
            if self.along == "x":
                other = lax.rem(place.y + step, place.ny)
                target = place.pix(other, place.x, place.c)
            else:
                other = lax.rem(place.x + step, place.nx)
                target = place.pix(place.y, other, place.c)
            self.waiting.append(
                self.links.push(
                    self.by_first.at[0, every, other],
                    self.by_second.at[step - 1],
                    place.z,
                    target,
                )
            )

    def push_z(self):
        place = self.place
        self.wait()
        mine = place.y if self.along == "x" else place.x
        held = self.by_first[0, :, mine].astype(jnp.float32)
        for slot in range(self.by_second.shape[0]):
            held = held + self.by_second[slot].astype(jnp.float32)
        self.by_second[0] = held.astype(BF)
        for step in range(1, place.nz):
            zz = lax.rem(place.z - step + place.nz, place.nz)
            self.waiting.append(
                self.links.push(self.by_second.at[0, zz], self.by_z.at[step - 1], zz, place.p)
            )

    def total(self):
        self.wait()
        held = self.by_second[0, self.place.z].astype(jnp.float32)
        return held, [self.by_z.at[slot] for slot in range(self.by_z.shape[0])]


class ReduceDown(Reduce):
    def push_z(self):
        place = self.place
        self.wait()

        @pl.loop(0, self.by_core.shape[0])
        def _(level):
            self.by_core[level] = add_low(
                self.by_core[level], self.term[level, :, :, place.c]
            )

        for step in range(1, place.nz):
            zz = lax.rem(place.z - step + place.nz, place.nz)
            self.waiting.append(
                self.links.push(self.by_core.at[zz], self.by_z.at[step - 1], zz, place.p)
            )

    def push_first(self):
        place = self.place
        self.wait()
        held = self.by_core[place.z].astype(jnp.float32)
        for slot in range(self.by_z.shape[0]):
            held = held + self.by_z[slot].astype(jnp.float32)
        self.by_z[0] = held.astype(BF)
        every = slice(None)
        for step in range(1, place.nx if self.along == "x" else place.ny):
            if self.along == "x":
                other = lax.rem(place.x + step, place.nx)
                source = self.by_z.at[0, every, other]
                target = place.pix(place.y, other, place.c)
            else:
                other = lax.rem(place.y + step, place.ny)
                source = self.by_z.at[0, other]
                target = place.pix(other, place.x, place.c)
            self.waiting.append(
                self.links.push(source, self.by_first.at[step - 1], place.z, target)
            )

    def push_second(self):
        place = self.place
        self.wait()
        if self.along == "x":
            held = self.by_z[0, :, place.x].astype(jnp.float32)
        else:
            held = self.by_z[0, place.y].astype(jnp.float32)
        for slot in range(self.by_first.shape[0]):
            held = held + self.by_first[slot].astype(jnp.float32)
        self.by_first[0] = held.astype(BF)
        for step in range(1, place.ny if self.along == "x" else place.nx):
            if self.along == "x":
                other = lax.rem(place.y + step, place.ny)
                target = place.pix(other, place.x, place.c)
            else:
                other = lax.rem(place.x + step, place.nx)
                target = place.pix(place.y, other, place.c)
            self.waiting.append(
                self.links.push(
                    self.by_first.at[0, other], self.by_second.at[step - 1], place.z, target
                )
            )

    def total(self):
        self.wait()
        mine = self.place.y if self.along == "x" else self.place.x
        held = self.by_first[0, mine].astype(jnp.float32)
        return held, [self.by_second.at[slot] for slot in range(self.by_second.shape[0])]


def block_index(block, col_blocks, owned):
    every = slice(None)
    if 2 * owned == col_blocks:
        return (every, every, every, block // owned, block % owned)
    return (every, every, block // 2, block % 2, 0)


def back_kernel(
    dims,
    channels,
    landed,
    all_keyval,
    all_mats,
    normed_all,
    inverse,
    weights_all,
    sent_all,
    pixel_query,
    latents,
    gain_rows,
    grad_rows,
    mixed,
    pixel_grad,
    mats_grad,
    chan_total,
    query_total,
    gain_total,
    residual_total,
    came,
    values,
    mats,
    normed,
    weights,
    tops,
    attended_chan,
    attended,
    middle,
    mid_hat,
    mid_inverse,
    mid_normed,
    slope,
    hidden,
    grad_pre,
    grad_mid_normed,
    grad_mid,
    grad_attended,
    shares,
    query_turned,
    query_acc,
    back_turned,
    grad_scores,
    gain_cols,
    staged,
    terms,
    buffers,
    query_low,
    query_came,
    query_levels,
    gain_plane,
    gain_levels,
    residual_parts,
    residual_came,
    residual_levels,
    send_sems,
    recv_sems,
    local_sems,
):
    place = Place(*dims)
    links = Links(send_sems, recv_sems)
    z, y, x, c, p = place.z, place.y, place.x, place.c, place.p
    chips, batches, lat_rows, lanes = landed.shape
    group = place.group
    rows = batches * lat_rows
    all_rows = group * lat_rows
    width = latents.shape[1]
    padded, shard_pixels = normed_all.shape[1:]
    owned, row_block, col_block = all_mats.shape[5:]
    col_blocks = width // col_block
    every = slice(None)
    tile = 256
    tiles = width // tile
    local = []

    def local_copy(source, target):
        copy = pltpu.make_async_copy(source, target, local_sems.at[len(local)])
        copy.start()
        local.append(copy)
        return copy

    came_copy = local_copy(landed, came)
    values_copy = local_copy(all_keyval.at[pl.ds(place.nz // 2, place.nz // 2)], values)
    mats_copies = []
    for mat in range(3):
        copies = []
        for block in range(col_blocks):
            where = block_index(block, col_blocks, owned)
            source = all_mats.at[where[:4] + (mat,) + where[4:]]
            cols = pl.ds(block * col_block, col_block)
            lead = (mat,) + (every,) * (len(mats.shape) - 2)
            copies.append(local_copy(source, mats.at[lead + (cols,)]))
        mats_copies.append(copies)
    tops_copy = local_copy(sent_all, tops)

    def fetch(image):
        slot = image % 2
        return [
            local_copy(normed_all.at[image], normed.at[slot]),
            local_copy(weights_all.at[image], weights.at[slot]),
        ]

    fetched = [fetch(0), fetch(1)]
    place.barrier()

    def columns_of(mat, index):
        lead = (mat,) + (every,) * (len(mats.shape) - 2)
        return mats[lead + (slice(index * tile, (index + 1) * tile),)].reshape(width, tile)

    def rows_of(mat, index):
        return mats[mat, index].reshape(-1, width)

    row_tile = width // place.nz

    came_copy.wait()
    lane = lax.broadcasted_iota(jnp.int32, (rows, lanes), 1)
    parts = [came[g].reshape(rows, lanes).astype(jnp.float32) for g in range(chips)]
    top = [part[:, channels : channels + 1] for part in parts]
    peak = functools.reduce(jnp.maximum, top)
    factor = [jnp.exp(value - peak) for value in top]
    denominator = sum(f * part[:, channels + 1 : channels + 2] for f, part in zip(factor, parts))
    summed = sum(f * part for f, part in zip(factor, parts))
    attended_chan[...] = jnp.where(lane < channels, summed / denominator, 0.0).astype(BF)

    values_copy.wait()
    value_t = values[...].reshape(width, lanes)
    attended[...] = lax.dot_general(
        attended_chan[...], value_t, NT, preferred_element_type=jnp.float32
    ).astype(BF)
    arrived_local(mats_copies[0])
    for index in range(tiles):
        cols = slice(index * tile, (index + 1) * tile)
        own = latents[:, cols]
        middle[:, cols] = jnp.concatenate([own] * batches, axis=0) + jnp.dot(
            attended[...], columns_of(0, index), preferred_element_type=jnp.float32
        )

    @pl.loop(0, rows // lat_rows)
    def _(step):
        part = pl.ds(pl.multiple_of(step * lat_rows, lat_rows), lat_rows)
        value = middle[part, :]
        value = value - jnp.mean(value, axis=1, keepdims=True)
        scale = lax.rsqrt(jnp.mean(value * value, axis=1, keepdims=True) + EPSILON)
        value = value * scale
        mid_hat[part, :] = value
        mid_inverse[part, :] = jnp.broadcast_to(scale, (lat_rows, 128))
        mid_normed[part, :] = (value * gain_rows[2:3, :]).astype(BF)

    arrived_local(mats_copies[1])
    for index in range(tiles):
        cols = slice(index * tile, (index + 1) * tile)
        pre = jnp.dot(mid_normed[...], columns_of(1, index), preferred_element_type=jnp.float32)
        below = 0.5 + 0.5 * lax.erf(pre * 0.5**0.5)
        hidden[:, cols] = (pre * below).astype(BF)
        slope[:, cols] = below + pre * jnp.exp(-0.5 * pre * pre) * (0.5 / math.pi) ** 0.5

    half_rows = row_block // 2

    def store_term(targets, left, right):
        turned = left[...].T
        for pair in range(col_blocks // 2):
            cols = slice(2 * pair * col_block, 2 * (pair + 1) * col_block)
            product = jnp.dot(turned, right[:, cols], preferred_element_type=jnp.float32).astype(
                BF
            )
            for side in range(2):
                where = block_index(2 * pair + side, col_blocks, owned)
                block = product[:, side * col_block : (side + 1) * col_block]
                taken = 0
                for target in targets:
                    height = target.shape[-2]
                    pieces = block.reshape(-1, row_block, col_block)[:, taken : taken + height]
                    taken += height
                    shape = target.shape
                    lead = shape[:3] if 2 * owned == col_blocks else shape[:2]
                    target[where] = pieces.reshape(lead + (height, col_block))

    pairs = []
    for index, kind in enumerate((ReduceDown, Reduce)):
        pairs.append(
            [
                kind(place, links, terms[2 * index + side], buffers[2 * index + side], along)
                for side, along in enumerate("xy")
            ]
        )
    down, inward = pairs
    chan_job = Reduce(place, links, terms[4], buffers[4], "x")
    store_term(terms[0:2], hidden, grad_rows)
    for job in down:
        job.push_core()

    arrived_local(mats_copies[2])
    for index in range(place.nz):
        cols = slice(index * row_tile, (index + 1) * row_tile)
        grad_hidden = lax.dot_general(
            grad_rows[...], rows_of(2, index), NT, preferred_element_type=jnp.float32
        )
        grad_pre[:, cols] = (
            grad_hidden.astype(BF).astype(jnp.float32) * slope[:, cols]
        ).astype(BF)
    for job in down:
        job.push_z()
    gain_plane[p] = jnp.zeros(gain_plane.shape[1:], jnp.float32)
    for index in range(place.nz):
        cols = slice(index * row_tile, (index + 1) * row_tile)
        part = lax.dot_general(
            grad_pre[...], rows_of(1, index), NT, preferred_element_type=jnp.float32
        )
        grad_mid_normed[:, cols] = part
        summed_rows = jnp.sum(part * mid_hat[:, cols], axis=0, keepdims=True)
        for sub in range(row_tile // 128):
            row = index * (row_tile // 128) + sub
            gain_plane[p, row : row + 1, :] = summed_rows[:, sub * 128 : (sub + 1) * 128]

    @pl.loop(0, rows // lat_rows)
    def _(step):
        part = pl.ds(pl.multiple_of(step * lat_rows, lat_rows), lat_rows)
        grad = grad_mid_normed[part, :] * gain_rows[2:3, :]
        hat = mid_hat[part, :]
        grad = (
            grad
            - jnp.mean(grad, axis=1, keepdims=True)
            - hat * jnp.mean(grad * hat, axis=1, keepdims=True)
        ) * mid_inverse[part, 0:1]
        grad_mid[part, :] = (grad_rows[part, :].astype(jnp.float32) + grad).astype(BF)

    for index in range(place.nz):
        cols = slice(index * row_tile, (index + 1) * row_tile)
        grad_attended[:, cols] = lax.dot_general(
            grad_mid[...], rows_of(0, index), NT, preferred_element_type=jnp.float32
        ).astype(BF)
    grad_chan = jnp.dot(grad_attended[...], value_t, preferred_element_type=jnp.float32)
    products = attended_chan[...].astype(jnp.float32) * grad_chan
    row_delta = jnp.sum(products, axis=1, keepdims=True)
    channel_sums = jnp.sum(products, axis=0, keepdims=True)
    for sub in range(lanes // 128):
        row = width // 128 + sub
        gain_plane[p, row : row + 1, :] = channel_sums[:, sub * 128 : (sub + 1) * 128]
    back = jnp.where(lane == channels + 1, row_delta, grad_chan) / denominator
    back = jnp.where(lane == channels, peak, back)
    shares[y, x, c] = back.astype(BF).reshape(batches, lat_rows, lanes)

    share_first = []
    for image in range(batches):
        share_first.append(
            place.push_first(links, shares, (), (image,), "xy"[image % 2])
        )
    gain_sent = []
    for step in range(1, group):
        own = gain_plane.at[p]
        gain_sent.append(links.push(own, own, z, lax.rem(p + step, group)))
    share_second = []
    share_core = []

    def share_on(image):
        arrived(share_first[image])
        share_second.append(place.push_second(links, shares, (), (image,), "xy"[image % 2]))

    def share_pair(image):
        arrived(share_second[image])
        held = shares.at[:, :, c, image]
        share_core.append([links.push(held, held, z, p + 1 - 2 * c)])

    terms[4][...] = (
        jnp.dot(grad_mid[...].T, attended_chan[...], preferred_element_type=jnp.float32)
        .astype(BF)
        .reshape(terms[4].shape)
    )
    chan_job.push_core()
    store_term(terms[2:4], mid_normed, grad_pre)
    for job in inward:
        job.push_core()
    for image in range(batches):
        share_on(image)
    chan_job.push_first()
    for job in inward:
        job.push_first()
    residual = sum(
        grad_mid[image * lat_rows : (image + 1) * lat_rows].astype(jnp.float32)
        for image in range(batches)
    )
    part_width = width // place.nz
    residual_sent = []
    for zz in range(place.nz):
        residual_parts[zz] = residual[:, zz * part_width : (zz + 1) * part_width].astype(BF)
    for step in range(1, place.nz):
        zz = lax.rem(z + step, place.nz)
        residual_sent.append(
            links.push(residual_parts.at[zz], residual_came.at[step - 1], zz, p)
        )

    lane_all = lax.broadcasted_iota(jnp.int32, (all_rows, lanes), 1)
    query_turned[...] = jnp.where(
        lane_all < channels, pixel_query[...].astype(jnp.float32), 0.0
    ).T[0:padded].astype(BF)
    query_acc[...] = jnp.zeros(query_acc.shape, jnp.float32)
    gain_cols[0] = jnp.broadcast_to(gain_rows[1:2, 0:lanes], (128, lanes)).T[0:padded]
    gain_cols[1] = jnp.broadcast_to(gain_rows[3:4, 0:lanes], (128, lanes)).T[0:padded]
    chunk = min(512, shard_pixels)
    tops_copy.wait()

    def attend_query(image):
        slot = image % 2
        arrived(share_core[image])
        arrived_local(fetched[image])
        back = shares[:, :, :, image].reshape(all_rows, lanes).astype(jnp.float32)
        top = tops[image].reshape(all_rows, 128).astype(jnp.float32)[
            :, channels - (lanes - 128) :
        ][:, 0:1]
        share = jnp.exp(top - back[:, channels : channels + 1])
        back = jnp.where(lane_all == channels, 0.0, back * share)
        back = jnp.where(lane_all > channels + 1, 0.0, back)
        back_low = jnp.where(lane_all == channels + 1, -back, back).astype(BF)[:, 0:padded]
        back_turned[image] = jnp.where(lane_all < channels, back, 0.0).T[0:padded].astype(BF)

        @pl.loop(0, shard_pixels // chunk)
        def _(step):
            cols = pl.ds(pl.multiple_of(step * chunk, chunk), chunk)
            normed_chunk = normed[slot, :, cols]
            grad_weights = jnp.dot(back_low, normed_chunk, preferred_element_type=jnp.float32)
            grad_chunk = (weights[slot, :, cols].astype(jnp.float32) * grad_weights).astype(BF)
            grad_scores[image, :, cols] = grad_chunk
            query_acc[:, 0:padded] += lax.dot_general(
                grad_chunk, normed_chunk, NT, preferred_element_type=jnp.float32
            )

        if image + 2 < batches:
            fetched.append(fetch(image + 2))

    order = list(range(2, batches)) + [0, 1]
    staged_out = []

    def attend_pixels(turn):
        image = order[turn]
        slot = image % 2
        if turn >= 2:
            arrived_local(fetched[batches + turn - 2])
            staged_out[turn - 2].wait()

        @pl.loop(0, shard_pixels // chunk)
        def _(step):
            cols = pl.ds(pl.multiple_of(step * chunk, chunk), chunk)
            grad_normed = jnp.dot(
                query_turned[...], grad_scores[image, :, cols], preferred_element_type=jnp.float32
            ) + jnp.dot(
                back_turned[image], weights[slot, :, cols], preferred_element_type=jnp.float32
            )
            normal = normed[slot, :, cols].astype(jnp.float32)
            second_mean = jnp.sum(grad_normed * normal, axis=0, keepdims=True) / channels
            spread = jnp.concatenate([gain_cols[0]] * (chunk // 128), axis=1)
            spread_back = jnp.concatenate([gain_cols[1]] * (chunk // 128), axis=1)
            grad_hat = grad_normed * spread
            first_mean = jnp.sum(grad_hat, axis=0, keepdims=True) / channels
            result = (grad_hat - first_mean - normal * spread_back * second_mean) * inverse[
                image : image + 1, cols
            ]
            staged[turn % 2, :, cols] = result[0:channels].astype(BF)

        staged_out.append(local_copy(staged.at[turn % 2], pixel_grad.at[image]))
        if turn + 2 < batches:
            fetched.append(fetch(order[turn + 2]))

    share_pair(0)
    share_pair(1)
    attend_query(0)
    share_pair(2)
    share_pair(3)
    chan_job.push_second()
    attend_query(1)
    arrived(gain_sent)
    gain_levels[z] = sum(gain_plane[g] for g in range(group))
    gain_up = []
    for step in range(1, place.nz):
        own = gain_levels.at[z]
        gain_up.append(links.push(own, own, lax.rem(z + step, place.nz), p))
    attend_query(2)
    chan_job.push_z()
    for job in inward:
        job.push_second()
    attend_query(3)

    query_low[...] = query_acc[...].astype(BF)
    query_sent = []
    for step in range(1, group):
        q = lax.rem(p + step, group)
        part = pl.ds(pl.multiple_of(q * lat_rows, lat_rows), lat_rows)
        query_sent.append(links.push(query_low.at[part], query_came.at[step - 1], z, q))
    attend_pixels(0)
    held, came_z = chan_job.total()
    for part in came_z:
        held = held + part[...].astype(jnp.float32)
    chan_total[z, y, x, c] = held.astype(BF)
    chan_z = []
    for step in range(1, place.nz):
        chan_z += place.push_z(links, chan_total, step)
    for job in down:
        job.push_first()
    arrived(query_sent)
    own_rows = pl.ds(pl.multiple_of(p * lat_rows, lat_rows), lat_rows)
    held = query_acc[own_rows, :]
    for slot in range(group - 1):
        held = held + query_came[slot].astype(jnp.float32)
    query_levels[z] = held.astype(BF)
    query_up = []
    for step in range(1, place.nz):
        own = query_levels.at[z]
        query_up.append(links.push(own, own, lax.rem(z + step, place.nz), p))
    attend_pixels(1)
    arrived(chan_z)
    chan_first = place.push_first(links, chan_total, (every,), (), "x")
    arrived(query_up)
    query_total[p] = sum(query_levels[zz].astype(jnp.float32) for zz in range(place.nz)).astype(BF)
    query_all = []
    for step in range(1, group):
        own = query_total.at[p]
        query_all.append(links.push(own, own, z, lax.rem(p + step, group)))
    for job in inward:
        job.push_z()
    for job in down:
        job.push_second()
    attend_pixels(2)
    arrived(chan_first)
    chan_second = place.push_second(links, chan_total, (every,), (), "x")
    arrived(residual_sent)
    residual_levels[z] = (
        residual_parts[z].astype(jnp.float32)
        + sum(residual_came[slot].astype(jnp.float32) for slot in range(place.nz - 1))
    ).astype(BF)
    residual_up = []
    for step in range(1, place.nz):
        own = residual_levels.at[z]
        residual_up.append(links.push(own, own, lax.rem(z + step, place.nz), p))
    attend_pixels(3)
    arrived(chan_second)
    chan_core = place.push_core(links, chan_total, (every,))
    for index in range(tiles):
        cols = slice(index * tile, (index + 1) * tile)
        mixed[:, cols] = (
            middle[:, cols]
            + jnp.dot(hidden[...], columns_of(2, index), preferred_element_type=jnp.float32)
        ).astype(BF)
    def finish(job, target):
        held, came_z = job.total()
        for part in came_z:
            held = held + part[...].astype(jnp.float32)
        target[...] = held

    def finish_mat(mat, jobs):
        for side, job in enumerate(jobs):
            finish(job, mats_grad.at[mat, :, pl.ds(side * half_rows, half_rows)])

    finish_mat(1, down)
    arrived(gain_up)
    gain_total[...] = sum(gain_levels[zz] for zz in range(place.nz))
    arrived(residual_up)
    for zz in range(place.nz):
        residual_total[:, zz * part_width : (zz + 1) * part_width] = residual_levels[zz].astype(
            jnp.float32
        )
    finish_mat(0, inward)
    arrived(chan_core)
    arrived(query_all)
    links.drain()
    for copy in staged_out[batches - 2 :]:
        copy.wait()


def arrived_local(copies):
    for copy in copies:
        copy.wait()


def back_copies(nz, ny, nx, batches):
    group = 2 * ny * nx
    both = nx + ny - 2
    count = batches // 2 * 2 * both + batches
    count += 5 * (1 + both + nz - 1) + nz - 1 + both + 1
    count += 4 * (nz - 1) + 3 * (group - 1)
    return count


def back(dims, channels, gathered, latents, gain_rows, mixed_grad):
    landed, all_keyval, all_mats, normed_all, inverse, weights_all, sent_all, pixel_query = gathered
    nz, ny, nx = dims
    batches, lat_rows, lanes = landed.shape[1:]
    group = 2 * ny * nx
    rows = batches * lat_rows
    all_rows = group * lat_rows
    width = latents.shape[1]
    padded, shard_pixels = normed_all.shape[1:]
    owned, row_block, col_block = all_mats.shape[5:]
    keyval_rows = all_keyval.shape[4]
    half_rows = row_block // 2
    vmem = pl.BlockSpec(memory_space=pltpu.VMEM)
    anywhere = pl.BlockSpec(memory_space=pl.ANY)
    lead = (nz, ny, nx) if 2 * owned * col_block == width else (nz, ny)
    cube = (nz, ny, nx, 2)
    inners = [(nz, (owned, half_rows, col_block), along) for along in "xyxy"]
    inners.append((nz, (width // (group * nz), lanes), "x"))
    terms = [pltpu.VMEM((levels, ny, nx, 2) + inner, BF) for levels, inner, _ in inners]
    buffers = []
    for index, (levels, inner, along) in enumerate(inners):
        one, two = (nx, ny) if along == "x" else (ny, nx)
        plane_last = index < 2
        buffers.append(
            [
                pltpu.VMEM((levels, ny, nx) + inner, BF),
                pltpu.VMEM((one - 1,) + (() if plane_last else (levels,)) + (two,) + inner, BF),
                pltpu.VMEM((two - 1,) + (() if plane_last else (levels,)) + inner, BF),
                pltpu.VMEM((nz - 1,) + ((ny, nx) if plane_last else ()) + inner, BF),
            ]
        )
    wide = lambda kind: pltpu.VMEM((rows, width), kind)
    copies = back_copies(nz, ny, nx, batches)
    return pl.pallas_call(
        functools.partial(back_kernel, dims, channels),
        out_shape=(
            jax.ShapeDtypeStruct((rows, width), BF),
            jax.ShapeDtypeStruct((batches, channels, shard_pixels), BF),
            jax.ShapeDtypeStruct((2, owned, row_block, col_block), jnp.float32),
            jax.ShapeDtypeStruct(cube + (width // (group * nz), lanes), BF),
            jax.ShapeDtypeStruct((group, lat_rows, lanes), BF),
            jax.ShapeDtypeStruct((16, 128), jnp.float32),
            jax.ShapeDtypeStruct((lat_rows, width), jnp.float32),
        ),
        in_specs=[
            anywhere,
            anywhere,
            anywhere,
            anywhere,
            vmem,
            anywhere,
            anywhere,
            vmem,
            vmem,
            vmem,
            vmem,
        ],
        out_specs=(vmem, anywhere, vmem, vmem, vmem, vmem, vmem),
        scratch_shapes=[
            pltpu.VMEM((ny * nx, batches, lat_rows, lanes), BF),
            pltpu.VMEM((nz // 2, ny, nx, 2, keyval_rows, lanes), BF),
            pltpu.VMEM((3,) + lead + (row_block, width), BF),
            pltpu.VMEM((2, padded, shard_pixels), BF),
            pltpu.VMEM((2, all_rows, shard_pixels), BF),
            pltpu.VMEM((batches, ny, nx, 2, lat_rows, 128), BF),
            pltpu.VMEM((rows, lanes), BF),
            wide(BF),
            wide(jnp.float32),
            wide(jnp.float32),
            pltpu.VMEM((rows, 128), jnp.float32),
            wide(BF),
            wide(jnp.float32),
            wide(BF),
            wide(BF),
            wide(jnp.float32),
            wide(BF),
            wide(BF),
            pltpu.VMEM(cube[1:] + (batches, lat_rows, lanes), BF),
            pltpu.VMEM((padded, all_rows), BF),
            pltpu.VMEM((all_rows, lanes), jnp.float32),
            pltpu.VMEM((batches, padded, all_rows), BF),
            pltpu.VMEM((batches, all_rows, shard_pixels), BF),
            pltpu.VMEM((2, padded, 128), jnp.float32),
            pltpu.VMEM((2, channels, shard_pixels), BF),
            terms,
            buffers,
            pltpu.VMEM((all_rows, lanes), BF),
            pltpu.VMEM((group - 1, lat_rows, lanes), BF),
            pltpu.VMEM((nz, lat_rows, lanes), BF),
            pltpu.VMEM((group, 16, 128), jnp.float32),
            pltpu.VMEM((nz, 16, 128), jnp.float32),
            pltpu.VMEM((nz, lat_rows, width // nz), BF),
            pltpu.VMEM((nz - 1, lat_rows, width // nz), BF),
            pltpu.VMEM((nz, lat_rows, width // nz), BF),
            pltpu.SemaphoreType.DMA((copies,)),
            pltpu.SemaphoreType.DMA((copies,)),
            pltpu.SemaphoreType.DMA((3 + 3 * (width // col_block) + 5 * batches,)),
        ],
        compiler_params=pltpu.CompilerParams(
            collective_id=1, has_side_effects=True, vmem_limit_bytes=61 * 2**20
        ),
    )(
        landed,
        all_keyval,
        all_mats,
        normed_all,
        inverse,
        weights_all,
        sent_all,
        pixel_query,
        latents,
        gain_rows,
        mixed_grad.reshape(rows, width),
    )


TN = (((0,), (0,)), ((), ()))


def tail_kernel(
    dims,
    channels,
    query_total,
    residual_total,
    mats_grad,
    chan_grad,
    proj_blocks,
    proj_left,
    proj_right,
    left_roots,
    right_roots,
    keyval_weight,
    keyval_second,
    latents,
    latent_second,
    gain_rows,
    query_in,
    lat_normed_in,
    query_blocks,
    all_keyval,
    pixel_low,
    pixel_query,
    gain_total,
    all_rows_keyval,
    all_mats,
    pixel_grad,
    proj_grad,
    left_new,
    right_new,
    proj_new,
    keyval_grad,
    keyval_second_new,
    keyval_new,
    latent_grad,
    latent_second_new,
    latent_new,
    lat_gain_grad,
    channel_gain_grad,
    query,
    lat_normed,
    query_weight,
    keys,
    pixel_came,
    pixel_wide,
    grad_query,
    grad_normed,
    query_grad,
    key_rows,
    value_block,
    output_block,
    local_sems,
):
    place = Place(*dims)
    group, lat_rows, lanes = query_total.shape
    all_rows = group * lat_rows
    width = latents.shape[1]
    batches = pixel_low.shape[0]
    owned, mats, row_block, col_block = proj_blocks.shape
    col_blocks = width // col_block
    keyval_rows = keyval_weight.shape[0]
    device = place.z * group + place.p
    every = slice(None)
    local = []

    def local_copy(source, target):
        copy = pltpu.make_async_copy(source, target, local_sems.at[len(local)])
        copy.start()
        local.append(copy)
        return copy

    keys_copy = local_copy(all_keyval.at[pl.ds(0, place.nz // 2)], keys)
    weight_copies = []
    for block in range(col_blocks):
        lead = (every,) * (len(query_weight.shape) - 1)
        weight_copies.append(
            local_copy(
                query_blocks.at[block_index(block, col_blocks, owned)],
                query_weight.at[lead + (pl.ds(block * col_block, col_block),)],
            )
        )
    normed_copy = local_copy(lat_normed_in, lat_normed)
    block_row = device * owned // col_blocks
    block_col = lax.rem(device * owned, col_blocks)
    half_devices = width // keyval_rows
    key_start = lax.rem(device, half_devices) * keyval_rows
    value_rows = pl.ds(pl.multiple_of(width + block_row * row_block, row_block), row_block)
    value_copy = local_copy(all_rows_keyval.at[value_rows], value_block)
    output_row = key_start // row_block
    if 2 * owned == col_blocks:
        across = lax.rem(output_row, place.nx)
        along = lax.rem(output_row // place.nx, place.ny)
        source = all_mats.at[output_row // (place.nx * place.ny), along, across, :, 0]
    else:
        source = all_mats.at[output_row // place.ny, lax.rem(output_row, place.ny), :, :, 0, 0]
    output_copy = local_copy(source, output_block)
    query_copy = local_copy(query_in, query)
    pixel_copies = [local_copy(pixel_low.at[i], pixel_came.at[i]) for i in range(batches)]
    pixel_sent = []

    def widen(image):
        pixel_copies[image].wait()

        @pl.loop(0, pixel_low.shape[2] // 256)
        def _(step):
            cols = pl.ds(pl.multiple_of(step * 256, 256), 256)
            pixel_wide[image, :, cols] = pixel_came[image, :, cols].astype(jnp.float32)

        pixel_sent.append(local_copy(pixel_wide.at[image], pixel_grad.at[:, image]))

    def moments(weight, grad, second, rate, second_out, weight_out):
        second_value = STAT_DECAY * second[...] + (1.0 - STAT_DECAY) * grad * grad
        second_out[...] = second_value
        weight_out[...] = weight[...] - rate * grad / (jnp.sqrt(second_value) + MOMENT_FLOOR)

    def precondition(mat, index, grad):
        low = grad.astype(BF)
        proj_grad[index, mat] = grad
        left_new[index, mat] = STAT_DECAY * proj_left[index, mat] + (
            1.0 - STAT_DECAY
        ) * lax.dot_general(low, low, NT, preferred_element_type=jnp.float32)
        right_new[index, mat] = STAT_DECAY * proj_right[index, mat] + (
            1.0 - STAT_DECAY
        ) * lax.dot_general(low, low, TN, preferred_element_type=jnp.float32)
        step = jnp.dot(
            left_roots[index, mat].astype(BF), low, preferred_element_type=jnp.float32
        ).astype(BF)
        step = jnp.dot(
            step, right_roots[index, mat].astype(BF), preferred_element_type=jnp.float32
        )
        proj_new[index, mat] = proj_blocks[index, mat] - MATRIX_RATE * step

    for mat in range(2):
        for index in range(owned):
            precondition(mat + 2, index, mats_grad[mat, index])
    widen(0)
    value_copy.wait()
    own_cols = pl.ds(pl.multiple_of(block_col * col_block, col_block), owned * col_block)
    output_grad = lax.dot_general(
        value_block[...], chan_grad[own_cols, :], NT, preferred_element_type=jnp.float32
    )
    for index in range(owned):
        precondition(1, index, output_grad[:, index * col_block : (index + 1) * col_block])
    keys_copy.wait()
    scale = width ** (-0.5)
    query_sum = query_total[...].reshape(all_rows, lanes)
    key_t = keys[...].reshape(width, lanes)
    products = query_sum.astype(jnp.float32) * pixel_query[...].astype(jnp.float32)
    sums = jnp.sum(products, axis=0, keepdims=True)
    first = width // 128
    for sub in range(lanes // 128):
        cols = slice(sub * 128, (sub + 1) * 128)
        channel_gain_grad[:, cols] = (
            sums[:, cols] + gain_total[first + sub : first + sub + 1, :]
        ) * gain_rows[3:4, cols]
    for start in range(0, width, 256):
        grad_query[:, start : start + 256] = (
            lax.dot_general(
                query_sum, key_t[start : start + 256], NT, preferred_element_type=jnp.float32
            )
            * scale
        ).astype(BF)
    widen(1)
    arrived_local(weight_copies)
    normed_copy.wait()
    row_tile = width // place.nz
    for index in range(place.nz):
        cols = slice(index * row_tile, (index + 1) * row_tile)
        part = lax.dot_general(
            grad_query[...],
            query_weight[index].reshape(row_tile, width),
            NT,
            preferred_element_type=jnp.float32,
        )
        grad_normed[:, cols] = part
        lat_gain_grad[:, cols] = (
            jnp.sum(part * lat_normed[:, cols].astype(jnp.float32), axis=0, keepdims=True)
            / gain_rows[0:1, cols]
        )
    widen(2)
    values = latents[...]
    centered = values - jnp.mean(values, axis=1, keepdims=True)
    inverse = lax.rsqrt(jnp.mean(centered * centered, axis=1, keepdims=True) + EPSILON)
    hat = centered * inverse
    own = pl.ds(pl.multiple_of(place.p * lat_rows, lat_rows), lat_rows)
    grad = grad_normed[own, :] * gain_rows[0:1, :]
    grad = (
        grad
        - jnp.mean(grad, axis=1, keepdims=True)
        - hat * jnp.mean(grad * hat, axis=1, keepdims=True)
    ) * inverse
    grad = residual_total[...] + grad
    latent_grad[...] = grad
    moments(latents, grad, latent_second, LATENT_RATE, latent_second_new, latent_new)

    per_lane = 128 // row_block
    rows = pl.ds(pl.multiple_of(block_row // per_lane * 128, 128), 128)
    cols = pl.ds(pl.multiple_of(block_col * col_block, col_block), owned * col_block)
    query_grad[...] = lax.dot_general(
        lat_normed[:, rows], grad_query[:, cols], TN, preferred_element_type=jnp.float32
    )
    part = pl.ds(pl.multiple_of(lax.rem(block_row, per_lane) * row_block, row_block), row_block)
    for index in range(owned):
        precondition(0, index, query_grad[part, index * col_block : (index + 1) * col_block])
    widen(3)

    query_copy.wait()
    cols = pl.ds(pl.multiple_of(key_start // 128 * 128, 128), 128)
    key_rows[...] = (
        lax.dot_general(query[:, cols], query_sum, TN, preferred_element_type=jnp.float32) * scale
    )
    part = pl.ds(pl.multiple_of(lax.rem(key_start, 128), keyval_rows), keyval_rows)
    grad = key_rows[part, :]
    output_copy.wait()
    blocks = output_block[...].reshape(col_blocks, row_block, col_block)
    key_rows[0:row_block, :] = sum(
        jnp.dot(
            blocks[block],
            chan_grad[block * col_block : (block + 1) * col_block, :],
            preferred_element_type=jnp.float32,
        )
        for block in range(col_blocks)
    )
    part = pl.ds(pl.multiple_of(lax.rem(key_start, row_block), keyval_rows), keyval_rows)
    grad = jnp.where(device < half_devices, grad, key_rows[part, :])[:, 0:channels]
    keyval_grad[...] = grad
    moments(keyval_weight, grad, keyval_second, KEYVAL_RATE, keyval_second_new, keyval_new)
    for copy in pixel_sent:
        copy.wait()


def tail(
    dims,
    query_total,
    residual_total,
    mats_grad,
    chan_grad,
    owned_arrays,
    gain_rows,
    query,
    lat_normed,
    query_blocks,
    all_keyval,
    pixel_low,
    pixel_query,
    gain_total,
    all_mats,
):
    nz, ny, nx = dims
    proj_blocks, keyval_weight, latents = owned_arrays[0], owned_arrays[5], owned_arrays[7]
    group, lat_rows, lanes = query_total.shape
    all_rows = group * lat_rows
    width = latents.shape[1]
    batches, channels, shard_pixels = pixel_low.shape
    owned, mats, row_block, col_block = proj_blocks.shape
    lead = (nz, ny, nx) if 2 * owned * col_block == width else (nz, ny)
    vmem = pl.BlockSpec(memory_space=pltpu.VMEM)
    anywhere = pl.BlockSpec(memory_space=pl.ANY)
    like = lambda array: jax.ShapeDtypeStruct(array.shape, array.dtype)
    wide = jax.ShapeDtypeStruct((channels, batches, shard_pixels), jnp.float32)
    results = [
        wide,
        like(proj_blocks),
        like(owned_arrays[1]),
        like(owned_arrays[2]),
        like(proj_blocks),
        like(keyval_weight),
        like(keyval_weight),
        like(keyval_weight),
        like(latents),
        like(latents),
        like(latents),
        jax.ShapeDtypeStruct((1, width), jnp.float32),
        jax.ShapeDtypeStruct((1, lanes), jnp.float32),
    ]
    return pl.pallas_call(
        functools.partial(tail_kernel, dims, channels),
        out_shape=results,
        in_specs=[vmem] * 14 + [anywhere] * 5 + [vmem] * 2 + [anywhere] * 2,
        out_specs=[anywhere] + [vmem] * 12,
        scratch_shapes=[
            pltpu.VMEM((all_rows, width), BF),
            pltpu.VMEM((all_rows, width), BF),
            pltpu.VMEM(lead + (row_block, width), BF),
            pltpu.VMEM((nz // 2, ny, nx, 2) + all_keyval.shape[4:], BF),
            pltpu.VMEM((batches, channels, shard_pixels), BF),
            pltpu.VMEM((batches, channels, shard_pixels), jnp.float32),
            pltpu.VMEM((all_rows, width), BF),
            pltpu.VMEM((all_rows, width), jnp.float32),
            pltpu.VMEM((128, owned * col_block), jnp.float32),
            pltpu.VMEM((128, lanes), jnp.float32),
            pltpu.VMEM((row_block, lanes), BF),
            pltpu.VMEM((2, owned, row_block, col_block) if len(lead) == 3 else (nx, 2, row_block, col_block), BF),
            pltpu.SemaphoreType.DMA((5 + width // col_block + 2 * batches,)),
        ],
        compiler_params=pltpu.CompilerParams(vmem_limit_bytes=56 * 2**20),
    )(
        query_total,
        residual_total,
        mats_grad,
        chan_grad.reshape(width, lanes),
        *owned_arrays,
        gain_rows,
        query,
        lat_normed,
        query_blocks,
        all_keyval,
        pixel_low,
        pixel_query,
        gain_total,
        all_keyval.reshape(2 * width, lanes),
        all_mats,
    )


def body(
    pixels,
    pixel_mask,
    proj_blocks,
    proj_left,
    proj_right,
    left_roots,
    right_roots,
    keyval_weight,
    keyval_second,
    latents,
    latent_second,
    gains,
    gain_second,
    mixed_grad,
):
    batches, channels, shard_pixels = pixels.shape
    lat_rows, width = latents.shape
    groups = lax.axis_size("pix")
    scale = width ** (-0.5)

    lat_gain = gains[:width]
    in_gain = gains[width : width + channels]
    mlp_gain = gains[width + channels :]
    side = math.isqrt(groups // 2)
    dims = (lax.axis_size("samp"), side, side)
    widen = lambda row: jnp.pad(row, (0, width - row.shape[0]))
    gain_rows = jnp.stack([lat_gain, widen(in_gain), mlp_gain, widen(1.0 / in_gain)])
    keyval_own = keyval_weight.T
    (
        query_blocks,
        keyval_t,
        lat_normed,
        mats,
        normed_all,
        inverse_all,
        weights_all,
        sent_all,
        landed,
        pixel_query,
        query,
    ) = front(
        dims, pixels.swapaxes(0, 1), pixel_mask, gain_rows, proj_blocks, keyval_own, latents
    )
    gathered = (
        landed,
        keyval_t,
        mats,
        normed_all,
        inverse_all,
        weights_all,
        sent_all,
        pixel_query,
    )
    mixed, pixel_low, mats_grad, chan_grad, query_total, gain_total, residual_total = back(
        dims, channels, gathered, latents, gain_rows, mixed_grad
    )
    (
        pixel_grad,
        proj_grad,
        left_new,
        right_new,
        proj_new,
        keyval_grad,
        keyval_second_new,
        keyval_new,
        latent_grad,
        latent_second_new,
        latent_new,
        lat_gain_grad,
        channel_gain_grad,
    ) = tail(
        dims,
        query_total,
        residual_total,
        mats_grad,
        chan_grad,
        (
            proj_blocks,
            proj_left,
            proj_right,
            left_roots,
            right_roots,
            keyval_own,
            keyval_second.T,
            latents,
            latent_second,
        ),
        gain_rows,
        query,
        lat_normed,
        query_blocks,
        keyval_t,
        pixel_low,
        pixel_query,
        gain_total,
        mats,
    )
    gain_sums = gain_total.reshape(-1)
    gain_grad = jnp.concatenate(
        [
            lat_gain_grad[0],
            channel_gain_grad[0, :channels],
            gain_sums[:width],
        ],
        axis=0,
    )
    gain_second_new, gain_new = moment_step(gains, gain_grad, gain_second, GAIN_RATE)
    return (
        mixed.reshape(batches, lat_rows, width),
        pixel_grad.swapaxes(0, 1),
        proj_grad,
        left_new,
        right_new,
        proj_new,
        keyval_grad.T,
        keyval_second_new.T,
        keyval_new.T,
        latent_grad,
        latent_second_new,
        latent_new,
        gain_grad,
        gain_second_new,
        gain_new,
    )


def solution(mesh):
    blocks = P(("samp", "pix"), None, None, None)
    columns = P(None, ("samp", "pix"))
    rows = P("pix", None)
    return jax.shard_map(
        body,
        mesh=mesh,
        in_specs=(
            P("samp", None, "pix"),
            P("samp", "pix"),
            blocks,
            blocks,
            blocks,
            blocks,
            blocks,
            columns,
            columns,
            rows,
            rows,
            P(),
            P(),
            P("samp", "pix", None),
        ),
        out_specs=(
            P("samp", "pix", None),
            P("samp", None, "pix"),
            blocks,
            blocks,
            blocks,
            blocks,
            columns,
            columns,
            columns,
            rows,
            rows,
            rows,
            P(),
            P(),
            P(),
        ),
        check_vma=False,
    )
```

```python
import functools
import math

import jax
import jax.numpy as jnp
from jax import lax
from jax.experimental import pallas as pl
from jax.experimental.pallas import tpu as pltpu
from jax.sharding import PartitionSpec as P

EPSILON = 1e-05
NEGATIVE = -1e30
HIGHEST = lax.Precision.HIGHEST
STAT_DECAY = 0.5
MATRIX_RATE = 0.5
KEYVAL_RATE = 0.05
LATENT_RATE = 0.7
GAIN_RATE = 0.6
MOMENT_FLOOR = 1e-08
BF = jnp.bfloat16
MESH = pl.DeviceIdType.MESH
NT = (((1,), (1,)), ((), ()))


def moment_step(weight, grad, second, rate):
    second_new = STAT_DECAY * second + (1.0 - STAT_DECAY) * grad * grad
    return (second_new, weight - rate * grad / (jnp.sqrt(second_new) + MOMENT_FLOOR))


def ceil_to(value, step):
    return -(-value // step) * step


class Links:
    def __init__(self, send_sems, recv_sems):
        self.send_sems = send_sems
        self.recv_sems = recv_sems
        self.used = 0
        self.started = []

    def make(self, source, target, samp, pix):
        copy = pltpu.make_async_remote_copy(
            src_ref=source,
            dst_ref=target,
            send_sem=self.send_sems.at[self.used],
            recv_sem=self.recv_sems.at[self.used],
            device_id=(samp, pix),
            device_id_type=MESH,
        )
        self.used += 1
        return copy

    def push(self, source, target, samp, pix):
        copy = self.make(source, target, samp, pix)
        copy.start()
        self.started.append(copy)
        return copy

    def drain(self):
        for copy in self.started:
            copy.wait_send()
        self.started = []


class Place:
    def __init__(self, nz, ny, nx):
        self.nz, self.ny, self.nx = nz, ny, nx
        self.group = ny * nx * 2
        self.z = lax.axis_index("samp")
        self.p = lax.axis_index("pix")
        self.c = lax.rem(self.p, 2)
        self.x = lax.rem(self.p // 2, nx)
        self.y = self.p // (2 * nx)

    def pix(self, y, x, c):
        return (y * self.nx + x) * 2 + c

    def barrier(self):
        semaphore = pltpu.get_barrier_semaphore()
        for step in range(1, self.nz):
            pl.semaphore_signal(
                semaphore,
                inc=1,
                device_id=(lax.rem(self.z + step, self.nz), self.p),
                device_id_type=MESH,
            )
        for step in range(1, self.group):
            pl.semaphore_signal(
                semaphore,
                inc=1,
                device_id=(self.z, lax.rem(self.p + step, self.group)),
                device_id_type=MESH,
            )
        pl.semaphore_wait(semaphore, self.nz - 1 + self.group - 1)

    def push_z(self, links, array, step):
        own = array.at[self.z, self.y, self.x, self.c]
        return [links.push(own, own, lax.rem(self.z - step + self.nz, self.nz), self.p)]

    def push_first(self, links, array, lead, sub, along):
        own = array.at[lead + (self.y, self.x, self.c) + sub]
        copies = []
        if along == "x":
            for step in range(1, self.nx):
                other = self.pix(self.y, lax.rem(self.x + step, self.nx), self.c)
                copies.append(links.push(own, own, self.z, other))
        else:
            for step in range(1, self.ny):
                other = self.pix(lax.rem(self.y + step, self.ny), self.x, self.c)
                copies.append(links.push(own, own, self.z, other))
        return copies

    def push_second(self, links, array, lead, sub, first):
        copies = []
        if first == "x":
            held = array.at[lead + (self.y, slice(None), self.c) + sub]
            for step in range(1, self.ny):
                other = self.pix(lax.rem(self.y + step, self.ny), self.x, self.c)
                copies.append(links.push(held, held, self.z, other))
        else:
            held = array.at[lead + (slice(None), self.x, self.c) + sub]
            for step in range(1, self.nx):
                other = self.pix(self.y, lax.rem(self.x + step, self.nx), self.c)
                copies.append(links.push(held, held, self.z, other))
        return copies

    def push_core(self, links, array, lead):
        held = array.at[lead + (slice(None), slice(None), self.c)]
        return [links.push(held, held, self.z, self.p + 1 - 2 * self.c)]


def arrived(copies):
    for copy in copies:
        copy.wait_recv()


def column_block(array, place, index, col_blocks, owned, sub=()):
    every = slice(None)
    if 2 * owned == col_blocks:
        block = array[(every, every, every, index // owned) + sub + (index % owned,)]
    else:
        block = array[(every, every, index // 2, index % 2) + sub + (0,)]
    return block.reshape(-1, block.shape[-1])


def column_pair(array, place, pair, col_blocks, owned, sub=()):
    return jnp.concatenate(
        [
            column_block(array, place, 2 * pair, col_blocks, owned, sub),
            column_block(array, place, 2 * pair + 1, col_blocks, owned, sub),
        ],
        axis=1,
    )


def front_kernel(
    dims,
    pixels,
    mask,
    gain_rows,
    own_proj,
    own_keyval,
    own_latents,
    all_query,
    all_keyval,
    all_latents,
    all_mats,
    normed_out,
    inverse_out,
    weights_out,
    sent_out,
    landed,
    pixel_query,
    query_out,
    raw,
    gain_cols,
    mats_own,
    g_query,
    g_keyval,
    g_latents,
    lat_normed,
    query,
    normed,
    weights,
    outgoing,
    paired,
    merged,
    send_sems,
    recv_sems,
    local_sems,
):
    channels, batches, shard_pixels = pixels.shape
    lat_rows, width = own_latents.shape
    owned, _, row_block, col_block = own_proj.shape
    col_blocks = width // col_block
    padded = normed.shape[1]
    main = channels // 16 * 16
    place = Place(*dims)
    links = Links(send_sems, recv_sems)
    z, y, x, c, p = place.z, place.y, place.x, place.c, place.p
    half_rows = row_block // 2
    half_width = width // 2
    every = slice(None)
    quarter = shard_pixels // 8
    local = []

    def local_copy(source, target):
        copy = pltpu.make_async_copy(source, target, local_sems.at[len(local)])
        copy.start()
        local.append(copy)
        return copy

    g_query[z, y, x, c] = own_proj[:, 0].astype(BF)
    pixel_copies = [
        local_copy(pixels.at[:, :, pl.ds(part, quarter)], raw.at[:, :, pl.ds(part, quarter)])
        for part in range(0, shard_pixels, quarter)
    ]
    keyval_rows, lanes = g_keyval.shape[4:]
    g_keyval[z, y, x, c] = jnp.zeros((keyval_rows, lanes), BF)
    g_keyval[z, y, x, c, :, 0:channels] = own_keyval[...].astype(BF)
    gain_cols[...] = jnp.broadcast_to(gain_rows[1:2, 0:lanes], (128, lanes)).T
    g_latents[y, x, c] = own_latents[...].astype(BF)
    for mat in range(3):
        mats_own[mat] = own_proj[:, mat + 1].astype(BF)
    own_mats_copy = local_copy(mats_own, all_mats.at[z, y, x, c])
    place.barrier()

    sub_a = (every, pl.ds(0, half_rows))
    sub_b = (every, pl.ds(half_rows, half_rows))
    mats_subs = [
        ((1,), "x"),
        ((2,), "y"),
        ((0, every, pl.ds(0, half_rows)), "x"),
        ((0, every, pl.ds(half_rows, half_rows)), "y"),
    ]

    def level(step):
        return lax.rem(z + step, place.nz)

    def hand_on(push, step):
        copies = push(links, g_query, (level(step),), sub_a, "x")
        copies += push(links, g_query, (level(step),), sub_b, "y")
        copies += push(links, g_keyval, (level(step),), (), "xy"[step % 2])
        return copies

    def hand_on_mats(push, step):
        copies = []
        for sub, along in mats_subs:
            copies += push(links, all_mats, (level(step),), sub, along)
        return copies

    z_group = []
    for step in range(1, place.nz):
        z_group.append(
            place.push_z(links, g_query, step) + place.push_z(links, g_keyval, step)
        )
    firsts = [hand_on(place.push_first, 0)]
    lat_a = (every, pl.ds(0, half_width))
    lat_b = (every, pl.ds(half_width, half_width))
    lat_first = place.push_first(links, g_latents, (), lat_a, "x")
    lat_first += place.push_first(links, g_latents, (), lat_b, "y")
    own_mats_copy.wait()
    z_mats = []
    firsts_m = []

    lane_chunk = 128
    bias_row = channels - main
    row = lax.broadcasted_iota(jnp.int32, (padded - main, lane_chunk), 0)

    def norm_quarter(part):
        pixel_copies[part].wait()

        @pl.loop(0, quarter // lane_chunk)
        def _(chunk):
            start = part * quarter + chunk * lane_chunk
            cols = pl.ds(pl.multiple_of(start, lane_chunk), lane_chunk)
            together = raw[:, :, cols].astype(jnp.float32)
            for image in range(batches):
                value = together[:, image, :]
                value = value - jnp.sum(value, axis=0, keepdims=True) / channels
                variance = jnp.sum(value * value, axis=0, keepdims=True) / channels
                inverse = lax.rsqrt(variance + EPSILON)
                inverse_out[image : image + 1, cols] = inverse
                value = value * inverse * gain_cols[0:channels, :]
                normed[image, 0:main, cols] = value[0:main].astype(BF)
                tail = value[main:channels]
                bias = jnp.where(mask[image : image + 1, cols] == 1, 0.0, NEGATIVE)
                rest = jnp.where(row == bias_row + 1, 1.0, 0.0)
                rest = jnp.where(row == bias_row, bias, rest)
                for index in range(channels - main):
                    rest = jnp.where(row == index, tail[index : index + 1], rest)
                normed[image, main:padded, cols] = rest.astype(BF)

    seconds = []
    seconds_m = []
    cores_m = []

    def first(step):
        arrived(z_group[step - 1])
        firsts.append(hand_on(place.push_first, step))

    def second(step):
        arrived(firsts[step])
        seconds.extend(hand_on(place.push_second, step))

    def first_m(step):
        arrived(z_mats[step - 1])
        firsts_m.append(hand_on_mats(place.push_first, step))

    def second_m(step):
        arrived(firsts_m[step])
        seconds_m.append(hand_on_mats(place.push_second, step))

    def core_m(step):
        arrived(seconds_m[step])
        cores_m.extend(place.push_core(links, all_mats, (level(step),)))

    norm_quarter(0)
    norm_quarter(1)
    second(0)
    arrived(lat_first)
    seconds += place.push_second(links, g_latents, (), lat_a, "x")
    seconds += place.push_second(links, g_latents, (), lat_b, "y")
    norm_quarter(2)
    first(1)
    norm_quarter(3)
    norm_quarter(4)
    first(2)
    second(1)
    norm_quarter(5)
    for step in range(3, place.nz):
        first(step)
    second(2)
    z_mats.extend(place.push_z(links, all_mats, step) for step in range(1, place.nz))
    firsts_m.append(hand_on_mats(place.push_first, 0))
    norm_quarter(6)
    for step in range(3, place.nz):
        second(step)
    norm_quarter(7)
    second_m(0)
    first_m(1)
    local_copy(normed, normed_out)
    arrived(seconds)
    cores = place.push_core(links, g_query, (every,))
    cores += place.push_core(links, g_keyval, (every,))
    cores += place.push_core(links, g_latents, ())
    second_m(1)
    first_m(2)

    arrived(cores)
    for yy in range(place.ny):
        for xx in range(place.nx):
            for cc in range(2):
                rows = pl.ds(((yy * place.nx + xx) * 2 + cc) * lat_rows, lat_rows)
                values = g_latents[yy, xx, cc].astype(jnp.float32)
                mean = jnp.mean(values, axis=1, keepdims=True)
                values = values - mean
                variance = jnp.mean(values * values, axis=1, keepdims=True)
                values = values * lax.rsqrt(variance + EPSILON) * gain_rows[0:1, :]
                lat_normed[rows, :] = values.astype(BF)
    second_m(2)
    local_copy(g_query, all_query)
    local_copy(g_keyval, all_keyval)
    local_copy(lat_normed, all_latents)
    for pair in range(col_blocks // 2):
        query[:, 2 * col_block * pair : 2 * col_block * (pair + 1)] = jnp.dot(
            lat_normed[...],
            column_pair(g_query, place, pair, col_blocks, owned),
            preferred_element_type=jnp.float32,
        ).astype(BF)
    local_copy(query, query_out)
    key_t = g_keyval[0 : place.nz // 2]
    key_t = key_t.reshape(width, key_t.shape[-1])
    projected = jnp.dot(query[...], key_t, preferred_element_type=jnp.float32) * width ** (-0.5)
    lane = lax.broadcasted_iota(jnp.int32, projected.shape, 1)
    pixel_query[...] = jnp.where(lane == channels, 1.0, projected).astype(BF)

    tile = place.nx * 2 * lat_rows
    rows_here = place.ny * place.nx * lat_rows

    def attend(image):
        @pl.loop(0, place.ny)
        def _(step):
            rows = pl.ds(pl.multiple_of(step * tile, tile), tile)
            scores = jnp.dot(
                pixel_query[rows, 0:padded], normed[image], preferred_element_type=jnp.float32
            )
            top = jnp.max(scores, axis=1, keepdims=True)
            top = jnp.maximum(top, 0.1 * NEGATIVE).astype(BF).astype(jnp.float32)
            share = jnp.exp(scores - top).astype(BF)
            weights[image, rows, :] = share
            numer = lax.dot_general(
                share, normed[image], NT, preferred_element_type=jnp.float32
            )
            lane = lax.broadcasted_iota(jnp.int32, numer.shape, 1)
            numer = jnp.where(lane == channels, top, numer).astype(BF)
            outgoing[image, step, :, :, :, 0:padded] = numer.reshape(
                place.nx, 2, lat_rows, padded
            )

        local_copy(weights.at[image], weights_out.at[image])
        last = pl.ds(lanes - 128, 128)
        local_copy(
            outgoing.at[image, :, :, :, :, last], sent_out.at[image]
        )
        return [
            links.push(
                outgoing.at[image, :, :, 1 - c], paired.at[image], z, p + 1 - 2 * c
            )
        ]

    def merge(image, pair):
        arrived(pair)
        mine = outgoing[image, :, :, c].reshape(rows_here, lanes).astype(jnp.float32)
        other = paired[image].reshape(rows_here, lanes).astype(jnp.float32)
        my_top = mine[:, channels : channels + 1]
        other_top = other[:, channels : channels + 1]
        top = jnp.maximum(my_top, other_top)
        lane = lax.broadcasted_iota(jnp.int32, mine.shape, 1)
        both = jnp.exp(my_top - top) * mine + jnp.exp(other_top - top) * other
        both = jnp.where(lane == channels, top, both)
        merged[image] = both.astype(BF).reshape(place.ny, place.nx, lat_rows, lanes)
        chip = y * place.nx + x
        chips = place.ny * place.nx
        local_copy(merged.at[image, y, x], landed.at[chip, image])
        copies = []
        for step in range(1, chips):
            q = lax.rem(chip + step, chips)
            copies.append(
                links.push(
                    merged.at[image, q // place.nx, lax.rem(q, place.nx)],
                    landed.at[chip, image],
                    z,
                    2 * q + c,
                )
            )
        return copies

    for step in range(3, place.nz):
        first_m(step)
    core_m(0)
    pair = attend(0)
    sent = []
    for step in range(3, place.nz):
        second_m(step)
    core_m(1)
    for image in range(1, batches):
        following = attend(image)
        sent += merge(image - 1, pair)
        pair = following
        if image == 1:
            core_m(2)
    sent += merge(batches - 1, pair)
    for step in range(3, place.nz):
        core_m(step)
    arrived(sent)
    arrived(cores_m)
    links.drain()
    for copy in local[9:]:
        copy.wait()


def front_copies(nz, ny, nx, batches):
    both = nx + ny - 2
    count = 3 * (nz - 1) + 2 * nz * (both + max(nx, ny) - 1) + 2 * both
    count += 2 * nz * 2 * both + 3 + nz
    return count + batches * nx * ny


def front(dims, pixels, pixel_mask, gain_rows, proj_blocks, keyval_t, latents):
    nz, ny, nx = dims
    channels, batches, shard_pixels = pixels.shape
    lat_rows, width = latents.shape
    owned, mats, row_block, col_block = proj_blocks.shape
    keyval_rows = keyval_t.shape[0]
    group = 2 * ny * nx
    all_rows = lat_rows * group
    padded = ceil_to(channels + 2, 16)
    lanes = ceil_to(padded, 128)
    vmem = pl.BlockSpec(memory_space=pltpu.VMEM)
    anywhere = pl.BlockSpec(memory_space=pl.ANY)
    cube = (nz, ny, nx, 2)
    copies = front_copies(nz, ny, nx, batches)
    return pl.pallas_call(
        functools.partial(front_kernel, dims),
        out_shape=(
            jax.ShapeDtypeStruct(cube + (owned, row_block, col_block), BF),
            jax.ShapeDtypeStruct(cube + (keyval_rows, lanes), BF),
            jax.ShapeDtypeStruct((all_rows, width), BF),
            jax.ShapeDtypeStruct(cube + (3, owned, row_block, col_block), BF),
            jax.ShapeDtypeStruct((batches, padded, shard_pixels), BF),
            jax.ShapeDtypeStruct((batches, shard_pixels), jnp.float32),
            jax.ShapeDtypeStruct((batches, all_rows, shard_pixels), BF),
            jax.ShapeDtypeStruct((batches, ny, nx, 2, lat_rows, 128), BF),
            jax.ShapeDtypeStruct((ny * nx, batches, lat_rows, lanes), BF),
            jax.ShapeDtypeStruct((all_rows, lanes), BF),
            jax.ShapeDtypeStruct((all_rows, width), BF),
        ),
        in_specs=[anywhere] + [vmem] * 5,
        out_specs=(
            anywhere,
            anywhere,
            anywhere,
            anywhere,
            anywhere,
            vmem,
            anywhere,
            anywhere,
            anywhere,
            vmem,
            anywhere,
        ),
        scratch_shapes=[
            pltpu.VMEM(pixels.shape, BF),
            pltpu.VMEM((lanes, 128), jnp.float32),
            pltpu.VMEM((3, owned, row_block, col_block), BF),
            pltpu.VMEM(cube + (owned, row_block, col_block), BF),
            pltpu.VMEM(cube + (keyval_rows, lanes), BF),
            pltpu.VMEM(cube[1:] + (lat_rows, width), BF),
            pltpu.VMEM((all_rows, width), BF),
            pltpu.VMEM((all_rows, width), BF),
            pltpu.VMEM((batches, padded, shard_pixels), BF),
            pltpu.VMEM((batches, all_rows, shard_pixels), BF),
            pltpu.VMEM((batches, ny, nx, 2, lat_rows, lanes), BF),
            pltpu.VMEM((batches, ny, nx, lat_rows, lanes), BF),
            pltpu.VMEM((batches, ny, nx, lat_rows, lanes), BF),
            pltpu.SemaphoreType.DMA((copies,)),
            pltpu.SemaphoreType.DMA((copies,)),
            pltpu.SemaphoreType.DMA((14 + 3 * batches,)),
        ],
        compiler_params=pltpu.CompilerParams(
            collective_id=0, has_side_effects=True, vmem_limit_bytes=56 * 2**20
        ),
    )(
        pixels,
        pixel_mask,
        gain_rows,
        proj_blocks,
        keyval_t,
        latents,
    )


def add_low(former, latter):
    return (former.astype(jnp.float32) + latter.astype(jnp.float32)).astype(BF)


class Reduce:
    def __init__(self, place, links, term, buffers, along):
        self.place, self.links, self.term, self.along = place, links, term, along
        self.by_core, self.by_first, self.by_second, self.by_z = buffers
        self.waiting = []

    def wait(self):
        arrived(self.waiting)
        self.waiting = []

    def push_core(self):
        place = self.place
        every = slice(None)
        self.waiting = [
            self.links.push(
                self.term.at[every, every, every, 1 - place.c],
                self.by_core,
                place.z,
                place.p + 1 - 2 * place.c,
            )
        ]

    def push_first(self):
        place = self.place
        self.wait()

        @pl.loop(0, self.by_core.shape[0])
        def _(level):
            self.by_core[level] = add_low(
                self.by_core[level], self.term[level, :, :, place.c]
            )

        every = slice(None)
        for step in range(1, place.nx if self.along == "x" else place.ny):
            if self.along == "x":
                xx = lax.rem(place.x + step, place.nx)
                source = self.by_core.at[every, every, xx]
                target = place.pix(place.y, xx, place.c)
            else:
                yy = lax.rem(place.y + step, place.ny)
                source = self.by_core.at[every, yy]
                target = place.pix(yy, place.x, place.c)
            self.waiting.append(
                self.links.push(source, self.by_first.at[step - 1], place.z, target)
            )

    def push_second(self):
        place = self.place
        self.wait()
        if self.along == "x":
            held = self.by_core[:, :, place.x].astype(jnp.float32)
        else:
            held = self.by_core[:, place.y].astype(jnp.float32)
        for slot in range(self.by_first.shape[0]):
            held = held + self.by_first[slot].astype(jnp.float32)
        self.by_first[0] = held.astype(BF)
        every = slice(None)
        for step in range(1, place.ny if self.along == "x" else place.nx):
            if self.along == "x":
                other = lax.rem(place.y + step, place.ny)
                target = place.pix(other, place.x, place.c)
            else:
                other = lax.rem(place.x + step, place.nx)
                target = place.pix(place.y, other, place.c)
            self.waiting.append(
                self.links.push(
                    self.by_first.at[0, every, other],
                    self.by_second.at[step - 1],
                    place.z,
                    target,
                )
            )

    def push_z(self):
        place = self.place
        self.wait()
        mine = place.y if self.along == "x" else place.x
        held = self.by_first[0, :, mine].astype(jnp.float32)
        for slot in range(self.by_second.shape[0]):
            held = held + self.by_second[slot].astype(jnp.float32)
        self.by_second[0] = held.astype(BF)
        for step in range(1, place.nz):
            zz = lax.rem(place.z - step + place.nz, place.nz)
            self.waiting.append(
                self.links.push(self.by_second.at[0, zz], self.by_z.at[step - 1], zz, place.p)
            )

    def total(self):
        self.wait()
        held = self.by_second[0, self.place.z].astype(jnp.float32)
        return held, [self.by_z.at[slot] for slot in range(self.by_z.shape[0])]


class ReduceDown(Reduce):
    def push_z(self):
        place = self.place
        self.wait()

        @pl.loop(0, self.by_core.shape[0])
        def _(level):
            self.by_core[level] = add_low(
                self.by_core[level], self.term[level, :, :, place.c]
            )

        for step in range(1, place.nz):
            zz = lax.rem(place.z - step + place.nz, place.nz)
            self.waiting.append(
                self.links.push(self.by_core.at[zz], self.by_z.at[step - 1], zz, place.p)
            )

    def push_first(self):
        place = self.place
        self.wait()
        held = self.by_core[place.z].astype(jnp.float32)
        for slot in range(self.by_z.shape[0]):
            held = held + self.by_z[slot].astype(jnp.float32)
        self.by_z[0] = held.astype(BF)
        every = slice(None)
        for step in range(1, place.nx if self.along == "x" else place.ny):
            if self.along == "x":
                other = lax.rem(place.x + step, place.nx)
                source = self.by_z.at[0, every, other]
                target = place.pix(place.y, other, place.c)
            else:
                other = lax.rem(place.y + step, place.ny)
                source = self.by_z.at[0, other]
                target = place.pix(other, place.x, place.c)
            self.waiting.append(
                self.links.push(source, self.by_first.at[step - 1], place.z, target)
            )

    def push_second(self):
        place = self.place
        self.wait()
        if self.along == "x":
            held = self.by_z[0, :, place.x].astype(jnp.float32)
        else:
            held = self.by_z[0, place.y].astype(jnp.float32)
        for slot in range(self.by_first.shape[0]):
            held = held + self.by_first[slot].astype(jnp.float32)
        self.by_first[0] = held.astype(BF)
        for step in range(1, place.ny if self.along == "x" else place.nx):
            if self.along == "x":
                other = lax.rem(place.y + step, place.ny)
                target = place.pix(other, place.x, place.c)
            else:
                other = lax.rem(place.x + step, place.nx)
                target = place.pix(place.y, other, place.c)
            self.waiting.append(
                self.links.push(
                    self.by_first.at[0, other], self.by_second.at[step - 1], place.z, target
                )
            )

    def total(self):
        self.wait()
        mine = self.place.y if self.along == "x" else self.place.x
        held = self.by_first[0, mine].astype(jnp.float32)
        return held, [self.by_second.at[slot] for slot in range(self.by_second.shape[0])]


def block_index(block, col_blocks, owned):
    every = slice(None)
    if 2 * owned == col_blocks:
        return (every, every, every, block // owned, block % owned)
    return (every, every, block // 2, block % 2, 0)


def back_kernel(
    dims,
    channels,
    landed,
    all_keyval,
    all_mats,
    normed_all,
    inverse,
    weights_all,
    sent_all,
    pixel_query,
    latents,
    gain_rows,
    grad_rows,
    mixed,
    pixel_grad,
    mats_grad,
    chan_total,
    query_total,
    gain_total,
    residual_total,
    came,
    values,
    mats,
    normed,
    weights,
    tops,
    attended_chan,
    attended,
    middle,
    mid_hat,
    mid_inverse,
    mid_normed,
    slope,
    hidden,
    grad_pre,
    grad_mid_normed,
    grad_mid,
    grad_attended,
    shares,
    query_turned,
    query_acc,
    turned_acc,
    back_turned,
    grad_scores,
    gain_cols,
    staged,
    terms,
    buffers,
    query_low,
    query_came,
    query_levels,
    gain_plane,
    gain_levels,
    residual_parts,
    residual_came,
    residual_levels,
    send_sems,
    recv_sems,
    local_sems,
):
    place = Place(*dims)
    links = Links(send_sems, recv_sems)
    z, y, x, c, p = place.z, place.y, place.x, place.c, place.p
    chips, batches, lat_rows, lanes = landed.shape
    group = place.group
    rows = batches * lat_rows
    all_rows = group * lat_rows
    width = latents.shape[1]
    padded, shard_pixels = normed_all.shape[1:]
    owned, row_block, col_block = all_mats.shape[5:]
    col_blocks = width // col_block
    every = slice(None)
    tile = 256
    tiles = width // tile
    local = []

    def local_copy(source, target):
        copy = pltpu.make_async_copy(source, target, local_sems.at[len(local)])
        copy.start()
        local.append(copy)
        return copy

    came_copy = local_copy(landed, came)
    values_copy = local_copy(all_keyval.at[pl.ds(place.nz // 2, place.nz // 2)], values)
    mats_copies = []
    for mat in range(3):
        copies = []
        for block in range(col_blocks):
            where = block_index(block, col_blocks, owned)
            source = all_mats.at[where[:4] + (mat,) + where[4:]]
            cols = pl.ds(block * col_block, col_block)
            lead = (mat,) + (every,) * (len(mats.shape) - 2)
            copies.append(local_copy(source, mats.at[lead + (cols,)]))
        mats_copies.append(copies)
    tops_copy = local_copy(sent_all, tops)

    def fetch(image):
        slot = image % 2
        return [
            local_copy(normed_all.at[image], normed.at[slot]),
            local_copy(weights_all.at[image], weights.at[slot]),
        ]

    fetched = [fetch(0), fetch(1)]
    place.barrier()

    def columns_of(mat, index):
        lead = (mat,) + (every,) * (len(mats.shape) - 2)
        return mats[lead + (slice(index * tile, (index + 1) * tile),)].reshape(width, tile)

    def rows_of(mat, index):
        return mats[mat, index].reshape(-1, width)

    row_tile = width // place.nz

    came_copy.wait()
    lane = lax.broadcasted_iota(jnp.int32, (rows, lanes), 1)
    parts = [came[g].reshape(rows, lanes).astype(jnp.float32) for g in range(chips)]
    top = [part[:, channels : channels + 1] for part in parts]
    peak = functools.reduce(jnp.maximum, top)
    factor = [jnp.exp(value - peak) for value in top]
    denominator = sum(f * part[:, channels + 1 : channels + 2] for f, part in zip(factor, parts))
    summed = sum(f * part for f, part in zip(factor, parts))
    attended_chan[...] = jnp.where(lane < channels, summed / denominator, 0.0).astype(BF)

    values_copy.wait()
    value_t = values[...].reshape(width, lanes)
    attended[...] = lax.dot_general(
        attended_chan[...], value_t, NT, preferred_element_type=jnp.float32
    ).astype(BF)
    arrived_local(mats_copies[0])
    for index in range(tiles):
        cols = slice(index * tile, (index + 1) * tile)
        own = latents[:, cols]
        middle[:, cols] = jnp.concatenate([own] * batches, axis=0) + jnp.dot(
            attended[...], columns_of(0, index), preferred_element_type=jnp.float32
        )

    @pl.loop(0, rows // lat_rows)
    def _(step):
        part = pl.ds(pl.multiple_of(step * lat_rows, lat_rows), lat_rows)
        value = middle[part, :]
        value = value - jnp.mean(value, axis=1, keepdims=True)
        scale = lax.rsqrt(jnp.mean(value * value, axis=1, keepdims=True) + EPSILON)
        value = value * scale
        mid_hat[part, :] = value
        mid_inverse[part, :] = jnp.broadcast_to(scale, (lat_rows, 128))
        mid_normed[part, :] = (value * gain_rows[2:3, :]).astype(BF)

    arrived_local(mats_copies[1])
    for index in range(tiles):
        cols = slice(index * tile, (index + 1) * tile)
        pre = jnp.dot(mid_normed[...], columns_of(1, index), preferred_element_type=jnp.float32)
        below = 0.5 + 0.5 * lax.erf(pre * 0.5**0.5)
        hidden[:, cols] = (pre * below).astype(BF)
        slope[:, cols] = below + pre * jnp.exp(-0.5 * pre * pre) * (0.5 / math.pi) ** 0.5

    half_rows = row_block // 2

    def store_term(targets, left, right):
        turned = left[...].T
        for pair in range(col_blocks // 2):
            cols = slice(2 * pair * col_block, 2 * (pair + 1) * col_block)
            product = jnp.dot(turned, right[:, cols], preferred_element_type=jnp.float32).astype(
                BF
            )
            for side in range(2):
                where = block_index(2 * pair + side, col_blocks, owned)
                block = product[:, side * col_block : (side + 1) * col_block]
                taken = 0
                for target in targets:
                    height = target.shape[-2]
                    pieces = block.reshape(-1, row_block, col_block)[:, taken : taken + height]
                    taken += height
                    shape = target.shape
                    lead = shape[:3] if 2 * owned == col_blocks else shape[:2]
                    target[where] = pieces.reshape(lead + (height, col_block))

    pairs = []
    for index, kind in enumerate((ReduceDown, Reduce)):
        pairs.append(
            [
                kind(place, links, terms[2 * index + side], buffers[2 * index + side], along)
                for side, along in enumerate("xy")
            ]
        )
    down, inward = pairs
    chan_job = Reduce(place, links, terms[4], buffers[4], "x")
    store_term(terms[0:2], hidden, grad_rows)
    for job in down:
        job.push_core()

    arrived_local(mats_copies[2])
    for index in range(place.nz):
        cols = slice(index * row_tile, (index + 1) * row_tile)
        grad_hidden = lax.dot_general(
            grad_rows[...], rows_of(2, index), NT, preferred_element_type=jnp.float32
        )
        grad_pre[:, cols] = (
            grad_hidden.astype(BF).astype(jnp.float32) * slope[:, cols]
        ).astype(BF)
    for job in down:
        job.push_z()
    gain_plane[p] = jnp.zeros(gain_plane.shape[1:], jnp.float32)
    for index in range(place.nz):
        cols = slice(index * row_tile, (index + 1) * row_tile)
        part = lax.dot_general(
            grad_pre[...], rows_of(1, index), NT, preferred_element_type=jnp.float32
        )
        grad_mid_normed[:, cols] = part
        summed_rows = jnp.sum(part * mid_hat[:, cols], axis=0, keepdims=True)
        for sub in range(row_tile // 128):
            row = index * (row_tile // 128) + sub
            gain_plane[p, row : row + 1, :] = summed_rows[:, sub * 128 : (sub + 1) * 128]

    @pl.loop(0, rows // lat_rows)
    def _(step):
        part = pl.ds(pl.multiple_of(step * lat_rows, lat_rows), lat_rows)
        grad = grad_mid_normed[part, :] * gain_rows[2:3, :]
        hat = mid_hat[part, :]
        grad = (
            grad
            - jnp.mean(grad, axis=1, keepdims=True)
            - hat * jnp.mean(grad * hat, axis=1, keepdims=True)
        ) * mid_inverse[part, 0:1]
        grad_mid[part, :] = (grad_rows[part, :].astype(jnp.float32) + grad).astype(BF)

    for index in range(place.nz):
        cols = slice(index * row_tile, (index + 1) * row_tile)
        grad_attended[:, cols] = lax.dot_general(
            grad_mid[...], rows_of(0, index), NT, preferred_element_type=jnp.float32
        ).astype(BF)
    grad_chan = jnp.dot(grad_attended[...], value_t, preferred_element_type=jnp.float32)
    products = attended_chan[...].astype(jnp.float32) * grad_chan
    row_delta = jnp.sum(products, axis=1, keepdims=True)
    channel_sums = jnp.sum(products, axis=0, keepdims=True)
    for sub in range(lanes // 128):
        row = width // 128 + sub
        gain_plane[p, row : row + 1, :] = channel_sums[:, sub * 128 : (sub + 1) * 128]
    back = jnp.where(lane == channels + 1, row_delta, grad_chan) / denominator
    back = jnp.where(lane == channels, peak, back)
    shares[y, x, c] = back.astype(BF).reshape(batches, lat_rows, lanes)

    share_first = []
    for image in range(batches):
        share_first.append(
            place.push_first(links, shares, (), (image,), "xy"[image % 2])
        )
    gain_sent = []
    for step in range(1, group):
        own = gain_plane.at[p]
        gain_sent.append(links.push(own, own, z, lax.rem(p + step, group)))
    share_second = []
    share_core = []

    def share_on(image):
        arrived(share_first[image])
        share_second.append(place.push_second(links, shares, (), (image,), "xy"[image % 2]))

    def share_pair(image):
        arrived(share_second[image])
        held = shares.at[:, :, c, image]
        share_core.append([links.push(held, held, z, p + 1 - 2 * c)])

    terms[4][...] = (
        jnp.dot(grad_mid[...].T, attended_chan[...], preferred_element_type=jnp.float32)
        .astype(BF)
        .reshape(terms[4].shape)
    )
    chan_job.push_core()
    store_term(terms[2:4], mid_normed, grad_pre)
    for job in inward:
        job.push_core()
    for image in range(batches):
        share_on(image)
    chan_job.push_first()
    for job in inward:
        job.push_first()
    residual = sum(
        grad_mid[image * lat_rows : (image + 1) * lat_rows].astype(jnp.float32)
        for image in range(batches)
    )
    part_width = width // place.nz
    residual_sent = []
    for zz in range(place.nz):
        residual_parts[zz] = residual[:, zz * part_width : (zz + 1) * part_width].astype(BF)
    for step in range(1, place.nz):
        zz = lax.rem(z + step, place.nz)
        residual_sent.append(
            links.push(residual_parts.at[zz], residual_came.at[step - 1], zz, p)
        )

    lane_all = lax.broadcasted_iota(jnp.int32, (all_rows, lanes), 1)
    query_turned[...] = jnp.where(
        lane_all < channels, pixel_query[...].astype(jnp.float32), 0.0
    ).T[0:padded].astype(BF)
    turned_acc[...] = jnp.zeros(turned_acc.shape, jnp.float32)
    gain_cols[0] = jnp.broadcast_to(gain_rows[1:2, 0:lanes], (128, lanes)).T[0:padded]
    gain_cols[1] = jnp.broadcast_to(gain_rows[3:4, 0:lanes], (128, lanes)).T[0:padded]
    chunk = min(512, shard_pixels)
    tops_copy.wait()

    def attend_query(image):
        slot = image % 2
        arrived(share_core[image])
        arrived_local(fetched[image])
        back = shares[:, :, :, image].reshape(all_rows, lanes).astype(jnp.float32)
        top = tops[image].reshape(all_rows, 128).astype(jnp.float32)[
            :, channels - (lanes - 128) :
        ][:, 0:1]
        share = jnp.exp(top - back[:, channels : channels + 1])
        back = jnp.where(lane_all == channels, 0.0, back * share)
        back = jnp.where(lane_all > channels + 1, 0.0, back)
        back_low = jnp.where(lane_all == channels + 1, -back, back).astype(BF)[:, 0:padded]
        back_turned[image] = jnp.where(lane_all < channels, back, 0.0).T[0:padded].astype(BF)

        @pl.loop(0, shard_pixels // chunk)
        def _(step):
            cols = pl.ds(pl.multiple_of(step * chunk, chunk), chunk)
            normed_chunk = normed[slot, :, cols]
            grad_weights = jnp.dot(back_low, normed_chunk, preferred_element_type=jnp.float32)
            grad_chunk = (weights[slot, :, cols].astype(jnp.float32) * grad_weights).astype(BF)
            grad_scores[image, :, cols] = grad_chunk
            turned_acc[0:padded, :] += lax.dot_general(
                normed_chunk, grad_chunk, NT, preferred_element_type=jnp.float32
            )

        if image + 2 < batches:
            fetched.append(fetch(image + 2))

    order = list(range(2, batches)) + [0, 1]
    staged_out = []

    def attend_pixels(turn):
        image = order[turn]
        slot = image % 2
        if turn >= 2:
            arrived_local(fetched[batches + turn - 2])
            staged_out[turn - 2].wait()

        @pl.loop(0, shard_pixels // chunk)
        def _(step):
            cols = pl.ds(pl.multiple_of(step * chunk, chunk), chunk)
            grad_normed = jnp.dot(
                query_turned[...], grad_scores[image, :, cols], preferred_element_type=jnp.float32
            ) + jnp.dot(
                back_turned[image], weights[slot, :, cols], preferred_element_type=jnp.float32
            )
            normal = normed[slot, :, cols].astype(jnp.float32)
            second_mean = jnp.sum(grad_normed * normal, axis=0, keepdims=True) / channels
            spread = jnp.concatenate([gain_cols[0]] * (chunk // 128), axis=1)
            spread_back = jnp.concatenate([gain_cols[1]] * (chunk // 128), axis=1)
            grad_hat = grad_normed * spread
            first_mean = jnp.sum(grad_hat, axis=0, keepdims=True) / channels
            result = (grad_hat - first_mean - normal * spread_back * second_mean) * inverse[
                image : image + 1, cols
            ]
            staged[turn % 2, :, cols] = result[0:channels].astype(BF)

        staged_out.append(local_copy(staged.at[turn % 2], pixel_grad.at[image]))
        if turn + 2 < batches:
            fetched.append(fetch(order[turn + 2]))

    share_pair(0)
    share_pair(1)
    attend_query(0)
    share_pair(2)
    share_pair(3)
    chan_job.push_second()
    attend_query(1)
    arrived(gain_sent)
    gain_levels[z] = sum(gain_plane[g] for g in range(group))
    gain_up = []
    for step in range(1, place.nz):
        own = gain_levels.at[z]
        gain_up.append(links.push(own, own, lax.rem(z + step, place.nz), p))
    attend_query(2)
    chan_job.push_z()
    for job in inward:
        job.push_second()
    attend_query(3)

    query_acc[...] = turned_acc[...].T
    query_low[...] = query_acc[...].astype(BF)
    query_sent = []
    for step in range(1, group):
        q = lax.rem(p + step, group)
        part = pl.ds(pl.multiple_of(q * lat_rows, lat_rows), lat_rows)
        query_sent.append(links.push(query_low.at[part], query_came.at[step - 1], z, q))
    attend_pixels(0)
    held, came_z = chan_job.total()
    for part in came_z:
        held = held + part[...].astype(jnp.float32)
    chan_total[z, y, x, c] = held.astype(BF)
    chan_z = []
    for step in range(1, place.nz):
        chan_z += place.push_z(links, chan_total, step)
    for job in down:
        job.push_first()
    arrived(query_sent)
    own_rows = pl.ds(pl.multiple_of(p * lat_rows, lat_rows), lat_rows)
    held = query_acc[own_rows, :]
    for slot in range(group - 1):
        held = held + query_came[slot].astype(jnp.float32)
    query_levels[z] = held.astype(BF)
    query_up = []
    for step in range(1, place.nz):
        own = query_levels.at[z]
        query_up.append(links.push(own, own, lax.rem(z + step, place.nz), p))
    attend_pixels(1)
    arrived(chan_z)
    chan_first = place.push_first(links, chan_total, (every,), (), "x")
    arrived(query_up)
    query_total[p] = sum(query_levels[zz].astype(jnp.float32) for zz in range(place.nz)).astype(BF)
    query_all = []
    for step in range(1, group):
        own = query_total.at[p]
        query_all.append(links.push(own, own, z, lax.rem(p + step, group)))
    for job in inward:
        job.push_z()
    for job in down:
        job.push_second()
    attend_pixels(2)
    arrived(chan_first)
    chan_second = place.push_second(links, chan_total, (every,), (), "x")
    arrived(residual_sent)
    residual_levels[z] = (
        residual_parts[z].astype(jnp.float32)
        + sum(residual_came[slot].astype(jnp.float32) for slot in range(place.nz - 1))
    ).astype(BF)
    residual_up = []
    for step in range(1, place.nz):
        own = residual_levels.at[z]
        residual_up.append(links.push(own, own, lax.rem(z + step, place.nz), p))
    attend_pixels(3)
    arrived(chan_second)
    chan_core = place.push_core(links, chan_total, (every,))
    for index in range(tiles):
        cols = slice(index * tile, (index + 1) * tile)
        mixed[:, cols] = (
            middle[:, cols]
            + jnp.dot(hidden[...], columns_of(2, index), preferred_element_type=jnp.float32)
        ).astype(BF)
    def finish(job, target):
        held, came_z = job.total()
        for part in came_z:
            held = held + part[...].astype(jnp.float32)
        target[...] = held

    def finish_mat(mat, jobs):
        for side, job in enumerate(jobs):
            finish(job, mats_grad.at[mat, :, pl.ds(side * half_rows, half_rows)])

    finish_mat(1, down)
    arrived(gain_up)
    gain_total[...] = sum(gain_levels[zz] for zz in range(place.nz))
    arrived(residual_up)
    for zz in range(place.nz):
        residual_total[:, zz * part_width : (zz + 1) * part_width] = residual_levels[zz].astype(
            jnp.float32
        )
    finish_mat(0, inward)
    arrived(chan_core)
    arrived(query_all)
    links.drain()
    for copy in staged_out[batches - 2 :]:
        copy.wait()


def arrived_local(copies):
    for copy in copies:
        copy.wait()


def back_copies(nz, ny, nx, batches):
    group = 2 * ny * nx
    both = nx + ny - 2
    count = batches // 2 * 2 * both + batches
    count += 5 * (1 + both + nz - 1) + nz - 1 + both + 1
    count += 4 * (nz - 1) + 3 * (group - 1)
    return count


def back(dims, channels, gathered, latents, gain_rows, mixed_grad):
    landed, all_keyval, all_mats, normed_all, inverse, weights_all, sent_all, pixel_query = gathered
    nz, ny, nx = dims
    batches, lat_rows, lanes = landed.shape[1:]
    group = 2 * ny * nx
    rows = batches * lat_rows
    all_rows = group * lat_rows
    width = latents.shape[1]
    padded, shard_pixels = normed_all.shape[1:]
    owned, row_block, col_block = all_mats.shape[5:]
    keyval_rows = all_keyval.shape[4]
    half_rows = row_block // 2
    vmem = pl.BlockSpec(memory_space=pltpu.VMEM)
    anywhere = pl.BlockSpec(memory_space=pl.ANY)
    lead = (nz, ny, nx) if 2 * owned * col_block == width else (nz, ny)
    cube = (nz, ny, nx, 2)
    inners = [(nz, (owned, half_rows, col_block), along) for along in "xyxy"]
    inners.append((nz, (width // (group * nz), lanes), "x"))
    terms = [pltpu.VMEM((levels, ny, nx, 2) + inner, BF) for levels, inner, _ in inners]
    buffers = []
    for index, (levels, inner, along) in enumerate(inners):
        one, two = (nx, ny) if along == "x" else (ny, nx)
        plane_last = index < 2
        buffers.append(
            [
                pltpu.VMEM((levels, ny, nx) + inner, BF),
                pltpu.VMEM((one - 1,) + (() if plane_last else (levels,)) + (two,) + inner, BF),
                pltpu.VMEM((two - 1,) + (() if plane_last else (levels,)) + inner, BF),
                pltpu.VMEM((nz - 1,) + ((ny, nx) if plane_last else ()) + inner, BF),
            ]
        )
    wide = lambda kind: pltpu.VMEM((rows, width), kind)
    copies = back_copies(nz, ny, nx, batches)
    return pl.pallas_call(
        functools.partial(back_kernel, dims, channels),
        out_shape=(
            jax.ShapeDtypeStruct((rows, width), BF),
            jax.ShapeDtypeStruct((batches, channels, shard_pixels), BF),
            jax.ShapeDtypeStruct((2, owned, row_block, col_block), jnp.float32),
            jax.ShapeDtypeStruct(cube + (width // (group * nz), lanes), BF),
            jax.ShapeDtypeStruct((group, lat_rows, lanes), BF),
            jax.ShapeDtypeStruct((16, 128), jnp.float32),
            jax.ShapeDtypeStruct((lat_rows, width), jnp.float32),
        ),
        in_specs=[
            anywhere,
            anywhere,
            anywhere,
            anywhere,
            vmem,
            anywhere,
            anywhere,
            vmem,
            vmem,
            vmem,
            vmem,
        ],
        out_specs=(vmem, anywhere, vmem, vmem, vmem, vmem, vmem),
        scratch_shapes=[
            pltpu.VMEM((ny * nx, batches, lat_rows, lanes), BF),
            pltpu.VMEM((nz // 2, ny, nx, 2, keyval_rows, lanes), BF),
            pltpu.VMEM((3,) + lead + (row_block, width), BF),
            pltpu.VMEM((2, padded, shard_pixels), BF),
            pltpu.VMEM((2, all_rows, shard_pixels), BF),
            pltpu.VMEM((batches, ny, nx, 2, lat_rows, 128), BF),
            pltpu.VMEM((rows, lanes), BF),
            wide(BF),
            wide(jnp.float32),
            wide(jnp.float32),
            pltpu.VMEM((rows, 128), jnp.float32),
            wide(BF),
            wide(jnp.float32),
            wide(BF),
            wide(BF),
            wide(jnp.float32),
            wide(BF),
            wide(BF),
            pltpu.VMEM(cube[1:] + (batches, lat_rows, lanes), BF),
            pltpu.VMEM((padded, all_rows), BF),
            pltpu.VMEM((all_rows, lanes), jnp.float32),
            pltpu.VMEM((lanes, all_rows), jnp.float32),
            pltpu.VMEM((batches, padded, all_rows), BF),
            pltpu.VMEM((batches, all_rows, shard_pixels), BF),
            pltpu.VMEM((2, padded, 128), jnp.float32),
            pltpu.VMEM((2, channels, shard_pixels), BF),
            terms,
            buffers,
            pltpu.VMEM((all_rows, lanes), BF),
            pltpu.VMEM((group - 1, lat_rows, lanes), BF),
            pltpu.VMEM((nz, lat_rows, lanes), BF),
            pltpu.VMEM((group, 16, 128), jnp.float32),
            pltpu.VMEM((nz, 16, 128), jnp.float32),
            pltpu.VMEM((nz, lat_rows, width // nz), BF),
            pltpu.VMEM((nz - 1, lat_rows, width // nz), BF),
            pltpu.VMEM((nz, lat_rows, width // nz), BF),
            pltpu.SemaphoreType.DMA((copies,)),
            pltpu.SemaphoreType.DMA((copies,)),
            pltpu.SemaphoreType.DMA((3 + 3 * (width // col_block) + 5 * batches,)),
        ],
        compiler_params=pltpu.CompilerParams(
            collective_id=1, has_side_effects=True, vmem_limit_bytes=61 * 2**20
        ),
    )(
        landed,
        all_keyval,
        all_mats,
        normed_all,
        inverse,
        weights_all,
        sent_all,
        pixel_query,
        latents,
        gain_rows,
        mixed_grad.reshape(rows, width),
    )


TN = (((0,), (0,)), ((), ()))


def tail_kernel(
    dims,
    channels,
    query_total,
    residual_total,
    mats_grad,
    chan_grad,
    proj_blocks,
    left_in,
    right_in,
    left_roots_in,
    right_roots_in,
    keyval_weight,
    keyval_second,
    latents,
    latent_second,
    gain_rows,
    query_in,
    lat_normed_in,
    query_blocks,
    all_keyval,
    pixel_low,
    pixel_query,
    gain_total,
    all_rows_keyval,
    all_mats,
    mixed_in,
    pixel_grad,
    proj_grad,
    left_new,
    right_new,
    proj_new,
    keyval_grad,
    keyval_second_new,
    keyval_new,
    latent_grad,
    latent_second_new,
    latent_new,
    gain_grad,
    mixed_out,
    query,
    lat_normed,
    query_weight,
    keys,
    pixel_came,
    pixel_wide,
    grad_query,
    grad_normed,
    query_grad,
    key_rows,
    value_block,
    output_block,
    proj_left,
    proj_right,
    left_roots,
    right_roots,
    local_sems,
):
    place = Place(*dims)
    group, lat_rows, lanes = query_total.shape
    all_rows = group * lat_rows
    width = latents.shape[1]
    batches = pixel_low.shape[0]
    owned, mats, row_block, col_block = proj_blocks.shape
    col_blocks = width // col_block
    keyval_rows = keyval_weight.shape[0]
    device = place.z * group + place.p
    every = slice(None)
    local = []

    def local_copy(source, target):
        copy = pltpu.make_async_copy(source, target, local_sems.at[len(local)])
        copy.start()
        local.append(copy)
        return copy

    keys_copy = local_copy(all_keyval.at[pl.ds(0, place.nz // 2)], keys)
    weight_copies = []
    for block in range(col_blocks):
        lead = (every,) * (len(query_weight.shape) - 1)
        weight_copies.append(
            local_copy(
                query_blocks.at[block_index(block, col_blocks, owned)],
                query_weight.at[lead + (pl.ds(block * col_block, col_block),)],
            )
        )
    normed_copy = local_copy(lat_normed_in, lat_normed)
    block_row = device * owned // col_blocks
    block_col = lax.rem(device * owned, col_blocks)
    half_devices = width // keyval_rows
    key_start = lax.rem(device, half_devices) * keyval_rows
    value_rows = pl.ds(pl.multiple_of(width + block_row * row_block, row_block), row_block)
    value_copy = local_copy(all_rows_keyval.at[value_rows], value_block)
    output_row = key_start // row_block
    if 2 * owned == col_blocks:
        across = lax.rem(output_row, place.nx)
        along = lax.rem(output_row // place.nx, place.ny)
        source = all_mats.at[output_row // (place.nx * place.ny), along, across, :, 0]
    else:
        source = all_mats.at[output_row // place.ny, lax.rem(output_row, place.ny), :, :, 0, 0]
    output_copy = local_copy(source, output_block)
    stat_copies = [
        local_copy(left_in, proj_left),
        local_copy(right_in, proj_right),
        local_copy(left_roots_in, left_roots),
        local_copy(right_roots_in, right_roots),
    ]
    query_copy = local_copy(query_in, query)
    mixed_out[...] = mixed_in[...]
    pixel_copies = [local_copy(pixel_low.at[i], pixel_came.at[i]) for i in range(batches)]
    pixel_sent = []

    def widen(image):
        pixel_copies[image].wait()

        @pl.loop(0, pixel_low.shape[2] // 256)
        def _(step):
            cols = pl.ds(pl.multiple_of(step * 256, 256), 256)
            pixel_wide[image, :, cols] = pixel_came[image, :, cols].astype(jnp.float32)

        pixel_sent.append(local_copy(pixel_wide.at[image], pixel_grad.at[:, image]))

    def moments(weight, grad, second, rate, second_out, weight_out):
        second_value = STAT_DECAY * second[...] + (1.0 - STAT_DECAY) * grad * grad
        second_out[...] = second_value
        weight_out[...] = weight[...] - rate * grad / (jnp.sqrt(second_value) + MOMENT_FLOOR)

    def precondition(mat, index, grad):
        low = grad.astype(BF)
        proj_grad[index, mat] = grad
        left_new[index, mat] = STAT_DECAY * proj_left[index, mat] + (
            1.0 - STAT_DECAY
        ) * lax.dot_general(low, low, NT, preferred_element_type=jnp.float32)
        right_new[index, mat] = STAT_DECAY * proj_right[index, mat] + (
            1.0 - STAT_DECAY
        ) * lax.dot_general(low, low, TN, preferred_element_type=jnp.float32)
        step = jnp.dot(
            left_roots[index, mat].astype(BF), low, preferred_element_type=jnp.float32
        ).astype(BF)
        step = jnp.dot(
            step, right_roots[index, mat].astype(BF), preferred_element_type=jnp.float32
        )
        proj_new[index, mat] = proj_blocks[index, mat] - MATRIX_RATE * step

    keys_copy.wait()
    scale = width ** (-0.5)
    query_sum = query_total[...].reshape(all_rows, lanes)
    key_t = keys[...].reshape(width, lanes)
    products = query_sum.astype(jnp.float32) * pixel_query[...].astype(jnp.float32)
    sums = jnp.sum(products, axis=0, keepdims=True)
    first = width // 128
    for sub in range(lanes // 128):
        cols = slice(sub * 128, (sub + 1) * 128)
        gain_grad[:, width + sub * 128 : width + (sub + 1) * 128] = (
            sums[:, cols] + gain_total[first + sub : first + sub + 1, :]
        ) * gain_rows[3:4, cols]
    for sub in range(first):
        at = width + lanes + sub * 128
        gain_grad[:, at : at + 128] = gain_total[sub : sub + 1, :]
    for start in range(0, width, 256):
        grad_query[:, start : start + 256] = (
            lax.dot_general(
                query_sum, key_t[start : start + 256], NT, preferred_element_type=jnp.float32
            )
            * scale
        ).astype(BF)
    widen(0)
    arrived_local(weight_copies)
    normed_copy.wait()
    row_tile = width // place.nz
    for index in range(place.nz):
        cols = slice(index * row_tile, (index + 1) * row_tile)
        part = lax.dot_general(
            grad_query[...],
            query_weight[index].reshape(row_tile, width),
            NT,
            preferred_element_type=jnp.float32,
        )
        grad_normed[:, cols] = part
        gain_grad[:, cols] = (
            jnp.sum(part * lat_normed[:, cols].astype(jnp.float32), axis=0, keepdims=True)
            / gain_rows[0:1, cols]
        )
    widen(1)
    arrived_local(stat_copies)
    for mat in range(2):
        for index in range(owned):
            precondition(mat + 2, index, mats_grad[mat, index])
    value_copy.wait()
    own_cols = pl.ds(pl.multiple_of(block_col * col_block, col_block), owned * col_block)
    output_grad = lax.dot_general(
        value_block[...], chan_grad[own_cols, :], NT, preferred_element_type=jnp.float32
    )
    for index in range(owned):
        precondition(1, index, output_grad[:, index * col_block : (index + 1) * col_block])
    widen(2)
    values = latents[...]
    centered = values - jnp.mean(values, axis=1, keepdims=True)
    inverse = lax.rsqrt(jnp.mean(centered * centered, axis=1, keepdims=True) + EPSILON)
    hat = centered * inverse
    own = pl.ds(pl.multiple_of(place.p * lat_rows, lat_rows), lat_rows)
    grad = grad_normed[own, :] * gain_rows[0:1, :]
    grad = (
        grad
        - jnp.mean(grad, axis=1, keepdims=True)
        - hat * jnp.mean(grad * hat, axis=1, keepdims=True)
    ) * inverse
    grad = residual_total[...] + grad
    latent_grad[...] = grad
    moments(latents, grad, latent_second, LATENT_RATE, latent_second_new, latent_new)

    per_lane = 128 // row_block
    rows = pl.ds(pl.multiple_of(block_row // per_lane * 128, 128), 128)
    cols = pl.ds(pl.multiple_of(block_col * col_block, col_block), owned * col_block)
    query_grad[...] = lax.dot_general(
        lat_normed[:, rows], grad_query[:, cols], TN, preferred_element_type=jnp.float32
    )
    part = pl.ds(pl.multiple_of(lax.rem(block_row, per_lane) * row_block, row_block), row_block)
    for index in range(owned):
        precondition(0, index, query_grad[part, index * col_block : (index + 1) * col_block])
    widen(3)

    query_copy.wait()
    cols = pl.ds(pl.multiple_of(key_start // 128 * 128, 128), 128)
    key_rows[...] = (
        lax.dot_general(query[:, cols], query_sum, TN, preferred_element_type=jnp.float32) * scale
    )
    part = pl.ds(pl.multiple_of(lax.rem(key_start, 128), keyval_rows), keyval_rows)
    grad = key_rows[part, :]
    output_copy.wait()
    blocks = output_block[...].reshape(col_blocks, row_block, col_block)
    key_rows[0:row_block, :] = sum(
        jnp.dot(
            blocks[block],
            chan_grad[block * col_block : (block + 1) * col_block, :],
            preferred_element_type=jnp.float32,
        )
        for block in range(col_blocks)
    )
    part = pl.ds(pl.multiple_of(lax.rem(key_start, row_block), keyval_rows), keyval_rows)
    grad = jnp.where(device < half_devices, grad, key_rows[part, :])[:, 0:channels]
    keyval_grad[...] = grad
    moments(keyval_weight, grad, keyval_second, KEYVAL_RATE, keyval_second_new, keyval_new)
    for copy in pixel_sent:
        copy.wait()


def tail(
    dims,
    query_total,
    residual_total,
    mats_grad,
    chan_grad,
    owned_arrays,
    gain_rows,
    query,
    lat_normed,
    query_blocks,
    all_keyval,
    pixel_low,
    pixel_query,
    gain_total,
    all_mats,
    mixed,
):
    nz, ny, nx = dims
    proj_blocks, keyval_weight, latents = owned_arrays[0], owned_arrays[5], owned_arrays[7]
    group, lat_rows, lanes = query_total.shape
    all_rows = group * lat_rows
    width = latents.shape[1]
    batches, channels, shard_pixels = pixel_low.shape
    owned, mats, row_block, col_block = proj_blocks.shape
    lead = (nz, ny, nx) if 2 * owned * col_block == width else (nz, ny)
    vmem = pl.BlockSpec(memory_space=pltpu.VMEM)
    anywhere = pl.BlockSpec(memory_space=pl.ANY)
    like = lambda array: jax.ShapeDtypeStruct(array.shape, array.dtype)
    wide = jax.ShapeDtypeStruct((channels, batches, shard_pixels), jnp.float32)
    results = [
        wide,
        like(proj_blocks),
        like(owned_arrays[1]),
        like(owned_arrays[2]),
        like(proj_blocks),
        like(keyval_weight),
        like(keyval_weight),
        like(keyval_weight),
        like(latents),
        like(latents),
        like(latents),
        jax.ShapeDtypeStruct((1, 2 * width + lanes), jnp.float32),
        like(mixed),
    ]
    return pl.pallas_call(
        functools.partial(tail_kernel, dims, channels),
        out_shape=results,
        in_specs=(
            [vmem] * 5
            + [anywhere] * 4
            + [vmem] * 5
            + [anywhere] * 5
            + [vmem] * 2
            + [anywhere] * 2
            + [vmem]
        ),
        out_specs=[anywhere] + [vmem] * 12,
        scratch_shapes=[
            pltpu.VMEM((all_rows, width), BF),
            pltpu.VMEM((all_rows, width), BF),
            pltpu.VMEM(lead + (row_block, width), BF),
            pltpu.VMEM((nz // 2, ny, nx, 2) + all_keyval.shape[4:], BF),
            pltpu.VMEM((batches, channels, shard_pixels), BF),
            pltpu.VMEM((batches, channels, shard_pixels), jnp.float32),
            pltpu.VMEM((all_rows, width), BF),
            pltpu.VMEM((all_rows, width), jnp.float32),
            pltpu.VMEM((128, owned * col_block), jnp.float32),
            pltpu.VMEM((128, lanes), jnp.float32),
            pltpu.VMEM((row_block, lanes), BF),
            pltpu.VMEM((2, owned, row_block, col_block) if len(lead) == 3 else (nx, 2, row_block, col_block), BF),
            *[pltpu.VMEM(array.shape, jnp.float32) for array in owned_arrays[1:5]],
            pltpu.SemaphoreType.DMA((10 + width // col_block + 2 * batches,)),
        ],
        compiler_params=pltpu.CompilerParams(vmem_limit_bytes=56 * 2**20),
    )(
        query_total,
        residual_total,
        mats_grad,
        chan_grad.reshape(width, lanes),
        *owned_arrays,
        gain_rows,
        query,
        lat_normed,
        query_blocks,
        all_keyval,
        pixel_low,
        pixel_query,
        gain_total,
        all_keyval.reshape(2 * width, lanes),
        all_mats,
        mixed,
    )


def body(
    pixels,
    pixel_mask,
    proj_blocks,
    proj_left,
    proj_right,
    left_roots,
    right_roots,
    keyval_weight,
    keyval_second,
    latents,
    latent_second,
    gains,
    gain_second,
    mixed_grad,
):
    batches, channels, shard_pixels = pixels.shape
    lat_rows, width = latents.shape
    groups = lax.axis_size("pix")
    scale = width ** (-0.5)

    lat_gain = gains[:width]
    in_gain = gains[width : width + channels]
    mlp_gain = gains[width + channels :]
    side = math.isqrt(groups // 2)
    dims = (lax.axis_size("samp"), side, side)
    widen = lambda row: jnp.pad(row, (0, width - row.shape[0]))
    gain_rows = jnp.stack([lat_gain, widen(in_gain), mlp_gain, widen(1.0 / in_gain)])
    keyval_own = keyval_weight.T
    (
        query_blocks,
        keyval_t,
        lat_normed,
        mats,
        normed_all,
        inverse_all,
        weights_all,
        sent_all,
        landed,
        pixel_query,
        query,
    ) = front(
        dims, pixels.swapaxes(0, 1), pixel_mask, gain_rows, proj_blocks, keyval_own, latents
    )
    gathered = (
        landed,
        keyval_t,
        mats,
        normed_all,
        inverse_all,
        weights_all,
        sent_all,
        pixel_query,
    )
    mixed, pixel_low, mats_grad, chan_grad, query_total, gain_total, residual_total = back(
        dims, channels, gathered, latents, gain_rows, mixed_grad
    )
    (
        pixel_grad,
        proj_grad,
        left_new,
        right_new,
        proj_new,
        keyval_grad,
        keyval_second_new,
        keyval_new,
        latent_grad,
        latent_second_new,
        latent_new,
        gain_row,
        mixed,
    ) = tail(
        dims,
        query_total,
        residual_total,
        mats_grad,
        chan_grad,
        (
            proj_blocks,
            proj_left,
            proj_right,
            left_roots,
            right_roots,
            keyval_own,
            keyval_second.T,
            latents,
            latent_second,
        ),
        gain_rows,
        query,
        lat_normed,
        query_blocks,
        keyval_t,
        pixel_low,
        pixel_query,
        gain_total,
        mats,
        mixed,
    )
    lanes = ceil_to(ceil_to(channels + 2, 16), 128)
    gain_grad = jnp.concatenate(
        [gain_row[0, : width + channels], gain_row[0, width + lanes :]], axis=0
    )
    gain_second_new, gain_new = moment_step(gains, gain_grad, gain_second, GAIN_RATE)
    return (
        mixed.reshape(batches, lat_rows, width),
        pixel_grad.swapaxes(0, 1),
        proj_grad,
        left_new,
        right_new,
        proj_new,
        keyval_grad.T,
        keyval_second_new.T,
        keyval_new.T,
        latent_grad,
        latent_second_new,
        latent_new,
        gain_grad,
        gain_second_new,
        gain_new,
    )


def solution(mesh):
    blocks = P(("samp", "pix"), None, None, None)
    columns = P(None, ("samp", "pix"))
    rows = P("pix", None)
    return jax.shard_map(
        body,
        mesh=mesh,
        in_specs=(
            P("samp", None, "pix"),
            P("samp", "pix"),
            blocks,
            blocks,
            blocks,
            blocks,
            blocks,
            columns,
            columns,
            rows,
            rows,
            P(),
            P(),
            P("samp", "pix", None),
        ),
        out_specs=(
            P("samp", "pix", None),
            P("samp", None, "pix"),
            blocks,
            blocks,
            blocks,
            blocks,
            columns,
            columns,
            columns,
            rows,
            rows,
            rows,
            P(),
            P(),
            P(),
        ),
        check_vma=False,
    )
```

```python
import functools
import math

import jax
import jax.numpy as jnp
from jax import lax
from jax.experimental import pallas as pl
from jax.experimental.pallas import tpu as pltpu
from jax.sharding import PartitionSpec as P

EPSILON = 1e-05
NEGATIVE = -1e30
HIGHEST = lax.Precision.HIGHEST
STAT_DECAY = 0.5
MATRIX_RATE = 0.5
KEYVAL_RATE = 0.05
LATENT_RATE = 0.7
GAIN_RATE = 0.6
MOMENT_FLOOR = 1e-08
BF = jnp.bfloat16
MESH = pl.DeviceIdType.MESH
NT = (((1,), (1,)), ((), ()))


def moment_step(weight, grad, second, rate):
    second_new = STAT_DECAY * second + (1.0 - STAT_DECAY) * grad * grad
    return (second_new, weight - rate * grad / (jnp.sqrt(second_new) + MOMENT_FLOOR))


def ceil_to(value, step):
    return -(-value // step) * step


class Links:
    def __init__(self, send_sems, recv_sems):
        self.send_sems = send_sems
        self.recv_sems = recv_sems
        self.used = 0
        self.started = []

    def make(self, source, target, samp, pix):
        copy = pltpu.make_async_remote_copy(
            src_ref=source,
            dst_ref=target,
            send_sem=self.send_sems.at[self.used],
            recv_sem=self.recv_sems.at[self.used],
            device_id=(samp, pix),
            device_id_type=MESH,
        )
        self.used += 1
        return copy

    def push(self, source, target, samp, pix):
        copy = self.make(source, target, samp, pix)
        copy.start()
        self.started.append(copy)
        return copy

    def drain(self):
        for copy in self.started:
            copy.wait_send()
        self.started = []


class Place:
    def __init__(self, nz, ny, nx):
        self.nz, self.ny, self.nx = nz, ny, nx
        self.group = ny * nx * 2
        self.z = lax.axis_index("samp")
        self.p = lax.axis_index("pix")
        self.c = lax.rem(self.p, 2)
        self.x = lax.rem(self.p // 2, nx)
        self.y = self.p // (2 * nx)

    def pix(self, y, x, c):
        return (y * self.nx + x) * 2 + c

    def barrier(self):
        semaphore = pltpu.get_barrier_semaphore()
        for step in range(1, self.nz):
            pl.semaphore_signal(
                semaphore,
                inc=1,
                device_id=(lax.rem(self.z + step, self.nz), self.p),
                device_id_type=MESH,
            )
        for step in range(1, self.group):
            pl.semaphore_signal(
                semaphore,
                inc=1,
                device_id=(self.z, lax.rem(self.p + step, self.group)),
                device_id_type=MESH,
            )
        pl.semaphore_wait(semaphore, self.nz - 1 + self.group - 1)

    def push_z(self, links, array, step):
        own = array.at[self.z, self.y, self.x, self.c]
        return [links.push(own, own, lax.rem(self.z - step + self.nz, self.nz), self.p)]

    def push_first(self, links, array, lead, sub, along):
        own = array.at[lead + (self.y, self.x, self.c) + sub]
        copies = []
        if along == "x":
            for step in range(1, self.nx):
                other = self.pix(self.y, lax.rem(self.x + step, self.nx), self.c)
                copies.append(links.push(own, own, self.z, other))
        else:
            for step in range(1, self.ny):
                other = self.pix(lax.rem(self.y + step, self.ny), self.x, self.c)
                copies.append(links.push(own, own, self.z, other))
        return copies

    def push_second(self, links, array, lead, sub, first):
        copies = []
        if first == "x":
            held = array.at[lead + (self.y, slice(None), self.c) + sub]
            for step in range(1, self.ny):
                other = self.pix(lax.rem(self.y + step, self.ny), self.x, self.c)
                copies.append(links.push(held, held, self.z, other))
        else:
            held = array.at[lead + (slice(None), self.x, self.c) + sub]
            for step in range(1, self.nx):
                other = self.pix(self.y, lax.rem(self.x + step, self.nx), self.c)
                copies.append(links.push(held, held, self.z, other))
        return copies

    def push_core(self, links, array, lead):
        held = array.at[lead + (slice(None), slice(None), self.c)]
        return [links.push(held, held, self.z, self.p + 1 - 2 * self.c)]


def arrived(copies):
    for copy in copies:
        copy.wait_recv()


def column_block(array, place, index, col_blocks, owned, sub=()):
    every = slice(None)
    if 2 * owned == col_blocks:
        block = array[(every, every, every, index // owned) + sub + (index % owned,)]
    else:
        block = array[(every, every, index // 2, index % 2) + sub + (0,)]
    return block.reshape(-1, block.shape[-1])


def column_pair(array, place, pair, col_blocks, owned, sub=()):
    return jnp.concatenate(
        [
            column_block(array, place, 2 * pair, col_blocks, owned, sub),
            column_block(array, place, 2 * pair + 1, col_blocks, owned, sub),
        ],
        axis=1,
    )


def front_kernel(
    dims,
    pixels,
    mask,
    gain_rows,
    own_proj,
    own_keyval,
    own_latents,
    all_query,
    all_keyval,
    all_latents,
    all_mats,
    normed_out,
    inverse_out,
    weights_out,
    sent_out,
    landed,
    pixel_query,
    query_out,
    raw,
    gain_cols,
    mats_own,
    g_query,
    g_keyval,
    g_latents,
    lat_normed,
    query,
    normed,
    weights,
    outgoing,
    paired,
    merged,
    send_sems,
    recv_sems,
    local_sems,
):
    channels, batches, shard_pixels = pixels.shape
    lat_rows, width = own_latents.shape
    owned, _, row_block, col_block = own_proj.shape
    col_blocks = width // col_block
    padded = normed.shape[1]
    main = channels // 16 * 16
    place = Place(*dims)
    links = Links(send_sems, recv_sems)
    z, y, x, c, p = place.z, place.y, place.x, place.c, place.p
    half_rows = row_block // 2
    half_width = width // 2
    every = slice(None)
    quarter = shard_pixels // 8
    local = []

    def local_copy(source, target):
        copy = pltpu.make_async_copy(source, target, local_sems.at[len(local)])
        copy.start()
        local.append(copy)
        return copy

    g_query[z, y, x, c] = own_proj[:, 0].astype(BF)
    pixel_copies = [
        local_copy(pixels.at[:, :, pl.ds(part, quarter)], raw.at[:, :, pl.ds(part, quarter)])
        for part in range(0, shard_pixels, quarter)
    ]
    keyval_rows, lanes = g_keyval.shape[4:]
    g_keyval[z, y, x, c] = jnp.zeros((keyval_rows, lanes), BF)
    g_keyval[z, y, x, c, :, 0:channels] = own_keyval[...].astype(BF)
    gain_cols[...] = jnp.broadcast_to(gain_rows[1:2, 0:lanes], (128, lanes)).T
    g_latents[y, x, c] = own_latents[...].astype(BF)
    for mat in range(3):
        mats_own[mat] = own_proj[:, mat + 1].astype(BF)
    own_mats_copy = local_copy(mats_own, all_mats.at[z, y, x, c])
    place.barrier()

    sub_a = (every, pl.ds(0, half_rows))
    sub_b = (every, pl.ds(half_rows, half_rows))
    mats_subs = [
        ((1,), "x"),
        ((2,), "y"),
        ((0, every, pl.ds(0, half_rows)), "x"),
        ((0, every, pl.ds(half_rows, half_rows)), "y"),
    ]

    def level(step):
        return lax.rem(z + step, place.nz)

    def hand_on(push, step):
        copies = push(links, g_query, (level(step),), sub_a, "x")
        copies += push(links, g_query, (level(step),), sub_b, "y")
        copies += push(links, g_keyval, (level(step),), (), "xy"[step % 2])
        return copies

    def hand_on_mats(push, step):
        copies = []
        for sub, along in mats_subs:
            copies += push(links, all_mats, (level(step),), sub, along)
        return copies

    z_group = []
    for step in range(1, place.nz):
        z_group.append(
            place.push_z(links, g_query, step) + place.push_z(links, g_keyval, step)
        )
    firsts = [hand_on(place.push_first, 0)]
    lat_a = (every, pl.ds(0, half_width))
    lat_b = (every, pl.ds(half_width, half_width))
    lat_first = place.push_first(links, g_latents, (), lat_a, "x")
    lat_first += place.push_first(links, g_latents, (), lat_b, "y")
    own_mats_copy.wait()
    z_mats = []
    firsts_m = []

    lane_chunk = 128
    bias_row = channels - main
    row = lax.broadcasted_iota(jnp.int32, (padded - main, lane_chunk), 0)

    def norm_quarter(part):
        pixel_copies[part].wait()

        @pl.loop(0, quarter // lane_chunk)
        def _(chunk):
            start = part * quarter + chunk * lane_chunk
            cols = pl.ds(pl.multiple_of(start, lane_chunk), lane_chunk)
            together = raw[:, :, cols].astype(jnp.float32)
            for image in range(batches):
                value = together[:, image, :]
                value = value - jnp.sum(value, axis=0, keepdims=True) / channels
                variance = jnp.sum(value * value, axis=0, keepdims=True) / channels
                inverse = lax.rsqrt(variance + EPSILON)
                inverse_out[image : image + 1, cols] = inverse
                value = value * inverse * gain_cols[0:channels, :]
                normed[image, 0:main, cols] = value[0:main].astype(BF)
                tail = value[main:channels]
                bias = jnp.where(mask[image : image + 1, cols] == 1, 0.0, NEGATIVE)
                rest = jnp.where(row == bias_row + 1, 1.0, 0.0)
                rest = jnp.where(row == bias_row, bias, rest)
                for index in range(channels - main):
                    rest = jnp.where(row == index, tail[index : index + 1], rest)
                normed[image, main:padded, cols] = rest.astype(BF)

    seconds = []
    seconds_m = []
    cores_m = []

    def first(step):
        arrived(z_group[step - 1])
        firsts.append(hand_on(place.push_first, step))

    def second(step):
        arrived(firsts[step])
        seconds.extend(hand_on(place.push_second, step))

    def first_m(step):
        arrived(z_mats[step - 1])
        firsts_m.append(hand_on_mats(place.push_first, step))

    def second_m(step):
        arrived(firsts_m[step])
        seconds_m.append(hand_on_mats(place.push_second, step))

    def core_m(step):
        arrived(seconds_m[step])
        cores_m.extend(place.push_core(links, all_mats, (level(step),)))

    norm_quarter(0)
    norm_quarter(1)
    second(0)
    arrived(lat_first)
    seconds += place.push_second(links, g_latents, (), lat_a, "x")
    seconds += place.push_second(links, g_latents, (), lat_b, "y")
    norm_quarter(2)
    first(1)
    norm_quarter(3)
    norm_quarter(4)
    first(2)
    second(1)
    norm_quarter(5)
    for step in range(3, place.nz):
        first(step)
    second(2)
    z_mats.extend(place.push_z(links, all_mats, step) for step in range(1, place.nz))
    firsts_m.append(hand_on_mats(place.push_first, 0))
    norm_quarter(6)
    for step in range(3, place.nz):
        second(step)
    norm_quarter(7)
    second_m(0)
    first_m(1)
    local_copy(normed, normed_out)
    arrived(seconds)
    cores = place.push_core(links, g_query, (every,))
    cores += place.push_core(links, g_keyval, (every,))
    cores += place.push_core(links, g_latents, ())
    second_m(1)
    first_m(2)

    arrived(cores)
    for yy in range(place.ny):
        for xx in range(place.nx):
            for cc in range(2):
                rows = pl.ds(((yy * place.nx + xx) * 2 + cc) * lat_rows, lat_rows)
                values = g_latents[yy, xx, cc].astype(jnp.float32)
                mean = jnp.mean(values, axis=1, keepdims=True)
                values = values - mean
                variance = jnp.mean(values * values, axis=1, keepdims=True)
                values = values * lax.rsqrt(variance + EPSILON) * gain_rows[0:1, :]
                lat_normed[rows, :] = values.astype(BF)
    second_m(2)
    local_copy(g_query, all_query)
    local_copy(g_keyval, all_keyval)
    local_copy(lat_normed, all_latents)
    for pair in range(col_blocks // 2):
        query[:, 2 * col_block * pair : 2 * col_block * (pair + 1)] = jnp.dot(
            lat_normed[...],
            column_pair(g_query, place, pair, col_blocks, owned),
            preferred_element_type=jnp.float32,
        ).astype(BF)
    local_copy(query, query_out)
    key_t = g_keyval[0 : place.nz // 2]
    key_t = key_t.reshape(width, key_t.shape[-1])
    projected = jnp.dot(query[...], key_t, preferred_element_type=jnp.float32) * width ** (-0.5)
    lane = lax.broadcasted_iota(jnp.int32, projected.shape, 1)
    pixel_query[...] = jnp.where(lane == channels, 1.0, projected).astype(BF)

    tile = place.nx * 2 * lat_rows
    rows_here = place.ny * place.nx * lat_rows

    def attend(image):
        @pl.loop(0, place.ny)
        def _(step):
            rows = pl.ds(pl.multiple_of(step * tile, tile), tile)
            scores = jnp.dot(
                pixel_query[rows, 0:padded], normed[image], preferred_element_type=jnp.float32
            )
            top = jnp.max(scores, axis=1, keepdims=True)
            top = jnp.maximum(top, 0.1 * NEGATIVE).astype(BF).astype(jnp.float32)
            share = jnp.exp(scores - top).astype(BF)
            weights[image, rows, :] = share
            numer = lax.dot_general(
                share, normed[image], NT, preferred_element_type=jnp.float32
            )
            lane = lax.broadcasted_iota(jnp.int32, numer.shape, 1)
            numer = jnp.where(lane == channels, top, numer).astype(BF)
            outgoing[image, step, :, :, :, 0:padded] = numer.reshape(
                place.nx, 2, lat_rows, padded
            )

        local_copy(weights.at[image], weights_out.at[image])
        last = pl.ds(lanes - 128, 128)
        local_copy(
            outgoing.at[image, :, :, :, :, last], sent_out.at[image]
        )
        return [
            links.push(
                outgoing.at[image, :, :, 1 - c], paired.at[image], z, p + 1 - 2 * c
            )
        ]

    def merge(image, pair):
        arrived(pair)
        mine = outgoing[image, :, :, c].reshape(rows_here, lanes).astype(jnp.float32)
        other = paired[image].reshape(rows_here, lanes).astype(jnp.float32)
        my_top = mine[:, channels : channels + 1]
        other_top = other[:, channels : channels + 1]
        top = jnp.maximum(my_top, other_top)
        lane = lax.broadcasted_iota(jnp.int32, mine.shape, 1)
        both = jnp.exp(my_top - top) * mine + jnp.exp(other_top - top) * other
        both = jnp.where(lane == channels, top, both)
        merged[image] = both.astype(BF).reshape(place.ny, place.nx, lat_rows, lanes)
        chip = y * place.nx + x
        chips = place.ny * place.nx
        local_copy(merged.at[image, y, x], landed.at[chip, image])
        copies = []
        for step in range(1, chips):
            q = lax.rem(chip + step, chips)
            copies.append(
                links.push(
                    merged.at[image, q // place.nx, lax.rem(q, place.nx)],
                    landed.at[chip, image],
                    z,
                    2 * q + c,
                )
            )
        return copies

    for step in range(3, place.nz):
        first_m(step)
    core_m(0)
    pair = attend(0)
    sent = []
    for step in range(3, place.nz):
        second_m(step)
    core_m(1)
    for image in range(1, batches):
        following = attend(image)
        sent += merge(image - 1, pair)
        pair = following
        if image == 1:
            core_m(2)
    sent += merge(batches - 1, pair)
    for step in range(3, place.nz):
        core_m(step)
    arrived(sent)
    arrived(cores_m)
    links.drain()
    for copy in local[9:]:
        copy.wait()


def front_copies(nz, ny, nx, batches):
    both = nx + ny - 2
    count = 3 * (nz - 1) + 2 * nz * (both + max(nx, ny) - 1) + 2 * both
    count += 2 * nz * 2 * both + 3 + nz
    return count + batches * nx * ny


def front(dims, pixels, pixel_mask, gain_rows, proj_blocks, keyval_t, latents):
    nz, ny, nx = dims
    channels, batches, shard_pixels = pixels.shape
    lat_rows, width = latents.shape
    owned, mats, row_block, col_block = proj_blocks.shape
    keyval_rows = keyval_t.shape[0]
    group = 2 * ny * nx
    all_rows = lat_rows * group
    padded = ceil_to(channels + 2, 16)
    lanes = ceil_to(padded, 128)
    vmem = pl.BlockSpec(memory_space=pltpu.VMEM)
    anywhere = pl.BlockSpec(memory_space=pl.ANY)
    cube = (nz, ny, nx, 2)
    copies = front_copies(nz, ny, nx, batches)
    return pl.pallas_call(
        functools.partial(front_kernel, dims),
        out_shape=(
            jax.ShapeDtypeStruct(cube + (owned, row_block, col_block), BF),
            jax.ShapeDtypeStruct(cube + (keyval_rows, lanes), BF),
            jax.ShapeDtypeStruct((all_rows, width), BF),
            jax.ShapeDtypeStruct(cube + (3, owned, row_block, col_block), BF),
            jax.ShapeDtypeStruct((batches, padded, shard_pixels), BF),
            jax.ShapeDtypeStruct((batches, shard_pixels), jnp.float32),
            jax.ShapeDtypeStruct((batches, all_rows, shard_pixels), BF),
            jax.ShapeDtypeStruct((batches, ny, nx, 2, lat_rows, 128), BF),
            jax.ShapeDtypeStruct((ny * nx, batches, lat_rows, lanes), BF),
            jax.ShapeDtypeStruct((all_rows, lanes), BF),
            jax.ShapeDtypeStruct((all_rows, width), BF),
        ),
        in_specs=[anywhere] + [vmem] * 5,
        out_specs=(
            anywhere,
            anywhere,
            anywhere,
            anywhere,
            anywhere,
            vmem,
            anywhere,
            anywhere,
            anywhere,
            vmem,
            anywhere,
        ),
        scratch_shapes=[
            pltpu.VMEM(pixels.shape, BF),
            pltpu.VMEM((lanes, 128), jnp.float32),
            pltpu.VMEM((3, owned, row_block, col_block), BF),
            pltpu.VMEM(cube + (owned, row_block, col_block), BF),
            pltpu.VMEM(cube + (keyval_rows, lanes), BF),
            pltpu.VMEM(cube[1:] + (lat_rows, width), BF),
            pltpu.VMEM((all_rows, width), BF),
            pltpu.VMEM((all_rows, width), BF),
            pltpu.VMEM((batches, padded, shard_pixels), BF),
            pltpu.VMEM((batches, all_rows, shard_pixels), BF),
            pltpu.VMEM((batches, ny, nx, 2, lat_rows, lanes), BF),
            pltpu.VMEM((batches, ny, nx, lat_rows, lanes), BF),
            pltpu.VMEM((batches, ny, nx, lat_rows, lanes), BF),
            pltpu.SemaphoreType.DMA((copies,)),
            pltpu.SemaphoreType.DMA((copies,)),
            pltpu.SemaphoreType.DMA((14 + 3 * batches,)),
        ],
        compiler_params=pltpu.CompilerParams(
            collective_id=0, has_side_effects=True, vmem_limit_bytes=56 * 2**20
        ),
    )(
        pixels,
        pixel_mask,
        gain_rows,
        proj_blocks,
        keyval_t,
        latents,
    )


def add_low(former, latter):
    return (former.astype(jnp.float32) + latter.astype(jnp.float32)).astype(BF)


class Reduce:
    def __init__(self, place, links, term, buffers, along):
        self.place, self.links, self.term, self.along = place, links, term, along
        self.by_core, self.by_first, self.by_second, self.by_z = buffers
        self.waiting = []

    def wait(self):
        arrived(self.waiting)
        self.waiting = []

    def push_core(self):
        place = self.place
        every = slice(None)
        self.waiting = [
            self.links.push(
                self.term.at[every, every, every, 1 - place.c],
                self.by_core,
                place.z,
                place.p + 1 - 2 * place.c,
            )
        ]

    def push_first(self):
        place = self.place
        self.wait()

        @pl.loop(0, self.by_core.shape[0])
        def _(level):
            self.by_core[level] = add_low(
                self.by_core[level], self.term[level, :, :, place.c]
            )

        every = slice(None)
        for step in range(1, place.nx if self.along == "x" else place.ny):
            if self.along == "x":
                xx = lax.rem(place.x + step, place.nx)
                source = self.by_core.at[every, every, xx]
                target = place.pix(place.y, xx, place.c)
            else:
                yy = lax.rem(place.y + step, place.ny)
                source = self.by_core.at[every, yy]
                target = place.pix(yy, place.x, place.c)
            self.waiting.append(
                self.links.push(source, self.by_first.at[step - 1], place.z, target)
            )

    def push_second(self):
        place = self.place
        self.wait()
        if self.along == "x":
            held = self.by_core[:, :, place.x].astype(jnp.float32)
        else:
            held = self.by_core[:, place.y].astype(jnp.float32)
        for slot in range(self.by_first.shape[0]):
            held = held + self.by_first[slot].astype(jnp.float32)
        self.by_first[0] = held.astype(BF)
        every = slice(None)
        for step in range(1, place.ny if self.along == "x" else place.nx):
            if self.along == "x":
                other = lax.rem(place.y + step, place.ny)
                target = place.pix(other, place.x, place.c)
            else:
                other = lax.rem(place.x + step, place.nx)
                target = place.pix(place.y, other, place.c)
            self.waiting.append(
                self.links.push(
                    self.by_first.at[0, every, other],
                    self.by_second.at[step - 1],
                    place.z,
                    target,
                )
            )

    def push_z(self):
        place = self.place
        self.wait()
        mine = place.y if self.along == "x" else place.x
        held = self.by_first[0, :, mine].astype(jnp.float32)
        for slot in range(self.by_second.shape[0]):
            held = held + self.by_second[slot].astype(jnp.float32)
        self.by_second[0] = held.astype(BF)
        for step in range(1, place.nz):
            zz = lax.rem(place.z - step + place.nz, place.nz)
            self.waiting.append(
                self.links.push(self.by_second.at[0, zz], self.by_z.at[step - 1], zz, place.p)
            )

    def total(self):
        self.wait()
        held = self.by_second[0, self.place.z].astype(jnp.float32)
        return held, [self.by_z.at[slot] for slot in range(self.by_z.shape[0])]


class ReduceDown(Reduce):
    def push_z(self):
        place = self.place
        self.wait()

        @pl.loop(0, self.by_core.shape[0])
        def _(level):
            self.by_core[level] = add_low(
                self.by_core[level], self.term[level, :, :, place.c]
            )

        for step in range(1, place.nz):
            zz = lax.rem(place.z - step + place.nz, place.nz)
            self.waiting.append(
                self.links.push(self.by_core.at[zz], self.by_z.at[step - 1], zz, place.p)
            )

    def push_first(self):
        place = self.place
        self.wait()
        held = self.by_core[place.z].astype(jnp.float32)
        for slot in range(self.by_z.shape[0]):
            held = held + self.by_z[slot].astype(jnp.float32)
        self.by_z[0] = held.astype(BF)
        every = slice(None)
        for step in range(1, place.nx if self.along == "x" else place.ny):
            if self.along == "x":
                other = lax.rem(place.x + step, place.nx)
                source = self.by_z.at[0, every, other]
                target = place.pix(place.y, other, place.c)
            else:
                other = lax.rem(place.y + step, place.ny)
                source = self.by_z.at[0, other]
                target = place.pix(other, place.x, place.c)
            self.waiting.append(
                self.links.push(source, self.by_first.at[step - 1], place.z, target)
            )

    def push_second(self):
        place = self.place
        self.wait()
        if self.along == "x":
            held = self.by_z[0, :, place.x].astype(jnp.float32)
        else:
            held = self.by_z[0, place.y].astype(jnp.float32)
        for slot in range(self.by_first.shape[0]):
            held = held + self.by_first[slot].astype(jnp.float32)
        self.by_first[0] = held.astype(BF)
        for step in range(1, place.ny if self.along == "x" else place.nx):
            if self.along == "x":
                other = lax.rem(place.y + step, place.ny)
                target = place.pix(other, place.x, place.c)
            else:
                other = lax.rem(place.x + step, place.nx)
                target = place.pix(place.y, other, place.c)
            self.waiting.append(
                self.links.push(
                    self.by_first.at[0, other], self.by_second.at[step - 1], place.z, target
                )
            )

    def total(self):
        self.wait()
        mine = self.place.y if self.along == "x" else self.place.x
        held = self.by_first[0, mine].astype(jnp.float32)
        return held, [self.by_second.at[slot] for slot in range(self.by_second.shape[0])]


def block_index(block, col_blocks, owned):
    every = slice(None)
    if 2 * owned == col_blocks:
        return (every, every, every, block // owned, block % owned)
    return (every, every, block // 2, block % 2, 0)


def back_kernel(
    dims,
    channels,
    landed,
    all_keyval,
    all_mats,
    normed_all,
    inverse,
    weights_all,
    sent_all,
    pixel_query,
    latents,
    gain_rows,
    grad_rows,
    mixed,
    pixel_grad,
    mats_grad,
    chan_total,
    query_total,
    gain_total,
    residual_total,
    came,
    values,
    mats,
    normed,
    weights,
    tops,
    attended_chan,
    attended,
    middle,
    mid_hat,
    mid_inverse,
    mid_normed,
    slope,
    hidden,
    grad_pre,
    grad_mid_normed,
    grad_mid,
    grad_attended,
    shares,
    query_turned,
    query_acc,
    turned_acc,
    back_turned,
    grad_scores,
    gain_cols,
    staged,
    terms,
    buffers,
    query_low,
    query_came,
    query_levels,
    gain_plane,
    gain_levels,
    residual_parts,
    residual_came,
    residual_levels,
    send_sems,
    recv_sems,
    local_sems,
):
    place = Place(*dims)
    links = Links(send_sems, recv_sems)
    z, y, x, c, p = place.z, place.y, place.x, place.c, place.p
    chips, batches, lat_rows, lanes = landed.shape
    group = place.group
    rows = batches * lat_rows
    all_rows = group * lat_rows
    width = latents.shape[1]
    padded, shard_pixels = normed_all.shape[1:]
    owned, row_block, col_block = all_mats.shape[5:]
    col_blocks = width // col_block
    every = slice(None)
    tile = 256
    tiles = width // tile
    local = []

    def local_copy(source, target):
        copy = pltpu.make_async_copy(source, target, local_sems.at[len(local)])
        copy.start()
        local.append(copy)
        return copy

    came_copy = local_copy(landed, came)
    values_copy = local_copy(all_keyval.at[pl.ds(place.nz // 2, place.nz // 2)], values)
    mats_copies = []
    for mat in range(3):
        copies = []
        for block in range(col_blocks):
            where = block_index(block, col_blocks, owned)
            source = all_mats.at[where[:4] + (mat,) + where[4:]]
            cols = pl.ds(block * col_block, col_block)
            lead = (mat,) + (every,) * (len(mats.shape) - 2)
            copies.append(local_copy(source, mats.at[lead + (cols,)]))
        mats_copies.append(copies)

    def fetch(image):
        slot = image % 2
        return [
            local_copy(normed_all.at[image], normed.at[slot]),
            local_copy(weights_all.at[image], weights.at[slot]),
        ]

    place.barrier()

    def columns_of(mat, index):
        lead = (mat,) + (every,) * (len(mats.shape) - 2)
        return mats[lead + (slice(index * tile, (index + 1) * tile),)].reshape(width, tile)

    def rows_of(mat, index):
        return mats[mat, index].reshape(-1, width)

    row_tile = width // place.nz

    came_copy.wait()
    lane = lax.broadcasted_iota(jnp.int32, (rows, lanes), 1)
    parts = [came[g].reshape(rows, lanes).astype(jnp.float32) for g in range(chips)]
    top = [part[:, channels : channels + 1] for part in parts]
    peak = functools.reduce(jnp.maximum, top)
    factor = [jnp.exp(value - peak) for value in top]
    denominator = sum(f * part[:, channels + 1 : channels + 2] for f, part in zip(factor, parts))
    summed = sum(f * part for f, part in zip(factor, parts))
    attended_chan[...] = jnp.where(lane < channels, summed / denominator, 0.0).astype(BF)

    values_copy.wait()
    value_t = values[...].reshape(width, lanes)
    attended[...] = lax.dot_general(
        attended_chan[...], value_t, NT, preferred_element_type=jnp.float32
    ).astype(BF)
    arrived_local(mats_copies[0])
    for index in range(tiles):
        cols = slice(index * tile, (index + 1) * tile)
        own = latents[:, cols]
        middle[:, cols] = jnp.concatenate([own] * batches, axis=0) + jnp.dot(
            attended[...], columns_of(0, index), preferred_element_type=jnp.float32
        )

    @pl.loop(0, rows // lat_rows)
    def _(step):
        part = pl.ds(pl.multiple_of(step * lat_rows, lat_rows), lat_rows)
        value = middle[part, :]
        value = value - jnp.mean(value, axis=1, keepdims=True)
        scale = lax.rsqrt(jnp.mean(value * value, axis=1, keepdims=True) + EPSILON)
        value = value * scale
        mid_hat[part, :] = value
        mid_inverse[part, :] = jnp.broadcast_to(scale, (lat_rows, 128))
        mid_normed[part, :] = (value * gain_rows[2:3, :]).astype(BF)

    arrived_local(mats_copies[1])
    for index in range(tiles):
        cols = slice(index * tile, (index + 1) * tile)
        pre = jnp.dot(mid_normed[...], columns_of(1, index), preferred_element_type=jnp.float32)
        below = 0.5 + 0.5 * lax.erf(pre * 0.5**0.5)
        hidden[:, cols] = (pre * below).astype(BF)
        slope[:, cols] = below + pre * jnp.exp(-0.5 * pre * pre) * (0.5 / math.pi) ** 0.5

    tops_copy = local_copy(sent_all, tops)
    fetched = [fetch(0), fetch(1)]

    half_rows = row_block // 2

    def store_term(targets, left, right):
        turned = left[...].T
        for pair in range(col_blocks // 2):
            cols = slice(2 * pair * col_block, 2 * (pair + 1) * col_block)
            product = jnp.dot(turned, right[:, cols], preferred_element_type=jnp.float32).astype(
                BF
            )
            for side in range(2):
                where = block_index(2 * pair + side, col_blocks, owned)
                block = product[:, side * col_block : (side + 1) * col_block]
                taken = 0
                for target in targets:
                    height = target.shape[-2]
                    pieces = block.reshape(-1, row_block, col_block)[:, taken : taken + height]
                    taken += height
                    shape = target.shape
                    lead = shape[:3] if 2 * owned == col_blocks else shape[:2]
                    target[where] = pieces.reshape(lead + (height, col_block))

    pairs = []
    for index, kind in enumerate((ReduceDown, Reduce)):
        pairs.append(
            [
                kind(place, links, terms[2 * index + side], buffers[2 * index + side], along)
                for side, along in enumerate("xy")
            ]
        )
    down, inward = pairs
    chan_job = Reduce(place, links, terms[4], buffers[4], "x")
    store_term(terms[0:2], hidden, grad_rows)
    for job in down:
        job.push_core()

    arrived_local(mats_copies[2])
    for index in range(place.nz):
        cols = slice(index * row_tile, (index + 1) * row_tile)
        grad_hidden = lax.dot_general(
            grad_rows[...], rows_of(2, index), NT, preferred_element_type=jnp.float32
        )
        grad_pre[:, cols] = (
            grad_hidden.astype(BF).astype(jnp.float32) * slope[:, cols]
        ).astype(BF)
    for job in down:
        job.push_z()
    gain_plane[p] = jnp.zeros(gain_plane.shape[1:], jnp.float32)
    for index in range(place.nz):
        cols = slice(index * row_tile, (index + 1) * row_tile)
        part = lax.dot_general(
            grad_pre[...], rows_of(1, index), NT, preferred_element_type=jnp.float32
        )
        grad_mid_normed[:, cols] = part
        summed_rows = jnp.sum(part * mid_hat[:, cols], axis=0, keepdims=True)
        for sub in range(row_tile // 128):
            row = index * (row_tile // 128) + sub
            gain_plane[p, row : row + 1, :] = summed_rows[:, sub * 128 : (sub + 1) * 128]

    @pl.loop(0, rows // lat_rows)
    def _(step):
        part = pl.ds(pl.multiple_of(step * lat_rows, lat_rows), lat_rows)
        grad = grad_mid_normed[part, :] * gain_rows[2:3, :]
        hat = mid_hat[part, :]
        grad = (
            grad
            - jnp.mean(grad, axis=1, keepdims=True)
            - hat * jnp.mean(grad * hat, axis=1, keepdims=True)
        ) * mid_inverse[part, 0:1]
        grad_mid[part, :] = (grad_rows[part, :].astype(jnp.float32) + grad).astype(BF)

    for index in range(place.nz):
        cols = slice(index * row_tile, (index + 1) * row_tile)
        grad_attended[:, cols] = lax.dot_general(
            grad_mid[...], rows_of(0, index), NT, preferred_element_type=jnp.float32
        ).astype(BF)
    grad_chan = jnp.dot(grad_attended[...], value_t, preferred_element_type=jnp.float32)
    products = attended_chan[...].astype(jnp.float32) * grad_chan
    row_delta = jnp.sum(products, axis=1, keepdims=True)
    channel_sums = jnp.sum(products, axis=0, keepdims=True)
    for sub in range(lanes // 128):
        row = width // 128 + sub
        gain_plane[p, row : row + 1, :] = channel_sums[:, sub * 128 : (sub + 1) * 128]
    back = jnp.where(lane == channels + 1, row_delta, grad_chan) / denominator
    back = jnp.where(lane == channels, peak, back)
    shares[y, x, c] = back.astype(BF).reshape(batches, lat_rows, lanes)

    share_first = []
    for image in range(batches):
        share_first.append(
            place.push_first(links, shares, (), (image,), "xy"[image % 2])
        )
    gain_sent = []
    for step in range(1, group):
        own = gain_plane.at[p]
        gain_sent.append(links.push(own, own, z, lax.rem(p + step, group)))
    share_second = []
    share_core = []

    def share_on(image):
        arrived(share_first[image])
        share_second.append(place.push_second(links, shares, (), (image,), "xy"[image % 2]))

    def share_pair(image):
        arrived(share_second[image])
        held = shares.at[:, :, c, image]
        share_core.append([links.push(held, held, z, p + 1 - 2 * c)])

    terms[4][...] = (
        jnp.dot(grad_mid[...].T, attended_chan[...], preferred_element_type=jnp.float32)
        .astype(BF)
        .reshape(terms[4].shape)
    )
    chan_job.push_core()
    store_term(terms[2:4], mid_normed, grad_pre)
    for job in inward:
        job.push_core()
    for image in range(batches):
        share_on(image)
    chan_job.push_first()
    for job in inward:
        job.push_first()
    residual = sum(
        grad_mid[image * lat_rows : (image + 1) * lat_rows].astype(jnp.float32)
        for image in range(batches)
    )
    part_width = width // place.nz
    residual_sent = []
    for zz in range(place.nz):
        residual_parts[zz] = residual[:, zz * part_width : (zz + 1) * part_width].astype(BF)
    for step in range(1, place.nz):
        zz = lax.rem(z + step, place.nz)
        residual_sent.append(
            links.push(residual_parts.at[zz], residual_came.at[step - 1], zz, p)
        )

    lane_all = lax.broadcasted_iota(jnp.int32, (all_rows, lanes), 1)
    query_turned[...] = jnp.where(
        lane_all < channels, pixel_query[...].astype(jnp.float32), 0.0
    ).T[0:padded].astype(BF)
    turned_acc[...] = jnp.zeros(turned_acc.shape, jnp.float32)
    gain_cols[0] = jnp.broadcast_to(gain_rows[1:2, 0:lanes], (128, lanes)).T[0:padded]
    gain_value = gain_cols[0]
    gain_cols[1] = jnp.where(gain_value > 0.0, 1.0 / gain_value, 0.0)
    chunk = min(512, shard_pixels)
    tops_copy.wait()

    def attend_query(image):
        slot = image % 2
        arrived(share_core[image])
        arrived_local(fetched[image])
        back = shares[:, :, :, image].reshape(all_rows, lanes).astype(jnp.float32)
        top = tops[image].reshape(all_rows, 128).astype(jnp.float32)[
            :, channels - (lanes - 128) :
        ][:, 0:1]
        share = jnp.exp(top - back[:, channels : channels + 1])
        back = jnp.where(lane_all == channels, 0.0, back * share)
        back = jnp.where(lane_all > channels + 1, 0.0, back)
        back_low = jnp.where(lane_all == channels + 1, -back, back).astype(BF)[:, 0:padded]
        back_turned[image] = jnp.where(lane_all < channels, back, 0.0).T[0:padded].astype(BF)

        @pl.loop(0, shard_pixels // chunk)
        def _(step):
            cols = pl.ds(pl.multiple_of(step * chunk, chunk), chunk)
            normed_chunk = normed[slot, :, cols]
            grad_weights = jnp.dot(back_low, normed_chunk, preferred_element_type=jnp.float32)
            grad_chunk = (weights[slot, :, cols].astype(jnp.float32) * grad_weights).astype(BF)
            grad_scores[image, :, cols] = grad_chunk
            turned_acc[0:padded, :] += lax.dot_general(
                normed_chunk, grad_chunk, NT, preferred_element_type=jnp.float32
            )

        if image + 2 < batches:
            fetched.append(fetch(image + 2))

    order = list(range(2, batches)) + [0, 1]
    staged_out = []

    def attend_pixels(turn):
        image = order[turn]
        slot = image % 2
        if turn >= 2:
            arrived_local(fetched[batches + turn - 2])
            staged_out[turn - 2].wait()

        @pl.loop(0, shard_pixels // chunk)
        def _(step):
            cols = pl.ds(pl.multiple_of(step * chunk, chunk), chunk)
            grad_normed = jnp.dot(
                query_turned[...], grad_scores[image, :, cols], preferred_element_type=jnp.float32
            ) + jnp.dot(
                back_turned[image], weights[slot, :, cols], preferred_element_type=jnp.float32
            )
            normal = normed[slot, :, cols].astype(jnp.float32)
            second_mean = jnp.sum(grad_normed * normal, axis=0, keepdims=True) / channels
            spread = jnp.concatenate([gain_cols[0]] * (chunk // 128), axis=1)
            spread_back = jnp.concatenate([gain_cols[1]] * (chunk // 128), axis=1)
            grad_hat = grad_normed * spread
            first_mean = jnp.sum(grad_hat, axis=0, keepdims=True) / channels
            result = (grad_hat - first_mean - normal * spread_back * second_mean) * inverse[
                image : image + 1, cols
            ]
            staged[turn % 2, :, cols] = result[0:channels].astype(BF)

        staged_out.append(local_copy(staged.at[turn % 2], pixel_grad.at[image]))
        if turn + 2 < batches:
            fetched.append(fetch(order[turn + 2]))

    for image in range(batches):
        share_pair(image)
    attend_query(0)
    chan_job.push_second()
    attend_query(1)
    arrived(gain_sent)
    gain_levels[z] = sum(gain_plane[g] for g in range(group))
    gain_up = []
    for step in range(1, place.nz):
        own = gain_levels.at[z]
        gain_up.append(links.push(own, own, lax.rem(z + step, place.nz), p))
    attend_query(2)
    chan_job.push_z()
    attend_query(3)

    query_acc[...] = turned_acc[...].T
    query_low[...] = query_acc[...].astype(BF)
    query_sent = []
    for step in range(1, group):
        q = lax.rem(p + step, group)
        part = pl.ds(pl.multiple_of(q * lat_rows, lat_rows), lat_rows)
        query_sent.append(links.push(query_low.at[part], query_came.at[step - 1], z, q))
    for job in inward:
        job.push_second()
    attend_pixels(0)
    held, came_z = chan_job.total()
    for part in came_z:
        held = held + part[...].astype(jnp.float32)
    chan_total[z, y, x, c] = held.astype(BF)
    chan_z = []
    for step in range(1, place.nz):
        chan_z += place.push_z(links, chan_total, step)
    for job in down:
        job.push_first()
    arrived(query_sent)
    own_rows = pl.ds(pl.multiple_of(p * lat_rows, lat_rows), lat_rows)
    held = query_acc[own_rows, :]
    for slot in range(group - 1):
        held = held + query_came[slot].astype(jnp.float32)
    query_levels[z] = held.astype(BF)
    query_up = []
    for step in range(1, place.nz):
        own = query_levels.at[z]
        query_up.append(links.push(own, own, lax.rem(z + step, place.nz), p))
    attend_pixels(1)
    arrived(chan_z)
    chan_first = place.push_first(links, chan_total, (every,), (), "x")
    arrived(query_up)
    query_total[p] = sum(query_levels[zz].astype(jnp.float32) for zz in range(place.nz)).astype(BF)
    query_all = []
    for step in range(1, group):
        own = query_total.at[p]
        query_all.append(links.push(own, own, z, lax.rem(p + step, group)))
    for job in inward:
        job.push_z()
    for job in down:
        job.push_second()
    attend_pixels(2)
    arrived(chan_first)
    chan_second = place.push_second(links, chan_total, (every,), (), "x")
    arrived(residual_sent)
    residual_levels[z] = (
        residual_parts[z].astype(jnp.float32)
        + sum(residual_came[slot].astype(jnp.float32) for slot in range(place.nz - 1))
    ).astype(BF)
    residual_up = []
    for step in range(1, place.nz):
        own = residual_levels.at[z]
        residual_up.append(links.push(own, own, lax.rem(z + step, place.nz), p))
    attend_pixels(3)
    arrived(chan_second)
    chan_core = place.push_core(links, chan_total, (every,))
    for index in range(tiles):
        cols = slice(index * tile, (index + 1) * tile)
        mixed[:, cols] = (
            middle[:, cols]
            + jnp.dot(hidden[...], columns_of(2, index), preferred_element_type=jnp.float32)
        ).astype(BF)
    def finish(job, target):
        held, came_z = job.total()
        for part in came_z:
            held = held + part[...].astype(jnp.float32)
        target[...] = held

    def finish_mat(mat, jobs):
        for side, job in enumerate(jobs):
            finish(job, mats_grad.at[mat, :, pl.ds(side * half_rows, half_rows)])

    finish_mat(1, down)
    arrived(gain_up)
    gain_total[...] = sum(gain_levels[zz] for zz in range(place.nz))
    arrived(residual_up)
    for zz in range(place.nz):
        residual_total[:, zz * part_width : (zz + 1) * part_width] = residual_levels[zz].astype(
            jnp.float32
        )
    finish_mat(0, inward)
    arrived(chan_core)
    arrived(query_all)
    links.drain()
    for copy in staged_out[batches - 2 :]:
        copy.wait()


def arrived_local(copies):
    for copy in copies:
        copy.wait()


def back_copies(nz, ny, nx, batches):
    group = 2 * ny * nx
    both = nx + ny - 2
    count = batches // 2 * 2 * both + batches
    count += 5 * (1 + both + nz - 1) + nz - 1 + both + 1
    count += 4 * (nz - 1) + 3 * (group - 1)
    return count


def back(dims, channels, gathered, latents, gain_rows, mixed_grad):
    landed, all_keyval, all_mats, normed_all, inverse, weights_all, sent_all, pixel_query = gathered
    nz, ny, nx = dims
    batches, lat_rows, lanes = landed.shape[1:]
    group = 2 * ny * nx
    rows = batches * lat_rows
    all_rows = group * lat_rows
    width = latents.shape[1]
    padded, shard_pixels = normed_all.shape[1:]
    owned, row_block, col_block = all_mats.shape[5:]
    keyval_rows = all_keyval.shape[4]
    half_rows = row_block // 2
    vmem = pl.BlockSpec(memory_space=pltpu.VMEM)
    anywhere = pl.BlockSpec(memory_space=pl.ANY)
    lead = (nz, ny, nx) if 2 * owned * col_block == width else (nz, ny)
    cube = (nz, ny, nx, 2)
    inners = [(nz, (owned, half_rows, col_block), along) for along in "xyxy"]
    inners.append((nz, (width // (group * nz), lanes), "x"))
    terms = [pltpu.VMEM((levels, ny, nx, 2) + inner, BF) for levels, inner, _ in inners]
    buffers = []
    for index, (levels, inner, along) in enumerate(inners):
        one, two = (nx, ny) if along == "x" else (ny, nx)
        plane_last = index < 2
        buffers.append(
            [
                pltpu.VMEM((levels, ny, nx) + inner, BF),
                pltpu.VMEM((one - 1,) + (() if plane_last else (levels,)) + (two,) + inner, BF),
                pltpu.VMEM((two - 1,) + (() if plane_last else (levels,)) + inner, BF),
                pltpu.VMEM((nz - 1,) + ((ny, nx) if plane_last else ()) + inner, BF),
            ]
        )
    wide = lambda kind: pltpu.VMEM((rows, width), kind)
    copies = back_copies(nz, ny, nx, batches)
    return pl.pallas_call(
        functools.partial(back_kernel, dims, channels),
        out_shape=(
            jax.ShapeDtypeStruct((rows, width), BF),
            jax.ShapeDtypeStruct((batches, channels, shard_pixels), BF),
            jax.ShapeDtypeStruct((2, owned, row_block, col_block), jnp.float32),
            jax.ShapeDtypeStruct(cube + (width // (group * nz), lanes), BF),
            jax.ShapeDtypeStruct((group, lat_rows, lanes), BF),
            jax.ShapeDtypeStruct((16, 128), jnp.float32),
            jax.ShapeDtypeStruct((lat_rows, width), jnp.float32),
        ),
        in_specs=[
            anywhere,
            anywhere,
            anywhere,
            anywhere,
            vmem,
            anywhere,
            anywhere,
            vmem,
            vmem,
            vmem,
            vmem,
        ],
        out_specs=(vmem, anywhere, vmem, vmem, vmem, vmem, vmem),
        scratch_shapes=[
            pltpu.VMEM((ny * nx, batches, lat_rows, lanes), BF),
            pltpu.VMEM((nz // 2, ny, nx, 2, keyval_rows, lanes), BF),
            pltpu.VMEM((3,) + lead + (row_block, width), BF),
            pltpu.VMEM((2, padded, shard_pixels), BF),
            pltpu.VMEM((2, all_rows, shard_pixels), BF),
            pltpu.VMEM((batches, ny, nx, 2, lat_rows, 128), BF),
            pltpu.VMEM((rows, lanes), BF),
            wide(BF),
            wide(jnp.float32),
            wide(jnp.float32),
            pltpu.VMEM((rows, 128), jnp.float32),
            wide(BF),
            wide(jnp.float32),
            wide(BF),
            wide(BF),
            wide(jnp.float32),
            wide(BF),
            wide(BF),
            pltpu.VMEM(cube[1:] + (batches, lat_rows, lanes), BF),
            pltpu.VMEM((padded, all_rows), BF),
            pltpu.VMEM((all_rows, lanes), jnp.float32),
            pltpu.VMEM((lanes, all_rows), jnp.float32),
            pltpu.VMEM((batches, padded, all_rows), BF),
            pltpu.VMEM((batches, all_rows, shard_pixels), BF),
            pltpu.VMEM((2, padded, 128), jnp.float32),
            pltpu.VMEM((2, channels, shard_pixels), BF),
            terms,
            buffers,
            pltpu.VMEM((all_rows, lanes), BF),
            pltpu.VMEM((group - 1, lat_rows, lanes), BF),
            pltpu.VMEM((nz, lat_rows, lanes), BF),
            pltpu.VMEM((group, 16, 128), jnp.float32),
            pltpu.VMEM((nz, 16, 128), jnp.float32),
            pltpu.VMEM((nz, lat_rows, width // nz), BF),
            pltpu.VMEM((nz - 1, lat_rows, width // nz), BF),
            pltpu.VMEM((nz, lat_rows, width // nz), BF),
            pltpu.SemaphoreType.DMA((copies,)),
            pltpu.SemaphoreType.DMA((copies,)),
            pltpu.SemaphoreType.DMA((3 + 3 * (width // col_block) + 5 * batches,)),
        ],
        compiler_params=pltpu.CompilerParams(
            collective_id=1, has_side_effects=True, vmem_limit_bytes=61 * 2**20
        ),
    )(
        landed,
        all_keyval,
        all_mats,
        normed_all,
        inverse,
        weights_all,
        sent_all,
        pixel_query,
        latents,
        gain_rows,
        mixed_grad.reshape(rows, width),
    )


TN = (((0,), (0,)), ((), ()))


def tail_kernel(
    dims,
    channels,
    query_total,
    residual_total,
    mats_grad,
    chan_grad,
    proj_blocks,
    left_in,
    right_in,
    left_roots_in,
    right_roots_in,
    keyval_weight,
    keyval_second,
    latents,
    latent_second,
    gain_rows,
    query_in,
    lat_normed_in,
    query_blocks,
    all_keyval,
    pixel_low,
    pixel_query,
    gain_total,
    all_rows_keyval,
    all_mats,
    mixed_in,
    pixel_grad,
    proj_grad,
    left_new,
    right_new,
    proj_new,
    keyval_grad,
    keyval_second_new,
    keyval_new,
    latent_grad,
    latent_second_new,
    latent_new,
    gain_grad,
    mixed_out,
    query,
    lat_normed,
    query_weight,
    keys,
    pixel_came,
    pixel_wide,
    grad_query,
    grad_normed,
    query_grad,
    key_rows,
    value_block,
    output_block,
    proj_left,
    proj_right,
    left_roots,
    right_roots,
    local_sems,
):
    place = Place(*dims)
    group, lat_rows, lanes = query_total.shape
    all_rows = group * lat_rows
    width = latents.shape[1]
    batches = pixel_low.shape[0]
    owned, mats, row_block, col_block = proj_blocks.shape
    col_blocks = width // col_block
    keyval_rows = keyval_weight.shape[0]
    device = place.z * group + place.p
    every = slice(None)
    local = []

    def local_copy(source, target):
        copy = pltpu.make_async_copy(source, target, local_sems.at[len(local)])
        copy.start()
        local.append(copy)
        return copy

    keys_copy = local_copy(all_keyval.at[pl.ds(0, place.nz // 2)], keys)
    weight_copies = []
    for block in range(col_blocks):
        lead = (every,) * (len(query_weight.shape) - 1)
        weight_copies.append(
            local_copy(
                query_blocks.at[block_index(block, col_blocks, owned)],
                query_weight.at[lead + (pl.ds(block * col_block, col_block),)],
            )
        )
    normed_copy = local_copy(lat_normed_in, lat_normed)
    block_row = device * owned // col_blocks
    block_col = lax.rem(device * owned, col_blocks)
    half_devices = width // keyval_rows
    key_start = lax.rem(device, half_devices) * keyval_rows
    value_rows = pl.ds(pl.multiple_of(width + block_row * row_block, row_block), row_block)
    value_copy = local_copy(all_rows_keyval.at[value_rows], value_block)
    output_row = key_start // row_block
    if 2 * owned == col_blocks:
        across = lax.rem(output_row, place.nx)
        along = lax.rem(output_row // place.nx, place.ny)
        source = all_mats.at[output_row // (place.nx * place.ny), along, across, :, 0]
    else:
        source = all_mats.at[output_row // place.ny, lax.rem(output_row, place.ny), :, :, 0, 0]
    output_copy = local_copy(source, output_block)
    stat_copies = [
        local_copy(left_in, proj_left),
        local_copy(right_in, proj_right),
        local_copy(left_roots_in, left_roots),
        local_copy(right_roots_in, right_roots),
    ]
    key_cols = pl.ds(pl.multiple_of(key_start // 128 * 128, 128), 128)
    query_copy = local_copy(query_in.at[:, key_cols], query)
    mixed_out[...] = mixed_in[...]
    pixel_copies = [local_copy(pixel_low.at[i], pixel_came.at[i]) for i in range(batches)]
    pixel_sent = []

    def widen(image):
        pixel_copies[image].wait()

        @pl.loop(0, pixel_low.shape[2] // 256)
        def _(step):
            cols = pl.ds(pl.multiple_of(step * 256, 256), 256)
            pixel_wide[image, :, cols] = pixel_came[image, :, cols].astype(jnp.float32)

        pixel_sent.append(local_copy(pixel_wide.at[image], pixel_grad.at[:, image]))

    def moments(weight, grad, second, rate, second_out, weight_out):
        second_value = STAT_DECAY * second[...] + (1.0 - STAT_DECAY) * grad * grad
        second_out[...] = second_value
        weight_out[...] = weight[...] - rate * grad / (jnp.sqrt(second_value) + MOMENT_FLOOR)

    def precondition(mat, index, grad):
        low = grad.astype(BF)
        proj_grad[index, mat] = grad
        left_new[index, mat] = STAT_DECAY * proj_left[index, mat] + (
            1.0 - STAT_DECAY
        ) * lax.dot_general(low, low, NT, preferred_element_type=jnp.float32)
        right_new[index, mat] = STAT_DECAY * proj_right[index, mat] + (
            1.0 - STAT_DECAY
        ) * lax.dot_general(low, low, TN, preferred_element_type=jnp.float32)
        step = jnp.dot(
            left_roots[index, mat].astype(BF), low, preferred_element_type=jnp.float32
        ).astype(BF)
        step = jnp.dot(
            step, right_roots[index, mat].astype(BF), preferred_element_type=jnp.float32
        )
        proj_new[index, mat] = proj_blocks[index, mat] - MATRIX_RATE * step

    keys_copy.wait()
    scale = width ** (-0.5)
    query_sum = query_total[...].reshape(all_rows, lanes)
    key_t = keys[...].reshape(width, lanes)
    products = query_sum.astype(jnp.float32) * pixel_query[...].astype(jnp.float32)
    sums = jnp.sum(products, axis=0, keepdims=True)
    first = width // 128
    for sub in range(lanes // 128):
        cols = slice(sub * 128, (sub + 1) * 128)
        gain_grad[:, width + sub * 128 : width + (sub + 1) * 128] = (
            sums[:, cols] + gain_total[first + sub : first + sub + 1, :]
        ) / jnp.where(gain_rows[1:2, cols] > 0.0, gain_rows[1:2, cols], 1.0)
    for sub in range(first):
        at = width + lanes + sub * 128
        gain_grad[:, at : at + 128] = gain_total[sub : sub + 1, :]
    for start in range(0, width, 256):
        grad_query[:, start : start + 256] = (
            lax.dot_general(
                query_sum, key_t[start : start + 256], NT, preferred_element_type=jnp.float32
            )
            * scale
        ).astype(BF)
    widen(0)
    arrived_local(weight_copies)
    normed_copy.wait()
    row_tile = width // place.nz
    for index in range(place.nz):
        cols = slice(index * row_tile, (index + 1) * row_tile)
        part = lax.dot_general(
            grad_query[...],
            query_weight[index].reshape(row_tile, width),
            NT,
            preferred_element_type=jnp.float32,
        )
        grad_normed[:, cols] = part
        gain_grad[:, cols] = (
            jnp.sum(part * lat_normed[:, cols].astype(jnp.float32), axis=0, keepdims=True)
            / gain_rows[0:1, cols]
        )
    widen(1)
    arrived_local(stat_copies)
    for mat in range(2):
        for index in range(owned):
            precondition(mat + 2, index, mats_grad[mat, index])
    value_copy.wait()
    own_cols = pl.ds(pl.multiple_of(block_col * col_block, col_block), owned * col_block)
    output_grad = lax.dot_general(
        value_block[...], chan_grad[own_cols, :], NT, preferred_element_type=jnp.float32
    )
    for index in range(owned):
        precondition(1, index, output_grad[:, index * col_block : (index + 1) * col_block])
    widen(2)
    values = latents[...]
    centered = values - jnp.mean(values, axis=1, keepdims=True)
    inverse = lax.rsqrt(jnp.mean(centered * centered, axis=1, keepdims=True) + EPSILON)
    hat = centered * inverse
    own = pl.ds(pl.multiple_of(place.p * lat_rows, lat_rows), lat_rows)
    grad = grad_normed[own, :] * gain_rows[0:1, :]
    grad = (
        grad
        - jnp.mean(grad, axis=1, keepdims=True)
        - hat * jnp.mean(grad * hat, axis=1, keepdims=True)
    ) * inverse
    grad = residual_total[...] + grad
    latent_grad[...] = grad
    moments(latents, grad, latent_second, LATENT_RATE, latent_second_new, latent_new)

    per_lane = 128 // row_block
    rows = pl.ds(pl.multiple_of(block_row // per_lane * 128, 128), 128)
    cols = pl.ds(pl.multiple_of(block_col * col_block, col_block), owned * col_block)
    query_grad[...] = lax.dot_general(
        lat_normed[:, rows], grad_query[:, cols], TN, preferred_element_type=jnp.float32
    )
    part = pl.ds(pl.multiple_of(lax.rem(block_row, per_lane) * row_block, row_block), row_block)
    for index in range(owned):
        precondition(0, index, query_grad[part, index * col_block : (index + 1) * col_block])
    widen(3)

    query_copy.wait()
    key_rows[...] = (
        lax.dot_general(query[...], query_sum, TN, preferred_element_type=jnp.float32) * scale
    )
    part = pl.ds(pl.multiple_of(lax.rem(key_start, 128), keyval_rows), keyval_rows)
    grad = key_rows[part, :]
    output_copy.wait()
    blocks = output_block[...].reshape(col_blocks, row_block, col_block)
    key_rows[0:row_block, :] = sum(
        jnp.dot(
            blocks[block],
            chan_grad[block * col_block : (block + 1) * col_block, :],
            preferred_element_type=jnp.float32,
        )
        for block in range(col_blocks)
    )
    part = pl.ds(pl.multiple_of(lax.rem(key_start, row_block), keyval_rows), keyval_rows)
    grad = jnp.where(device < half_devices, grad, key_rows[part, :])[:, 0:channels]
    keyval_grad[...] = grad
    moments(keyval_weight, grad, keyval_second, KEYVAL_RATE, keyval_second_new, keyval_new)
    for copy in pixel_sent:
        copy.wait()


def tail(
    dims,
    query_total,
    residual_total,
    mats_grad,
    chan_grad,
    owned_arrays,
    gain_rows,
    query,
    lat_normed,
    query_blocks,
    all_keyval,
    pixel_low,
    pixel_query,
    gain_total,
    all_mats,
    mixed,
):
    nz, ny, nx = dims
    proj_blocks, keyval_weight, latents = owned_arrays[0], owned_arrays[5], owned_arrays[7]
    group, lat_rows, lanes = query_total.shape
    all_rows = group * lat_rows
    width = latents.shape[1]
    batches, channels, shard_pixels = pixel_low.shape
    owned, mats, row_block, col_block = proj_blocks.shape
    lead = (nz, ny, nx) if 2 * owned * col_block == width else (nz, ny)
    vmem = pl.BlockSpec(memory_space=pltpu.VMEM)
    anywhere = pl.BlockSpec(memory_space=pl.ANY)
    like = lambda array: jax.ShapeDtypeStruct(array.shape, array.dtype)
    wide = jax.ShapeDtypeStruct((channels, batches, shard_pixels), jnp.float32)
    results = [
        wide,
        like(proj_blocks),
        like(owned_arrays[1]),
        like(owned_arrays[2]),
        like(proj_blocks),
        like(keyval_weight),
        like(keyval_weight),
        like(keyval_weight),
        like(latents),
        like(latents),
        like(latents),
        jax.ShapeDtypeStruct((1, 2 * width + lanes), jnp.float32),
        like(mixed),
    ]
    return pl.pallas_call(
        functools.partial(tail_kernel, dims, channels),
        out_shape=results,
        in_specs=(
            [vmem] * 5
            + [anywhere] * 4
            + [vmem] * 5
            + [anywhere] * 5
            + [vmem] * 2
            + [anywhere] * 2
            + [vmem]
        ),
        out_specs=[anywhere] + [vmem] * 12,
        scratch_shapes=[
            pltpu.VMEM((all_rows, 128), BF),
            pltpu.VMEM((all_rows, width), BF),
            pltpu.VMEM(lead + (row_block, width), BF),
            pltpu.VMEM((nz // 2, ny, nx, 2) + all_keyval.shape[4:], BF),
            pltpu.VMEM((batches, channels, shard_pixels), BF),
            pltpu.VMEM((batches, channels, shard_pixels), jnp.float32),
            pltpu.VMEM((all_rows, width), BF),
            pltpu.VMEM((all_rows, width), jnp.float32),
            pltpu.VMEM((128, owned * col_block), jnp.float32),
            pltpu.VMEM((128, lanes), jnp.float32),
            pltpu.VMEM((row_block, lanes), BF),
            pltpu.VMEM((2, owned, row_block, col_block) if len(lead) == 3 else (nx, 2, row_block, col_block), BF),
            *[pltpu.VMEM(array.shape, jnp.float32) for array in owned_arrays[1:5]],
            pltpu.SemaphoreType.DMA((10 + width // col_block + 2 * batches,)),
        ],
        compiler_params=pltpu.CompilerParams(vmem_limit_bytes=56 * 2**20),
    )(
        query_total,
        residual_total,
        mats_grad,
        chan_grad.reshape(width, lanes),
        *owned_arrays,
        gain_rows,
        query,
        lat_normed,
        query_blocks,
        all_keyval,
        pixel_low,
        pixel_query,
        gain_total,
        all_keyval.reshape(2 * width, lanes),
        all_mats,
        mixed,
    )


def body(
    pixels,
    pixel_mask,
    proj_blocks,
    proj_left,
    proj_right,
    left_roots,
    right_roots,
    keyval_weight,
    keyval_second,
    latents,
    latent_second,
    gains,
    gain_second,
    mixed_grad,
):
    batches, channels, shard_pixels = pixels.shape
    lat_rows, width = latents.shape
    groups = lax.axis_size("pix")
    scale = width ** (-0.5)

    lat_gain = gains[:width]
    in_gain = gains[width : width + channels]
    mlp_gain = gains[width + channels :]
    side = math.isqrt(groups // 2)
    dims = (lax.axis_size("samp"), side, side)
    widen = lambda row: jnp.pad(row, (0, width - row.shape[0]))
    gain_rows = jnp.stack([lat_gain, widen(in_gain), mlp_gain])
    keyval_own = keyval_weight.T
    (
        query_blocks,
        keyval_t,
        lat_normed,
        mats,
        normed_all,
        inverse_all,
        weights_all,
        sent_all,
        landed,
        pixel_query,
        query,
    ) = front(
        dims, pixels.swapaxes(0, 1), pixel_mask, gain_rows, proj_blocks, keyval_own, latents
    )
    gathered = (
        landed,
        keyval_t,
        mats,
        normed_all,
        inverse_all,
        weights_all,
        sent_all,
        pixel_query,
    )
    mixed, pixel_low, mats_grad, chan_grad, query_total, gain_total, residual_total = back(
        dims, channels, gathered, latents, gain_rows, mixed_grad
    )
    (
        pixel_grad,
        proj_grad,
        left_new,
        right_new,
        proj_new,
        keyval_grad,
        keyval_second_new,
        keyval_new,
        latent_grad,
        latent_second_new,
        latent_new,
        gain_row,
        mixed,
    ) = tail(
        dims,
        query_total,
        residual_total,
        mats_grad,
        chan_grad,
        (
            proj_blocks,
            proj_left,
            proj_right,
            left_roots,
            right_roots,
            keyval_own,
            keyval_second.T,
            latents,
            latent_second,
        ),
        gain_rows,
        query,
        lat_normed,
        query_blocks,
        keyval_t,
        pixel_low,
        pixel_query,
        gain_total,
        mats,
        mixed,
    )
    lanes = ceil_to(ceil_to(channels + 2, 16), 128)
    gain_grad = jnp.concatenate(
        [gain_row[0, : width + channels], gain_row[0, width + lanes :]], axis=0
    )
    gain_second_new, gain_new = moment_step(gains, gain_grad, gain_second, GAIN_RATE)
    return (
        mixed.reshape(batches, lat_rows, width),
        pixel_grad.swapaxes(0, 1),
        proj_grad,
        left_new,
        right_new,
        proj_new,
        keyval_grad.T,
        keyval_second_new.T,
        keyval_new.T,
        latent_grad,
        latent_second_new,
        latent_new,
        gain_grad,
        gain_second_new,
        gain_new,
    )


def solution(mesh):
    blocks = P(("samp", "pix"), None, None, None)
    columns = P(None, ("samp", "pix"))
    rows = P("pix", None)
    return jax.shard_map(
        body,
        mesh=mesh,
        in_specs=(
            P("samp", None, "pix"),
            P("samp", "pix"),
            blocks,
            blocks,
            blocks,
            blocks,
            blocks,
            columns,
            columns,
            rows,
            rows,
            P(),
            P(),
            P("samp", "pix", None),
        ),
        out_specs=(
            P("samp", "pix", None),
            P("samp", None, "pix"),
            blocks,
            blocks,
            blocks,
            blocks,
            columns,
            columns,
            columns,
            rows,
            rows,
            rows,
            P(),
            P(),
            P(),
        ),
        check_vma=False,
    )
```
